32 devices in a mesh: groups: 2 (over x), dp: 8 (over z, y), tensor: 2 (over core).
Axes of the slice: x: 2, y: 2, z: 4, core: 2. Of those that a mesh axis runs over, the one named last changes fastest.
Arguments:
- hidden: bfloat16 [4096, 28672], P(('groups', 'dp'), 'tensor'), parts along dimension 0, may hold values from -6 to 6
- out_grad: bfloat16 [4096, 8192], P(('groups', 'dp'), 'tensor'), parts along dimension 0, may hold values from -6 to 6
- proj_in: bfloat16 [28672, 64], P('tensor'), may hold values from -0.03125 to 0.03125
- proj_out: bfloat16 [8192, 64], P('tensor'), may hold values from -0.0625 to 0.0625
- doc_ids: int32 [4096], P(('groups', 'dp')), parts along dimension 0, may hold values from 0 to 63, as said below
- queries: float32 [32, 4096], P(('groups', 'dp')), parts along dimension 0, may hold values from -6 to 6
Outputs:
- scores: float32 [32, 64], P('groups', 'dp'), parts along dimension 0
The draws below stay inside these ranges and needn't reach their ends.
There are 2 independent parts, one for each index of `groups`. The reference program is written for one: setup_inputs(seed, part) draws one part's arguments, and reference() takes and returns one part's arrays. A program takes and returns all parts, laid end to end along the dimension named above; an argument that names none is the same for every part. Nothing has to cross between parts.
Inputs may be any that keep to these rules, and one draw needn't show every extreme that they name: `doc_ids`: document ids never fall along the window and every id from 0 to 63 occurs; each document has 1 to 512 tokens, one exactly that many.
All inputs are finite; a program needn't handle non-finite values.
Results may differ from the reference program's by a relative error of at most 0.0003.
Values sent between devices are 32-bit elements; how exact they have to be, the bound alone decides.
No kernel may reach another device: no remote copies, remote signals or barrier semaphores. Data moves between devices by JAX's collectives and lax.ppermute only.
A program may use at most 64 MiB of HBM per device.

```python
import jax
import jax.numpy as jnp
from jax import lax

D = 8192
FF = 28672
R_IN = 64
R_OUT = 64
TOK_DEV = 256
TOKENS = 2048
NDOC = 64
NQ = 16


def draw_doc_ids(key, part):
    key = jax.random.fold_in(key, 11)
    least_long = 3 * TOKENS // (4 * TOK_DEV - 8) + 1
    single_docs = min(TOK_DEV, NDOC - 2 - least_long)
    long_docs = NDOC - single_docs - 2
    span = TOKENS - single_docs - 2 * TOK_DEV
    extra = span - 2 * long_docs
    key_weight, key_slot = jax.random.split(key)
    weights = jax.random.randint(key_weight, (long_docs,), 2, 4, dtype=jnp.int32)
    cumulative = jnp.cumsum(weights).astype(jnp.int32)
    total_weight = cumulative[long_docs - 1]
    counter = jnp.arange(1, long_docs + 1, dtype=jnp.int32)
    ends = 2 * counter + extra * cumulative // total_weight
    starts = jnp.concatenate([jnp.zeros((1,), jnp.int32), ends[:long_docs - 1]]).astype(jnp.int32)
    moved = jnp.logical_and(starts % TOK_DEV == 0, starts > 0)
    starts = jnp.where(moved, starts + 1, starts).astype(jnp.int32)
    marks = jnp.zeros((span,), jnp.int32).at[starts].set(1)
    slot = jax.random.randint(key_slot, (), 1, (span - 1) // TOK_DEV + 1, dtype=jnp.int32)
    place = slot * TOK_DEV
    positions = jnp.arange(TOKENS, dtype=jnp.int32)
    in_run = jnp.logical_and(positions >= place, positions < place + single_docs)
    longest_start = place + single_docs
    after_start = longest_start + 2 * TOK_DEV
    in_longest = jnp.logical_and(positions >= longest_start, positions < after_start)
    virtual = jnp.where(positions < place, positions, positions - single_docs - 2 * TOK_DEV)
    virtual = jnp.clip(virtual, 0, span - 1).astype(jnp.int32)
    from_marks = marks[virtual]
    starting = jnp.where(in_run, 1, jnp.where(in_longest, (positions == longest_start).astype(jnp.int32), from_marks))
    starting = jnp.maximum(starting, (positions == after_start).astype(jnp.int32))
    return (jnp.cumsum(starting) - 1).astype(jnp.int32)


def shard_levels(key, shape, cuts, low, high):
    level, own = 1.0, jax.random.fold_in(key, 6)
    for position, blocks in cuts:
        draws = jnp.exp(jax.random.uniform(jax.random.fold_in(own, position), (blocks,), jnp.float32, low / len(cuts), high / len(cuts)))
        level = level * jnp.repeat(draws, shape[position] // blocks).reshape([-1 if axis == position else 1 for axis in range(len(shape))])
    return level


def bell_draw(key, shape, deviation, most, pieces=(), kind=jnp.bfloat16):
    factor_of = shard_levels(key, shape, pieces, -0.22, 0.18) if pieces else 1.0
    entries = jax.random.normal(key, shape, jnp.float32) * deviation * factor_of
    return jnp.minimum(jnp.maximum(entries, -most), most).astype(kind)


def setup_inputs(seed: int = 0, part: int = 0) -> dict:
    arg_keys = jax.random.split(jax.random.key(seed), 7)
    part_keys = jax.random.split(jax.random.fold_in(arg_keys[6], part), 7)
    return {
        "hidden": bell_draw(part_keys[0], (TOKENS, FF), 1.0, 6.0, ((0, 8), (1, 2))),
        "out_grad": bell_draw(part_keys[1], (TOKENS, D), 1.0, 6.0, ((0, 8), (1, 2))),
        "proj_in": bell_draw(arg_keys[2], (FF, R_IN), FF ** -0.5, 0.03125, ((0, 2),)),
        "proj_out": bell_draw(arg_keys[3], (D, R_OUT), D ** -0.5, 0.0625, ((0, 2),)),
        "doc_ids": draw_doc_ids(jax.random.fold_in(jax.random.fold_in(arg_keys[6], part), 71), part),
        "queries": bell_draw(part_keys[5], (NQ, R_OUT * R_IN), 1.0, 6.0, ((0, 8),), jnp.float32),
    }


def reference(hidden, out_grad, proj_in, proj_out, doc_ids, queries):
    input_proj = jnp.dot(hidden.astype(jnp.float32), proj_in.astype(jnp.float32), preferred_element_type=jnp.float32)
    grad_proj = jnp.dot(out_grad.astype(jnp.float32), proj_out.astype(jnp.float32), preferred_element_type=jnp.float32)
    outer = (grad_proj[:, :, None] * input_proj[:, None, :]).reshape(grad_proj.shape[0], R_OUT * R_IN)
    member = (doc_ids[None, :] == jnp.arange(NDOC, dtype=jnp.int32)[:, None]).astype(jnp.float32)
    doc_grads = jnp.dot(member, outer, precision=lax.Precision.HIGHEST) / jnp.sqrt(jnp.float32(TOK_DEV))
    kernel = jnp.dot(doc_grads, doc_grads.T, precision=lax.Precision.HIGHEST)
    mean_diag = jnp.trace(kernel) / NDOC
    damping = 0.1 * mean_diag
    cross = jnp.dot(queries, doc_grads.T, precision=lax.Precision.HIGHEST)
    factor = jnp.linalg.cholesky(kernel + damping * jnp.eye(NDOC, dtype=jnp.float32))
    solved = jax.scipy.linalg.cho_solve((factor, True), cross.T).T
    return solved * (mean_diag / jnp.sqrt(jnp.float32(R_IN * R_OUT)))
```

```python
import functools

import jax
import jax.numpy as jnp
from jax import lax
from jax.experimental import pallas as pl
from jax.experimental.pallas import tpu as pltpu
from jax.sharding import PartitionSpec as P

TOK_DEV = 256
DOC_DEV = 8
LANES = 128
NT = (((1,), (1,)), ((), ()))
HIGHEST = lax.Precision.HIGHEST
VMEM = pl.BlockSpec(memory_space=pltpu.VMEM)
ANY = pl.BlockSpec(memory_space=pl.ANY)


def vmem_params(mib):
    return pltpu.CompilerParams(vmem_limit_bytes=mib << 20)


def chunks_of(length, most=1024):
    size = most
    while length % size:
        size //= 2
    return size, length // size


def project_kernel(sizes, h_ref, g_ref, pin_ref, pout_ref, keep_ref, send_ref, h_buf, g_buf, pin_buf, pout_buf, sems):
    h_size, h_count, g_size, g_count = sizes
    copies = {}
    slot = 0
    for name, src, dst in (("po", pout_ref, pout_buf), ("pi", pin_ref, pin_buf)):
        copies[name] = pltpu.make_async_copy(src, dst, sems.at[slot])
        slot += 1
    for i in range(g_count):
        at = pl.ds(i * g_size, g_size)
        copies["g", i] = pltpu.make_async_copy(g_ref.at[:, at], g_buf.at[:, at], sems.at[slot])
        slot += 1
    for i in range(h_count):
        at = pl.ds(i * h_size, h_size)
        copies["h", i] = pltpu.make_async_copy(h_ref.at[:, at], h_buf.at[:, at], sems.at[slot])
        slot += 1
    order = ["po"] + [("g", i) for i in range(g_count)] + ["pi"] + [("h", i) for i in range(h_count)]
    for name in order:
        copies[name].start()

    def run(tag, count, size, proj, data):
        total = None
        for i in range(count):
            copies[tag, i].wait()
            at = pl.ds(i * size, size)
            part = lax.dot_general(proj[:, at], data[:, at], NT, preferred_element_type=jnp.float32)
            total = part if total is None else total + part
        return total

    copies["po"].wait()
    grad = run("g", g_count, g_size, pout_buf, g_buf)
    copies["pi"].wait()
    inp = run("h", h_count, h_size, pin_buf, h_buf)
    both = jnp.concatenate([grad, inp], axis=0)
    half = both.shape[1] // 2
    first, second = both[:, :half], both[:, half:]
    lead = lax.axis_index("tensor") == 0
    keep_ref[...] = jnp.where(lead, first, second)
    send_ref[...] = jnp.where(lead, second, first)


def project(hidden, out_grad, pin_t, pout_t):
    tokens, units = hidden.shape
    width = out_grad.shape[1]
    ranks = pin_t.shape[0] + pout_t.shape[0]
    h_size, h_count = chunks_of(units)
    g_size, g_count = chunks_of(width)
    half = jax.ShapeDtypeStruct((ranks, tokens // 2), jnp.float32)
    return pl.pallas_call(
        functools.partial(project_kernel, (h_size, h_count, g_size, g_count)),
        out_shape=(half, half),
        in_specs=[ANY] * 4,
        out_specs=(VMEM, VMEM),
        scratch_shapes=[
            pltpu.VMEM(hidden.shape, hidden.dtype),
            pltpu.VMEM(out_grad.shape, out_grad.dtype),
            pltpu.VMEM(pin_t.shape, pin_t.dtype),
            pltpu.VMEM(pout_t.shape, pout_t.dtype),
            pltpu.SemaphoreType.DMA((2 + g_count + h_count,)),
        ],
        compiler_params=vmem_params(40),
        cost_estimate=pl.CostEstimate(
            flops=2 * tokens * 64 * (units + width),
            bytes_accessed=2 * (tokens + 64) * (units + width),
            transcendentals=0,
        ),
        name="project",
    )(hidden, out_grad, pin_t, pout_t)


def pack_kernel(pa, pb, keep_ref, recv_ref, extra_ref, out_ref):
    total = keep_ref[...] + recv_ref[...]
    ranks = total.shape[0] // 2
    rows_a, rows_b = ranks // pa, ranks // pb
    for s in range(pa * pb):
        p, q = s // pb, s % pb
        out_ref[s, 0:rows_a, :] = total[p * rows_a:(p + 1) * rows_a, :]
        out_ref[s, rows_a:rows_a + rows_b, :] = total[ranks + q * rows_b:ranks + (q + 1) * rows_b, :]
        out_ref[s, rows_a + rows_b:, :] = extra_ref[s]


def pack(keep, recv, extra, pa, pb):
    ranks = keep.shape[0] // 2
    rows = ranks // pa + ranks // pb + extra.shape[1]
    return pl.pallas_call(
        functools.partial(pack_kernel, pa, pb),
        out_shape=jax.ShapeDtypeStruct((pa * pb, rows, keep.shape[1]), jnp.float32),
        in_specs=[VMEM] * 3,
        out_specs=VMEM,
        compiler_params=vmem_params(16),
        name="pack",
    )(keep, recv, extra)


def gram_kernel(rows_a, rows_b, docs, copies, x_ref, out_ref, outer_ref, member_ref):
    n, _, lanes = x_ref.shape
    wide = rows_a * rows_b
    doc = lax.broadcasted_iota(jnp.int32, (docs, lanes), 0)

    def place(s):
        at = pl.ds(pl.multiple_of(s * lanes, lanes), lanes)
        g = x_ref[s, 0:rows_a, :]
        b = x_ref[s, rows_a:rows_a + rows_b, :]
        ids = x_ref[s, rows_a + rows_b:rows_a + rows_b + 1, :].astype(jnp.int32)
        member_ref[:, at] = jnp.where(doc == ids, 1.0, 0.0).astype(jnp.bfloat16)
        outer = (g[:, None, :] * b[None, :, :]).reshape(wide, lanes)
        high = outer.astype(jnp.bfloat16)
        rest = outer - high.astype(jnp.float32)
        mid = rest.astype(jnp.bfloat16)
        outer_ref[0:wide, at] = high
        outer_ref[wide:2 * wide, at] = mid
        outer_ref[2 * wide:, at] = (rest - mid.astype(jnp.float32)).astype(jnp.bfloat16)

    if n <= 16:
        for s in range(n):
            place(s)
    else:
        pl.loop(0, n)(place)
    sums = lax.dot_general(member_ref[...], outer_ref[...], NT, preferred_element_type=jnp.float32)
    grads = (sums[:, 2 * wide:] + sums[:, wide:2 * wide] + sums[:, :wide]) * (TOK_DEV ** -0.5)
    first = rows_a + rows_b + 1
    if wide >= lanes:
        queries = jnp.concatenate([x_ref[:, first + j, :] for j in range(wide // lanes)], axis=1)
    else:
        queries = x_ref[:, first, :][:, :wide]
    both = jnp.concatenate([grads, queries], axis=0)
    share = lax.dot_general(grads, both, NT, precision=HIGHEST, preferred_element_type=jnp.float32)
    for s in range(copies):
        out_ref[s, :, 0:docs + n] = share
        if out_ref.shape[2] > docs + n:
            out_ref[s, :, docs + n:] = jnp.zeros((docs, out_ref.shape[2] - docs - n), jnp.float32)


def gram(x, rows_a, rows_b, docs, copies):
    n, _, lanes = x.shape
    wide = rows_a * rows_b
    cols = -(-(docs + n) // LANES) * LANES
    return pl.pallas_call(
        functools.partial(gram_kernel, rows_a, rows_b, docs, copies),
        out_shape=jax.ShapeDtypeStruct((copies, docs, cols), jnp.float32),
        in_specs=[VMEM],
        out_specs=VMEM,
        scratch_shapes=[
            pltpu.VMEM((3 * wide, n * lanes), jnp.bfloat16),
            pltpu.VMEM((docs, n * lanes), jnp.bfloat16),
        ],
        compiler_params=vmem_params(40),
        name="gram",
    )(x)


def solve_kernel(docs, queries, scale, x_ref, out_ref, done_ref):
    total = x_ref[0]
    for s in range(1, x_ref.shape[0]):
        total = total + x_ref[s]
    rows, cols = total.shape
    row = lax.broadcasted_iota(jnp.int32, (rows, cols), 0)
    col = lax.broadcasted_iota(jnp.int32, (rows, cols), 1)
    mean_diag = jnp.sum(jnp.where(row == col, total, 0.0)) * (1.0 / docs)
    work = total + jnp.where(row == col, 0.1 * mean_diag, 0.0)
    here = lax.broadcasted_iota(jnp.int32, (rows, 1), 0)
    for k in range(docs):
        line = work[k:k + 1, :]
        inverse = 1.0 / line[:, k:k + 1]
        factor = jnp.where(here == k, 1.0 - inverse, work[:, k:k + 1] * inverse)
        work = work - factor * line
    done_ref[...] = work * (mean_diag * scale)
    mine = pl.ds(pl.multiple_of(lax.axis_index("dp") * DOC_DEV, DOC_DEV), DOC_DEV)
    out_ref[...] = done_ref[mine, :][:, docs:docs + queries]


def solve(x, docs, queries, scale):
    return pl.pallas_call(
        functools.partial(solve_kernel, docs, queries, scale),
        out_shape=jax.ShapeDtypeStruct((DOC_DEV, queries), jnp.float32),
        in_specs=[VMEM],
        out_specs=VMEM,
        scratch_shapes=[pltpu.VMEM(x.shape[1:], jnp.float32)],
        compiler_params=vmem_params(16),
        name="solve",
    )(x)


def solve_large(total, docs, queries, scale):
    kernel = total[:, :docs]
    mean_diag = jnp.trace(kernel) / docs
    factor = jnp.linalg.cholesky(kernel + 0.1 * mean_diag * jnp.eye(docs, dtype=jnp.float32))
    solved = jax.scipy.linalg.cho_solve((factor, True), total[:, docs:docs + queries]) * (mean_diag * scale)
    return lax.dynamic_slice_in_dim(solved, lax.axis_index("dp") * DOC_DEV, DOC_DEV, 0)


def local(hidden, out_grad, proj_in, proj_out, doc_ids, queries):
    dp, tensor = lax.axis_size("dp"), lax.axis_size("tensor")
    n = dp * tensor
    docs = DOC_DEV * dp
    ranks = proj_in.shape[1]
    pa = 1
    while pa * pa < n:
        pa *= 2
    pb = n // pa
    rows_a, rows_b = ranks // pa, ranks // pb
    wide = rows_a * rows_b
    core = lax.axis_index("tensor")
    all_axes = ("dp", "tensor")

    keep, send = project(hidden, out_grad, proj_in.T, proj_out.T)
    recv = lax.ppermute(send, "tensor", [(i, tensor - 1 - i) for i in range(tensor)])

    lanes = keep.shape[1]
    ids = lax.dynamic_slice_in_dim(doc_ids, core * lanes, lanes).astype(jnp.float32)
    query = lax.dynamic_slice_in_dim(queries, core, 1, 0).reshape(pa, rows_a, pb, rows_b)
    query = query.transpose(0, 2, 1, 3).reshape(n, wide)
    q_rows = -(-wide // lanes)
    query = jnp.pad(query, ((0, 0), (0, q_rows * lanes - wide))).reshape(n, q_rows, lanes)
    extra = jnp.concatenate([jnp.broadcast_to(ids, (n, 1, lanes)), query], axis=1)
    extra = jnp.pad(extra, ((0, 0), (0, -(1 + q_rows) % 8), (0, 0)))

    block = pack(keep, recv, extra, pa, pb)
    block = lax.all_to_all(block, all_axes, 0, 0, tiled=True)
    scale = float(ranks * ranks) ** -0.5
    if docs <= 64:
        share = gram(block, rows_a, rows_b, docs, n)
        share = lax.all_to_all(share, all_axes, 0, 0, tiled=True)
        return solve(share, docs, n, scale).T
    share = gram(block, rows_a, rows_b, docs, 1)[0]
    return solve_large(lax.psum(share, all_axes), docs, n, scale).T


def solution(mesh):
    return jax.shard_map(
        local,
        mesh=mesh,
        in_specs=(
            P(("groups", "dp"), "tensor"),
            P(("groups", "dp"), "tensor"),
            P("tensor", None),
            P("tensor", None),
            P(("groups", "dp")),
            P(("groups", "dp"), None),
        ),
        out_specs=P("groups", "dp"),
        check_vma=False,
    )
```

```python
import functools

import jax
import jax.numpy as jnp
from jax import lax
from jax.experimental import pallas as pl
from jax.experimental.pallas import tpu as pltpu
from jax.sharding import PartitionSpec as P

TOK_DEV = 256
DOC_DEV = 8
LANES = 128
NT = (((1,), (1,)), ((), ()))
HIGHEST = lax.Precision.HIGHEST
VMEM = pl.BlockSpec(memory_space=pltpu.VMEM)
HBM = pl.BlockSpec(memory_space=pltpu.HBM)


def vmem_params(mib):
    return pltpu.CompilerParams(vmem_limit_bytes=mib << 20)


def chunks_of(length, most=1024):
    size = most
    while length % size:
        size //= 2
    return size, length // size


def project_kernel(sizes, h_ref, g_ref, pin_ref, pout_ref, keep_ref, send_ref, h_buf, g_buf, pin_buf, pout_buf, sems):
    h_size, h_count, g_size, g_count = sizes
    copies = {}
    slot = 0
    for name, src, dst in (("po", pout_ref, pout_buf), ("pi", pin_ref, pin_buf)):
        copies[name] = pltpu.make_async_copy(src, dst, sems.at[slot])
        slot += 1
    for i in range(g_count):
        at = pl.ds(i * g_size, g_size)
        copies["g", i] = pltpu.make_async_copy(g_ref.at[:, at], g_buf.at[:, at], sems.at[slot])
        slot += 1
    for i in range(h_count):
        at = pl.ds(i * h_size, h_size)
        copies["h", i] = pltpu.make_async_copy(h_ref.at[:, at], h_buf.at[:, at], sems.at[slot])
        slot += 1
    order = ["po"] + [("g", i) for i in range(g_count)] + ["pi"] + [("h", i) for i in range(h_count)]
    for name in order:
        copies[name].start()

    def run(tag, count, size, proj, data):
        total = None
        for i in range(count):
            copies[tag, i].wait()
            at = pl.ds(i * size, size)
            part = lax.dot_general(proj[:, at], data[:, at], NT, preferred_element_type=jnp.float32)
            total = part if total is None else total + part
        return total

    copies["po"].wait()
    grad = run("g", g_count, g_size, pout_buf, g_buf)
    copies["pi"].wait()
    inp = run("h", h_count, h_size, pin_buf, h_buf)
    both = jnp.concatenate([grad, inp], axis=0)
    half = both.shape[1] // 2
    first, second = both[:, :half], both[:, half:]
    lead = lax.axis_index("tensor") == 0
    keep_ref[...] = jnp.where(lead, first, second)
    send_ref[...] = jnp.where(lead, second, first)


def project(hidden, out_grad, pin_t, pout_t):
    tokens, units = hidden.shape
    width = out_grad.shape[1]
    ranks = pin_t.shape[0] + pout_t.shape[0]
    h_size, h_count = chunks_of(units)
    g_size, g_count = chunks_of(width)
    half = jax.ShapeDtypeStruct((ranks, tokens // 2), jnp.float32)
    return pl.pallas_call(
        functools.partial(project_kernel, (h_size, h_count, g_size, g_count)),
        out_shape=(half, half),
        in_specs=[HBM] * 4,
        out_specs=(VMEM, VMEM),
        scratch_shapes=[
            pltpu.VMEM(hidden.shape, hidden.dtype),
            pltpu.VMEM(out_grad.shape, out_grad.dtype),
            pltpu.VMEM(pin_t.shape, pin_t.dtype),
            pltpu.VMEM(pout_t.shape, pout_t.dtype),
            pltpu.SemaphoreType.DMA((2 + g_count + h_count,)),
        ],
        compiler_params=vmem_params(56),
        cost_estimate=pl.CostEstimate(
            flops=2 * tokens * 64 * (units + width),
            bytes_accessed=2 * (tokens + 64) * (units + width),
            transcendentals=0,
        ),
        name="project",
    )(hidden, out_grad, pin_t, pout_t)


def pack_kernel(pa, pb, keep_ref, recv_ref, extra_ref, *refs):
    outs, total_ref = refs[:-1], refs[-1]
    total_ref[...] = keep_ref[...] + recv_ref[...]
    ranks = total_ref.shape[0] // 2
    rows_a, rows_b = ranks // pa, ranks // pb
    me = lax.axis_index("dp")
    for m, out_ref in enumerate(outs):
        owner = me ^ m
        p, q = owner // pb, owner % pb
        out_ref[0:rows_a, :] = total_ref[pl.ds(pl.multiple_of(p * rows_a, rows_a), rows_a), :]
        out_ref[rows_a:rows_a + rows_b, :] = total_ref[pl.ds(pl.multiple_of(ranks + q * rows_b, rows_b), rows_b), :]
        out_ref[rows_a + rows_b:, :] = extra_ref[owner]


def pack(keep, recv, extra, pa, pb):
    ranks = keep.shape[0] // 2
    rows = ranks // pa + ranks // pb + extra.shape[1]
    out = jax.ShapeDtypeStruct((rows, keep.shape[1]), jnp.float32)
    return pl.pallas_call(
        functools.partial(pack_kernel, pa, pb),
        out_shape=(out,) * (pa * pb),
        in_specs=[VMEM] * 3,
        out_specs=(VMEM,) * (pa * pb),
        scratch_shapes=[pltpu.VMEM(keep.shape, jnp.float32)],
        compiler_params=vmem_params(16),
        name="pack",
    )(keep, recv, extra)


def grads_kernel(rows_a, rows_b, docs, *refs):
    xs, (keep_ref, send_ref, outer_ref, member_ref) = refs[:-4], refs[-4:]
    lanes = xs[0].shape[1]
    wide = rows_a * rows_b
    doc = lax.broadcasted_iota(jnp.int32, (docs, lanes), 0)
    source = lax.broadcasted_iota(jnp.int32, (len(xs), lanes), 0)
    queries = [jnp.zeros((len(xs), lanes), jnp.float32)] * (wide // lanes)
    first = rows_a + rows_b
    me = lax.axis_index("dp")
    for m, x_ref in enumerate(xs):
        at = slice(m * lanes, (m + 1) * lanes)
        g, b = x_ref[0:rows_a, :], x_ref[rows_a:first, :]
        ids = x_ref[first:first + 1, :].astype(jnp.int32)
        member_ref[:, at] = jnp.where(doc == ids, 1.0, 0.0).astype(jnp.bfloat16)
        outer = (g[:, None, :] * b[None, :, :]).reshape(wide, lanes)
        high = outer.astype(jnp.bfloat16)
        outer_ref[0:wide, at] = high
        outer_ref[wide:, at] = (outer - high.astype(jnp.float32)).astype(jnp.bfloat16)
        for j in range(wide // lanes):
            line = x_ref[first + 1 + j:first + 2 + j, :]
            queries[j] = jnp.where(source == (me ^ m), line, queries[j])
    sums = lax.dot_general(member_ref[...], outer_ref[...], NT, preferred_element_type=jnp.float32)
    grads = (sums[:, wide:] + sums[:, :wide]) * (TOK_DEV ** -0.5)
    lead = lax.axis_index("tensor") == 0
    half = wide // 2
    for part, at in ((grads, slice(0, docs)), (jnp.concatenate(queries, axis=1), slice(docs, docs + len(xs)))):
        keep_ref[at, :] = jnp.where(lead, part[:, :half], part[:, half:])
        send_ref[at, :] = jnp.where(lead, part[:, half:], part[:, :half])


def grads_of(xs, rows_a, rows_b, docs):
    lanes = xs[0].shape[1]
    wide = rows_a * rows_b
    out = jax.ShapeDtypeStruct((docs + len(xs), wide // 2), jnp.float32)
    return pl.pallas_call(
        functools.partial(grads_kernel, rows_a, rows_b, docs),
        out_shape=(out, out),
        in_specs=[VMEM] * len(xs),
        out_specs=(VMEM, VMEM),
        scratch_shapes=[
            pltpu.VMEM((2 * wide, len(xs) * lanes), jnp.bfloat16),
            pltpu.VMEM((docs, len(xs) * lanes), jnp.bfloat16),
        ],
        compiler_params=vmem_params(40),
        name="grads",
    )(*xs)


def gram_kernel(docs, keep_ref, recv_ref, out_ref):
    pairs = keep_ref.shape[0] - docs
    grads = keep_ref[0:docs, :] + recv_ref[0:docs, :]
    lead = lax.axis_index("tensor") == 0
    mine, other = keep_ref[docs:, :], recv_ref[docs:, :]
    even, odd = jnp.where(lead, mine, other), jnp.where(lead, other, mine)
    lines = [x[i:i + 1, :] for i in range(pairs) for x in (even, odd)]
    both = jnp.concatenate([grads] + lines, axis=0)
    share = lax.dot_general(both, grads, NT, precision=HIGHEST, preferred_element_type=jnp.float32)
    half = share.shape[0] // 2
    out_ref[...] = jnp.concatenate([share[:half], share[half:]], axis=1)


def gram(keep, recv, docs):
    rows = docs + 2 * (keep.shape[0] - docs)
    return pl.pallas_call(
        functools.partial(gram_kernel, docs),
        out_shape=jax.ShapeDtypeStruct((rows // 2, 2 * docs), jnp.float32),
        in_specs=[VMEM] * 2,
        out_specs=VMEM,
        compiler_params=vmem_params(16),
        name="gram",
    )(keep, recv)


def solve_kernel(docs, queries, scale, *refs):
    xs, out_ref, done_ref = refs[:-2], refs[-2], refs[-1]
    total = xs[0][...]
    for x_ref in xs[1:]:
        total = total + x_ref[...]
    stack = jnp.concatenate([total[:, :docs], total[:, docs:]], axis=0)
    cols = done_ref.shape[1]
    stack = jnp.concatenate([stack, jnp.zeros((cols - stack.shape[0], docs), jnp.float32)], axis=0)
    total = stack.T
    rows = docs
    row = lax.broadcasted_iota(jnp.int32, (rows, cols), 0)
    col = lax.broadcasted_iota(jnp.int32, (rows, cols), 1)
    mean_diag = jnp.sum(jnp.where(row == col, total, 0.0)) * (1.0 / docs)
    work = total + jnp.where(row == col, 0.1 * mean_diag, 0.0)
    here = lax.broadcasted_iota(jnp.int32, (rows, 1), 0)
    for k in range(docs):
        line = work[k:k + 1, :]
        inverse = 1.0 / line[:, k:k + 1]
        factor = jnp.where(here == k, 1.0 - inverse, work[:, k:k + 1] * inverse)
        work = work - factor * line
    done_ref[...] = work * (mean_diag * scale)
    mine = pl.ds(pl.multiple_of(lax.axis_index("dp") * DOC_DEV, DOC_DEV), DOC_DEV)
    out_ref[...] = done_ref[mine, :][:, docs:docs + queries]


def solve(xs, docs, queries, scale):
    return pl.pallas_call(
        functools.partial(solve_kernel, docs, queries, scale),
        out_shape=jax.ShapeDtypeStruct((DOC_DEV, queries), jnp.float32),
        in_specs=[VMEM] * len(xs),
        out_specs=VMEM,
        scratch_shapes=[pltpu.VMEM((docs, -(-(docs + queries) // LANES) * LANES), jnp.float32)],
        compiler_params=vmem_params(16),
        name="solve",
    )(*xs)


def solve_large(total, docs, queries, scale):
    kernel = total[:, :docs]
    mean_diag = jnp.trace(kernel) / docs
    factor = jnp.linalg.cholesky(kernel + 0.1 * mean_diag * jnp.eye(docs, dtype=jnp.float32))
    solved = jax.scipy.linalg.cho_solve((factor, True), total[:, docs:docs + queries]) * (mean_diag * scale)
    return lax.dynamic_slice_in_dim(solved, lax.axis_index("dp") * DOC_DEV, DOC_DEV, 0)


def swap_cores(x):
    cores = lax.axis_size("tensor")
    return lax.ppermute(x, "tensor", [(i, cores - 1 - i) for i in range(cores)])


def trade(xs):
    dp = lax.axis_size("dp")
    return [xs[0]] + [lax.ppermute(xs[m], "dp", [(i, i ^ m) for i in range(dp)]) for m in range(1, dp)]


def local(hidden, out_grad, proj_in, proj_out, doc_ids, queries):
    dp, tensor = lax.axis_size("dp"), lax.axis_size("tensor")
    docs, num_queries = DOC_DEV * dp, queries.shape[0] * dp
    ranks = proj_in.shape[1]
    pa = 1
    while pa * pa < dp:
        pa *= 2
    pb = dp // pa
    rows_a, rows_b = ranks // pa, ranks // pb
    wide = rows_a * rows_b
    core = lax.axis_index("tensor")

    keep, send = project(hidden, out_grad, proj_in.T, proj_out.T)
    recv = swap_cores(send)

    lanes = keep.shape[1]
    ids = lax.dynamic_slice_in_dim(doc_ids, core * lanes, lanes).astype(jnp.float32)
    query = lax.dynamic_slice_in_dim(queries, core, 1, 0).reshape(pa, rows_a, pb, rows_b)
    query = query.transpose(0, 2, 1, 3).reshape(dp, wide // lanes, lanes)
    extra = jnp.concatenate([jnp.broadcast_to(ids, (dp, 1, lanes)), query], axis=1)
    extra = jnp.pad(extra, ((0, 0), (0, -extra.shape[1] % 8), (0, 0)))

    blocks = trade(pack(keep, recv, extra, pa, pb))
    keep, send = grads_of(blocks, rows_a, rows_b, docs)
    share = gram(keep, swap_cores(send), docs)
    scale = float(ranks * ranks) ** -0.5
    if docs <= 64:
        share = share + swap_cores(share)
        return solve(trade([share] * dp), docs, num_queries, scale).T
    share = lax.psum(share, ("dp", "tensor"))
    return solve_large(jnp.concatenate([share[:, :docs], share[:, docs:]], axis=0).T, docs, num_queries, scale).T


def solution(mesh):
    return jax.shard_map(
        local,
        mesh=mesh,
        in_specs=(
            P(("groups", "dp"), "tensor"),
            P(("groups", "dp"), "tensor"),
            P("tensor", None),
            P("tensor", None),
            P(("groups", "dp")),
            P(("groups", "dp"), None),
        ),
        out_specs=P("groups", "dp"),
        check_vma=False,
    )
```

```python
import functools

import jax
import jax.numpy as jnp
from jax import lax
from jax.experimental import pallas as pl
from jax.experimental.pallas import tpu as pltpu
from jax.sharding import PartitionSpec as P

TOK_DEV = 256
DOC_DEV = 8
LANES = 128
NT = (((1,), (1,)), ((), ()))
HIGHEST = lax.Precision.HIGHEST
VMEM = pl.BlockSpec(memory_space=pltpu.VMEM)
HBM = pl.BlockSpec(memory_space=pltpu.HBM)


def vmem_params(mib):
    return pltpu.CompilerParams(vmem_limit_bytes=mib << 20)


def chunks_of(length, most=1024):
    size = most
    while length % size:
        size //= 2
    return size, length // size


def project_kernel(sizes, h_ref, g_ref, pin_ref, pout_ref, keep_ref, send_ref, h_buf, g_buf, pin_buf, pout_buf, sems):
    h_size, h_count, g_size, g_count = sizes
    copies = {}
    slot = 0
    for name, src, dst in (("po", pout_ref, pout_buf), ("pi", pin_ref, pin_buf)):
        copies[name] = pltpu.make_async_copy(src, dst, sems.at[slot])
        slot += 1
    for i in range(g_count):
        at = pl.ds(i * g_size, g_size)
        copies["g", i] = pltpu.make_async_copy(g_ref.at[:, at], g_buf.at[:, at], sems.at[slot])
        slot += 1
    for i in range(h_count):
        at = pl.ds(i * h_size, h_size)
        copies["h", i] = pltpu.make_async_copy(h_ref.at[:, at], h_buf.at[:, at], sems.at[slot])
        slot += 1
    order = ["po"] + [("g", i) for i in range(g_count)] + ["pi"] + [("h", i) for i in range(h_count)]
    for name in order:
        copies[name].start()

    def run(tag, count, size, proj, data):
        total = None
        for i in range(count):
            copies[tag, i].wait()
            at = pl.ds(i * size, size)
            part = lax.dot_general(data[:, at], proj[:, at], NT, preferred_element_type=jnp.float32)
            total = part if total is None else total + part
        return total

    copies["po"].wait()
    grad = run("g", g_count, g_size, pout_buf, g_buf)
    copies["pi"].wait()
    inp = run("h", h_count, h_size, pin_buf, h_buf)
    both = jnp.concatenate([grad, inp], axis=1).T
    half = both.shape[1] // 2
    first, second = both[:, :half], both[:, half:]
    lead = lax.axis_index("tensor") == 0
    keep_ref[...] = jnp.where(lead, first, second)
    send_ref[...] = jnp.where(lead, second, first)


def project(hidden, out_grad, pin_t, pout_t):
    tokens, units = hidden.shape
    width = out_grad.shape[1]
    ranks = pin_t.shape[0] + pout_t.shape[0]
    h_size, h_count = chunks_of(units)
    g_size, g_count = chunks_of(width)
    half = jax.ShapeDtypeStruct((ranks, tokens // 2), jnp.float32)
    return pl.pallas_call(
        functools.partial(project_kernel, (h_size, h_count, g_size, g_count)),
        out_shape=(half, half),
        in_specs=[HBM] * 4,
        out_specs=(VMEM, VMEM),
        scratch_shapes=[
            pltpu.VMEM(hidden.shape, hidden.dtype),
            pltpu.VMEM(out_grad.shape, out_grad.dtype),
            pltpu.VMEM(pin_t.shape, pin_t.dtype),
            pltpu.VMEM(pout_t.shape, pout_t.dtype),
            pltpu.SemaphoreType.DMA((2 + g_count + h_count,)),
        ],
        compiler_params=vmem_params(56),
        cost_estimate=pl.CostEstimate(
            flops=2 * tokens * 64 * (units + width),
            bytes_accessed=2 * (tokens + 64) * (units + width),
            transcendentals=0,
        ),
        name="project",
    )(hidden, out_grad, pin_t, pout_t)


def pack_kernel(pb, rows_a, rows_b, keep_ref, recv_ref, extra_ref, out_ref):
    total = keep_ref[...] + recv_ref[...]
    ranks = total.shape[0] // 2
    for owner in range(out_ref.shape[0]):
        p, q = owner // pb, owner % pb
        out_ref[owner, 0:rows_a, :] = total[p * rows_a:(p + 1) * rows_a, :]
        out_ref[owner, rows_a:rows_a + rows_b, :] = total[ranks + q * rows_b:ranks + (q + 1) * rows_b, :]
        out_ref[owner, rows_a + rows_b:, :] = extra_ref[owner]


def pack(keep, recv, extra, pa, pb):
    ranks = keep.shape[0] // 2
    rows_a, rows_b = ranks // pa, ranks // pb
    rows = rows_a + rows_b + extra.shape[1]
    return pl.pallas_call(
        functools.partial(pack_kernel, pb, rows_a, rows_b),
        out_shape=jax.ShapeDtypeStruct((pa * pb, rows, keep.shape[1]), jnp.float32),
        in_specs=[VMEM] * 3,
        out_specs=VMEM,
        compiler_params=vmem_params(16),
        name="pack",
    )(keep, recv, extra)


def grads_kernel(rows_a, rows_b, docs, x_ref, keep_ref, send_ref, outer_ref, member_ref):
    sources, _, lanes = x_ref.shape
    wide = rows_a * rows_b
    doc = lax.broadcasted_iota(jnp.int32, (docs, lanes), 0)
    first = rows_a + rows_b
    for s in range(sources):
        at = slice(s * lanes, (s + 1) * lanes)
        g, b = x_ref[s, 0:rows_a, :], x_ref[s, rows_a:first, :]
        ids = x_ref[s, first:first + 1, :].astype(jnp.int32)
        member_ref[:, at] = jnp.where(doc == ids, 1.0, 0.0).astype(jnp.bfloat16)
        outer = (g[:, None, :] * b[None, :, :]).reshape(wide, lanes)
        high = outer.astype(jnp.bfloat16)
        outer_ref[0:wide, at] = high
        outer_ref[wide:, at] = (outer - high.astype(jnp.float32)).astype(jnp.bfloat16)
    queries = [x_ref[:, first + 1 + j, :] for j in range(wide // lanes)]
    sums = lax.dot_general(member_ref[...], outer_ref[...], NT, preferred_element_type=jnp.float32)
    grads = (sums[:, wide:] + sums[:, :wide]) * (TOK_DEV ** -0.5)
    lead = lax.axis_index("tensor") == 0
    half = wide // 2
    for part, at in ((grads, slice(0, docs)), (jnp.concatenate(queries, axis=1), slice(docs, docs + sources))):
        keep_ref[at, :] = jnp.where(lead, part[:, :half], part[:, half:])
        send_ref[at, :] = jnp.where(lead, part[:, half:], part[:, :half])


def grads_of(x, rows_a, rows_b, docs):
    sources, _, lanes = x.shape
    wide = rows_a * rows_b
    out = jax.ShapeDtypeStruct((docs + sources, wide // 2), jnp.float32)
    return pl.pallas_call(
        functools.partial(grads_kernel, rows_a, rows_b, docs),
        out_shape=(out, out),
        in_specs=[VMEM],
        out_specs=(VMEM, VMEM),
        scratch_shapes=[
            pltpu.VMEM((2 * wide, sources * lanes), jnp.bfloat16),
            pltpu.VMEM((docs, sources * lanes), jnp.bfloat16),
        ],
        compiler_params=vmem_params(40),
        name="grads",
    )(x)


def gram_kernel(docs, keep_ref, recv_ref, out_ref):
    pairs = keep_ref.shape[0] - docs
    grads = keep_ref[0:docs, :] + recv_ref[0:docs, :]
    lead = lax.axis_index("tensor") == 0
    mine, other = keep_ref[docs:, :], recv_ref[docs:, :]
    even, odd = jnp.where(lead, mine, other), jnp.where(lead, other, mine)
    lines = [x[i:i + 1, :] for i in range(pairs) for x in (even, odd)]
    both = jnp.concatenate([grads] + lines, axis=0)
    share = lax.dot_general(both, grads, NT, precision=HIGHEST, preferred_element_type=jnp.float32)
    half = share.shape[0] // 2
    out_ref[...] = jnp.concatenate([share[:half], share[half:]], axis=1)


def gram(keep, recv, docs):
    rows = docs + 2 * (keep.shape[0] - docs)
    return pl.pallas_call(
        functools.partial(gram_kernel, docs),
        out_shape=jax.ShapeDtypeStruct((rows // 2, 2 * docs), jnp.float32),
        in_specs=[VMEM] * 2,
        out_specs=VMEM,
        compiler_params=vmem_params(16),
        name="gram",
    )(keep, recv)


def solve_kernel(docs, queries, scale, x_ref, recv_ref, out_ref, done_ref):
    total = x_ref[...] + recv_ref[...]
    stack = jnp.concatenate([total[:, :docs], total[:, docs:]], axis=0)
    cols = done_ref.shape[1]
    stack = jnp.concatenate([stack, jnp.zeros((cols - stack.shape[0], docs), jnp.float32)], axis=0)
    total = stack.T
    rows = docs
    row = lax.broadcasted_iota(jnp.int32, (rows, cols), 0)
    col = lax.broadcasted_iota(jnp.int32, (rows, cols), 1)
    mean_diag = jnp.sum(jnp.where(row == col, total, 0.0)) * (1.0 / docs)
    work = total + jnp.where(row == col, 0.1 * mean_diag, 0.0)
    here = lax.broadcasted_iota(jnp.int32, (rows, 1), 0)
    for k in range(docs):
        line = work[k:k + 1, :]
        inverse = 1.0 / line[:, k:k + 1]
        factor = jnp.where(here == k, 1.0 - inverse, work[:, k:k + 1] * inverse)
        work = work - factor * line
    done_ref[...] = work * (mean_diag * scale)
    mine = pl.ds(pl.multiple_of(lax.axis_index("dp") * DOC_DEV, DOC_DEV), DOC_DEV)
    out_ref[...] = done_ref[mine, :][:, docs:docs + queries]


def solve(x, recv, docs, queries, scale):
    return pl.pallas_call(
        functools.partial(solve_kernel, docs, queries, scale),
        out_shape=jax.ShapeDtypeStruct((DOC_DEV, queries), jnp.float32),
        in_specs=[VMEM] * 2,
        out_specs=VMEM,
        scratch_shapes=[pltpu.VMEM((docs, -(-(docs + queries) // LANES) * LANES), jnp.float32)],
        compiler_params=vmem_params(16),
        name="solve",
    )(x, recv)


def solve_large(total, docs, queries, scale):
    kernel = total[:, :docs]
    mean_diag = jnp.trace(kernel) / docs
    factor = jnp.linalg.cholesky(kernel + 0.1 * mean_diag * jnp.eye(docs, dtype=jnp.float32))
    solved = jax.scipy.linalg.cho_solve((factor, True), total[:, docs:docs + queries]) * (mean_diag * scale)
    return lax.dynamic_slice_in_dim(solved, lax.axis_index("dp") * DOC_DEV, DOC_DEV, 0)


def swap_cores(x):
    cores = lax.axis_size("tensor")
    return lax.ppermute(x, "tensor", [(i, cores - 1 - i) for i in range(cores)])


def swap_dp(x, m):
    return lax.ppermute(x, "dp", [(i, i ^ m) for i in range(lax.axis_size("dp"))])


def local(hidden, out_grad, proj_in, proj_out, doc_ids, queries):
    dp, tensor = lax.axis_size("dp"), lax.axis_size("tensor")
    docs, num_queries = DOC_DEV * dp, queries.shape[0] * dp
    ranks = proj_in.shape[1]
    pa = 1
    while pa * pa < dp:
        pa *= 2
    pb = dp // pa
    rows_a, rows_b = ranks // pa, ranks // pb
    wide = rows_a * rows_b
    core = lax.axis_index("tensor")

    keep, send = project(hidden, out_grad, proj_in.T, proj_out.T)
    recv = swap_cores(send)

    lanes = keep.shape[1]
    ids = lax.dynamic_slice_in_dim(doc_ids, core * lanes, lanes).astype(jnp.float32)
    query = lax.dynamic_slice_in_dim(queries, core, 1, 0).reshape(pa, rows_a, pb, rows_b)
    query = query.transpose(0, 2, 1, 3).reshape(dp, wide // lanes, lanes)
    extra = jnp.concatenate([jnp.broadcast_to(ids, (dp, 1, lanes)), query], axis=1)
    extra = jnp.pad(extra, ((0, 0), (0, -extra.shape[1] % 8), (0, 0)))

    blocks = lax.all_to_all(pack(keep, recv, extra, pa, pb), "dp", 0, 0, tiled=True)
    keep, send = grads_of(blocks, rows_a, rows_b, docs)
    share = gram(keep, swap_cores(send), docs)
    scale = float(ranks * ranks) ** -0.5
    if docs <= 64:
        share = share + swap_cores(share)
        m = 1
        while 2 * m < dp:
            share = share + swap_dp(share, m)
            m *= 2
        return solve(share, swap_dp(share, m), docs, num_queries, scale).T
    share = lax.psum(share, ("dp", "tensor"))
    return solve_large(jnp.concatenate([share[:, :docs], share[:, docs:]], axis=0).T, docs, num_queries, scale).T


def solution(mesh):
    return jax.shard_map(
        local,
        mesh=mesh,
        in_specs=(
            P(("groups", "dp"), "tensor"),
            P(("groups", "dp"), "tensor"),
            P("tensor", None),
            P("tensor", None),
            P(("groups", "dp")),
            P(("groups", "dp"), None),
        ),
        out_specs=P("groups", "dp"),
        check_vma=False,
    )
```

```python
import functools

import jax
import jax.numpy as jnp
from jax import lax
from jax.experimental import pallas as pl
from jax.experimental.pallas import tpu as pltpu
from jax.sharding import PartitionSpec as P

TOK_DEV = 256
DOC_DEV = 8
LANES = 128
DEPTH = 256
NT = (((1,), (1,)), ((), ()))
HIGHEST = lax.Precision.HIGHEST
VMEM = pl.BlockSpec(memory_space=pltpu.VMEM)
HBM = pl.BlockSpec(memory_space=pltpu.HBM)


def vmem_params(mib):
    return pltpu.CompilerParams(vmem_limit_bytes=int(mib * (1 << 20)))


def chunks_of(length, most=1024):
    size = most
    while length % size:
        size //= 2
    return size, length // size


def project_kernel(sizes, h_ref, g_ref, pin_ref, pout_ref, out_ref, h_buf, g_buf, pin_buf, pout_buf, sems):
    h_size, h_count, g_size, g_count = sizes
    copies = {}

    def copy(name, src, dst):
        copies[name] = pltpu.make_async_copy(src, dst, sems.at[len(copies)])
        copies[name].start()

    copy("po", pout_ref, pout_buf)
    for i in range(g_count):
        at = pl.ds(i * g_size, g_size)
        copy(("g", i), g_ref.at[:, at], g_buf.at[:, at])
    copy("pi", pin_ref, pin_buf)
    for i in range(h_count):
        at = pl.ds(i * h_size, h_size)
        copy(("h", i), h_ref.at[:, at], h_buf.at[:, at])

    def run(tag, count, size, proj, data):
        total = None
        depth = min(size, DEPTH)
        for i in range(count):
            copies[tag, i].wait()
            parts = []
            for j in range(size // depth):
                at = pl.ds(i * size + j * depth, depth)
                parts.append(lax.dot_general(data[:, at], proj[:, at], NT, preferred_element_type=jnp.float32))
            part = sum(parts[1:], parts[0])
            total = part if total is None else total + part
        return total

    copies["po"].wait()
    grad = run("g", g_count, g_size, pout_buf, g_buf)
    copies["pi"].wait()
    inp = run("h", h_count, h_size, pin_buf, h_buf)
    out_ref[...] = jnp.concatenate([grad, inp], axis=1).T


def project(hidden, out_grad, pin_t, pout_t):
    tokens, units = hidden.shape
    width = out_grad.shape[1]
    ranks = pin_t.shape[0] + pout_t.shape[0]
    h_size, h_count = chunks_of(units)
    g_size, g_count = chunks_of(width)
    return pl.pallas_call(
        functools.partial(project_kernel, (h_size, h_count, g_size, g_count)),
        out_shape=jax.ShapeDtypeStruct((ranks, tokens), jnp.float32),
        in_specs=[HBM] * 4,
        out_specs=VMEM,
        scratch_shapes=[
            pltpu.VMEM(hidden.shape, hidden.dtype),
            pltpu.VMEM(out_grad.shape, out_grad.dtype),
            pltpu.VMEM(pin_t.shape, pin_t.dtype),
            pltpu.VMEM(pout_t.shape, pout_t.dtype),
            pltpu.SemaphoreType.DMA((2 + g_count + h_count,)),
        ],
        compiler_params=vmem_params(53.5),
        cost_estimate=pl.CostEstimate(
            flops=2 * tokens * 64 * (units + width),
            bytes_accessed=2 * (tokens + 64) * (units + width),
            transcendentals=0,
        ),
        name="project",
    )(hidden, out_grad, pin_t, pout_t)


def pack_kernel(pb, rows_a, rows_b, part_ref, recv_ref, extra_ref, *refs):
    outs, total_ref = refs[:-1], refs[-1]
    total_ref[...] = part_ref[...] + recv_ref[...]
    ranks = total_ref.shape[0] // 2
    first = lax.axis_index("tensor") * len(outs)
    me = lax.axis_index("dp")
    for t, out_ref in enumerate(outs):
        owner = me ^ (first + t)
        p, q = owner // pb, owner % pb
        out_ref[0:rows_a, :] = total_ref[pl.ds(pl.multiple_of(p * rows_a, rows_a), rows_a), :]
        out_ref[rows_a:rows_a + rows_b, :] = total_ref[pl.ds(pl.multiple_of(ranks + q * rows_b, rows_b), rows_b), :]
        out_ref[rows_a + rows_b:, :] = extra_ref[owner]


def pack(part, recv, extra, pa, pb):
    ranks, lanes = part.shape[0] // 2, part.shape[1]
    rows_a, rows_b = ranks // pa, ranks // pb
    rows = rows_a + rows_b + extra.shape[1]
    count = pa * pb // 2
    return pl.pallas_call(
        functools.partial(pack_kernel, pb, rows_a, rows_b),
        out_shape=(jax.ShapeDtypeStruct((rows, lanes), jnp.float32),) * count,
        in_specs=[VMEM] * 3,
        out_specs=(VMEM,) * count,
        scratch_shapes=[pltpu.VMEM(part.shape, jnp.float32)],
        compiler_params=vmem_params(16),
        name="pack",
    )(part, recv, extra)


def grads_kernel(rows_a, rows_b, docs, *refs):
    xs, (out_ref, outer_ref, member_ref) = refs[:-3], refs[-3:]
    lanes = xs[0].shape[1]
    wide = rows_a * rows_b
    first = rows_a + rows_b
    queries = out_ref.shape[0] - docs
    per = queries // (2 * len(xs))
    doc = lax.broadcasted_iota(jnp.int32, (docs, lanes), 0)
    place = lax.broadcasted_iota(jnp.int32, (queries, wide), 0)
    begin = lax.axis_index("tensor") * len(xs)
    me = lax.axis_index("dp")
    asked = jnp.zeros((queries, wide), jnp.float32)
    for t, x_ref in enumerate(xs):
        at = slice(t * lanes, (t + 1) * lanes)
        g, b = x_ref[0:rows_a, :], x_ref[rows_a:first, :]
        ids = x_ref[first:first + 1, :].astype(jnp.int32)
        member_ref[:, at] = jnp.where(doc == ids, 1.0, 0.0).astype(jnp.bfloat16)
        outer = (g[:, None, :] * b[None, :, :]).reshape(wide, lanes)
        high = outer.astype(jnp.bfloat16)
        outer_ref[0:wide, at] = high
        outer_ref[wide:, at] = (outer - high.astype(jnp.float32)).astype(jnp.bfloat16)
        source = me ^ (begin + t)
        for q in range(per):
            if wide >= lanes:
                span = wide // lanes
                row = first + 1 + q * span
                line = jnp.concatenate([x_ref[row + j:row + j + 1, :] for j in range(span)], axis=1)
            else:
                line = x_ref[first + 1:first + 2, q * wide:(q + 1) * wide]
            asked = jnp.where(place == source * per + q, line, asked)
    sums = lax.dot_general(member_ref[...], outer_ref[...], NT, preferred_element_type=jnp.float32)
    out_ref[0:docs, :] = (sums[:, wide:] + sums[:, :wide]) * (TOK_DEV ** -0.5)
    out_ref[docs:, :] = asked


def grads_of(xs, rows_a, rows_b, docs, queries):
    lanes = xs[0].shape[1]
    wide = rows_a * rows_b
    return pl.pallas_call(
        functools.partial(grads_kernel, rows_a, rows_b, docs),
        out_shape=jax.ShapeDtypeStruct((docs + queries, wide), jnp.float32),
        in_specs=[VMEM] * len(xs),
        out_specs=VMEM,
        scratch_shapes=[
            pltpu.VMEM((2 * wide, len(xs) * lanes), jnp.bfloat16),
            pltpu.VMEM((docs, len(xs) * lanes), jnp.bfloat16),
        ],
        compiler_params=vmem_params(40),
        name="grads",
    )(*xs)


def gram_kernel(docs, part_ref, recv_ref, out_ref):
    both = part_ref[...] + recv_ref[...]
    share = lax.dot_general(both, both[:docs], NT, precision=HIGHEST, preferred_element_type=jnp.float32)
    half = share.shape[0] // 2
    out_ref[...] = jnp.concatenate([share[:half], share[half:]], axis=1)


def gram(part, recv, docs):
    return pl.pallas_call(
        functools.partial(gram_kernel, docs),
        out_shape=jax.ShapeDtypeStruct((part.shape[0] // 2, 2 * docs), jnp.float32),
        in_specs=[VMEM] * 2,
        out_specs=VMEM,
        compiler_params=vmem_params(16),
        name="gram",
    )(part, recv)


def solve_kernel(docs, queries, scale, x_ref, recv_ref, out_ref, done_ref):
    total = x_ref[...] + recv_ref[...]
    stack = jnp.concatenate([total[:, :docs], total[:, docs:]], axis=0)
    cols = done_ref.shape[1]
    stack = jnp.concatenate([stack, jnp.zeros((cols - stack.shape[0], docs), jnp.float32)], axis=0)
    total = stack.T
    row = lax.broadcasted_iota(jnp.int32, (docs, cols), 0)
    col = lax.broadcasted_iota(jnp.int32, (docs, cols), 1)
    mean_diag = jnp.sum(jnp.where(row == col, total, 0.0)) * (1.0 / docs)
    work = total + jnp.where(row == col, 0.1 * mean_diag, 0.0)
    size = 8
    here = lax.broadcasted_iota(jnp.int32, (size, cols), 0)
    rows = [work[i:i + size] for i in range(0, docs, size)]
    for r in range(len(rows)):
        wide = [[jnp.broadcast_to(x[:, c:c + 1], (size, cols)) for c in range(r * size, (r + 1) * size)] for x in rows]
        pivot, line = wide[r], rows[r]
        for j in range(size):
            inverse = 1.0 / pivot[j][j:j + 1]
            factor = jnp.where(here == j, 1.0 - inverse, pivot[j] * inverse)
            pivot = [x if i <= j else x - factor * x[j:j + 1] for i, x in enumerate(pivot)]
            line = line - factor * line[j:j + 1]
        for s in range(len(rows)):
            if s == r:
                rows[s] = line
            else:
                terms = [wide[s][j] * line[j:j + 1] for j in range(size)]
                rows[s] = rows[s] - (((terms[0] + terms[1]) + (terms[2] + terms[3]))
                                     + ((terms[4] + terms[5]) + (terms[6] + terms[7])))
    for r, x in enumerate(rows):
        done_ref[r * size:(r + 1) * size, :] = x * (mean_diag * scale)
    mine = pl.ds(pl.multiple_of(lax.axis_index("dp") * DOC_DEV, DOC_DEV), DOC_DEV)
    out_ref[...] = done_ref[mine, :][:, docs:docs + queries]


def solve(x, recv, docs, queries, scale):
    return pl.pallas_call(
        functools.partial(solve_kernel, docs, queries, scale),
        out_shape=jax.ShapeDtypeStruct((DOC_DEV, queries), jnp.float32),
        in_specs=[VMEM] * 2,
        out_specs=VMEM,
        scratch_shapes=[pltpu.VMEM((docs, -(-(docs + queries) // LANES) * LANES), jnp.float32)],
        compiler_params=vmem_params(16),
        name="solve",
    )(x, recv)


def solve_large(total, docs, queries, scale):
    kernel = total[:, :docs]
    mean_diag = jnp.trace(kernel) / docs
    factor = jnp.linalg.cholesky(kernel + 0.1 * mean_diag * jnp.eye(docs, dtype=jnp.float32))
    solved = jax.scipy.linalg.cho_solve((factor, True), total[:, docs:docs + queries]) * (mean_diag * scale)
    return lax.dynamic_slice_in_dim(solved, lax.axis_index("dp") * DOC_DEV, DOC_DEV, 0)


def swap_cores(x):
    cores = lax.axis_size("tensor")
    return lax.ppermute(x, "tensor", [(i, cores - 1 - i) for i in range(cores)])


def trade(xs):
    dp, count = lax.axis_size("dp"), len(xs)
    got = []
    for t, x in enumerate(xs):
        pairs = [(i * 2 + k, (i ^ (k * count + t)) * 2 + k) for i in range(dp) for k in range(2)]
        got.append(lax.ppermute(x, ("dp", "tensor"), pairs))
    return got


def local(hidden, out_grad, proj_in, proj_out, doc_ids, queries):
    dp = lax.axis_size("dp")
    docs, num_queries = DOC_DEV * dp, queries.shape[0] * dp
    ranks = proj_in.shape[1]
    pa = 1
    while pa * pa < dp:
        pa *= 2
    pb = dp // pa
    rows_a, rows_b = ranks // pa, ranks // pb

    part = project(hidden, out_grad, proj_in.T, proj_out.T)
    recv = swap_cores(part)

    lanes = part.shape[1]
    ids = doc_ids.astype(jnp.float32)
    asked = queries.reshape(-1, pa, rows_a, pb, rows_b).transpose(1, 3, 0, 2, 4).reshape(dp, -1, lanes)
    extra = jnp.concatenate([jnp.broadcast_to(ids, (dp, 1, lanes)), asked], axis=1)
    extra = jnp.pad(extra, ((0, 0), (0, -extra.shape[1] % 8), (0, 0)))

    blocks = trade(pack(part, recv, extra, pa, pb))
    grads = grads_of(blocks, rows_a, rows_b, docs, num_queries)
    share = gram(grads, swap_cores(grads), docs)
    scale = float(ranks * ranks) ** -0.5
    if docs <= 64:
        share = sum(trade([share] * (dp // 2)))
        return solve(share, swap_cores(share), docs, num_queries, scale).T
    share = lax.psum(share, "dp")
    return solve_large(jnp.concatenate([share[:, :docs], share[:, docs:]], axis=0).T, docs, num_queries, scale).T


def solution(mesh):
    return jax.shard_map(
        local,
        mesh=mesh,
        in_specs=(
            P(("groups", "dp"), "tensor"),
            P(("groups", "dp"), "tensor"),
            P("tensor", None),
            P("tensor", None),
            P(("groups", "dp")),
            P(("groups", "dp"), None),
        ),
        out_specs=P("groups", "dp"),
        check_vma=False,
    )
```

```python
import functools

import jax
import jax.numpy as jnp
from jax import lax
from jax.experimental import pallas as pl
from jax.experimental.pallas import tpu as pltpu
from jax.sharding import PartitionSpec as P

TOK_DEV = 256
DOC_DEV = 8
LANES = 128
DEPTH = 256
FLIGHT = 8
NT = (((1,), (1,)), ((), ()))
HIGHEST = lax.Precision.HIGHEST
VMEM = pl.BlockSpec(memory_space=pltpu.VMEM)
HBM = pl.BlockSpec(memory_space=pltpu.HBM)


def vmem_params(mib):
    return pltpu.CompilerParams(vmem_limit_bytes=int(mib * (1 << 20)))


def chunks_of(length, most=1024):
    size = most
    while length % size:
        size //= 2
    return size, length // size


def project_kernel(sizes, h_ref, g_ref, pin_ref, pout_ref, out_ref, h_buf, g_buf, pin_buf, pout_buf, sems):
    h_size, h_count, g_size, g_count = sizes
    copies, order = {}, []

    def copy(name, src, dst):
        copies[name] = pltpu.make_async_copy(src, dst, sems.at[len(copies)])
        order.append(name)
        if len(order) <= FLIGHT:
            copies[name].start()

    def arrive(name):
        copies[name].wait()
        ahead = order.index(name) + FLIGHT
        if ahead < len(order):
            copies[order[ahead]].start()

    copy("po", pout_ref, pout_buf)
    for i in range(g_count):
        at = pl.ds(i * g_size, g_size)
        copy(("g", i), g_ref.at[:, at], g_buf.at[:, at])
    copy("pi", pin_ref, pin_buf)
    for i in range(h_count):
        at = pl.ds(i * h_size, h_size)
        copy(("h", i), h_ref.at[:, at], h_buf.at[:, at])

    def run(tag, count, size, proj, data):
        total = None
        depth = min(size, DEPTH)
        for i in range(count):
            arrive((tag, i))
            parts = []
            for j in range(size // depth):
                at = pl.ds(i * size + j * depth, depth)
                parts.append(lax.dot_general(data[:, at], proj[:, at], NT, preferred_element_type=jnp.float32))
            part = sum(parts[1:], parts[0])
            total = part if total is None else total + part
        return total

    arrive("po")
    grad = run("g", g_count, g_size, pout_buf, g_buf)
    arrive("pi")
    inp = run("h", h_count, h_size, pin_buf, h_buf)
    out_ref[...] = jnp.concatenate([grad, inp], axis=1).T


def project(hidden, out_grad, pin_t, pout_t):
    tokens, units = hidden.shape
    width = out_grad.shape[1]
    ranks = pin_t.shape[0] + pout_t.shape[0]
    h_size, h_count = chunks_of(units)
    g_size, g_count = chunks_of(width)
    return pl.pallas_call(
        functools.partial(project_kernel, (h_size, h_count, g_size, g_count)),
        out_shape=jax.ShapeDtypeStruct((ranks, tokens), jnp.float32),
        in_specs=[HBM] * 4,
        out_specs=VMEM,
        scratch_shapes=[
            pltpu.VMEM(hidden.shape, hidden.dtype),
            pltpu.VMEM(out_grad.shape, out_grad.dtype),
            pltpu.VMEM(pin_t.shape, pin_t.dtype),
            pltpu.VMEM(pout_t.shape, pout_t.dtype),
            pltpu.SemaphoreType.DMA((2 + g_count + h_count,)),
        ],
        compiler_params=vmem_params(53.5),
        cost_estimate=pl.CostEstimate(
            flops=2 * tokens * 64 * (units + width),
            bytes_accessed=2 * (tokens + 64) * (units + width),
            transcendentals=0,
        ),
        name="project",
    )(hidden, out_grad, pin_t, pout_t)


def partners(dp):
    order = [m for far in (True, False) for m in range(1, dp - 1) if (2 * m >= dp) == far]
    return order[0::2], order[1::2]


def partner(dp, t):
    first, second = partners(dp)
    return jnp.where(lax.axis_index("tensor") == 0, first[t], second[t])


def pack_kernel(pb, rows_a, rows_b, part_ref, recv_ref, extra_ref, *refs):
    outs, total_ref = refs[:-1], refs[-1]
    total_ref[...] = part_ref[...] + recv_ref[...]
    ranks, lanes = total_ref.shape[0] // 2, total_ref.shape[1]
    dp = extra_ref.shape[0]
    me = lax.axis_index("dp")
    lead = lax.axis_index("tensor") == 0

    def rows(out_ref, owner, pick):
        p, q = owner // pb, owner % pb
        out_ref[0:rows_a, :] = pick(total_ref[pl.ds(pl.multiple_of(p * rows_a, rows_a), rows_a), :])
        out_ref[rows_a:rows_a + rows_b, :] = pick(total_ref[pl.ds(pl.multiple_of(ranks + q * rows_b, rows_b), rows_b), :])
        out_ref[rows_a + rows_b:, :] = pick(extra_ref[owner])

    def half(x):
        return jnp.where(lead, x[:, :lanes // 2], x[:, lanes // 2:])

    for t, out_ref in enumerate(outs[:-2]):
        rows(out_ref, me ^ partner(dp, t), lambda x: x)
    rows(outs[-2], me ^ (dp - 1), half)
    rows(outs[-1], me, half)


def pack(part, recv, extra, pa, pb):
    ranks, lanes = part.shape[0] // 2, part.shape[1]
    rows_a, rows_b = ranks // pa, ranks // pb
    rows = rows_a + rows_b + extra.shape[1]
    count = pa * pb // 2 - 1
    whole, half = (jax.ShapeDtypeStruct((rows, n), jnp.float32) for n in (lanes, lanes // 2))
    return pl.pallas_call(
        functools.partial(pack_kernel, pb, rows_a, rows_b),
        out_shape=(whole,) * count + (half, half),
        in_specs=[VMEM] * 3,
        out_specs=(VMEM,) * (count + 2),
        scratch_shapes=[pltpu.VMEM(part.shape, jnp.float32)],
        compiler_params=vmem_params(16),
        name="pack",
    )(part, recv, extra)


def grads_kernel(rows_a, rows_b, docs, dp, *refs):
    xs, (out_ref, outer_ref, member_ref) = refs[:-3], refs[-3:]
    whole = xs[0].shape[1]
    wide = rows_a * rows_b
    first = rows_a + rows_b
    queries = out_ref.shape[0] - docs
    per = queries // dp
    place = lax.broadcasted_iota(jnp.int32, (queries, whole), 0)
    lane = lax.broadcasted_iota(jnp.int32, (queries, whole), 1)
    me = lax.axis_index("dp")
    core = lax.axis_index("tensor")
    mine = lane // (whole // 2) == core
    flat = [jnp.zeros((queries, whole), jnp.float32)] * (per * wide // whole)
    start = 0
    for t, x_ref in enumerate(xs):
        lanes = x_ref.shape[1]
        at = slice(start, start + lanes)
        start += lanes
        g, b = x_ref[0:rows_a, :], x_ref[rows_a:first, :]
        ids = x_ref[first:first + 1, :].astype(jnp.int32)
        doc = lax.broadcasted_iota(jnp.int32, (docs, lanes), 0)
        member_ref[:, at] = jnp.where(doc == ids, 1.0, 0.0).astype(jnp.bfloat16)
        outer = (g[:, None, :] * b[None, :, :]).reshape(wide, lanes)
        high = outer.astype(jnp.bfloat16)
        outer_ref[0:wide, at] = high
        outer_ref[wide:, at] = (outer - high.astype(jnp.float32)).astype(jnp.bfloat16)
        gap = partner(dp, t) if t < len(xs) - 2 else dp - 1 if t == len(xs) - 2 else 0
        held = place // per == me ^ gap
        if lanes < whole:
            held = jnp.logical_and(held, mine)
        for j in range(len(flat)):
            line = x_ref[first + 1 + j:first + 2 + j, :]
            if lanes < whole:
                line = jnp.concatenate([line, line], axis=1)
            flat[j] = jnp.where(held, line, flat[j])
    sums = lax.dot_general(member_ref[...], outer_ref[...], NT, preferred_element_type=jnp.float32)
    out_ref[0:docs, :] = (sums[:, wide:] + sums[:, :wide]) * (TOK_DEV ** -0.5)
    flat = jnp.concatenate(flat, axis=1)
    asked = jnp.zeros((queries, wide), jnp.float32)
    which = lax.broadcasted_iota(jnp.int32, (queries, wide), 0) % per
    for q in range(per):
        asked = jnp.where(which == q, flat[:, q * wide:(q + 1) * wide], asked)
    out_ref[docs:, :] = asked


def grads_of(xs, rows_a, rows_b, docs, queries, dp):
    tokens = sum(x.shape[1] for x in xs)
    wide = rows_a * rows_b
    return pl.pallas_call(
        functools.partial(grads_kernel, rows_a, rows_b, docs, dp),
        out_shape=jax.ShapeDtypeStruct((docs + queries, wide), jnp.float32),
        in_specs=[VMEM] * len(xs),
        out_specs=VMEM,
        scratch_shapes=[
            pltpu.VMEM((2 * wide, tokens), jnp.bfloat16),
            pltpu.VMEM((docs, tokens), jnp.bfloat16),
        ],
        compiler_params=vmem_params(40),
        name="grads",
    )(*xs)


def gram_kernel(docs, part_ref, recv_ref, out_ref):
    both = part_ref[...] + recv_ref[...]
    share = lax.dot_general(both, both[:docs], NT, precision=HIGHEST, preferred_element_type=jnp.float32)
    half = share.shape[0] // 2
    out_ref[...] = jnp.concatenate([share[:half], share[half:]], axis=1)


def gram(part, recv, docs):
    return pl.pallas_call(
        functools.partial(gram_kernel, docs),
        out_shape=jax.ShapeDtypeStruct((part.shape[0] // 2, 2 * docs), jnp.float32),
        in_specs=[VMEM] * 2,
        out_specs=VMEM,
        compiler_params=vmem_params(16),
        name="gram",
    )(part, recv)


def solve_kernel(docs, queries, scale, x_ref, recv_ref, out_ref, done_ref):
    total = x_ref[...] + recv_ref[...]
    stack = jnp.concatenate([total[:, :docs], total[:, docs:]], axis=0)
    cols = done_ref.shape[1]
    stack = jnp.concatenate([stack, jnp.zeros((cols - stack.shape[0], docs), jnp.float32)], axis=0)
    total = stack.T
    row = lax.broadcasted_iota(jnp.int32, (docs, cols), 0)
    col = lax.broadcasted_iota(jnp.int32, (docs, cols), 1)
    mean_diag = jnp.sum(jnp.where(row == col, total, 0.0)) * (1.0 / docs)
    work = total + jnp.where(row == col, 0.1 * mean_diag, 0.0)
    size = 8
    here = lax.broadcasted_iota(jnp.int32, (size, cols), 0)
    rows = [work[i:i + size] for i in range(0, docs, size)]
    for r in range(len(rows)):
        wide = [[jnp.broadcast_to(x[:, c:c + 1], (size, cols)) for c in range(r * size, (r + 1) * size)] for x in rows]
        pivot, line = wide[r], rows[r]
        for j in range(size):
            inverse = 1.0 / pivot[j][j:j + 1]
            factor = jnp.where(here == j, 1.0 - inverse, pivot[j] * inverse)
            pivot = [x if i <= j else x - factor * x[j:j + 1] for i, x in enumerate(pivot)]
            line = line - factor * line[j:j + 1]
        for s in range(len(rows)):
            if s == r:
                rows[s] = line
            else:
                terms = [wide[s][j] * line[j:j + 1] for j in range(size)]
                rows[s] = rows[s] - (((terms[0] + terms[1]) + (terms[2] + terms[3]))
                                     + ((terms[4] + terms[5]) + (terms[6] + terms[7])))
    for r, x in enumerate(rows):
        done_ref[r * size:(r + 1) * size, :] = x * (mean_diag * scale)
    mine = pl.ds(pl.multiple_of(lax.axis_index("dp") * DOC_DEV, DOC_DEV), DOC_DEV)
    out_ref[...] = done_ref[mine, :][:, docs:docs + queries]


def solve(x, recv, docs, queries, scale):
    return pl.pallas_call(
        functools.partial(solve_kernel, docs, queries, scale),
        out_shape=jax.ShapeDtypeStruct((DOC_DEV, queries), jnp.float32),
        in_specs=[VMEM] * 2,
        out_specs=VMEM,
        scratch_shapes=[pltpu.VMEM((docs, -(-(docs + queries) // LANES) * LANES), jnp.float32)],
        compiler_params=vmem_params(16),
        name="solve",
    )(x, recv)


def solve_large(total, docs, queries, scale):
    kernel = total[:, :docs]
    mean_diag = jnp.trace(kernel) / docs
    factor = jnp.linalg.cholesky(kernel + 0.1 * mean_diag * jnp.eye(docs, dtype=jnp.float32))
    solved = jax.scipy.linalg.cho_solve((factor, True), total[:, docs:docs + queries]) * (mean_diag * scale)
    return lax.dynamic_slice_in_dim(solved, lax.axis_index("dp") * DOC_DEV, DOC_DEV, 0)


def swap_cores(x):
    cores = lax.axis_size("tensor")
    return lax.ppermute(x, "tensor", [(i, cores - 1 - i) for i in range(cores)])


def trade(xs):
    dp = lax.axis_size("dp")
    got = []
    for x, ms in zip(xs, zip(*partners(dp))):
        pairs = [(i * 2 + k, (i ^ m) * 2 + k) for i in range(dp) for k, m in enumerate(ms)]
        got.append(lax.ppermute(x, ("dp", "tensor"), pairs))
    return got


def trade_last(x):
    dp = lax.axis_size("dp")
    return lax.ppermute(x, "dp", [(i, i ^ (dp - 1)) for i in range(dp)])


def local(hidden, out_grad, proj_in, proj_out, doc_ids, queries):
    dp = lax.axis_size("dp")
    docs, num_queries = DOC_DEV * dp, queries.shape[0] * dp
    ranks = proj_in.shape[1]
    pa = 1
    while pa * pa < dp:
        pa *= 2
    pb = dp // pa
    rows_a, rows_b = ranks // pa, ranks // pb

    part = project(hidden, out_grad, proj_in.T, proj_out.T)
    recv = swap_cores(part)

    lanes = part.shape[1]
    ids = doc_ids.astype(jnp.float32)
    asked = queries.reshape(-1, pa, rows_a, pb, rows_b).transpose(1, 3, 0, 2, 4).reshape(dp, -1, lanes)
    extra = jnp.concatenate([jnp.broadcast_to(ids, (dp, 1, lanes)), asked], axis=1)
    extra = jnp.pad(extra, ((0, 0), (0, -extra.shape[1] % 8), (0, 0)))

    *blocks, last, own = pack(part, recv, extra, pa, pb)
    blocks = trade(blocks) + [trade_last(last), own]
    grads = grads_of(blocks, rows_a, rows_b, docs, num_queries, dp)
    share = gram(grads, swap_cores(grads), docs)
    scale = float(ranks * ranks) ** -0.5
    if docs <= 64:
        halves = jnp.where(lax.axis_index("tensor") == 0, share, trade_last(share))
        share = sum(trade([share] * (dp // 2 - 1)), halves)
        return solve(share, swap_cores(share), docs, num_queries, scale).T
    share = lax.psum(share, "dp")
    return solve_large(jnp.concatenate([share[:, :docs], share[:, docs:]], axis=0).T, docs, num_queries, scale).T


def solution(mesh):
    return jax.shard_map(
        local,
        mesh=mesh,
        in_specs=(
            P(("groups", "dp"), "tensor"),
            P(("groups", "dp"), "tensor"),
            P("tensor", None),
            P("tensor", None),
            P(("groups", "dp")),
            P(("groups", "dp"), None),
        ),
        out_specs=P("groups", "dp"),
        check_vma=False,
    )
```

```python
import functools

import jax
import jax.numpy as jnp
from jax import lax
from jax.experimental import pallas as pl
from jax.experimental.pallas import tpu as pltpu
from jax.sharding import PartitionSpec as P

TOK_DEV = 256
DOC_DEV = 8
LANES = 128
ROWS = 64
PIECES = 4
FLIGHT = 5
NT = (((1,), (1,)), ((), ()))
HIGHEST = lax.Precision.HIGHEST
VMEM = pl.BlockSpec(memory_space=pltpu.VMEM)
HBM = pl.BlockSpec(memory_space=pltpu.HBM)


def vmem_params(mib):
    return pltpu.CompilerParams(vmem_limit_bytes=int(mib * (1 << 20)))


def project_kernel(h_ref, g_ref, pin_ref, pout_ref, out_ref, h_buf, g_buf, pin_buf, pout_buf, sems):
    copies, order = {}, []

    def copy(name, src, dst):
        copies[name] = pltpu.make_async_copy(src, dst, sems.at[len(copies)])
        order.append(name)
        if len(order) <= FLIGHT:
            copies[name].start()

    def arrive(name):
        copies[name].wait()
        ahead = order.index(name) + FLIGHT
        if ahead < len(order):
            copies[order[ahead]].start()

    chunks = [pl.ds(i, ROWS) for i in range(0, h_ref.shape[0], ROWS)]
    copy("po", pout_ref, pout_buf)
    for i, at in enumerate(chunks):
        copy(("g", i), g_ref.at[at], g_buf.at[at])
    copy("pi", pin_ref, pin_buf)
    for i, at in enumerate(chunks):
        copy(("h", i), h_ref.at[at], h_buf.at[at])

    def run(tag, proj, data):
        depth = data.shape[1] // PIECES
        done = []
        for i, at in enumerate(chunks):
            arrive((tag, i))
            parts = []
            for j in range(PIECES):
                units = pl.ds(j * depth, depth)
                parts.append(lax.dot_general(proj[:, units], data[at, units], NT, preferred_element_type=jnp.float32))
            done.append(sum(parts[1:], parts[0]))
        return jnp.concatenate(done, axis=1)

    ranks = pout_ref.shape[0]
    arrive("po")
    out_ref[0:ranks, :] = run("g", pout_buf, g_buf)
    arrive("pi")
    out_ref[ranks:, :] = run("h", pin_buf, h_buf)


def project(hidden, out_grad, pin_t, pout_t):
    tokens, units = hidden.shape
    width = out_grad.shape[1]
    ranks = pin_t.shape[0] + pout_t.shape[0]
    return pl.pallas_call(
        project_kernel,
        out_shape=jax.ShapeDtypeStruct((ranks, tokens), jnp.float32),
        in_specs=[HBM] * 4,
        out_specs=VMEM,
        scratch_shapes=[
            pltpu.VMEM(hidden.shape, hidden.dtype),
            pltpu.VMEM(out_grad.shape, out_grad.dtype),
            pltpu.VMEM(pin_t.shape, pin_t.dtype),
            pltpu.VMEM(pout_t.shape, pout_t.dtype),
            pltpu.SemaphoreType.DMA((2 + 2 * tokens // ROWS,)),
        ],
        compiler_params=vmem_params(53.5),
        cost_estimate=pl.CostEstimate(
            flops=2 * tokens * 64 * (units + width),
            bytes_accessed=2 * (tokens + 64) * (units + width),
            transcendentals=0,
        ),
        name="project",
    )(hidden, out_grad, pin_t, pout_t)


def partners(dp):
    order = [m for far in (True, False) for m in range(1, dp - 1) if (2 * m >= dp) == far]
    return order[0::2], order[1::2]


def partner(dp, t):
    first, second = partners(dp)
    return jnp.where(lax.axis_index("tensor") == 0, first[t], second[t])


def pack_kernel(pb, rows_a, rows_b, part_ref, recv_ref, extra_ref, *refs):
    outs, total_ref = refs[:-1], refs[-1]
    total_ref[...] = part_ref[...] + recv_ref[...]
    ranks, lanes = total_ref.shape[0] // 2, total_ref.shape[1]
    dp = extra_ref.shape[0]
    me = lax.axis_index("dp")
    lead = lax.axis_index("tensor") == 0

    def rows(out_ref, owner, pick):
        p, q = owner // pb, owner % pb
        out_ref[0:rows_a, :] = pick(total_ref[pl.ds(pl.multiple_of(p * rows_a, rows_a), rows_a), :])
        out_ref[rows_a:rows_a + rows_b, :] = pick(total_ref[pl.ds(pl.multiple_of(ranks + q * rows_b, rows_b), rows_b), :])
        out_ref[rows_a + rows_b:, :] = pick(extra_ref[owner])

    def half(x):
        return jnp.where(lead, x[:, :lanes // 2], x[:, lanes // 2:])

    for t, out_ref in enumerate(outs[:-2]):
        rows(out_ref, me ^ partner(dp, t), lambda x: x)
    rows(outs[-2], me ^ (dp - 1), half)
    rows(outs[-1], me, half)


def pack(part, recv, extra, pa, pb):
    ranks, lanes = part.shape[0] // 2, part.shape[1]
    rows_a, rows_b = ranks // pa, ranks // pb
    rows = rows_a + rows_b + extra.shape[1]
    count = pa * pb // 2 - 1
    whole, half = (jax.ShapeDtypeStruct((rows, n), jnp.float32) for n in (lanes, lanes // 2))
    return pl.pallas_call(
        functools.partial(pack_kernel, pb, rows_a, rows_b),
        out_shape=(whole,) * count + (half, half),
        in_specs=[VMEM] * 3,
        out_specs=(VMEM,) * (count + 2),
        scratch_shapes=[pltpu.VMEM(part.shape, jnp.float32)],
        compiler_params=vmem_params(16),
        name="pack",
    )(part, recv, extra)


def grads_kernel(rows_a, rows_b, docs, dp, *refs):
    xs, (out_ref, outer_ref, member_ref) = refs[:-3], refs[-3:]
    whole = xs[0].shape[1]
    wide = rows_a * rows_b
    first = rows_a + rows_b
    queries = out_ref.shape[0] - docs
    per = queries // dp
    place = lax.broadcasted_iota(jnp.int32, (queries, whole), 0)
    lane = lax.broadcasted_iota(jnp.int32, (queries, whole), 1)
    me = lax.axis_index("dp")
    core = lax.axis_index("tensor")
    mine = lane // (whole // 2) == core
    flat = [jnp.zeros((queries, whole), jnp.float32)] * (per * wide // whole)
    start = 0
    for t, x_ref in enumerate(xs):
        lanes = x_ref.shape[1]
        at = slice(start, start + lanes)
        start += lanes
        g, b = x_ref[0:rows_a, :], x_ref[rows_a:first, :]
        ids = x_ref[first:first + 1, :].astype(jnp.int32)
        doc = lax.broadcasted_iota(jnp.int32, (docs, lanes), 0)
        member_ref[:, at] = jnp.where(doc == ids, 1.0, 0.0).astype(jnp.bfloat16)
        outer = (g[:, None, :] * b[None, :, :]).reshape(wide, lanes)
        high = outer.astype(jnp.bfloat16)
        outer_ref[0:wide, at] = high
        outer_ref[wide:, at] = (outer - high.astype(jnp.float32)).astype(jnp.bfloat16)
        gap = partner(dp, t) if t < len(xs) - 2 else dp - 1 if t == len(xs) - 2 else 0
        held = place // per == me ^ gap
        if lanes < whole:
            held = jnp.logical_and(held, mine)
        for j in range(len(flat)):
            line = x_ref[first + 1 + j:first + 2 + j, :]
            if lanes < whole:
                line = jnp.concatenate([line, line], axis=1)
            flat[j] = jnp.where(held, line, flat[j])
    sums = lax.dot_general(member_ref[...], outer_ref[...], NT, preferred_element_type=jnp.float32)
    out_ref[0:docs, :] = (sums[:, wide:] + sums[:, :wide]) * (TOK_DEV ** -0.5)
    flat = jnp.concatenate(flat, axis=1)
    asked = jnp.zeros((queries, wide), jnp.float32)
    which = lax.broadcasted_iota(jnp.int32, (queries, wide), 0) % per
    for q in range(per):
        asked = jnp.where(which == q, flat[:, q * wide:(q + 1) * wide], asked)
    out_ref[docs:, :] = asked


def grads_of(xs, rows_a, rows_b, docs, queries, dp):
    tokens = sum(x.shape[1] for x in xs)
    wide = rows_a * rows_b
    return pl.pallas_call(
        functools.partial(grads_kernel, rows_a, rows_b, docs, dp),
        out_shape=jax.ShapeDtypeStruct((docs + queries, wide), jnp.float32),
        in_specs=[VMEM] * len(xs),
        out_specs=VMEM,
        scratch_shapes=[
            pltpu.VMEM((2 * wide, tokens), jnp.bfloat16),
            pltpu.VMEM((docs, tokens), jnp.bfloat16),
        ],
        compiler_params=vmem_params(40),
        name="grads",
    )(*xs)


def gram_kernel(docs, part_ref, recv_ref, out_ref):
    both = part_ref[...] + recv_ref[...]
    share = lax.dot_general(both, both[:docs], NT, precision=HIGHEST, preferred_element_type=jnp.float32)
    half = share.shape[0] // 2
    out_ref[...] = jnp.concatenate([share[:half], share[half:]], axis=1)


def gram(part, recv, docs):
    return pl.pallas_call(
        functools.partial(gram_kernel, docs),
        out_shape=jax.ShapeDtypeStruct((part.shape[0] // 2, 2 * docs), jnp.float32),
        in_specs=[VMEM] * 2,
        out_specs=VMEM,
        compiler_params=vmem_params(16),
        name="gram",
    )(part, recv)


def solve_kernel(docs, queries, scale, x_ref, recv_ref, out_ref, done_ref):
    total = x_ref[...] + recv_ref[...]
    stack = jnp.concatenate([total[:, :docs], total[:, docs:]], axis=0)
    cols = done_ref.shape[1]
    stack = jnp.concatenate([stack, jnp.zeros((cols - stack.shape[0], docs), jnp.float32)], axis=0)
    total = stack.T
    row = lax.broadcasted_iota(jnp.int32, (docs, cols), 0)
    col = lax.broadcasted_iota(jnp.int32, (docs, cols), 1)
    mean_diag = jnp.sum(jnp.where(row == col, total, 0.0)) * (1.0 / docs)
    work = total + jnp.where(row == col, 0.1 * mean_diag, 0.0)
    size = 8
    here = lax.broadcasted_iota(jnp.int32, (size, cols), 0)
    rows = [work[i:i + size] for i in range(0, docs, size)]
    for r in range(len(rows)):
        wide = [[jnp.broadcast_to(x[:, c:c + 1], (size, cols)) for c in range(r * size, (r + 1) * size)] for x in rows]
        pivot, line = wide[r], rows[r]
        for j in range(size):
            inverse = 1.0 / pivot[j][j:j + 1]
            factor = jnp.where(here == j, 1.0 - inverse, pivot[j] * inverse)
            pivot = [x if i <= j else x - factor * x[j:j + 1] for i, x in enumerate(pivot)]
            line = line - factor * line[j:j + 1]
        for s in range(len(rows)):
            if s == r:
                rows[s] = line
            else:
                terms = [wide[s][j] * line[j:j + 1] for j in range(size)]
                rows[s] = rows[s] - (((terms[0] + terms[1]) + (terms[2] + terms[3]))
                                     + ((terms[4] + terms[5]) + (terms[6] + terms[7])))
    for r, x in enumerate(rows):
        done_ref[r * size:(r + 1) * size, :] = x * (mean_diag * scale)
    mine = pl.ds(pl.multiple_of(lax.axis_index("dp") * DOC_DEV, DOC_DEV), DOC_DEV)
    out_ref[...] = done_ref[mine, :][:, docs:docs + queries]


def solve(x, recv, docs, queries, scale):
    return pl.pallas_call(
        functools.partial(solve_kernel, docs, queries, scale),
        out_shape=jax.ShapeDtypeStruct((DOC_DEV, queries), jnp.float32),
        in_specs=[VMEM] * 2,
        out_specs=VMEM,
        scratch_shapes=[pltpu.VMEM((docs, -(-(docs + queries) // LANES) * LANES), jnp.float32)],
        compiler_params=vmem_params(16),
        name="solve",
    )(x, recv)


def solve_large(total, docs, queries, scale):
    kernel = total[:, :docs]
    mean_diag = jnp.trace(kernel) / docs
    factor = jnp.linalg.cholesky(kernel + 0.1 * mean_diag * jnp.eye(docs, dtype=jnp.float32))
    solved = jax.scipy.linalg.cho_solve((factor, True), total[:, docs:docs + queries]) * (mean_diag * scale)
    return lax.dynamic_slice_in_dim(solved, lax.axis_index("dp") * DOC_DEV, DOC_DEV, 0)


def swap_cores(x):
    cores = lax.axis_size("tensor")
    return lax.ppermute(x, "tensor", [(i, cores - 1 - i) for i in range(cores)])


def trade(xs):
    dp = lax.axis_size("dp")
    got = []
    for x, ms in zip(xs, zip(*partners(dp))):
        pairs = [(i * 2 + k, (i ^ m) * 2 + k) for i in range(dp) for k, m in enumerate(ms)]
        got.append(lax.ppermute(x, ("dp", "tensor"), pairs))
    return got


def trade_last(x):
    dp = lax.axis_size("dp")
    return lax.ppermute(x, "dp", [(i, i ^ (dp - 1)) for i in range(dp)])


def local(hidden, out_grad, proj_in, proj_out, doc_ids, queries):
    dp = lax.axis_size("dp")
    docs, num_queries = DOC_DEV * dp, queries.shape[0] * dp
    ranks = proj_in.shape[1]
    pa = 1
    while pa * pa < dp:
        pa *= 2
    pb = dp // pa
    rows_a, rows_b = ranks // pa, ranks // pb

    part = project(hidden, out_grad, proj_in.T, proj_out.T)
    recv = swap_cores(part)

    lanes = part.shape[1]
    ids = doc_ids.astype(jnp.float32)
    asked = queries.reshape(-1, pa, rows_a, pb, rows_b).transpose(1, 3, 0, 2, 4).reshape(dp, -1, lanes)
    extra = jnp.concatenate([jnp.broadcast_to(ids, (dp, 1, lanes)), asked], axis=1)
    extra = jnp.pad(extra, ((0, 0), (0, -extra.shape[1] % 8), (0, 0)))

    *blocks, last, own = pack(part, recv, extra, pa, pb)
    blocks = trade(blocks) + [trade_last(last), own]
    grads = grads_of(blocks, rows_a, rows_b, docs, num_queries, dp)
    share = gram(grads, swap_cores(grads), docs)
    scale = float(ranks * ranks) ** -0.5
    if docs <= 64:
        halves = jnp.where(lax.axis_index("tensor") == 0, share, trade_last(share))
        share = sum(trade([share] * (dp // 2 - 1)), halves)
        return solve(share, swap_cores(share), docs, num_queries, scale).T
    share = lax.psum(share, "dp")
    return solve_large(jnp.concatenate([share[:, :docs], share[:, docs:]], axis=0).T, docs, num_queries, scale).T


def solution(mesh):
    return jax.shard_map(
        local,
        mesh=mesh,
        in_specs=(
            P(("groups", "dp"), "tensor"),
            P(("groups", "dp"), "tensor"),
            P("tensor", None),
            P("tensor", None),
            P(("groups", "dp")),
            P(("groups", "dp"), None),
        ),
        out_specs=P("groups", "dp"),
        check_vma=False,
    )
```

```python
import functools

import jax
import jax.numpy as jnp
from jax import lax
from jax.experimental import pallas as pl
from jax.experimental.pallas import tpu as pltpu
from jax.sharding import PartitionSpec as P

TOK_DEV = 256
DOC_DEV = 8
LANES = 128
STACK = 2
FLIGHT = 10
NT = (((1,), (1,)), ((), ()))
HIGHEST = lax.Precision.HIGHEST
VMEM = pl.BlockSpec(memory_space=pltpu.VMEM)
HBM = pl.BlockSpec(memory_space=pltpu.HBM)


def vmem_params(mib):
    return pltpu.CompilerParams(vmem_limit_bytes=int(mib * (1 << 20)))


def chunks_of(length, most=1024):
    size = most
    while length % size:
        size //= 2
    return size, length // size


def project_kernel(h_ref, g_ref, pin_ref, pout_ref, out_ref, h_buf, g_buf, pin_buf, pout_buf, sems):
    copies, order = {}, []

    def copy(name, src, dst):
        copies[name] = pltpu.make_async_copy(src, dst, sems.at[len(copies)])
        order.append(name)
        if len(order) <= FLIGHT:
            copies[name].start()

    def arrive(name):
        copies[name].wait()
        ahead = order.index(name) + FLIGHT
        if ahead < len(order):
            copies[order[ahead]].start()

    def plan(tag, proj, proj_buf, data, data_buf):
        depth = data_buf.shape[1]
        ranks, tokens = proj.shape[0], data.shape[0]
        size, count = chunks_of(depth)
        for s in range(STACK):
            copy((tag, s), proj.at[:, pl.ds(s * depth, depth)], proj_buf.at[pl.ds(s * ranks, ranks)])
        for i in range(count):
            for s in range(STACK):
                copy(
                    (tag, s, i),
                    data.at[:, pl.ds(s * depth + i * size, size)],
                    data_buf.at[pl.ds(s * tokens, tokens), pl.ds(i * size, size)],
                )

    def run(tag, proj_buf, data_buf):
        ranks, tokens = proj_buf.shape[0] // STACK, data_buf.shape[0] // STACK
        size, count = chunks_of(data_buf.shape[1])
        for s in range(STACK):
            arrive((tag, s))
        total = None
        for i in range(count):
            for s in range(STACK):
                arrive((tag, s, i))
            at = pl.ds(i * size, size)
            part = lax.dot_general(proj_buf[:, at], data_buf[:, at], NT, preferred_element_type=jnp.float32)
            for s in range(STACK):
                block = part[s * ranks:(s + 1) * ranks, s * tokens:(s + 1) * tokens]
                total = block if total is None else total + block
        return total

    plan("g", pout_ref, pout_buf, g_ref, g_buf)
    plan("h", pin_ref, pin_buf, h_ref, h_buf)
    ranks = pout_ref.shape[0]
    out_ref[0:ranks, :] = run("g", pout_buf, g_buf)
    out_ref[ranks:, :] = run("h", pin_buf, h_buf)


def project(hidden, out_grad, pin_t, pout_t):
    tokens, units = hidden.shape
    width = out_grad.shape[1]
    ranks = pin_t.shape[0] + pout_t.shape[0]
    operands = (hidden, out_grad, pin_t, pout_t)
    copies = sum(STACK * (1 + chunks_of(x.shape[1] // STACK)[1]) for x in operands[:2])
    return pl.pallas_call(
        project_kernel,
        out_shape=jax.ShapeDtypeStruct((ranks, tokens), jnp.float32),
        in_specs=[HBM] * 4,
        out_specs=VMEM,
        scratch_shapes=[pltpu.VMEM((x.shape[0] * STACK, x.shape[1] // STACK), x.dtype) for x in operands]
        + [pltpu.SemaphoreType.DMA((copies,))],
        compiler_params=vmem_params(53.5),
        cost_estimate=pl.CostEstimate(
            flops=2 * tokens * 64 * (units + width),
            bytes_accessed=2 * (tokens + 64) * (units + width),
            transcendentals=0,
        ),
        name="project",
    )(*operands)


def partners(dp):
    order = [m for far in (True, False) for m in range(1, dp - 1) if (2 * m >= dp) == far]
    return order[0::2], order[1::2]


def partner(dp, t):
    first, second = partners(dp)
    return jnp.where(lax.axis_index("tensor") == 0, first[t], second[t])


def pack_kernel(pb, rows_a, rows_b, part_ref, recv_ref, extra_ref, *refs):
    outs, total_ref = refs[:-1], refs[-1]
    total_ref[...] = part_ref[...] + recv_ref[...]
    ranks, lanes = total_ref.shape[0] // 2, total_ref.shape[1]
    dp = extra_ref.shape[0]
    me = lax.axis_index("dp")
    lead = lax.axis_index("tensor") == 0

    def rows(out_ref, owner, pick):
        p, q = owner // pb, owner % pb
        out_ref[0:rows_a, :] = pick(total_ref[pl.ds(pl.multiple_of(p * rows_a, rows_a), rows_a), :])
        out_ref[rows_a:rows_a + rows_b, :] = pick(total_ref[pl.ds(pl.multiple_of(ranks + q * rows_b, rows_b), rows_b), :])
        out_ref[rows_a + rows_b:, :] = pick(extra_ref[owner])

    def half(x):
        return jnp.where(lead, x[:, :lanes // 2], x[:, lanes // 2:])

    for t, out_ref in enumerate(outs[:-2]):
        rows(out_ref, me ^ partner(dp, t), lambda x: x)
    rows(outs[-2], me ^ (dp - 1), half)
    rows(outs[-1], me, half)


def pack(part, recv, extra, pa, pb):
    ranks, lanes = part.shape[0] // 2, part.shape[1]
    rows_a, rows_b = ranks // pa, ranks // pb
    rows = rows_a + rows_b + extra.shape[1]
    count = pa * pb // 2 - 1
    whole, half = (jax.ShapeDtypeStruct((rows, n), jnp.float32) for n in (lanes, lanes // 2))
    return pl.pallas_call(
        functools.partial(pack_kernel, pb, rows_a, rows_b),
        out_shape=(whole,) * count + (half, half),
        in_specs=[VMEM] * 3,
        out_specs=(VMEM,) * (count + 2),
        scratch_shapes=[pltpu.VMEM(part.shape, jnp.float32)],
        compiler_params=vmem_params(16),
        name="pack",
    )(part, recv, extra)


def grads_kernel(rows_a, rows_b, docs, dp, *refs):
    xs, (out_ref, outer_ref, member_ref) = refs[:-3], refs[-3:]
    whole = xs[0].shape[1]
    wide = rows_a * rows_b
    first = rows_a + rows_b
    queries = out_ref.shape[0] - docs
    per = queries // dp
    place = lax.broadcasted_iota(jnp.int32, (queries, whole), 0)
    lane = lax.broadcasted_iota(jnp.int32, (queries, whole), 1)
    me = lax.axis_index("dp")
    core = lax.axis_index("tensor")
    mine = lane // (whole // 2) == core
    flat = [jnp.zeros((queries, whole), jnp.float32)] * (per * wide // whole)
    start = 0
    for t, x_ref in enumerate(xs):
        lanes = x_ref.shape[1]
        at = slice(start, start + lanes)
        start += lanes
        g, b = x_ref[0:rows_a, :], x_ref[rows_a:first, :]
        ids = x_ref[first:first + 1, :].astype(jnp.int32)
        doc = lax.broadcasted_iota(jnp.int32, (docs, lanes), 0)
        member_ref[:, at] = jnp.where(doc == ids, 1.0, 0.0).astype(jnp.bfloat16)
        outer = (g[:, None, :] * b[None, :, :]).reshape(wide, lanes)
        high = outer.astype(jnp.bfloat16)
        outer_ref[0:wide, at] = high
        outer_ref[wide:, at] = (outer - high.astype(jnp.float32)).astype(jnp.bfloat16)
        gap = partner(dp, t) if t < len(xs) - 2 else dp - 1 if t == len(xs) - 2 else 0
        held = place // per == me ^ gap
        if lanes < whole:
            held = jnp.logical_and(held, mine)
        for j in range(len(flat)):
            line = x_ref[first + 1 + j:first + 2 + j, :]
            if lanes < whole:
                line = jnp.concatenate([line, line], axis=1)
            flat[j] = jnp.where(held, line, flat[j])
    sums = lax.dot_general(member_ref[...], outer_ref[...], NT, preferred_element_type=jnp.float32)
    out_ref[0:docs, :] = (sums[:, wide:] + sums[:, :wide]) * (TOK_DEV ** -0.5)
    flat = jnp.concatenate(flat, axis=1)
    asked = jnp.zeros((queries, wide), jnp.float32)
    which = lax.broadcasted_iota(jnp.int32, (queries, wide), 0) % per
    for q in range(per):
        asked = jnp.where(which == q, flat[:, q * wide:(q + 1) * wide], asked)
    out_ref[docs:, :] = asked


def grads_of(xs, rows_a, rows_b, docs, queries, dp):
    tokens = sum(x.shape[1] for x in xs)
    wide = rows_a * rows_b
    return pl.pallas_call(
        functools.partial(grads_kernel, rows_a, rows_b, docs, dp),
        out_shape=jax.ShapeDtypeStruct((docs + queries, wide), jnp.float32),
        in_specs=[VMEM] * len(xs),
        out_specs=VMEM,
        scratch_shapes=[
            pltpu.VMEM((2 * wide, tokens), jnp.bfloat16),
            pltpu.VMEM((docs, tokens), jnp.bfloat16),
        ],
        compiler_params=vmem_params(40),
        name="grads",
    )(*xs)


def gram_kernel(docs, part_ref, recv_ref, out_ref):
    both = part_ref[...] + recv_ref[...]
    share = lax.dot_general(both, both[:docs], NT, precision=HIGHEST, preferred_element_type=jnp.float32)
    half = share.shape[0] // 2
    out_ref[...] = jnp.concatenate([share[:half], share[half:]], axis=1)


def gram(part, recv, docs):
    return pl.pallas_call(
        functools.partial(gram_kernel, docs),
        out_shape=jax.ShapeDtypeStruct((part.shape[0] // 2, 2 * docs), jnp.float32),
        in_specs=[VMEM] * 2,
        out_specs=VMEM,
        compiler_params=vmem_params(16),
        name="gram",
    )(part, recv)


def solve_kernel(docs, queries, scale, x_ref, recv_ref, out_ref, done_ref):
    total = x_ref[...] + recv_ref[...]
    stack = jnp.concatenate([total[:, :docs], total[:, docs:]], axis=0)
    cols = done_ref.shape[1]
    stack = jnp.concatenate([stack, jnp.zeros((cols - stack.shape[0], docs), jnp.float32)], axis=0)
    total = stack.T
    row = lax.broadcasted_iota(jnp.int32, (docs, cols), 0)
    col = lax.broadcasted_iota(jnp.int32, (docs, cols), 1)
    mean_diag = jnp.sum(jnp.where(row == col, total, 0.0)) * (1.0 / docs)
    work = total + jnp.where(row == col, 0.1 * mean_diag, 0.0)
    size = 8
    here = lax.broadcasted_iota(jnp.int32, (size, cols), 0)
    rows = [work[i:i + size] for i in range(0, docs, size)]
    for r in range(len(rows)):
        wide = [[jnp.broadcast_to(x[:, c:c + 1], (size, cols)) for c in range(r * size, (r + 1) * size)] for x in rows]
        pivot, line = wide[r], rows[r]
        for j in range(size):
            inverse = 1.0 / pivot[j][j:j + 1]
            factor = jnp.where(here == j, 1.0 - inverse, pivot[j] * inverse)
            pivot = [x if i <= j else x - factor * x[j:j + 1] for i, x in enumerate(pivot)]
            line = line - factor * line[j:j + 1]
        for s in range(len(rows)):
            if s == r:
                rows[s] = line
            else:
                terms = [wide[s][j] * line[j:j + 1] for j in range(size)]
                rows[s] = rows[s] - (((terms[0] + terms[1]) + (terms[2] + terms[3]))
                                     + ((terms[4] + terms[5]) + (terms[6] + terms[7])))
    for r, x in enumerate(rows):
        done_ref[r * size:(r + 1) * size, :] = x * (mean_diag * scale)
    mine = pl.ds(pl.multiple_of(lax.axis_index("dp") * DOC_DEV, DOC_DEV), DOC_DEV)
    out_ref[...] = done_ref[mine, :][:, docs:docs + queries]


def solve(x, recv, docs, queries, scale):
    return pl.pallas_call(
        functools.partial(solve_kernel, docs, queries, scale),
        out_shape=jax.ShapeDtypeStruct((DOC_DEV, queries), jnp.float32),
        in_specs=[VMEM] * 2,
        out_specs=VMEM,
        scratch_shapes=[pltpu.VMEM((docs, -(-(docs + queries) // LANES) * LANES), jnp.float32)],
        compiler_params=vmem_params(16),
        name="solve",
    )(x, recv)


def solve_large(total, docs, queries, scale):
    kernel = total[:, :docs]
    mean_diag = jnp.trace(kernel) / docs
    factor = jnp.linalg.cholesky(kernel + 0.1 * mean_diag * jnp.eye(docs, dtype=jnp.float32))
    solved = jax.scipy.linalg.cho_solve((factor, True), total[:, docs:docs + queries]) * (mean_diag * scale)
    return lax.dynamic_slice_in_dim(solved, lax.axis_index("dp") * DOC_DEV, DOC_DEV, 0)


def swap_cores(x):
    cores = lax.axis_size("tensor")
    return lax.ppermute(x, "tensor", [(i, cores - 1 - i) for i in range(cores)])


def trade(xs):
    dp = lax.axis_size("dp")
    got = []
    for x, ms in zip(xs, zip(*partners(dp))):
        pairs = [(i * 2 + k, (i ^ m) * 2 + k) for i in range(dp) for k, m in enumerate(ms)]
        got.append(lax.ppermute(x, ("dp", "tensor"), pairs))
    return got


def trade_last(x):
    dp = lax.axis_size("dp")
    return lax.ppermute(x, "dp", [(i, i ^ (dp - 1)) for i in range(dp)])


def local(hidden, out_grad, proj_in, proj_out, doc_ids, queries):
    dp = lax.axis_size("dp")
    docs, num_queries = DOC_DEV * dp, queries.shape[0] * dp
    ranks = proj_in.shape[1]
    pa = 1
    while pa * pa < dp:
        pa *= 2
    pb = dp // pa
    rows_a, rows_b = ranks // pa, ranks // pb

    part = project(hidden, out_grad, proj_in.T, proj_out.T)
    recv = swap_cores(part)

    lanes = part.shape[1]
    ids = doc_ids.astype(jnp.float32)
    asked = queries.reshape(-1, pa, rows_a, pb, rows_b).transpose(1, 3, 0, 2, 4).reshape(dp, -1, lanes)
    extra = jnp.concatenate([jnp.broadcast_to(ids, (dp, 1, lanes)), asked], axis=1)
    extra = jnp.pad(extra, ((0, 0), (0, -extra.shape[1] % 8), (0, 0)))

    *blocks, last, own = pack(part, recv, extra, pa, pb)
    blocks = trade(blocks) + [trade_last(last), own]
    grads = grads_of(blocks, rows_a, rows_b, docs, num_queries, dp)
    share = gram(grads, swap_cores(grads), docs)
    scale = float(ranks * ranks) ** -0.5
    if docs <= 64:
        halves = jnp.where(lax.axis_index("tensor") == 0, share, trade_last(share))
        share = sum(trade([share] * (dp // 2 - 1)), halves)
        return solve(share, swap_cores(share), docs, num_queries, scale).T
    share = lax.psum(share, "dp")
    return solve_large(jnp.concatenate([share[:, :docs], share[:, docs:]], axis=0).T, docs, num_queries, scale).T


def solution(mesh):
    return jax.shard_map(
        local,
        mesh=mesh,
        in_specs=(
            P(("groups", "dp"), "tensor"),
            P(("groups", "dp"), "tensor"),
            P("tensor", None),
            P("tensor", None),
            P(("groups", "dp")),
            P(("groups", "dp"), None),
        ),
        out_specs=P("groups", "dp"),
        check_vma=False,
    )
```

```python
import functools

import jax
import jax.numpy as jnp
from jax import lax
from jax.experimental import pallas as pl
from jax.experimental.pallas import tpu as pltpu
from jax.sharding import PartitionSpec as P

TOK_DEV = 256
DOC_DEV = 8
LANES = 128
DEPTH = 256
FLIGHT = 8
NT = (((1,), (1,)), ((), ()))
HIGHEST = lax.Precision.HIGHEST
VMEM = pl.BlockSpec(memory_space=pltpu.VMEM)
HBM = pl.BlockSpec(memory_space=pltpu.HBM)


def vmem_params(mib):
    return pltpu.CompilerParams(vmem_limit_bytes=int(mib * (1 << 20)))


def chunks_of(length, most=1024):
    size = most
    while length % size:
        size //= 2
    return size, length // size


def project_kernel(sizes, h_ref, g_ref, pin_ref, pout_ref, out_ref, h_buf, g_buf, pin_buf, pout_buf, sems):
    h_size, h_count, g_size, g_count = sizes
    copies, order = {}, []

    def copy(name, src, dst):
        copies[name] = pltpu.make_async_copy(src, dst, sems.at[len(copies)])
        order.append(name)
        if len(order) <= FLIGHT:
            copies[name].start(priority=(len(order) - 1) % 2)

    def arrive(name):
        copies[name].wait()
        ahead = order.index(name) + FLIGHT
        if ahead < len(order):
            copies[order[ahead]].start(priority=ahead % 2)

    copy("po", pout_ref, pout_buf)
    for i in range(g_count):
        at = pl.ds(i * g_size, g_size)
        copy(("g", i), g_ref.at[:, at], g_buf.at[:, at])
    copy("pi", pin_ref, pin_buf)
    for i in range(h_count):
        at = pl.ds(i * h_size, h_size)
        copy(("h", i), h_ref.at[:, at], h_buf.at[:, at])

    def run(tag, count, size, proj, data):
        total = None
        depth = min(size, DEPTH)
        for i in range(count):
            arrive((tag, i))
            parts = []
            for j in range(size // depth):
                at = pl.ds(i * size + j * depth, depth)
                parts.append(lax.dot_general(data[:, at], proj[:, at], NT, preferred_element_type=jnp.float32))
            part = sum(parts[1:], parts[0])
            total = part if total is None else total + part
        return total

    arrive("po")
    grad = run("g", g_count, g_size, pout_buf, g_buf)
    arrive("pi")
    inp = run("h", h_count, h_size, pin_buf, h_buf)
    out_ref[...] = jnp.concatenate([grad, inp], axis=1).T


def project(hidden, out_grad, pin_t, pout_t):
    tokens, units = hidden.shape
    width = out_grad.shape[1]
    ranks = pin_t.shape[0] + pout_t.shape[0]
    h_size, h_count = chunks_of(units)
    g_size, g_count = chunks_of(width)
    return pl.pallas_call(
        functools.partial(project_kernel, (h_size, h_count, g_size, g_count)),
        out_shape=jax.ShapeDtypeStruct((ranks, tokens), jnp.float32),
        in_specs=[HBM] * 4,
        out_specs=VMEM,
        scratch_shapes=[
            pltpu.VMEM(hidden.shape, hidden.dtype),
            pltpu.VMEM(out_grad.shape, out_grad.dtype),
            pltpu.VMEM(pin_t.shape, pin_t.dtype),
            pltpu.VMEM(pout_t.shape, pout_t.dtype),
            pltpu.SemaphoreType.DMA((2 + g_count + h_count,)),
        ],
        compiler_params=vmem_params(53.5),
        cost_estimate=pl.CostEstimate(
            flops=2 * tokens * 64 * (units + width),
            bytes_accessed=2 * (tokens + 64) * (units + width),
            transcendentals=0,
        ),
        name="project",
    )(hidden, out_grad, pin_t, pout_t)


def partners(dp):
    order = [m for far in (True, False) for m in range(1, dp - 1) if (2 * m >= dp) == far]
    return order[0::2], order[1::2]


def partner(dp, t):
    first, second = partners(dp)
    return jnp.where(lax.axis_index("tensor") == 0, first[t], second[t])


def pack_kernel(pb, rows_a, rows_b, part_ref, recv_ref, extra_ref, *refs):
    outs, total_ref = refs[:-1], refs[-1]
    total_ref[...] = part_ref[...] + recv_ref[...]
    ranks, lanes = total_ref.shape[0] // 2, total_ref.shape[1]
    dp = extra_ref.shape[0]
    me = lax.axis_index("dp")
    lead = lax.axis_index("tensor") == 0

    def rows(out_ref, owner, pick):
        p, q = owner // pb, owner % pb
        out_ref[0:rows_a, :] = pick(total_ref[pl.ds(pl.multiple_of(p * rows_a, rows_a), rows_a), :])
        out_ref[rows_a:rows_a + rows_b, :] = pick(total_ref[pl.ds(pl.multiple_of(ranks + q * rows_b, rows_b), rows_b), :])
        out_ref[rows_a + rows_b:, :] = pick(extra_ref[owner])

    def half(x):
        return jnp.where(lead, x[:, :lanes // 2], x[:, lanes // 2:])

    for t, out_ref in enumerate(outs[:-2]):
        rows(out_ref, me ^ partner(dp, t), lambda x: x)
    rows(outs[-2], me ^ (dp - 1), half)
    rows(outs[-1], me, half)


def pack(part, recv, extra, pa, pb):
    ranks, lanes = part.shape[0] // 2, part.shape[1]
    rows_a, rows_b = ranks // pa, ranks // pb
    rows = rows_a + rows_b + extra.shape[1]
    count = pa * pb // 2 - 1
    whole, half = (jax.ShapeDtypeStruct((rows, n), jnp.float32) for n in (lanes, lanes // 2))
    return pl.pallas_call(
        functools.partial(pack_kernel, pb, rows_a, rows_b),
        out_shape=(whole,) * count + (half, half),
        in_specs=[VMEM] * 3,
        out_specs=(VMEM,) * (count + 2),
        scratch_shapes=[pltpu.VMEM(part.shape, jnp.float32)],
        compiler_params=vmem_params(16),
        name="pack",
    )(part, recv, extra)


def grads_kernel(rows_a, rows_b, docs, dp, whole, gaps, *refs):
    xs, before, (out_ref, outer_ref, member_ref) = refs[:len(gaps)], refs[len(gaps):-3], refs[-3:]
    wide = rows_a * rows_b
    first = rows_a + rows_b
    queries = out_ref.shape[0] - docs
    per = queries // dp
    place = lax.broadcasted_iota(jnp.int32, (queries, whole), 0)
    lane = lax.broadcasted_iota(jnp.int32, (queries, whole), 1)
    me = lax.axis_index("dp")
    core = lax.axis_index("tensor")
    mine = lane // (whole // 2) == core
    flat = [jnp.zeros((queries, whole), jnp.float32)] * (per * wide // whole)
    start = 0
    for x_ref, gap in zip(xs, gaps):
        lanes = x_ref.shape[1]
        at = slice(start, start + lanes)
        start += lanes
        g, b = x_ref[0:rows_a, :], x_ref[rows_a:first, :]
        ids = x_ref[first:first + 1, :].astype(jnp.int32)
        doc = lax.broadcasted_iota(jnp.int32, (docs, lanes), 0)
        member_ref[:, at] = jnp.where(doc == ids, 1.0, 0.0).astype(jnp.bfloat16)
        outer = (g[:, None, :] * b[None, :, :]).reshape(wide, lanes)
        high = outer.astype(jnp.bfloat16)
        outer_ref[0:wide, at] = high
        outer_ref[wide:, at] = (outer - high.astype(jnp.float32)).astype(jnp.bfloat16)
        held = place // per == me ^ jnp.where(core == 0, gap[0], gap[1])
        if lanes < whole:
            held = jnp.logical_and(held, mine)
        for j in range(len(flat)):
            line = x_ref[first + 1 + j:first + 2 + j, :]
            if lanes < whole:
                line = jnp.concatenate([line, line], axis=1)
            flat[j] = jnp.where(held, line, flat[j])
    sums = lax.dot_general(member_ref[...], outer_ref[...], NT, preferred_element_type=jnp.float32)
    sums = (sums[:, wide:] + sums[:, :wide]) * (TOK_DEV ** -0.5)
    flat = jnp.concatenate(flat, axis=1)
    asked = jnp.zeros((queries, wide), jnp.float32)
    which = lax.broadcasted_iota(jnp.int32, (queries, wide), 0) % per
    for q in range(per):
        asked = jnp.where(which == q, flat[:, q * wide:(q + 1) * wide], asked)
    if before:
        sums, asked = sums + before[0][0:docs, :], asked + before[0][docs:, :]
    out_ref[0:docs, :] = sums
    out_ref[docs:, :] = asked


def grads_of(xs, gaps, before, rows_a, rows_b, docs, queries, dp, whole):
    tokens = sum(x.shape[1] for x in xs)
    wide = rows_a * rows_b
    operands = (*xs, *before)
    return pl.pallas_call(
        functools.partial(grads_kernel, rows_a, rows_b, docs, dp, whole, gaps),
        out_shape=jax.ShapeDtypeStruct((docs + queries, wide), jnp.float32),
        in_specs=[VMEM] * len(operands),
        out_specs=VMEM,
        scratch_shapes=[
            pltpu.VMEM((2 * wide, tokens), jnp.bfloat16),
            pltpu.VMEM((docs, tokens), jnp.bfloat16),
        ],
        compiler_params=vmem_params(40),
        cost_estimate=pl.CostEstimate(
            flops=4 * docs * wide * tokens, bytes_accessed=4 * (rows_a + rows_b) * tokens, transcendentals=0
        ),
        name="grads",
    )(*operands)


def gram_kernel(docs, part_ref, recv_ref, out_ref):
    both = part_ref[...] + recv_ref[...]
    share = lax.dot_general(both, both[:docs], NT, precision=HIGHEST, preferred_element_type=jnp.float32)
    half = share.shape[0] // 2
    out_ref[...] = jnp.concatenate([share[:half], share[half:]], axis=1)


def gram(part, recv, docs):
    return pl.pallas_call(
        functools.partial(gram_kernel, docs),
        out_shape=jax.ShapeDtypeStruct((part.shape[0] // 2, 2 * docs), jnp.float32),
        in_specs=[VMEM] * 2,
        out_specs=VMEM,
        compiler_params=vmem_params(16),
        name="gram",
    )(part, recv)


def solve_kernel(docs, queries, scale, x_ref, recv_ref, out_ref, done_ref):
    total = x_ref[...] + recv_ref[...]
    stack = jnp.concatenate([total[:, :docs], total[:, docs:]], axis=0)
    cols = done_ref.shape[1]
    stack = jnp.concatenate([stack, jnp.zeros((cols - stack.shape[0], docs), jnp.float32)], axis=0)
    total = stack.T
    row = lax.broadcasted_iota(jnp.int32, (docs, cols), 0)
    col = lax.broadcasted_iota(jnp.int32, (docs, cols), 1)
    mean_diag = jnp.sum(jnp.where(row == col, total, 0.0)) * (1.0 / docs)
    work = total + jnp.where(row == col, 0.1 * mean_diag, 0.0)
    size = 8
    here = lax.broadcasted_iota(jnp.int32, (size, cols), 0)
    rows = [work[i:i + size] for i in range(0, docs, size)]
    for r in range(len(rows)):
        wide = [[jnp.broadcast_to(x[:, c:c + 1], (size, cols)) for c in range(r * size, (r + 1) * size)] for x in rows]
        pivot, line = wide[r], rows[r]
        for j in range(size):
            inverse = 1.0 / pivot[j][j:j + 1]
            factor = jnp.where(here == j, 1.0 - inverse, pivot[j] * inverse)
            pivot = [x if i <= j else x - factor * x[j:j + 1] for i, x in enumerate(pivot)]
            line = line - factor * line[j:j + 1]
        for s in range(len(rows)):
            if s == r:
                rows[s] = line
            else:
                terms = [wide[s][j] * line[j:j + 1] for j in range(size)]
                rows[s] = rows[s] - (((terms[0] + terms[1]) + (terms[2] + terms[3]))
                                     + ((terms[4] + terms[5]) + (terms[6] + terms[7])))
    for r, x in enumerate(rows):
        done_ref[r * size:(r + 1) * size, :] = x * (mean_diag * scale)
    mine = pl.ds(pl.multiple_of(lax.axis_index("dp") * DOC_DEV, DOC_DEV), DOC_DEV)
    out_ref[...] = done_ref[mine, :][:, docs:docs + queries]


def solve(x, recv, docs, queries, scale):
    return pl.pallas_call(
        functools.partial(solve_kernel, docs, queries, scale),
        out_shape=jax.ShapeDtypeStruct((DOC_DEV, queries), jnp.float32),
        in_specs=[VMEM] * 2,
        out_specs=VMEM,
        scratch_shapes=[pltpu.VMEM((docs, -(-(docs + queries) // LANES) * LANES), jnp.float32)],
        compiler_params=vmem_params(16),
        name="solve",
    )(x, recv)


def solve_large(total, docs, queries, scale):
    kernel = total[:, :docs]
    mean_diag = jnp.trace(kernel) / docs
    factor = jnp.linalg.cholesky(kernel + 0.1 * mean_diag * jnp.eye(docs, dtype=jnp.float32))
    solved = jax.scipy.linalg.cho_solve((factor, True), total[:, docs:docs + queries]) * (mean_diag * scale)
    return lax.dynamic_slice_in_dim(solved, lax.axis_index("dp") * DOC_DEV, DOC_DEV, 0)


def swap_cores(x):
    cores = lax.axis_size("tensor")
    return lax.ppermute(x, "tensor", [(i, cores - 1 - i) for i in range(cores)])


def trade(xs):
    dp = lax.axis_size("dp")
    got = []
    for x, ms in zip(xs, zip(*partners(dp))):
        pairs = [(i * 2 + k, (i ^ m) * 2 + k) for i in range(dp) for k, m in enumerate(ms)]
        got.append(lax.ppermute(x, ("dp", "tensor"), pairs))
    return got


def trade_last(x):
    dp = lax.axis_size("dp")
    return lax.ppermute(x, "dp", [(i, i ^ (dp - 1)) for i in range(dp)])


def local(hidden, out_grad, proj_in, proj_out, doc_ids, queries):
    dp = lax.axis_size("dp")
    docs, num_queries = DOC_DEV * dp, queries.shape[0] * dp
    ranks = proj_in.shape[1]
    pa = 1
    while pa * pa < dp:
        pa *= 2
    pb = dp // pa
    rows_a, rows_b = ranks // pa, ranks // pb

    part = project(hidden, out_grad, proj_in.T, proj_out.T)
    recv = swap_cores(part)

    lanes = part.shape[1]
    ids = doc_ids.astype(jnp.float32)
    asked = queries.reshape(-1, pa, rows_a, pb, rows_b).transpose(1, 3, 0, 2, 4).reshape(dp, -1, lanes)
    extra = jnp.concatenate([jnp.broadcast_to(ids, (dp, 1, lanes)), asked], axis=1)
    extra = jnp.pad(extra, ((0, 0), (0, -extra.shape[1] % 8), (0, 0)))

    *blocks, last, own = pack(part, recv, extra, pa, pb)
    gaps = list(zip(*partners(dp)))
    sizes = (rows_a, rows_b, docs, num_queries, dp, lanes)
    last = trade_last(last)
    grads = grads_of(trade(blocks) + [own], gaps + [(0, 0)], (), *sizes)
    grads = grads_of([last], [(dp - 1, dp - 1)], (grads,), *sizes)
    share = gram(grads, swap_cores(grads), docs)
    scale = float(ranks * ranks) ** -0.5
    if docs <= 64:
        halves = jnp.where(lax.axis_index("tensor") == 0, share, trade_last(share))
        share = sum(trade([share] * (dp // 2 - 1)), halves)
        return solve(share, swap_cores(share), docs, num_queries, scale).T
    share = lax.psum(share, "dp")
    return solve_large(jnp.concatenate([share[:, :docs], share[:, docs:]], axis=0).T, docs, num_queries, scale).T


def solution(mesh):
    return jax.shard_map(
        local,
        mesh=mesh,
        in_specs=(
            P(("groups", "dp"), "tensor"),
            P(("groups", "dp"), "tensor"),
            P("tensor", None),
            P("tensor", None),
            P(("groups", "dp")),
            P(("groups", "dp"), None),
        ),
        out_specs=P("groups", "dp"),
        check_vma=False,
    )
```

```python
import functools

import jax
import jax.numpy as jnp
from jax import lax
from jax.experimental import pallas as pl
from jax.experimental.pallas import tpu as pltpu
from jax.sharding import PartitionSpec as P

TOK_DEV = 256
DOC_DEV = 8
LANES = 128
DEPTH = 256
FLIGHT = 7
NT = (((1,), (1,)), ((), ()))
HIGHEST = lax.Precision.HIGHEST
VMEM = pl.BlockSpec(memory_space=pltpu.VMEM)
HBM = pl.BlockSpec(memory_space=pltpu.HBM)


def vmem_params(mib):
    return pltpu.CompilerParams(vmem_limit_bytes=int(mib * (1 << 20)))


def chunks_of(length, ramp, tail):
    left = length // DEPTH - sum(ramp) - sum(tail)
    sizes = [*ramp, *([4] * (left // 4)), *([left % 4] if left % 4 else []), *tail]
    starts = [sum(sizes[:i]) for i in range(len(sizes))]
    return [(start * DEPTH, size * DEPTH) for start, size in zip(starts, sizes)]


def project_kernel(g_chunks, h_chunks, h_ref, g_ref, pin_ref, pout_ref, out_ref, h_buf, g_buf, pin_buf, pout_buf, sems):
    plan = [(pout_ref, pout_buf, g_ref, g_buf, at) for at in g_chunks] + [(pin_ref, pin_buf, h_ref, h_buf, at) for at in h_chunks]
    copies = []
    for i, (proj, proj_buf, data, data_buf, (start, size)) in enumerate(plan):
        at = pl.ds(start, size)
        copies.append((
            pltpu.make_async_copy(proj.at[:, at], proj_buf.at[:, at], sems.at[2 * i]),
            pltpu.make_async_copy(data.at[:, at], data_buf.at[:, at], sems.at[2 * i + 1]),
        ))

    def start(i):
        if i < len(copies):
            for copy in copies[i]:
                copy.start()

    for i in range(FLIGHT):
        start(i)
    totals = [None, None]
    for i, (_, proj_buf, _, data_buf, (first, size)) in enumerate(plan):
        for copy in copies[i]:
            copy.wait()
        start(i + FLIGHT)
        which = 0 if i < len(g_chunks) else 1
        for j in range(first, first + size, DEPTH):
            at = pl.ds(j, DEPTH)
            part = lax.dot_general(proj_buf[:, at], data_buf[:, at], NT, preferred_element_type=jnp.float32)
            totals[which] = part if totals[which] is None else totals[which] + part
    ranks = totals[0].shape[0]
    out_ref[0:ranks, :] = totals[0]
    out_ref[ranks:, :] = totals[1]


def project(hidden, out_grad, pin_t, pout_t):
    tokens, units = hidden.shape
    width = out_grad.shape[1]
    ranks = pin_t.shape[0] + pout_t.shape[0]
    operands = (hidden, out_grad, pin_t, pout_t)
    g_chunks = chunks_of(width, (1, 2, 3), ())
    h_chunks = chunks_of(units, (), (3, 1))
    return pl.pallas_call(
        functools.partial(project_kernel, g_chunks, h_chunks),
        out_shape=jax.ShapeDtypeStruct((ranks, tokens), jnp.float32),
        in_specs=[HBM] * 4,
        out_specs=VMEM,
        scratch_shapes=[pltpu.VMEM(x.shape, x.dtype) for x in operands]
        + [pltpu.SemaphoreType.DMA((2 * len(g_chunks + h_chunks),))],
        compiler_params=vmem_params(53.5),
        cost_estimate=pl.CostEstimate(
            flops=2 * tokens * 64 * (units + width),
            bytes_accessed=2 * (tokens + 64) * (units + width),
            transcendentals=0,
        ),
        name="project",
    )(*operands)


def partners(dp):
    order = [m for far in (True, False) for m in range(1, dp - 1) if (2 * m >= dp) == far]
    return order[0::2], order[1::2]


def partner(dp, t):
    first, second = partners(dp)
    return jnp.where(lax.axis_index("tensor") == 0, first[t], second[t])


def pack_kernel(pb, rows_a, rows_b, part_ref, recv_ref, extra_ref, *refs):
    outs, total_ref = refs[:-1], refs[-1]
    total_ref[...] = part_ref[...] + recv_ref[...]
    ranks, lanes = total_ref.shape[0] // 2, total_ref.shape[1]
    dp = extra_ref.shape[0]
    me = lax.axis_index("dp")
    lead = lax.axis_index("tensor") == 0

    def rows(out_ref, owner, pick):
        p, q = owner // pb, owner % pb
        out_ref[0:rows_a, :] = pick(total_ref[pl.ds(pl.multiple_of(p * rows_a, rows_a), rows_a), :])
        out_ref[rows_a:rows_a + rows_b, :] = pick(total_ref[pl.ds(pl.multiple_of(ranks + q * rows_b, rows_b), rows_b), :])
        out_ref[rows_a + rows_b:, :] = pick(extra_ref[owner])

    def half(x):
        return jnp.where(lead, x[:, :lanes // 2], x[:, lanes // 2:])

    for t, out_ref in enumerate(outs[:-2]):
        rows(out_ref, me ^ partner(dp, t), lambda x: x)
    rows(outs[-2], me ^ (dp - 1), half)
    rows(outs[-1], me, half)


def pack(part, recv, extra, pa, pb):
    ranks, lanes = part.shape[0] // 2, part.shape[1]
    rows_a, rows_b = ranks // pa, ranks // pb
    rows = rows_a + rows_b + extra.shape[1]
    count = pa * pb // 2 - 1
    whole, half = (jax.ShapeDtypeStruct((rows, n), jnp.float32) for n in (lanes, lanes // 2))
    return pl.pallas_call(
        functools.partial(pack_kernel, pb, rows_a, rows_b),
        out_shape=(whole,) * count + (half, half),
        in_specs=[VMEM] * 3,
        out_specs=(VMEM,) * (count + 2),
        scratch_shapes=[pltpu.VMEM(part.shape, jnp.float32)],
        compiler_params=vmem_params(16),
        name="pack",
    )(part, recv, extra)


def grads_kernel(rows_a, rows_b, docs, dp, whole, gaps, *refs):
    xs, before, (out_ref, outer_ref, member_ref) = refs[:len(gaps)], refs[len(gaps):-3], refs[-3:]
    wide = rows_a * rows_b
    first = rows_a + rows_b
    queries = out_ref.shape[0] - docs
    per = queries // dp
    place = lax.broadcasted_iota(jnp.int32, (queries, whole), 0)
    lane = lax.broadcasted_iota(jnp.int32, (queries, whole), 1)
    me = lax.axis_index("dp")
    core = lax.axis_index("tensor")
    mine = lane // (whole // 2) == core
    flat = [jnp.zeros((queries, whole), jnp.float32)] * (per * wide // whole)
    start = 0
    for x_ref, gap in zip(xs, gaps):
        lanes = x_ref.shape[1]
        at = slice(start, start + lanes)
        start += lanes
        g, b = x_ref[0:rows_a, :], x_ref[rows_a:first, :]
        ids = x_ref[first:first + 1, :].astype(jnp.int32)
        doc = lax.broadcasted_iota(jnp.int32, (docs, lanes), 0)
        member_ref[:, at] = jnp.where(doc == ids, 1.0, 0.0).astype(jnp.bfloat16)
        outer = (g[:, None, :] * b[None, :, :]).reshape(wide, lanes)
        high = outer.astype(jnp.bfloat16)
        outer_ref[0:wide, at] = high
        outer_ref[wide:, at] = (outer - high.astype(jnp.float32)).astype(jnp.bfloat16)
        held = place // per == me ^ jnp.where(core == 0, gap[0], gap[1])
        if lanes < whole:
            held = jnp.logical_and(held, mine)
        for j in range(len(flat)):
            line = x_ref[first + 1 + j:first + 2 + j, :]
            if lanes < whole:
                line = jnp.concatenate([line, line], axis=1)
            flat[j] = jnp.where(held, line, flat[j])
    sums = lax.dot_general(member_ref[...], outer_ref[...], NT, preferred_element_type=jnp.float32)
    sums = (sums[:, wide:] + sums[:, :wide]) * (TOK_DEV ** -0.5)
    flat = jnp.concatenate(flat, axis=1)
    asked = jnp.zeros((queries, wide), jnp.float32)
    which = lax.broadcasted_iota(jnp.int32, (queries, wide), 0) % per
    for q in range(per):
        asked = jnp.where(which == q, flat[:, q * wide:(q + 1) * wide], asked)
    if before:
        sums, asked = sums + before[0][0:docs, :], asked + before[0][docs:, :]
    out_ref[0:docs, :] = sums
    out_ref[docs:, :] = asked


def grads_of(xs, gaps, before, rows_a, rows_b, docs, queries, dp, whole):
    tokens = sum(x.shape[1] for x in xs)
    wide = rows_a * rows_b
    operands = (*xs, *before)
    return pl.pallas_call(
        functools.partial(grads_kernel, rows_a, rows_b, docs, dp, whole, gaps),
        out_shape=jax.ShapeDtypeStruct((docs + queries, wide), jnp.float32),
        in_specs=[VMEM] * len(operands),
        out_specs=VMEM,
        scratch_shapes=[
            pltpu.VMEM((2 * wide, tokens), jnp.bfloat16),
            pltpu.VMEM((docs, tokens), jnp.bfloat16),
        ],
        compiler_params=vmem_params(40),
        cost_estimate=pl.CostEstimate(
            flops=4 * docs * wide * tokens, bytes_accessed=4 * (rows_a + rows_b) * tokens, transcendentals=0
        ),
        name="grads",
    )(*operands)


def gram_kernel(docs, part_ref, recv_ref, out_ref):
    both = part_ref[...] + recv_ref[...]
    share = lax.dot_general(both, both[:docs], NT, precision=HIGHEST, preferred_element_type=jnp.float32)
    half = share.shape[0] // 2
    out_ref[...] = jnp.concatenate([share[:half], share[half:]], axis=1)


def gram(part, recv, docs):
    return pl.pallas_call(
        functools.partial(gram_kernel, docs),
        out_shape=jax.ShapeDtypeStruct((part.shape[0] // 2, 2 * docs), jnp.float32),
        in_specs=[VMEM] * 2,
        out_specs=VMEM,
        compiler_params=vmem_params(16),
        name="gram",
    )(part, recv)


def solve_kernel(docs, queries, scale, x_ref, recv_ref, out_ref, done_ref):
    total = x_ref[...] + recv_ref[...]
    stack = jnp.concatenate([total[:, :docs], total[:, docs:]], axis=0)
    cols = done_ref.shape[1]
    stack = jnp.concatenate([stack, jnp.zeros((cols - stack.shape[0], docs), jnp.float32)], axis=0)
    total = stack.T
    row = lax.broadcasted_iota(jnp.int32, (docs, cols), 0)
    col = lax.broadcasted_iota(jnp.int32, (docs, cols), 1)
    mean_diag = jnp.sum(jnp.where(row == col, total, 0.0)) * (1.0 / docs)
    work = total + jnp.where(row == col, 0.1 * mean_diag, 0.0)
    size = 8
    here = lax.broadcasted_iota(jnp.int32, (size, cols), 0)
    rows = [work[i:i + size] for i in range(0, docs, size)]
    for r in range(len(rows)):
        wide = [[jnp.broadcast_to(x[:, c:c + 1], (size, cols)) for c in range(r * size, (r + 1) * size)] for x in rows]
        pivot, line = wide[r], rows[r]
        scale_rows = jnp.ones((size, cols), jnp.float32)
        for j in range(size):
            inverse = 1.0 / pivot[j][j:j + 1]
            factor = jnp.where(here == j, 0.0, pivot[j]) * inverse
            pivot = [x if i <= j else x - factor * x[j:j + 1] for i, x in enumerate(pivot)]
            line = line - factor * line[j:j + 1]
            scale_rows = jnp.where(here == j, inverse, scale_rows)
        line = line * scale_rows
        for s in range(len(rows)):
            if s == r:
                rows[s] = line
            else:
                terms = [wide[s][j] * line[j:j + 1] for j in range(size)]
                rows[s] = rows[s] - (((terms[0] + terms[1]) + (terms[2] + terms[3]))
                                     + ((terms[4] + terms[5]) + (terms[6] + terms[7])))
    for r, x in enumerate(rows):
        done_ref[r * size:(r + 1) * size, :] = x * (mean_diag * scale)
    mine = pl.ds(pl.multiple_of(lax.axis_index("dp") * DOC_DEV, DOC_DEV), DOC_DEV)
    out_ref[...] = done_ref[mine, :][:, docs:docs + queries]


def solve(x, recv, docs, queries, scale):
    return pl.pallas_call(
        functools.partial(solve_kernel, docs, queries, scale),
        out_shape=jax.ShapeDtypeStruct((DOC_DEV, queries), jnp.float32),
        in_specs=[VMEM] * 2,
        out_specs=VMEM,
        scratch_shapes=[pltpu.VMEM((docs, -(-(docs + queries) // LANES) * LANES), jnp.float32)],
        compiler_params=vmem_params(16),
        name="solve",
    )(x, recv)


def solve_large(total, docs, queries, scale):
    kernel = total[:, :docs]
    mean_diag = jnp.trace(kernel) / docs
    factor = jnp.linalg.cholesky(kernel + 0.1 * mean_diag * jnp.eye(docs, dtype=jnp.float32))
    solved = jax.scipy.linalg.cho_solve((factor, True), total[:, docs:docs + queries]) * (mean_diag * scale)
    return lax.dynamic_slice_in_dim(solved, lax.axis_index("dp") * DOC_DEV, DOC_DEV, 0)


def swap_cores(x):
    cores = lax.axis_size("tensor")
    return lax.ppermute(x, "tensor", [(i, cores - 1 - i) for i in range(cores)])


def trade(xs):
    dp = lax.axis_size("dp")
    got = []
    for x, ms in zip(xs, zip(*partners(dp))):
        pairs = [(i * 2 + k, (i ^ m) * 2 + k) for i in range(dp) for k, m in enumerate(ms)]
        got.append(lax.ppermute(x, ("dp", "tensor"), pairs))
    return got


def trade_last(x):
    dp = lax.axis_size("dp")
    return lax.ppermute(x, "dp", [(i, i ^ (dp - 1)) for i in range(dp)])


def local(hidden, out_grad, proj_in, proj_out, doc_ids, queries):
    dp = lax.axis_size("dp")
    docs, num_queries = DOC_DEV * dp, queries.shape[0] * dp
    ranks = proj_in.shape[1]
    pa = 1
    while pa * pa < dp:
        pa *= 2
    pb = dp // pa
    rows_a, rows_b = ranks // pa, ranks // pb

    part = project(hidden, out_grad, proj_in.T, proj_out.T)
    recv = swap_cores(part)

    lanes = part.shape[1]
    ids = doc_ids.astype(jnp.float32)
    asked = queries.reshape(-1, pa, rows_a, pb, rows_b).transpose(1, 3, 0, 2, 4).reshape(dp, -1, lanes)
    extra = jnp.concatenate([jnp.broadcast_to(ids, (dp, 1, lanes)), asked], axis=1)
    extra = jnp.pad(extra, ((0, 0), (0, -extra.shape[1] % 8), (0, 0)))

    *blocks, last, own = pack(part, recv, extra, pa, pb)
    gaps = list(zip(*partners(dp)))
    sizes = (rows_a, rows_b, docs, num_queries, dp, lanes)
    last = trade_last(last)
    grads = grads_of(trade(blocks) + [own], gaps + [(0, 0)], (), *sizes)
    grads = grads_of([last], [(dp - 1, dp - 1)], (grads,), *sizes)
    share = gram(grads, swap_cores(grads), docs)
    scale = float(ranks * ranks) ** -0.5
    if docs <= 64:
        halves = jnp.where(lax.axis_index("tensor") == 0, share, trade_last(share))
        share = sum(trade([share] * (dp // 2 - 1)), halves)
        return solve(share, swap_cores(share), docs, num_queries, scale).T
    share = lax.psum(share, "dp")
    return solve_large(jnp.concatenate([share[:, :docs], share[:, docs:]], axis=0).T, docs, num_queries, scale).T


def solution(mesh):
    return jax.shard_map(
        local,
        mesh=mesh,
        in_specs=(
            P(("groups", "dp"), "tensor"),
            P(("groups", "dp"), "tensor"),
            P("tensor", None),
            P("tensor", None),
            P(("groups", "dp")),
            P(("groups", "dp"), None),
        ),
        out_specs=P("groups", "dp"),
        check_vma=False,
    )
```

```python
import functools

import jax
import jax.numpy as jnp
from jax import lax
from jax.experimental import pallas as pl
from jax.experimental.pallas import tpu as pltpu
from jax.sharding import PartitionSpec as P

TOK_DEV = 256
DOC_DEV = 8
LANES = 128
FLIGHT = 7
NT = (((1,), (1,)), ((), ()))
HIGHEST = lax.Precision.HIGHEST
VMEM = pl.BlockSpec(memory_space=pltpu.VMEM)
HBM = pl.BlockSpec(memory_space=pltpu.HBM)


def vmem_params(mib):
    return pltpu.CompilerParams(vmem_limit_bytes=int(mib * (1 << 20)))


def pieces(x):
    rows, units = x.shape
    split = x.reshape(rows // 8, 8, units // (2 * LANES), 2, LANES).transpose(0, 2, 3, 1, 4)
    return split.reshape(rows // 8, units // (2 * LANES), 16, LANES)


def chunks_of(length, ramp, tail):
    left = length - sum(ramp) - sum(tail)
    sizes = [*ramp, *([4] * (left // 4)), *([left % 4] if left % 4 else []), *tail]
    return [(sum(sizes[:i]), size) for i, size in enumerate(sizes)]


def project_kernel(g_chunks, h_chunks, h_ref, g_ref, pin_ref, pout_ref, out_ref, h_buf, g_buf, pin_buf, pout_buf, sems):
    plan = [(pout_ref, pout_buf, g_ref, g_buf, at) for at in g_chunks] + [(pin_ref, pin_buf, h_ref, h_buf, at) for at in h_chunks]
    copies = []
    for i, (proj, proj_buf, data, data_buf, (start, size)) in enumerate(plan):
        at = pl.ds(start, size)
        copies.append((
            pltpu.make_async_copy(proj.at[:, at], proj_buf.at[:, at], sems.at[2 * i]),
            pltpu.make_async_copy(data.at[:, at], data_buf.at[:, at], sems.at[2 * i + 1]),
        ))

    def start(i):
        if i < len(copies):
            for copy in copies[i]:
                copy.start()

    for i in range(FLIGHT):
        start(i)

    def line_up(ref, first, size):
        blocks = [ref[:, j].reshape(ref.shape[0] * 16, LANES) for j in range(first, first + size)]
        return jnp.concatenate(blocks, axis=1)

    totals = [None, None]
    for i, (_, proj_buf, _, data_buf, (first, size)) in enumerate(plan):
        for copy in copies[i]:
            copy.wait()
        start(i + FLIGHT)
        which = 0 if i < len(g_chunks) else 1
        for j in range(first, first + size, 2):
            n = min(2, first + size - j)
            part = lax.dot_general(
                line_up(proj_buf, j, n), line_up(data_buf, j, n), NT, preferred_element_type=jnp.float32
            )
            totals[which] = part if totals[which] is None else totals[which] + part

    spread = totals[0].shape[1]
    even = lax.broadcasted_iota(jnp.int32, (8, spread), 1) % 16 < 8
    lines = []
    for total in totals:
        for g in range(total.shape[0] // 16):
            lines.append(jnp.where(even, total[16 * g:16 * g + 8], total[16 * g + 8:16 * g + 16]))
    lane = lax.broadcasted_iota(jnp.int32, (spread, spread // 2), 0)
    token = lax.broadcasted_iota(jnp.int32, (spread, spread // 2), 1)
    fold = jnp.where(lane // 16 * 8 + lane % 8 == token, 1.0, 0.0)
    out_ref[...] = jnp.dot(
        jnp.concatenate(lines, axis=0), fold, precision=HIGHEST, preferred_element_type=jnp.float32
    )


def project(hidden, out_grad, pin_t, pout_t):
    tokens, units = hidden.shape
    width = out_grad.shape[1]
    ranks = pin_t.shape[0] + pout_t.shape[0]
    operands = [pieces(x) for x in (hidden, out_grad, pin_t, pout_t)]
    g_chunks = chunks_of(operands[1].shape[1], (2,), ())
    h_chunks = chunks_of(operands[0].shape[1], (), (2, 2))
    return pl.pallas_call(
        functools.partial(project_kernel, g_chunks, h_chunks),
        out_shape=jax.ShapeDtypeStruct((ranks, tokens), jnp.float32),
        in_specs=[HBM] * 4,
        out_specs=VMEM,
        scratch_shapes=[pltpu.VMEM(x.shape, x.dtype) for x in operands]
        + [pltpu.SemaphoreType.DMA((2 * len(g_chunks + h_chunks),))],
        compiler_params=vmem_params(53.5),
        cost_estimate=pl.CostEstimate(
            flops=2 * tokens * 64 * (units + width),
            bytes_accessed=2 * (tokens + 64) * (units + width),
            transcendentals=0,
        ),
        name="project",
    )(*operands)


def partners(dp):
    order = [m for far in (True, False) for m in range(1, dp - 1) if (2 * m >= dp) == far]
    return order[0::2], order[1::2]


def partner(dp, t):
    first, second = partners(dp)
    return jnp.where(lax.axis_index("tensor") == 0, first[t], second[t])


def pack_kernel(pb, rows_a, rows_b, part_ref, recv_ref, extra_ref, *refs):
    outs, total_ref = refs[:-1], refs[-1]
    total_ref[...] = part_ref[...] + recv_ref[...]
    ranks, lanes = total_ref.shape[0] // 2, total_ref.shape[1]
    dp = extra_ref.shape[0]
    me = lax.axis_index("dp")
    lead = lax.axis_index("tensor") == 0

    def rows(out_ref, owner, pick):
        p, q = owner // pb, owner % pb
        out_ref[0:rows_a, :] = pick(total_ref[pl.ds(pl.multiple_of(p * rows_a, rows_a), rows_a), :])
        out_ref[rows_a:rows_a + rows_b, :] = pick(total_ref[pl.ds(pl.multiple_of(ranks + q * rows_b, rows_b), rows_b), :])
        out_ref[rows_a + rows_b:, :] = pick(extra_ref[owner])

    def half(x):
        return jnp.where(lead, x[:, :lanes // 2], x[:, lanes // 2:])

    for t, out_ref in enumerate(outs[:-2]):
        rows(out_ref, me ^ partner(dp, t), lambda x: x)
    rows(outs[-2], me ^ (dp - 1), half)
    rows(outs[-1], me, half)


def pack(part, recv, extra, pa, pb):
    ranks, lanes = part.shape[0] // 2, part.shape[1]
    rows_a, rows_b = ranks // pa, ranks // pb
    rows = rows_a + rows_b + extra.shape[1]
    count = pa * pb // 2 - 1
    whole, half = (jax.ShapeDtypeStruct((rows, n), jnp.float32) for n in (lanes, lanes // 2))
    return pl.pallas_call(
        functools.partial(pack_kernel, pb, rows_a, rows_b),
        out_shape=(whole,) * count + (half, half),
        in_specs=[VMEM] * 3,
        out_specs=(VMEM,) * (count + 2),
        scratch_shapes=[pltpu.VMEM(part.shape, jnp.float32)],
        compiler_params=vmem_params(16),
        name="pack",
    )(part, recv, extra)


def grads_kernel(rows_a, rows_b, docs, dp, whole, gaps, *refs):
    xs, before, (out_ref, outer_ref, member_ref) = refs[:len(gaps)], refs[len(gaps):-3], refs[-3:]
    wide = rows_a * rows_b
    first = rows_a + rows_b
    queries = out_ref.shape[0] - docs
    per = queries // dp
    place = lax.broadcasted_iota(jnp.int32, (queries, whole), 0)
    lane = lax.broadcasted_iota(jnp.int32, (queries, whole), 1)
    me = lax.axis_index("dp")
    core = lax.axis_index("tensor")
    mine = lane // (whole // 2) == core
    flat = [jnp.zeros((queries, whole), jnp.float32)] * (per * wide // whole)
    start = 0
    for x_ref, gap in zip(xs, gaps):
        lanes = x_ref.shape[1]
        at = slice(start, start + lanes)
        start += lanes
        g, b = x_ref[0:rows_a, :], x_ref[rows_a:first, :]
        ids = x_ref[first:first + 1, :].astype(jnp.int32)
        doc = lax.broadcasted_iota(jnp.int32, (docs, lanes), 0)
        member_ref[:, at] = jnp.where(doc == ids, 1.0, 0.0).astype(jnp.bfloat16)
        outer = (g[:, None, :] * b[None, :, :]).reshape(wide, lanes)
        high = outer.astype(jnp.bfloat16)
        outer_ref[0:wide, at] = high
        outer_ref[wide:, at] = (outer - high.astype(jnp.float32)).astype(jnp.bfloat16)
        held = place // per == me ^ jnp.where(core == 0, gap[0], gap[1])
        if lanes < whole:
            held = jnp.logical_and(held, mine)
        for j in range(len(flat)):
            line = x_ref[first + 1 + j:first + 2 + j, :]
            if lanes < whole:
                line = jnp.concatenate([line, line], axis=1)
            flat[j] = jnp.where(held, line, flat[j])
    sums = lax.dot_general(member_ref[...], outer_ref[...], NT, preferred_element_type=jnp.float32)
    sums = (sums[:, wide:] + sums[:, :wide]) * (TOK_DEV ** -0.5)
    flat = jnp.concatenate(flat, axis=1)
    asked = jnp.zeros((queries, wide), jnp.float32)
    which = lax.broadcasted_iota(jnp.int32, (queries, wide), 0) % per
    for q in range(per):
        asked = jnp.where(which == q, flat[:, q * wide:(q + 1) * wide], asked)
    if before:
        sums, asked = sums + before[0][0:docs, :], asked + before[0][docs:, :]
    out_ref[0:docs, :] = sums
    out_ref[docs:, :] = asked


def grads_of(xs, gaps, before, rows_a, rows_b, docs, queries, dp, whole):
    tokens = sum(x.shape[1] for x in xs)
    wide = rows_a * rows_b
    operands = (*xs, *before)
    return pl.pallas_call(
        functools.partial(grads_kernel, rows_a, rows_b, docs, dp, whole, gaps),
        out_shape=jax.ShapeDtypeStruct((docs + queries, wide), jnp.float32),
        in_specs=[VMEM] * len(operands),
        out_specs=VMEM,
        scratch_shapes=[
            pltpu.VMEM((2 * wide, tokens), jnp.bfloat16),
            pltpu.VMEM((docs, tokens), jnp.bfloat16),
        ],
        compiler_params=vmem_params(40),
        cost_estimate=pl.CostEstimate(
            flops=4 * docs * wide * tokens, bytes_accessed=4 * (rows_a + rows_b) * tokens, transcendentals=0
        ),
        name="grads",
    )(*operands)


def gram_kernel(docs, part_ref, recv_ref, out_ref):
    both = part_ref[...] + recv_ref[...]
    share = lax.dot_general(both, both[:docs], NT, precision=HIGHEST, preferred_element_type=jnp.float32)
    half = share.shape[0] // 2
    out_ref[...] = jnp.concatenate([share[:half], share[half:]], axis=1)


def gram(part, recv, docs):
    return pl.pallas_call(
        functools.partial(gram_kernel, docs),
        out_shape=jax.ShapeDtypeStruct((part.shape[0] // 2, 2 * docs), jnp.float32),
        in_specs=[VMEM] * 2,
        out_specs=VMEM,
        compiler_params=vmem_params(16),
        name="gram",
    )(part, recv)


def solve_kernel(docs, queries, scale, x_ref, recv_ref, out_ref, done_ref):
    total = x_ref[...] + recv_ref[...]
    stack = jnp.concatenate([total[:, :docs], total[:, docs:]], axis=0)
    cols = done_ref.shape[1]
    stack = jnp.concatenate([stack, jnp.zeros((cols - stack.shape[0], docs), jnp.float32)], axis=0)
    total = stack.T
    row = lax.broadcasted_iota(jnp.int32, (docs, cols), 0)
    col = lax.broadcasted_iota(jnp.int32, (docs, cols), 1)
    mean_diag = jnp.sum(jnp.where(row == col, total, 0.0)) * (1.0 / docs)
    work = total + jnp.where(row == col, 0.1 * mean_diag, 0.0)
    size = 8
    here = lax.broadcasted_iota(jnp.int32, (size, cols), 0)
    rows = [work[i:i + size] for i in range(0, docs, size)]
    for r in range(len(rows)):
        wide = [[jnp.broadcast_to(x[:, c:c + 1], (size, cols)) for c in range(r * size, (r + 1) * size)] for x in rows]
        pivot, line = wide[r], rows[r]
        scale_rows = jnp.ones((size, cols), jnp.float32)
        for j in range(size):
            inverse = 1.0 / pivot[j][j:j + 1]
            factor = jnp.where(here == j, 0.0, pivot[j]) * inverse
            pivot = [x if i <= j else x - factor * x[j:j + 1] for i, x in enumerate(pivot)]
            line = line - factor * line[j:j + 1]
            scale_rows = jnp.where(here == j, inverse, scale_rows)
        line = line * scale_rows
        for s in range(len(rows)):
            if s == r:
                rows[s] = line
            else:
                terms = [wide[s][j] * line[j:j + 1] for j in range(size)]
                rows[s] = rows[s] - (((terms[0] + terms[1]) + (terms[2] + terms[3]))
                                     + ((terms[4] + terms[5]) + (terms[6] + terms[7])))
    for r, x in enumerate(rows):
        done_ref[r * size:(r + 1) * size, :] = x * (mean_diag * scale)
    mine = pl.ds(pl.multiple_of(lax.axis_index("dp") * DOC_DEV, DOC_DEV), DOC_DEV)
    out_ref[...] = done_ref[mine, :][:, docs:docs + queries]


def solve(x, recv, docs, queries, scale):
    return pl.pallas_call(
        functools.partial(solve_kernel, docs, queries, scale),
        out_shape=jax.ShapeDtypeStruct((DOC_DEV, queries), jnp.float32),
        in_specs=[VMEM] * 2,
        out_specs=VMEM,
        scratch_shapes=[pltpu.VMEM((docs, -(-(docs + queries) // LANES) * LANES), jnp.float32)],
        compiler_params=vmem_params(16),
        name="solve",
    )(x, recv)


def solve_large(total, docs, queries, scale):
    kernel = total[:, :docs]
    mean_diag = jnp.trace(kernel) / docs
    factor = jnp.linalg.cholesky(kernel + 0.1 * mean_diag * jnp.eye(docs, dtype=jnp.float32))
    solved = jax.scipy.linalg.cho_solve((factor, True), total[:, docs:docs + queries]) * (mean_diag * scale)
    return lax.dynamic_slice_in_dim(solved, lax.axis_index("dp") * DOC_DEV, DOC_DEV, 0)


def swap_cores(x):
    cores = lax.axis_size("tensor")
    return lax.ppermute(x, "tensor", [(i, cores - 1 - i) for i in range(cores)])


def trade(xs):
    dp = lax.axis_size("dp")
    got = []
    for x, ms in zip(xs, zip(*partners(dp))):
        pairs = [(i * 2 + k, (i ^ m) * 2 + k) for i in range(dp) for k, m in enumerate(ms)]
        got.append(lax.ppermute(x, ("dp", "tensor"), pairs))
    return got


def trade_last(x):
    dp = lax.axis_size("dp")
    return lax.ppermute(x, "dp", [(i, i ^ (dp - 1)) for i in range(dp)])


def local(hidden, out_grad, proj_in, proj_out, doc_ids, queries):
    dp = lax.axis_size("dp")
    docs, num_queries = DOC_DEV * dp, queries.shape[0] * dp
    ranks = proj_in.shape[1]
    pa = 1
    while pa * pa < dp:
        pa *= 2
    pb = dp // pa
    rows_a, rows_b = ranks // pa, ranks // pb

    part = project(hidden, out_grad, proj_in.T, proj_out.T)
    recv = swap_cores(part)

    lanes = part.shape[1]
    ids = doc_ids.astype(jnp.float32)
    asked = queries.reshape(-1, pa, rows_a, pb, rows_b).transpose(1, 3, 0, 2, 4).reshape(dp, -1, lanes)
    extra = jnp.concatenate([jnp.broadcast_to(ids, (dp, 1, lanes)), asked], axis=1)
    extra = jnp.pad(extra, ((0, 0), (0, -extra.shape[1] % 8), (0, 0)))

    *blocks, last, own = pack(part, recv, extra, pa, pb)
    gaps = list(zip(*partners(dp)))
    sizes = (rows_a, rows_b, docs, num_queries, dp, lanes)
    last = trade_last(last)
    grads = grads_of(trade(blocks) + [own], gaps + [(0, 0)], (), *sizes)
    grads = grads_of([last], [(dp - 1, dp - 1)], (grads,), *sizes)
    share = gram(grads, swap_cores(grads), docs)
    scale = float(ranks * ranks) ** -0.5
    if docs <= 64:
        halves = jnp.where(lax.axis_index("tensor") == 0, share, trade_last(share))
        share = sum(trade([share] * (dp // 2 - 1)), halves)
        return solve(share, swap_cores(share), docs, num_queries, scale).T
    share = lax.psum(share, "dp")
    return solve_large(jnp.concatenate([share[:, :docs], share[:, docs:]], axis=0).T, docs, num_queries, scale).T


def solution(mesh):
    return jax.shard_map(
        local,
        mesh=mesh,
        in_specs=(
            P(("groups", "dp"), "tensor"),
            P(("groups", "dp"), "tensor"),
            P("tensor", None),
            P("tensor", None),
            P(("groups", "dp")),
            P(("groups", "dp"), None),
        ),
        out_specs=P("groups", "dp"),
        check_vma=False,
    )
```

```python
import functools

import jax
import jax.numpy as jnp
from jax import lax
from jax.experimental import pallas as pl
from jax.experimental.pallas import tpu as pltpu
from jax.sharding import PartitionSpec as P

TOK_DEV = 256
DOC_DEV = 8
LANES = 128
FLIGHT = 7
SHARED = 1
NT = (((1,), (1,)), ((), ()))
HIGHEST = lax.Precision.HIGHEST
VMEM = pl.BlockSpec(memory_space=pltpu.VMEM)
HBM = pl.BlockSpec(memory_space=pltpu.HBM)


def vmem_params(mib):
    return pltpu.CompilerParams(vmem_limit_bytes=int(mib * (1 << 20)))


def pieces(x):
    rows, units = x.shape
    split = x.reshape(rows // 8, 8, units // (2 * LANES), 2, LANES).transpose(0, 2, 3, 1, 4)
    return split.reshape(rows // 8, units // (2 * LANES), 16, LANES)


def chunks_of(length, ramp, tail):
    left = length - sum(ramp) - sum(tail)
    sizes = [*ramp, *([4] * (left // 4)), *([left % 4] if left % 4 else []), *tail]
    return [(sum(sizes[:i]), size) for i, size in enumerate(sizes)]


def project_kernel(g_chunks, h_chunks, h_ref, g_ref, pin_ref, pout_ref, out_ref, h_buf, g_buf, pin_buf, pout_buf, fold_ref, sems):
    plan = [(pout_ref, pout_buf, g_ref, g_buf, at) for at in g_chunks] + [(pin_ref, pin_buf, h_ref, h_buf, at) for at in h_chunks]
    copies = []
    for i, (proj, proj_buf, data, data_buf, (start, size)) in enumerate(plan):
        at = pl.ds(start, size)
        copies.append((
            pltpu.make_async_copy(proj.at[:, at], proj_buf.at[:, at], sems.at[2 * i]),
            pltpu.make_async_copy(data.at[:, at], data_buf.at[:, at], sems.at[2 * i + 1]),
        ))

    def start(i):
        if i < len(copies):
            for copy in copies[i]:
                copy.start()

    for i in range(FLIGHT):
        start(i)
    lane = lax.broadcasted_iota(jnp.int32, fold_ref.shape, 0)
    token = lax.broadcasted_iota(jnp.int32, fold_ref.shape, 1)
    fold_ref[...] = jnp.where(lane // 16 * 8 + lane % 8 == token, 1.0, 0.0).astype(jnp.bfloat16)

    def line_up(ref, first, size):
        blocks = [ref[:, j].reshape(ref.shape[0] * 16, LANES) for j in range(first, first + size)]
        return jnp.concatenate(blocks, axis=1)

    totals = [None, None]
    for i, (_, proj_buf, _, data_buf, (first, size)) in enumerate(plan):
        for copy in copies[i]:
            copy.wait()
        start(i + FLIGHT)
        which = 0 if i < len(g_chunks) else 1
        part = lax.dot_general(
            line_up(proj_buf, first, size), line_up(data_buf, first, size), NT, preferred_element_type=jnp.float32
        )
        totals[which] = part if totals[which] is None else totals[which] + part

    spread = totals[0].shape[1]
    even = lax.broadcasted_iota(jnp.int32, (8, spread), 1) % 16 < 8
    lines = []
    for total in totals:
        for g in range(total.shape[0] // 16):
            lines.append(jnp.where(even, total[16 * g:16 * g + 8], total[16 * g + 8:16 * g + 16]))
    lines = jnp.concatenate(lines, axis=0)
    split = []
    for _ in range(3):
        split.append(lines.astype(jnp.bfloat16))
        lines = lines - split[-1].astype(jnp.float32)
    rows = out_ref.shape[0]
    sums = jnp.dot(jnp.concatenate(split, axis=0), fold_ref[...], preferred_element_type=jnp.float32)
    out_ref[...] = sums[2 * rows:] + sums[rows:2 * rows] + sums[:rows]


def project(hidden, out_grad, pin_t, pout_t):
    tokens, units = hidden.shape
    width = out_grad.shape[1]
    ranks = pin_t.shape[0] + pout_t.shape[0]
    operands = [pieces(x) for x in (hidden, out_grad, pin_t, pout_t)]
    g_chunks = chunks_of(operands[1].shape[1], (2,), ())
    h_chunks = chunks_of(operands[0].shape[1], (), (2, 2))
    return pl.pallas_call(
        functools.partial(project_kernel, g_chunks, h_chunks),
        out_shape=jax.ShapeDtypeStruct((ranks, tokens), jnp.float32),
        in_specs=[HBM] * 4,
        out_specs=VMEM,
        scratch_shapes=[pltpu.VMEM(x.shape, x.dtype) for x in operands]
        + [pltpu.VMEM((2 * tokens, tokens), jnp.bfloat16), pltpu.SemaphoreType.DMA((2 * len(g_chunks + h_chunks),))],
        compiler_params=vmem_params(53.5),
        cost_estimate=pl.CostEstimate(
            flops=2 * tokens * 64 * (units + width),
            bytes_accessed=2 * (tokens + 64) * (units + width),
            transcendentals=0,
        ),
        name="project",
    )(*operands)


def partners(dp):
    order = [m for far in (True, False) for m in range(1, dp) if m != SHARED and (2 * m >= dp) == far]
    return order[0::2], order[1::2]


def partner(dp, t):
    first, second = partners(dp)
    return jnp.where(lax.axis_index("tensor") == 0, first[t], second[t])


def pack_kernel(pb, rows_a, rows_b, part_ref, recv_ref, extra_ref, *refs):
    outs, total_ref = refs[:-1], refs[-1]
    total_ref[...] = part_ref[...] + recv_ref[...]
    ranks, lanes = total_ref.shape[0] // 2, total_ref.shape[1]
    dp = extra_ref.shape[0]
    me = lax.axis_index("dp")
    lead = lax.axis_index("tensor") == 0

    def rows(out_ref, owner, pick):
        p, q = owner // pb, owner % pb
        out_ref[0:rows_a, :] = pick(total_ref[pl.ds(pl.multiple_of(p * rows_a, rows_a), rows_a), :])
        out_ref[rows_a:rows_a + rows_b, :] = pick(total_ref[pl.ds(pl.multiple_of(ranks + q * rows_b, rows_b), rows_b), :])
        out_ref[rows_a + rows_b:, :] = pick(extra_ref[owner])

    def half(x):
        return jnp.where(lead, x[:, :lanes // 2], x[:, lanes // 2:])

    for t, out_ref in enumerate(outs[:-2]):
        rows(out_ref, me ^ partner(dp, t), lambda x: x)
    rows(outs[-2], me ^ SHARED, half)
    rows(outs[-1], me, half)


def pack(part, recv, extra, pa, pb):
    ranks, lanes = part.shape[0] // 2, part.shape[1]
    rows_a, rows_b = ranks // pa, ranks // pb
    rows = rows_a + rows_b + extra.shape[1]
    count = pa * pb // 2 - 1
    whole, half = (jax.ShapeDtypeStruct((rows, n), jnp.float32) for n in (lanes, lanes // 2))
    return pl.pallas_call(
        functools.partial(pack_kernel, pb, rows_a, rows_b),
        out_shape=(whole,) * count + (half, half),
        in_specs=[VMEM] * 3,
        out_specs=(VMEM,) * (count + 2),
        scratch_shapes=[pltpu.VMEM(part.shape, jnp.float32)],
        compiler_params=vmem_params(16),
        name="pack",
    )(part, recv, extra)


def grads_kernel(rows_a, rows_b, docs, dp, whole, gaps, *refs):
    xs, before, (out_ref, outer_ref, member_ref) = refs[:len(gaps)], refs[len(gaps):-3], refs[-3:]
    wide = rows_a * rows_b
    first = rows_a + rows_b
    queries = out_ref.shape[0] - docs
    per = queries // dp
    place = lax.broadcasted_iota(jnp.int32, (queries, whole), 0)
    lane = lax.broadcasted_iota(jnp.int32, (queries, whole), 1)
    me = lax.axis_index("dp")
    core = lax.axis_index("tensor")
    mine = lane // (whole // 2) == core
    flat = [jnp.zeros((queries, whole), jnp.float32)] * (per * wide // whole)
    start = 0
    for x_ref, gap in zip(xs, gaps):
        lanes = x_ref.shape[1]
        at = slice(start, start + lanes)
        start += lanes
        g, b = x_ref[0:rows_a, :], x_ref[rows_a:first, :]
        ids = x_ref[first:first + 1, :].astype(jnp.int32)
        doc = lax.broadcasted_iota(jnp.int32, (docs, lanes), 0)
        member_ref[:, at] = jnp.where(doc == ids, 1.0, 0.0).astype(jnp.bfloat16)
        outer = (g[:, None, :] * b[None, :, :]).reshape(wide, lanes)
        high = outer.astype(jnp.bfloat16)
        outer_ref[0:wide, at] = high
        outer_ref[wide:, at] = (outer - high.astype(jnp.float32)).astype(jnp.bfloat16)
        held = place // per == me ^ jnp.where(core == 0, gap[0], gap[1])
        if lanes < whole:
            held = jnp.logical_and(held, mine)
        for j in range(len(flat)):
            line = x_ref[first + 1 + j:first + 2 + j, :]
            if lanes < whole:
                line = jnp.concatenate([line, line], axis=1)
            flat[j] = jnp.where(held, line, flat[j])
    sums = lax.dot_general(member_ref[...], outer_ref[...], NT, preferred_element_type=jnp.float32)
    sums = (sums[:, wide:] + sums[:, :wide]) * (TOK_DEV ** -0.5)
    flat = jnp.concatenate(flat, axis=1)
    asked = jnp.zeros((queries, wide), jnp.float32)
    which = lax.broadcasted_iota(jnp.int32, (queries, wide), 0) % per
    for q in range(per):
        asked = jnp.where(which == q, flat[:, q * wide:(q + 1) * wide], asked)
    if before:
        sums, asked = sums + before[0][0:docs, :], asked + before[0][docs:, :]
    out_ref[0:docs, :] = sums
    out_ref[docs:, :] = asked


def grads_of(xs, gaps, before, rows_a, rows_b, docs, queries, dp, whole):
    tokens = sum(x.shape[1] for x in xs)
    wide = rows_a * rows_b
    operands = (*xs, *before)
    return pl.pallas_call(
        functools.partial(grads_kernel, rows_a, rows_b, docs, dp, whole, gaps),
        out_shape=jax.ShapeDtypeStruct((docs + queries, wide), jnp.float32),
        in_specs=[VMEM] * len(operands),
        out_specs=VMEM,
        scratch_shapes=[
            pltpu.VMEM((2 * wide, tokens), jnp.bfloat16),
            pltpu.VMEM((docs, tokens), jnp.bfloat16),
        ],
        compiler_params=vmem_params(40),
        cost_estimate=pl.CostEstimate(
            flops=4 * docs * wide * tokens, bytes_accessed=4 * (rows_a + rows_b) * tokens, transcendentals=0
        ),
        name="grads",
    )(*operands)


def gram_kernel(docs, part_ref, recv_ref, out_ref):
    both = part_ref[...] + recv_ref[...]
    share = lax.dot_general(both, both[:docs], NT, precision=HIGHEST, preferred_element_type=jnp.float32)
    half = share.shape[0] // 2
    out_ref[...] = jnp.concatenate([share[:half], share[half:]], axis=1)


def gram(part, recv, docs):
    return pl.pallas_call(
        functools.partial(gram_kernel, docs),
        out_shape=jax.ShapeDtypeStruct((part.shape[0] // 2, 2 * docs), jnp.float32),
        in_specs=[VMEM] * 2,
        out_specs=VMEM,
        compiler_params=vmem_params(16),
        name="gram",
    )(part, recv)


def solve_kernel(docs, queries, scale, x_ref, recv_ref, out_ref, done_ref):
    total = x_ref[...] + recv_ref[...]
    stack = jnp.concatenate([total[:, :docs], total[:, docs:]], axis=0)
    cols = done_ref.shape[1]
    stack = jnp.concatenate([stack, jnp.zeros((cols - stack.shape[0], docs), jnp.float32)], axis=0)
    total = stack.T
    row = lax.broadcasted_iota(jnp.int32, (docs, cols), 0)
    col = lax.broadcasted_iota(jnp.int32, (docs, cols), 1)
    mean_diag = jnp.sum(jnp.where(row == col, total, 0.0)) * (1.0 / docs)
    work = total + jnp.where(row == col, 0.1 * mean_diag, 0.0)
    size = 8
    here = lax.broadcasted_iota(jnp.int32, (size, cols), 0)
    rows = [work[i:i + size] for i in range(0, docs, size)]
    for r in range(len(rows)):
        wide = [[jnp.broadcast_to(x[:, c:c + 1], (size, cols)) for c in range(r * size, (r + 1) * size)] for x in rows]
        pivot, line = wide[r], rows[r]
        pairs = []
        for j in range(0, size, 2):
            left, right = pivot[j], pivot[j + 1]
            a, b, c, d = left[j:j + 1], right[j:j + 1], left[j + 1:j + 2], right[j + 1:j + 2]
            inverse = 1.0 / (a * d - b * c)
            left, right = (jnp.where(here // 2 == j // 2, 0.0, x) for x in (left, right))
            first, second = (left * d - right * c) * inverse, (right * a - left * b) * inverse
            pairs.append((a * inverse, b * inverse, c * inverse, d * inverse))
            pivot = [x if i <= j + 1 else x - (first * x[j:j + 1] + second * x[j + 1:j + 2]) for i, x in enumerate(pivot)]
            line = line - (first * line[j:j + 1] + second * line[j + 1:j + 2])
        lines = []
        for j, (a, b, c, d) in zip(range(0, size, 2), pairs):
            upper, lower = line[j:j + 1], line[j + 1:j + 2]
            lines += [upper * d - lower * b, lower * a - upper * c]
        for s in range(len(rows)):
            if s == r:
                rows[s] = jnp.concatenate(lines, axis=0)
            else:
                terms = [wide[s][j] * lines[j] for j in range(size)]
                rows[s] = rows[s] - (((terms[0] + terms[1]) + (terms[2] + terms[3]))
                                     + ((terms[4] + terms[5]) + (terms[6] + terms[7])))
    for r, x in enumerate(rows):
        done_ref[r * size:(r + 1) * size, :] = x * (mean_diag * scale)
    mine = pl.ds(pl.multiple_of(lax.axis_index("dp") * DOC_DEV, DOC_DEV), DOC_DEV)
    out_ref[...] = done_ref[mine, :][:, docs:docs + queries]


def solve(x, recv, docs, queries, scale):
    return pl.pallas_call(
        functools.partial(solve_kernel, docs, queries, scale),
        out_shape=jax.ShapeDtypeStruct((DOC_DEV, queries), jnp.float32),
        in_specs=[VMEM] * 2,
        out_specs=VMEM,
        scratch_shapes=[pltpu.VMEM((docs, -(-(docs + queries) // LANES) * LANES), jnp.float32)],
        compiler_params=vmem_params(16),
        name="solve",
    )(x, recv)


def solve_large(total, docs, queries, scale):
    kernel = total[:, :docs]
    mean_diag = jnp.trace(kernel) / docs
    factor = jnp.linalg.cholesky(kernel + 0.1 * mean_diag * jnp.eye(docs, dtype=jnp.float32))
    solved = jax.scipy.linalg.cho_solve((factor, True), total[:, docs:docs + queries]) * (mean_diag * scale)
    return lax.dynamic_slice_in_dim(solved, lax.axis_index("dp") * DOC_DEV, DOC_DEV, 0)


def swap_cores(x):
    cores = lax.axis_size("tensor")
    return lax.ppermute(x, "tensor", [(i, cores - 1 - i) for i in range(cores)])


def trade(xs):
    dp = lax.axis_size("dp")
    got = []
    for x, ms in zip(xs, zip(*partners(dp))):
        pairs = [(i * 2 + k, (i ^ m) * 2 + k) for i in range(dp) for k, m in enumerate(ms)]
        got.append(lax.ppermute(x, ("dp", "tensor"), pairs))
    return got


def trade_shared(x):
    dp = lax.axis_size("dp")
    return lax.ppermute(x, "dp", [(i, i ^ SHARED) for i in range(dp)])


def local(hidden, out_grad, proj_in, proj_out, doc_ids, queries):
    dp = lax.axis_size("dp")
    docs, num_queries = DOC_DEV * dp, queries.shape[0] * dp
    ranks = proj_in.shape[1]
    pa = 1
    while pa * pa < dp:
        pa *= 2
    pb = dp // pa
    rows_a, rows_b = ranks // pa, ranks // pb

    part = project(hidden, out_grad, proj_in.T, proj_out.T)
    recv = swap_cores(part)

    lanes = part.shape[1]
    ids = doc_ids.astype(jnp.float32)
    asked = queries.reshape(-1, pa, rows_a, pb, rows_b).transpose(1, 3, 0, 2, 4).reshape(dp, -1, lanes)
    extra = jnp.concatenate([jnp.broadcast_to(ids, (dp, 1, lanes)), asked], axis=1)
    extra = jnp.pad(extra, ((0, 0), (0, -extra.shape[1] % 8), (0, 0)))

    *blocks, last, own = pack(part, recv, extra, pa, pb)
    gaps = list(zip(*partners(dp)))
    sizes = (rows_a, rows_b, docs, num_queries, dp, lanes)
    last = trade_shared(last)
    grads = grads_of(trade(blocks) + [own], gaps + [(0, 0)], (), *sizes)
    grads = grads_of([last], [(SHARED, SHARED)], (grads,), *sizes)
    share = gram(grads, swap_cores(grads), docs)
    scale = float(ranks * ranks) ** -0.5
    if docs <= 64:
        halves = jnp.where(lax.axis_index("tensor") == 0, share, trade_shared(share))
        share = sum(trade([share] * (dp // 2 - 1)), halves)
        return solve(share, swap_cores(share), docs, num_queries, scale).T
    share = lax.psum(share, "dp")
    return solve_large(jnp.concatenate([share[:, :docs], share[:, docs:]], axis=0).T, docs, num_queries, scale).T


def solution(mesh):
    return jax.shard_map(
        local,
        mesh=mesh,
        in_specs=(
            P(("groups", "dp"), "tensor"),
            P(("groups", "dp"), "tensor"),
            P("tensor", None),
            P("tensor", None),
            P(("groups", "dp")),
            P(("groups", "dp"), None),
        ),
        out_specs=P("groups", "dp"),
        check_vma=False,
    )
```

```python
import functools

import jax
import jax.numpy as jnp
from jax import lax
from jax.experimental import pallas as pl
from jax.experimental.pallas import tpu as pltpu
from jax.sharding import PartitionSpec as P

TOK_DEV = 256
DOC_DEV = 8
LANES = 128
FLIGHT = 7
SHARED = 1
NT = (((1,), (1,)), ((), ()))
HIGHEST = lax.Precision.HIGHEST
VMEM = pl.BlockSpec(memory_space=pltpu.VMEM)
HBM = pl.BlockSpec(memory_space=pltpu.HBM)


def vmem_params(mib):
    return pltpu.CompilerParams(vmem_limit_bytes=int(mib * (1 << 20)))


def pieces(x):
    rows, units = x.shape
    split = x.reshape(rows // 8, 8, units // (2 * LANES), 2, LANES).transpose(0, 2, 3, 1, 4)
    return split.reshape(rows // 8, units // (2 * LANES), 16, LANES)


def chunks_of(length, ramp, tail):
    left = length - sum(ramp) - sum(tail)
    sizes = [*ramp, *([4] * (left // 4)), *([left % 4] if left % 4 else []), *tail]
    return [(sum(sizes[:i]), size) for i, size in enumerate(sizes)]


def project_kernel(g_chunks, h_chunks, h_ref, g_ref, pin_ref, pout_ref, out_ref, h_buf, g_buf, pin_buf, pout_buf, fold_ref, sems):
    plan = [(pout_ref, pout_buf, g_ref, g_buf, at) for at in g_chunks] + [(pin_ref, pin_buf, h_ref, h_buf, at) for at in h_chunks]
    copies = []
    for i, (proj, proj_buf, data, data_buf, (start, size)) in enumerate(plan):
        at = pl.ds(start, size)
        copies.append((
            pltpu.make_async_copy(proj.at[:, at], proj_buf.at[:, at], sems.at[2 * i]),
            pltpu.make_async_copy(data.at[:, at], data_buf.at[:, at], sems.at[2 * i + 1]),
        ))

    def start(i):
        if i < len(copies):
            for copy in copies[i]:
                copy.start()

    for i in range(FLIGHT):
        start(i)
    lane = lax.broadcasted_iota(jnp.int32, fold_ref.shape, 0)
    token = lax.broadcasted_iota(jnp.int32, fold_ref.shape, 1)
    fold_ref[...] = jnp.where(lane // 16 * 8 + lane % 8 == token, 1.0, 0.0).astype(jnp.bfloat16)

    def line_up(ref, first, size):
        blocks = [ref[:, j].reshape(ref.shape[0] * 16, LANES) for j in range(first, first + size)]
        return jnp.concatenate(blocks, axis=1)

    even = lax.broadcasted_iota(jnp.int32, (8, fold_ref.shape[0]), 1) % 16 < 8

    def run(chunks):
        total = None
        for i in chunks:
            _, proj_buf, _, data_buf, (first, size) = plan[i]
            for copy in copies[i]:
                copy.wait()
            start(i + FLIGHT)
            part = lax.dot_general(
                line_up(proj_buf, first, size), line_up(data_buf, first, size), NT, preferred_element_type=jnp.float32
            )
            lines = [jnp.where(even, part[j:j + 8], part[j + 8:j + 16]) for j in range(0, part.shape[0], 16)]
            total = lines if total is None else [x + y for x, y in zip(total, lines)]
        lines = jnp.concatenate(total, axis=0)
        rows = lines.shape[0]
        split = []
        for _ in range(3):
            split.append(lines.astype(jnp.bfloat16))
            lines = lines - split[-1].astype(jnp.float32)
        sums = jnp.dot(jnp.concatenate(split, axis=0), fold_ref[...], preferred_element_type=jnp.float32)
        return sums[2 * rows:] + sums[rows:2 * rows] + sums[:rows]

    grad = run(range(len(g_chunks)))
    ranks = grad.shape[0]
    out_ref[0:ranks, :] = grad
    out_ref[ranks:, :] = run(range(len(g_chunks), len(plan)))


def project(hidden, out_grad, pin_t, pout_t):
    tokens, units = hidden.shape
    width = out_grad.shape[1]
    ranks = pin_t.shape[0] + pout_t.shape[0]
    operands = [pieces(x) for x in (hidden, out_grad, pin_t, pout_t)]
    g_chunks = chunks_of(operands[1].shape[1], (2,), ())
    h_chunks = chunks_of(operands[0].shape[1], (), (2, 2))
    return pl.pallas_call(
        functools.partial(project_kernel, g_chunks, h_chunks),
        out_shape=jax.ShapeDtypeStruct((ranks, tokens), jnp.float32),
        in_specs=[HBM] * 4,
        out_specs=VMEM,
        scratch_shapes=[pltpu.VMEM(x.shape, x.dtype) for x in operands]
        + [pltpu.VMEM((2 * tokens, tokens), jnp.bfloat16), pltpu.SemaphoreType.DMA((2 * len(g_chunks + h_chunks),))],
        compiler_params=vmem_params(53.5),
        cost_estimate=pl.CostEstimate(
            flops=2 * tokens * 64 * (units + width),
            bytes_accessed=2 * (tokens + 64) * (units + width),
            transcendentals=0,
        ),
        name="project",
    )(*operands)


def partners(dp):
    order = [m for far in (True, False) for m in range(1, dp) if m != SHARED and (2 * m >= dp) == far]
    return order[0::2], order[1::2]


def partner(dp, t):
    first, second = partners(dp)
    return jnp.where(lax.axis_index("tensor") == 0, first[t], second[t])


def pack_kernel(pb, rows_a, rows_b, part_ref, recv_ref, extra_ref, *refs):
    outs, total_ref = refs[:-1], refs[-1]
    total_ref[...] = part_ref[...] + recv_ref[...]
    ranks, lanes = total_ref.shape[0] // 2, total_ref.shape[1]
    dp = extra_ref.shape[0]
    me = lax.axis_index("dp")
    lead = lax.axis_index("tensor") == 0

    def rows(out_ref, owner, pick):
        p, q = owner // pb, owner % pb
        out_ref[0:rows_a, :] = pick(total_ref[pl.ds(pl.multiple_of(p * rows_a, rows_a), rows_a), :])
        out_ref[rows_a:rows_a + rows_b, :] = pick(total_ref[pl.ds(pl.multiple_of(ranks + q * rows_b, rows_b), rows_b), :])
        out_ref[rows_a + rows_b:, :] = pick(extra_ref[owner])

    def half(x):
        return jnp.where(lead, x[:, :lanes // 2], x[:, lanes // 2:])

    for t, out_ref in enumerate(outs[:-2]):
        rows(out_ref, me ^ partner(dp, t), lambda x: x)
    rows(outs[-2], me ^ SHARED, half)
    rows(outs[-1], me, half)


def pack(part, recv, extra, pa, pb):
    ranks, lanes = part.shape[0] // 2, part.shape[1]
    rows_a, rows_b = ranks // pa, ranks // pb
    rows = rows_a + rows_b + extra.shape[1]
    count = pa * pb // 2 - 1
    whole, half = (jax.ShapeDtypeStruct((rows, n), jnp.float32) for n in (lanes, lanes // 2))
    return pl.pallas_call(
        functools.partial(pack_kernel, pb, rows_a, rows_b),
        out_shape=(whole,) * count + (half, half),
        in_specs=[VMEM] * 3,
        out_specs=(VMEM,) * (count + 2),
        scratch_shapes=[pltpu.VMEM(part.shape, jnp.float32)],
        compiler_params=vmem_params(16),
        name="pack",
    )(part, recv, extra)


def grads_kernel(rows_a, rows_b, docs, dp, whole, gaps, *refs):
    xs, before, (out_ref, outer_ref, member_ref) = refs[:len(gaps)], refs[len(gaps):-3], refs[-3:]
    wide = rows_a * rows_b
    first = rows_a + rows_b
    queries = out_ref.shape[0] - docs
    per = queries // dp
    place = lax.broadcasted_iota(jnp.int32, (queries, whole), 0)
    lane = lax.broadcasted_iota(jnp.int32, (queries, whole), 1)
    me = lax.axis_index("dp")
    core = lax.axis_index("tensor")
    mine = lane // (whole // 2) == core
    flat = [jnp.zeros((queries, whole), jnp.float32)] * (per * wide // whole)
    start = 0
    for x_ref, gap in zip(xs, gaps):
        lanes = x_ref.shape[1]
        at = slice(start, start + lanes)
        start += lanes
        g, b = x_ref[0:rows_a, :], x_ref[rows_a:first, :]
        ids = x_ref[first:first + 1, :].astype(jnp.int32)
        doc = lax.broadcasted_iota(jnp.int32, (docs, lanes), 0)
        member_ref[:, at] = jnp.where(doc == ids, 1.0, 0.0).astype(jnp.bfloat16)
        outer = (g[:, None, :] * b[None, :, :]).reshape(wide, lanes)
        high = outer.astype(jnp.bfloat16)
        outer_ref[0:wide, at] = high
        outer_ref[wide:, at] = (outer - high.astype(jnp.float32)).astype(jnp.bfloat16)
        held = place // per == me ^ jnp.where(core == 0, gap[0], gap[1])
        if lanes < whole:
            held = jnp.logical_and(held, mine)
        for j in range(len(flat)):
            line = x_ref[first + 1 + j:first + 2 + j, :]
            if lanes < whole:
                line = jnp.concatenate([line, line], axis=1)
            flat[j] = jnp.where(held, line, flat[j])
    sums = lax.dot_general(member_ref[...], outer_ref[...], NT, preferred_element_type=jnp.float32)
    sums = (sums[:, wide:] + sums[:, :wide]) * (TOK_DEV ** -0.5)
    flat = jnp.concatenate(flat, axis=1)
    asked = jnp.zeros((queries, wide), jnp.float32)
    which = lax.broadcasted_iota(jnp.int32, (queries, wide), 0) % per
    for q in range(per):
        asked = jnp.where(which == q, flat[:, q * wide:(q + 1) * wide], asked)
    if before:
        sums, asked = sums + before[0][0:docs, :], asked + before[0][docs:, :]
    out_ref[0:docs, :] = sums
    out_ref[docs:, :] = asked


def grads_of(xs, gaps, before, rows_a, rows_b, docs, queries, dp, whole):
    tokens = sum(x.shape[1] for x in xs)
    wide = rows_a * rows_b
    operands = (*xs, *before)
    return pl.pallas_call(
        functools.partial(grads_kernel, rows_a, rows_b, docs, dp, whole, gaps),
        out_shape=jax.ShapeDtypeStruct((docs + queries, wide), jnp.float32),
        in_specs=[VMEM] * len(operands),
        out_specs=VMEM,
        scratch_shapes=[
            pltpu.VMEM((2 * wide, tokens), jnp.bfloat16),
            pltpu.VMEM((docs, tokens), jnp.bfloat16),
        ],
        compiler_params=vmem_params(40),
        cost_estimate=pl.CostEstimate(
            flops=4 * docs * wide * tokens, bytes_accessed=4 * (rows_a + rows_b) * tokens, transcendentals=0
        ),
        name="grads",
    )(*operands)


def gram_kernel(docs, part_ref, recv_ref, out_ref):
    both = part_ref[...] + recv_ref[...]
    share = lax.dot_general(both, both[:docs], NT, precision=HIGHEST, preferred_element_type=jnp.float32)
    half = share.shape[0] // 2
    out_ref[...] = jnp.concatenate([share[:half], share[half:]], axis=1)


def gram(part, recv, docs):
    return pl.pallas_call(
        functools.partial(gram_kernel, docs),
        out_shape=jax.ShapeDtypeStruct((part.shape[0] // 2, 2 * docs), jnp.float32),
        in_specs=[VMEM] * 2,
        out_specs=VMEM,
        compiler_params=vmem_params(16),
        name="gram",
    )(part, recv)


def solve_kernel(docs, queries, scale, x_ref, recv_ref, out_ref, done_ref):
    total = x_ref[...] + recv_ref[...]
    stack = jnp.concatenate([total[:, :docs], total[:, docs:]], axis=0)
    cols = done_ref.shape[1]
    stack = jnp.concatenate([stack, jnp.zeros((cols - stack.shape[0], docs), jnp.float32)], axis=0)
    total = stack.T
    row = lax.broadcasted_iota(jnp.int32, (docs, cols), 0)
    col = lax.broadcasted_iota(jnp.int32, (docs, cols), 1)
    mean_diag = jnp.sum(jnp.where(row == col, total, 0.0)) * (1.0 / docs)
    work = total + jnp.where(row == col, 0.1 * mean_diag, 0.0)
    size = 8
    here = lax.broadcasted_iota(jnp.int32, (size, cols), 0)
    rows = [work[i:i + size] for i in range(0, docs, size)]
    for r in range(len(rows)):
        wide = [[jnp.broadcast_to(x[:, c:c + 1], (size, cols)) for c in range(r * size, (r + 1) * size)] for x in rows]
        pivot, line = wide[r], rows[r]
        scale_rows = jnp.ones((size, cols), jnp.float32)
        for j in range(size):
            inverse = 1.0 / pivot[j][j:j + 1]
            factor = jnp.where(here == j, 0.0, pivot[j]) * inverse
            pivot = [x if i <= j else x - factor * x[j:j + 1] for i, x in enumerate(pivot)]
            line = line - factor * line[j:j + 1]
            scale_rows = jnp.where(here == j, inverse, scale_rows)
        line = line * scale_rows
        for s in range(len(rows)):
            if s == r:
                rows[s] = line
            else:
                terms = [wide[s][j] * line[j:j + 1] for j in range(size)]
                rows[s] = rows[s] - (((terms[0] + terms[1]) + (terms[2] + terms[3]))
                                     + ((terms[4] + terms[5]) + (terms[6] + terms[7])))
    for r, x in enumerate(rows):
        done_ref[r * size:(r + 1) * size, :] = x * (mean_diag * scale)
    mine = pl.ds(pl.multiple_of(lax.axis_index("dp") * DOC_DEV, DOC_DEV), DOC_DEV)
    out_ref[...] = done_ref[mine, :][:, docs:docs + queries]


def solve(x, recv, docs, queries, scale):
    return pl.pallas_call(
        functools.partial(solve_kernel, docs, queries, scale),
        out_shape=jax.ShapeDtypeStruct((DOC_DEV, queries), jnp.float32),
        in_specs=[VMEM] * 2,
        out_specs=VMEM,
        scratch_shapes=[pltpu.VMEM((docs, -(-(docs + queries) // LANES) * LANES), jnp.float32)],
        compiler_params=vmem_params(16),
        name="solve",
    )(x, recv)


def solve_large(total, docs, queries, scale):
    kernel = total[:, :docs]
    mean_diag = jnp.trace(kernel) / docs
    factor = jnp.linalg.cholesky(kernel + 0.1 * mean_diag * jnp.eye(docs, dtype=jnp.float32))
    solved = jax.scipy.linalg.cho_solve((factor, True), total[:, docs:docs + queries]) * (mean_diag * scale)
    return lax.dynamic_slice_in_dim(solved, lax.axis_index("dp") * DOC_DEV, DOC_DEV, 0)


def swap_cores(x):
    cores = lax.axis_size("tensor")
    return lax.ppermute(x, "tensor", [(i, cores - 1 - i) for i in range(cores)])


def trade(xs):
    dp = lax.axis_size("dp")
    got = []
    for x, ms in zip(xs, zip(*partners(dp))):
        pairs = [(i * 2 + k, (i ^ m) * 2 + k) for i in range(dp) for k, m in enumerate(ms)]
        got.append(lax.ppermute(x, ("dp", "tensor"), pairs))
    return got


def trade_shared(x):
    dp = lax.axis_size("dp")
    return lax.ppermute(x, "dp", [(i, i ^ SHARED) for i in range(dp)])


def local(hidden, out_grad, proj_in, proj_out, doc_ids, queries):
    dp = lax.axis_size("dp")
    docs, num_queries = DOC_DEV * dp, queries.shape[0] * dp
    ranks = proj_in.shape[1]
    pa = 1
    while pa * pa < dp:
        pa *= 2
    pb = dp // pa
    rows_a, rows_b = ranks // pa, ranks // pb

    part = project(hidden, out_grad, proj_in.T, proj_out.T)
    recv = swap_cores(part)

    lanes = part.shape[1]
    ids = doc_ids.astype(jnp.float32)
    asked = queries.reshape(-1, pa, rows_a, pb, rows_b).transpose(1, 3, 0, 2, 4).reshape(dp, -1, lanes)
    extra = jnp.concatenate([jnp.broadcast_to(ids, (dp, 1, lanes)), asked], axis=1)
    extra = jnp.pad(extra, ((0, 0), (0, -extra.shape[1] % 8), (0, 0)))

    *blocks, shared, own = pack(part, recv, extra, pa, pb)
    gaps = list(zip(*partners(dp)))
    sizes = (rows_a, rows_b, docs, num_queries, dp, lanes)
    blocks = trade(blocks) + [trade_shared(shared), own]
    gaps += [(SHARED, SHARED), (0, 0)]
    late = min(1, len(blocks) - 3)
    rest = [t for t in range(len(blocks)) if t != late]
    grads = grads_of([blocks[t] for t in rest], [gaps[t] for t in rest], (), *sizes)
    grads = grads_of([blocks[late]], [gaps[late]], (grads,), *sizes)
    share = gram(grads, swap_cores(grads), docs)
    scale = float(ranks * ranks) ** -0.5
    if docs <= 64:
        others = sum(trade([share] * (dp // 2 - 1)))
        share = others + jnp.where(lax.axis_index("tensor") == 0, share, trade_shared(share))
        return solve(share, swap_cores(share), docs, num_queries, scale).T
    share = lax.psum(share, "dp")
    return solve_large(jnp.concatenate([share[:, :docs], share[:, docs:]], axis=0).T, docs, num_queries, scale).T


def solution(mesh):
    return jax.shard_map(
        local,
        mesh=mesh,
        in_specs=(
            P(("groups", "dp"), "tensor"),
            P(("groups", "dp"), "tensor"),
            P("tensor", None),
            P("tensor", None),
            P(("groups", "dp")),
            P(("groups", "dp"), None),
        ),
        out_specs=P("groups", "dp"),
        check_vma=False,
    )
```

```python
import functools

import jax
import jax.numpy as jnp
from jax import lax
from jax.experimental import pallas as pl
from jax.experimental.pallas import tpu as pltpu
from jax.sharding import PartitionSpec as P

TOK_DEV = 256
DOC_DEV = 8
LANES = 128
FLIGHT = 7
SHARED = 1
NT = (((1,), (1,)), ((), ()))
HIGHEST = lax.Precision.HIGHEST
VMEM = pl.BlockSpec(memory_space=pltpu.VMEM)
HBM = pl.BlockSpec(memory_space=pltpu.HBM)


def vmem_params(mib):
    return pltpu.CompilerParams(vmem_limit_bytes=int(mib * (1 << 20)))


def pieces(x):
    rows, units = x.shape
    split = x.reshape(rows // 8, 8, units // (2 * LANES), 2, LANES).transpose(0, 2, 3, 1, 4)
    return split.reshape(rows // 8, units // (2 * LANES), 16, LANES)


def chunks_of(length, ramp, tail):
    left = length - sum(ramp) - sum(tail)
    sizes = [*ramp, *([4] * (left // 4)), *([left % 4] if left % 4 else []), *tail]
    return [(sum(sizes[:i]), size) for i, size in enumerate(sizes)]


def project_kernel(g_chunks, h_chunks, h_ref, g_ref, pin_ref, pout_ref, out_ref, h_buf, g_buf, pin_buf, pout_buf, fold_ref, sems):
    plan = [(pout_ref, pout_buf, g_ref, g_buf, at) for at in g_chunks] + [(pin_ref, pin_buf, h_ref, h_buf, at) for at in h_chunks]
    copies = []
    for i, (proj, proj_buf, data, data_buf, (start, size)) in enumerate(plan):
        at = pl.ds(start, size)
        copies.append((
            pltpu.make_async_copy(proj.at[:, at], proj_buf.at[:, at], sems.at[2 * i]),
            pltpu.make_async_copy(data.at[:, at], data_buf.at[:, at], sems.at[2 * i + 1]),
        ))

    def start(i):
        if i < len(copies):
            for copy in copies[i]:
                copy.start()

    for i in range(FLIGHT):
        start(i)
    lane = lax.broadcasted_iota(jnp.int32, fold_ref.shape, 0)
    token = lax.broadcasted_iota(jnp.int32, fold_ref.shape, 1)
    fold_ref[...] = jnp.where(lane // 16 * 8 + lane % 8 == token, 1.0, 0.0).astype(jnp.bfloat16)

    def line_up(ref, first, size):
        blocks = [ref[:, j].reshape(ref.shape[0] * 16, LANES) for j in range(first, first + size)]
        return jnp.concatenate(blocks, axis=1)

    even = lax.broadcasted_iota(jnp.int32, (8, fold_ref.shape[0]), 1) % 16 < 8

    def run(chunks):
        total = None
        for i in chunks:
            _, proj_buf, _, data_buf, (first, size) = plan[i]
            for copy in copies[i]:
                copy.wait()
            start(i + FLIGHT)
            part = lax.dot_general(
                line_up(proj_buf, first, size), line_up(data_buf, first, size), NT, preferred_element_type=jnp.float32
            )
            total = part if total is None else total + part
        lines = [jnp.where(even, total[j:j + 8], total[j + 8:j + 16]) for j in range(0, total.shape[0], 16)]
        lines = jnp.concatenate(lines, axis=0)
        rows = lines.shape[0]
        split = []
        for _ in range(3):
            split.append(lines.astype(jnp.bfloat16))
            lines = lines - split[-1].astype(jnp.float32)
        sums = jnp.dot(jnp.concatenate(split, axis=0), fold_ref[...], preferred_element_type=jnp.float32)
        return sums[2 * rows:] + sums[rows:2 * rows] + sums[:rows]

    grad = run(range(len(g_chunks)))
    ranks = grad.shape[0]
    out_ref[0:ranks, :] = grad
    out_ref[ranks:, :] = run(range(len(g_chunks), len(plan)))


def project(hidden, out_grad, pin_t, pout_t):
    tokens, units = hidden.shape
    width = out_grad.shape[1]
    ranks = pin_t.shape[0] + pout_t.shape[0]
    operands = [pieces(x) for x in (hidden, out_grad, pin_t, pout_t)]
    g_chunks = chunks_of(operands[1].shape[1], (2,), ())
    h_chunks = chunks_of(operands[0].shape[1], (), (2, 2))
    return pl.pallas_call(
        functools.partial(project_kernel, g_chunks, h_chunks),
        out_shape=jax.ShapeDtypeStruct((ranks, tokens), jnp.float32),
        in_specs=[HBM] * 4,
        out_specs=VMEM,
        scratch_shapes=[pltpu.VMEM(x.shape, x.dtype) for x in operands]
        + [pltpu.VMEM((2 * tokens, tokens), jnp.bfloat16), pltpu.SemaphoreType.DMA((2 * len(g_chunks + h_chunks),))],
        compiler_params=vmem_params(53.5),
        cost_estimate=pl.CostEstimate(
            flops=2 * tokens * 64 * (units + width),
            bytes_accessed=2 * (tokens + 64) * (units + width),
            transcendentals=0,
        ),
        name="project",
    )(*operands)


def owners_of(dp):
    return max(dp // 2, 1)


def partners(dp):
    order = [m for far in (True, False) for m in range(1, dp) if m != SHARED and (2 * m >= dp) == far]
    return order[0::2], order[1::2]


def partner(dp, t):
    first, second = partners(dp)
    return jnp.where(lax.axis_index("tensor") == 0, first[t], second[t])


def pack_kernel(dp, pb, rows_a, rows_b, part_ref, recv_ref, extra_ref, *refs):
    outs, total_ref = refs[:-1], refs[-1]
    total_ref[...] = part_ref[...] + recv_ref[...]
    ranks, lanes = total_ref.shape[0] // 2, total_ref.shape[1]
    me = lax.axis_index("dp")
    lead = lax.axis_index("tensor") == 0

    def rows(out_ref, to, pick):
        owner = to % extra_ref.shape[0]
        p, q = owner // pb, owner % pb
        out_ref[0:rows_a, :] = pick(total_ref[pl.ds(pl.multiple_of(p * rows_a, rows_a), rows_a), :])
        out_ref[rows_a:rows_a + rows_b, :] = pick(total_ref[pl.ds(pl.multiple_of(ranks + q * rows_b, rows_b), rows_b), :])
        out_ref[rows_a + rows_b:, :] = pick(extra_ref[owner])

    def half(x):
        return jnp.where(lead, x[:, :lanes // 2], x[:, lanes // 2:])

    for t, out_ref in enumerate(outs[:-2]):
        rows(out_ref, me ^ partner(dp, t), lambda x: x)
    rows(outs[-2], me ^ SHARED, half)
    rows(outs[-1], me, half)


def pack(part, recv, extra, dp, pa, pb):
    ranks, lanes = part.shape[0] // 2, part.shape[1]
    rows_a, rows_b = ranks // pa, ranks // pb
    rows = rows_a + rows_b + extra.shape[1]
    count = dp // 2 - 1
    whole, half = (jax.ShapeDtypeStruct((rows, n), jnp.float32) for n in (lanes, lanes // 2))
    return pl.pallas_call(
        functools.partial(pack_kernel, dp, pb, rows_a, rows_b),
        out_shape=(whole,) * count + (half, half),
        in_specs=[VMEM] * 3,
        out_specs=(VMEM,) * (count + 2),
        scratch_shapes=[pltpu.VMEM(part.shape, jnp.float32)],
        compiler_params=vmem_params(16),
        name="pack",
    )(part, recv, extra)


def grads_kernel(rows_a, rows_b, docs, dp, whole, gaps, *refs):
    xs, before, (out_ref, outer_ref, member_ref) = refs[:len(gaps)], refs[len(gaps):-3], refs[-3:]
    wide = rows_a * rows_b
    first = rows_a + rows_b
    queries = out_ref.shape[0] - docs
    per = queries // dp
    place = lax.broadcasted_iota(jnp.int32, (queries, whole), 0)
    lane = lax.broadcasted_iota(jnp.int32, (queries, whole), 1)
    me = lax.axis_index("dp")
    core = lax.axis_index("tensor")
    mine = lane // (whole // 2) == core
    flat = [jnp.zeros((queries, whole), jnp.float32)] * (per * wide // whole)
    start = 0
    for x_ref, gap in zip(xs, gaps):
        lanes = x_ref.shape[1]
        at = slice(start, start + lanes)
        start += lanes
        g, b = x_ref[0:rows_a, :], x_ref[rows_a:first, :]
        ids = x_ref[first:first + 1, :].astype(jnp.int32)
        doc = lax.broadcasted_iota(jnp.int32, (docs, lanes), 0)
        member_ref[:, at] = jnp.where(doc == ids, 1.0, 0.0).astype(jnp.bfloat16)
        outer = (g[:, None, :] * b[None, :, :]).reshape(wide, lanes)
        high = outer.astype(jnp.bfloat16)
        outer_ref[0:wide, at] = high
        outer_ref[wide:, at] = (outer - high.astype(jnp.float32)).astype(jnp.bfloat16)
        held = place // per == me ^ jnp.where(core == 0, gap[0], gap[1])
        if lanes < whole:
            held = jnp.logical_and(held, mine)
        for j in range(len(flat)):
            line = x_ref[first + 1 + j:first + 2 + j, :]
            if lanes < whole:
                line = jnp.concatenate([line, line], axis=1)
            flat[j] = jnp.where(held, line, flat[j])
    sums = lax.dot_general(member_ref[...], outer_ref[...], NT, preferred_element_type=jnp.float32)
    sums = (sums[:, wide:] + sums[:, :wide]) * (TOK_DEV ** -0.5)
    flat = jnp.concatenate(flat, axis=1)
    asked = jnp.zeros((queries, wide), jnp.float32)
    which = lax.broadcasted_iota(jnp.int32, (queries, wide), 0) % per
    for q in range(per):
        asked = jnp.where(which == q, flat[:, q * wide:(q + 1) * wide], asked)
    if before:
        sums, asked = sums + before[0][0:docs, :], asked + before[0][docs:, :]
    out_ref[0:docs, :] = sums
    out_ref[docs:, :] = asked


def grads_of(xs, gaps, before, rows_a, rows_b, docs, queries, dp, whole):
    tokens = sum(x.shape[1] for x in xs)
    wide = rows_a * rows_b
    operands = (*xs, *before)
    return pl.pallas_call(
        functools.partial(grads_kernel, rows_a, rows_b, docs, dp, whole, gaps),
        out_shape=jax.ShapeDtypeStruct((docs + queries, wide), jnp.float32),
        in_specs=[VMEM] * len(operands),
        out_specs=VMEM,
        scratch_shapes=[
            pltpu.VMEM((2 * wide, tokens), jnp.bfloat16),
            pltpu.VMEM((docs, tokens), jnp.bfloat16),
        ],
        compiler_params=vmem_params(40),
        cost_estimate=pl.CostEstimate(
            flops=4 * docs * wide * tokens, bytes_accessed=4 * (rows_a + rows_b) * tokens, transcendentals=0
        ),
        name="grads",
    )(*operands)


def gram_kernel(docs, part_ref, recv_ref, out_ref):
    both = part_ref[...] + recv_ref[...]
    share = lax.dot_general(both, both[:docs], NT, precision=HIGHEST, preferred_element_type=jnp.float32)
    half = share.shape[0] // 2
    out_ref[...] = jnp.concatenate([share[:half], share[half:]], axis=1)


def gram(part, recv, docs):
    return pl.pallas_call(
        functools.partial(gram_kernel, docs),
        out_shape=jax.ShapeDtypeStruct((part.shape[0] // 2, 2 * docs), jnp.float32),
        in_specs=[VMEM] * 2,
        out_specs=VMEM,
        compiler_params=vmem_params(16),
        name="gram",
    )(part, recv)


def solve_kernel(docs, queries, scale, x_ref, recv_ref, out_ref, done_ref):
    total = x_ref[...] + recv_ref[...]
    stack = jnp.concatenate([total[:, :docs], total[:, docs:]], axis=0)
    cols = done_ref.shape[1]
    stack = jnp.concatenate([stack, jnp.zeros((cols - stack.shape[0], docs), jnp.float32)], axis=0)
    total = stack.T
    row = lax.broadcasted_iota(jnp.int32, (docs, cols), 0)
    col = lax.broadcasted_iota(jnp.int32, (docs, cols), 1)
    mean_diag = jnp.sum(jnp.where(row == col, total, 0.0)) * (1.0 / docs)
    work = total + jnp.where(row == col, 0.1 * mean_diag, 0.0)
    size = 8
    here = lax.broadcasted_iota(jnp.int32, (size, cols), 0)
    rows = [work[i:i + size] for i in range(0, docs, size)]
    for r in range(len(rows)):
        wide = [[jnp.broadcast_to(x[:, c:c + 1], (size, cols)) for c in range(r * size, (r + 1) * size)] for x in rows]
        pivot, line = wide[r], rows[r]
        scale_rows = jnp.ones((size, cols), jnp.float32)
        for j in range(size):
            inverse = 1.0 / pivot[j][j:j + 1]
            factor = jnp.where(here == j, 0.0, pivot[j]) * inverse
            pivot = [x if i <= j else x - factor * x[j:j + 1] for i, x in enumerate(pivot)]
            line = line - factor * line[j:j + 1]
            scale_rows = jnp.where(here == j, inverse, scale_rows)
        line = line * scale_rows
        for s in range(len(rows)):
            if s == r:
                rows[s] = line
            else:
                terms = [wide[s][j] * line[j:j + 1] for j in range(size)]
                rows[s] = rows[s] - (((terms[0] + terms[1]) + (terms[2] + terms[3]))
                                     + ((terms[4] + terms[5]) + (terms[6] + terms[7])))
    for r, x in enumerate(rows):
        done_ref[r * size:(r + 1) * size, :] = x * (mean_diag * scale)
    mine = pl.ds(pl.multiple_of(lax.axis_index("dp") * DOC_DEV, DOC_DEV), DOC_DEV)
    out_ref[...] = done_ref[mine, :][:, docs:docs + queries]


def solve(x, recv, docs, queries, scale):
    return pl.pallas_call(
        functools.partial(solve_kernel, docs, queries, scale),
        out_shape=jax.ShapeDtypeStruct((DOC_DEV, queries), jnp.float32),
        in_specs=[VMEM] * 2,
        out_specs=VMEM,
        scratch_shapes=[pltpu.VMEM((docs, -(-(docs + queries) // LANES) * LANES), jnp.float32)],
        compiler_params=vmem_params(16),
        name="solve",
    )(x, recv)


def solve_large(total, docs, queries, scale):
    kernel = total[:, :docs]
    mean_diag = jnp.trace(kernel) / docs
    factor = jnp.linalg.cholesky(kernel + 0.1 * mean_diag * jnp.eye(docs, dtype=jnp.float32))
    solved = jax.scipy.linalg.cho_solve((factor, True), total[:, docs:docs + queries]) * (mean_diag * scale)
    return lax.dynamic_slice_in_dim(solved, lax.axis_index("dp") * DOC_DEV, DOC_DEV, 0)


def swap_cores(x):
    cores = lax.axis_size("tensor")
    return lax.ppermute(x, "tensor", [(i, cores - 1 - i) for i in range(cores)])


def trade(xs, group):
    dp = lax.axis_size("dp")
    got = []
    for x, ms in zip(xs, zip(*partners(group))):
        pairs = [(i * 2 + k, (i ^ m) * 2 + k) for i in range(dp) for k, m in enumerate(ms)]
        got.append(lax.ppermute(x, ("dp", "tensor"), pairs))
    return got


def trade_shared(x):
    dp = lax.axis_size("dp")
    return lax.ppermute(x, "dp", [(i, i ^ SHARED) for i in range(dp)])


def local(hidden, out_grad, proj_in, proj_out, doc_ids, queries):
    dp = lax.axis_size("dp")
    docs, num_queries = DOC_DEV * dp, queries.shape[0] * dp
    ranks = proj_in.shape[1]
    owners = owners_of(dp)
    pa = 1
    while pa * pa < owners:
        pa *= 2
    pb = owners // pa
    rows_a, rows_b = ranks // pa, ranks // pb

    part = project(hidden, out_grad, proj_in.T, proj_out.T)
    recv = swap_cores(part)

    lanes = part.shape[1]
    ids = doc_ids.astype(jnp.float32)
    asked = queries.reshape(-1, pa, rows_a, pb, rows_b).transpose(1, 3, 0, 2, 4).reshape(owners, -1, lanes)
    extra = jnp.concatenate([jnp.broadcast_to(ids, (owners, 1, lanes)), asked], axis=1)
    extra = jnp.pad(extra, ((0, 0), (0, -extra.shape[1] % 8), (0, 0)))

    *blocks, shared, own = pack(part, recv, extra, dp, pa, pb)
    gaps = list(zip(*partners(dp)))
    sizes = (rows_a, rows_b, docs, num_queries, dp, lanes)
    blocks = trade(blocks, dp) + [trade_shared(shared), own]
    gaps += [(SHARED, SHARED), (0, 0)]
    late = min(1, len(blocks) - 3)
    rest = [t for t in range(len(blocks)) if t != late]
    grads = grads_of([blocks[t] for t in rest], [gaps[t] for t in rest], (), *sizes)
    grads = grads_of([blocks[late]], [gaps[late]], (grads,), *sizes)
    share = gram(grads, swap_cores(grads), docs)
    scale = float(ranks * ranks) ** -0.5
    if docs <= 64:
        others = sum(trade([share] * (owners // 2 - 1), owners))
        share = others + jnp.where(lax.axis_index("tensor") == 0, share, trade_shared(share))
        return solve(share, swap_cores(share), docs, num_queries, scale).T
    share = lax.psum(share, "dp") * (owners / dp)
    return solve_large(jnp.concatenate([share[:, :docs], share[:, docs:]], axis=0).T, docs, num_queries, scale).T


def solution(mesh):
    return jax.shard_map(
        local,
        mesh=mesh,
        in_specs=(
            P(("groups", "dp"), "tensor"),
            P(("groups", "dp"), "tensor"),
            P("tensor", None),
            P("tensor", None),
            P(("groups", "dp")),
            P(("groups", "dp"), None),
        ),
        out_specs=P("groups", "dp"),
        check_vma=False,
    )
```

```python
import functools

import jax
import jax.numpy as jnp
from jax import lax
from jax.experimental import pallas as pl
from jax.experimental.pallas import tpu as pltpu
from jax.sharding import PartitionSpec as P

TOK_DEV = 256
DOC_DEV = 8
LANES = 128
FLIGHT = 7
SHARED = 1
NT = (((1,), (1,)), ((), ()))
HIGHEST = lax.Precision.HIGHEST
VMEM = pl.BlockSpec(memory_space=pltpu.VMEM)
HBM = pl.BlockSpec(memory_space=pltpu.HBM)


def vmem_params(mib):
    return pltpu.CompilerParams(vmem_limit_bytes=int(mib * (1 << 20)))


def pieces(x):
    rows, units = x.shape
    split = x.reshape(rows // 8, 8, units // (2 * LANES), 2, LANES).transpose(0, 2, 3, 1, 4)
    return split.reshape(rows // 8, units // (2 * LANES), 16, LANES)


def chunks_of(length, ramp, tail):
    left = length - sum(ramp) - sum(tail)
    sizes = [*ramp, *([4] * (left // 4)), *([left % 4] if left % 4 else []), *tail]
    return [(sum(sizes[:i]), size) for i, size in enumerate(sizes)]


def project_kernel(g_chunks, h_chunks, h_ref, g_ref, pin_ref, pout_ref, out_ref, h_buf, g_buf, pin_buf, pout_buf, fold_ref, sems):
    plan = [(pout_ref, pout_buf, g_ref, g_buf, at) for at in g_chunks] + [(pin_ref, pin_buf, h_ref, h_buf, at) for at in h_chunks]
    copies = []
    for i, (proj, proj_buf, data, data_buf, (start, size)) in enumerate(plan):
        at = pl.ds(start, size)
        copies.append((
            pltpu.make_async_copy(proj.at[:, at], proj_buf.at[:, at], sems.at[2 * i]),
            pltpu.make_async_copy(data.at[:, at], data_buf.at[:, at], sems.at[2 * i + 1]),
        ))

    def start(i):
        if i < len(copies):
            for copy in copies[i]:
                copy.start()

    for i in range(FLIGHT):
        start(i)
    lane = lax.broadcasted_iota(jnp.int32, fold_ref.shape, 0)
    token = lax.broadcasted_iota(jnp.int32, fold_ref.shape, 1)
    fold_ref[...] = jnp.where(lane // 16 * 8 + lane % 8 == token, 1.0, 0.0).astype(jnp.bfloat16)

    def line_up(ref, first, size):
        blocks = [ref[:, j].reshape(ref.shape[0] * 16, LANES) for j in range(first, first + size)]
        return jnp.concatenate(blocks, axis=1)

    totals = [None, None]
    for i, (_, proj_buf, _, data_buf, (first, size)) in enumerate(plan):
        for copy in copies[i]:
            copy.wait()
        start(i + FLIGHT)
        which = 0 if i < len(g_chunks) else 1
        part = lax.dot_general(
            line_up(proj_buf, first, size), line_up(data_buf, first, size), NT, preferred_element_type=jnp.float32
        )
        totals[which] = part if totals[which] is None else totals[which] + part

    spread = totals[0].shape[1]
    even = lax.broadcasted_iota(jnp.int32, (8, spread), 1) % 16 < 8
    lines = []
    for total in totals:
        for g in range(total.shape[0] // 16):
            lines.append(jnp.where(even, total[16 * g:16 * g + 8], total[16 * g + 8:16 * g + 16]))
    lines = jnp.concatenate(lines, axis=0)
    split = []
    for _ in range(3):
        split.append(lines.astype(jnp.bfloat16))
        lines = lines - split[-1].astype(jnp.float32)
    rows = out_ref.shape[0]
    sums = jnp.dot(jnp.concatenate(split, axis=0), fold_ref[...], preferred_element_type=jnp.float32)
    out_ref[...] = sums[2 * rows:] + sums[rows:2 * rows] + sums[:rows]


def project(hidden, out_grad, pin_t, pout_t):
    tokens, units = hidden.shape
    width = out_grad.shape[1]
    ranks = pin_t.shape[0] + pout_t.shape[0]
    operands = [pieces(x) for x in (hidden, out_grad, pin_t, pout_t)]
    g_chunks = chunks_of(operands[1].shape[1], (2,), ())
    h_chunks = chunks_of(operands[0].shape[1], (), (2, 2))
    return pl.pallas_call(
        functools.partial(project_kernel, g_chunks, h_chunks),
        out_shape=jax.ShapeDtypeStruct((ranks, tokens), jnp.float32),
        in_specs=[HBM] * 4,
        out_specs=VMEM,
        scratch_shapes=[pltpu.VMEM(x.shape, x.dtype) for x in operands]
        + [pltpu.VMEM((2 * tokens, tokens), jnp.bfloat16), pltpu.SemaphoreType.DMA((2 * len(g_chunks + h_chunks),))],
        compiler_params=vmem_params(53.5),
        cost_estimate=pl.CostEstimate(
            flops=2 * tokens * 64 * (units + width),
            bytes_accessed=2 * (tokens + 64) * (units + width),
            transcendentals=0,
        ),
        name="project",
    )(*operands)


def owners_of(dp):
    return max(dp // 2, 1)


def partners(dp):
    order = [m for far in (True, False) for m in range(1, dp) if m != SHARED and (2 * m >= dp) == far]
    return order[0::2], order[1::2]


def partner(dp, t):
    first, second = partners(dp)
    return jnp.where(lax.axis_index("tensor") == 0, first[t], second[t])


def pack_kernel(dp, pb, rows_a, rows_b, part_ref, recv_ref, extra_ref, *refs):
    outs, total_ref = refs[:-1], refs[-1]
    total_ref[...] = part_ref[...] + recv_ref[...]
    ranks, lanes = total_ref.shape[0] // 2, total_ref.shape[1]
    me = lax.axis_index("dp")
    lead = lax.axis_index("tensor") == 0

    def rows(out_ref, to, pick):
        owner = to % extra_ref.shape[0]
        p, q = owner // pb, owner % pb
        out_ref[0:rows_a, :] = pick(total_ref[pl.ds(pl.multiple_of(p * rows_a, rows_a), rows_a), :])
        out_ref[rows_a:rows_a + rows_b, :] = pick(total_ref[pl.ds(pl.multiple_of(ranks + q * rows_b, rows_b), rows_b), :])
        out_ref[rows_a + rows_b:, :] = pick(extra_ref[owner])

    def half(x):
        return jnp.where(lead, x[:, :lanes // 2], x[:, lanes // 2:])

    for t, out_ref in enumerate(outs[:-2]):
        rows(out_ref, me ^ partner(dp, t), lambda x: x)
    rows(outs[-2], me ^ SHARED, half)
    rows(outs[-1], me, half)


def pack(part, recv, extra, dp, pa, pb):
    ranks, lanes = part.shape[0] // 2, part.shape[1]
    rows_a, rows_b = ranks // pa, ranks // pb
    rows = rows_a + rows_b + extra.shape[1]
    count = dp // 2 - 1
    whole, half = (jax.ShapeDtypeStruct((rows, n), jnp.float32) for n in (lanes, lanes // 2))
    return pl.pallas_call(
        functools.partial(pack_kernel, dp, pb, rows_a, rows_b),
        out_shape=(whole,) * count + (half, half),
        in_specs=[VMEM] * 3,
        out_specs=(VMEM,) * (count + 2),
        scratch_shapes=[pltpu.VMEM(part.shape, jnp.float32)],
        compiler_params=vmem_params(16),
        name="pack",
    )(part, recv, extra)


def grads_kernel(rows_a, rows_b, docs, dp, whole, gaps, *refs):
    xs, before, (out_ref, outer_ref, member_ref) = refs[:len(gaps)], refs[len(gaps):-3], refs[-3:]
    wide = rows_a * rows_b
    first = rows_a + rows_b
    queries = out_ref.shape[0] - docs
    per = queries // dp
    place = lax.broadcasted_iota(jnp.int32, (queries, whole), 0)
    lane = lax.broadcasted_iota(jnp.int32, (queries, whole), 1)
    me = lax.axis_index("dp")
    core = lax.axis_index("tensor")
    mine = lane // (whole // 2) == core
    flat = [jnp.zeros((queries, whole), jnp.float32)] * (per * wide // whole)
    start = 0
    for x_ref, gap in zip(xs, gaps):
        lanes = x_ref.shape[1]
        at = slice(start, start + lanes)
        start += lanes
        g, b = x_ref[0:rows_a, :], x_ref[rows_a:first, :]
        ids = x_ref[first:first + 1, :].astype(jnp.int32)
        doc = lax.broadcasted_iota(jnp.int32, (docs, lanes), 0)
        member_ref[:, at] = jnp.where(doc == ids, 1.0, 0.0).astype(jnp.bfloat16)
        outer = (g[:, None, :] * b[None, :, :]).reshape(wide, lanes)
        high = outer.astype(jnp.bfloat16)
        outer_ref[0:wide, at] = high
        outer_ref[wide:, at] = (outer - high.astype(jnp.float32)).astype(jnp.bfloat16)
        held = place // per == me ^ jnp.where(core == 0, gap[0], gap[1])
        if lanes < whole:
            held = jnp.logical_and(held, mine)
        for j in range(len(flat)):
            line = x_ref[first + 1 + j:first + 2 + j, :]
            if lanes < whole:
                line = jnp.concatenate([line, line], axis=1)
            flat[j] = jnp.where(held, line, flat[j])
    sums = lax.dot_general(member_ref[...], outer_ref[...], NT, preferred_element_type=jnp.float32)
    sums = (sums[:, wide:] + sums[:, :wide]) * (TOK_DEV ** -0.5)
    flat = jnp.concatenate(flat, axis=1)
    asked = jnp.zeros((queries, wide), jnp.float32)
    which = lax.broadcasted_iota(jnp.int32, (queries, wide), 0) % per
    for q in range(per):
        asked = jnp.where(which == q, flat[:, q * wide:(q + 1) * wide], asked)
    if before:
        sums, asked = sums + before[0][0:docs, :], asked + before[0][docs:, :]
    out_ref[0:docs, :] = sums
    out_ref[docs:, :] = asked


def grads_of(xs, gaps, before, rows_a, rows_b, docs, queries, dp, whole):
    tokens = sum(x.shape[1] for x in xs)
    wide = rows_a * rows_b
    operands = (*xs, *before)
    return pl.pallas_call(
        functools.partial(grads_kernel, rows_a, rows_b, docs, dp, whole, gaps),
        out_shape=jax.ShapeDtypeStruct((docs + queries, wide), jnp.float32),
        in_specs=[VMEM] * len(operands),
        out_specs=VMEM,
        scratch_shapes=[
            pltpu.VMEM((2 * wide, tokens), jnp.bfloat16),
            pltpu.VMEM((docs, tokens), jnp.bfloat16),
        ],
        compiler_params=vmem_params(40),
        cost_estimate=pl.CostEstimate(
            flops=4 * docs * wide * tokens, bytes_accessed=4 * (rows_a + rows_b) * tokens, transcendentals=0
        ),
        name="grads",
    )(*operands)


def gram_kernel(docs, part_ref, recv_ref, out_ref):
    both = part_ref[...] + recv_ref[...]
    share = lax.dot_general(both, both[:docs], NT, precision=HIGHEST, preferred_element_type=jnp.float32)
    half = share.shape[0] // 2
    out_ref[...] = jnp.concatenate([share[:half], share[half:]], axis=1)


def gram(part, recv, docs):
    return pl.pallas_call(
        functools.partial(gram_kernel, docs),
        out_shape=jax.ShapeDtypeStruct((part.shape[0] // 2, 2 * docs), jnp.float32),
        in_specs=[VMEM] * 2,
        out_specs=VMEM,
        compiler_params=vmem_params(16),
        name="gram",
    )(part, recv)


def reciprocal(x):
    y = pl.reciprocal(x, approx=True)
    for _ in range(2):
        y = y * (2.0 - x * y)
    return y


def solve_kernel(docs, queries, scale, x_ref, recv_ref, out_ref, done_ref):
    total = x_ref[...] + recv_ref[...]
    stack = jnp.concatenate([total[:, :docs], total[:, docs:]], axis=0)
    cols = done_ref.shape[1]
    diagonal = [lax.broadcasted_iota(jnp.int32, (docs, docs), i) for i in range(2)]
    mean_diag = jnp.sum(jnp.where(diagonal[0] == diagonal[1], stack[:docs], 0.0)) * (1.0 / docs)
    stack = jnp.concatenate([stack, jnp.zeros((cols - stack.shape[0], docs), jnp.float32)], axis=0)
    total = stack.T
    row = lax.broadcasted_iota(jnp.int32, (docs, cols), 0)
    col = lax.broadcasted_iota(jnp.int32, (docs, cols), 1)
    work = total + jnp.where(row == col, 0.1 * mean_diag, 0.0)
    size = 8
    here = lax.broadcasted_iota(jnp.int32, (size, cols), 0)
    rows = [work[i:i + size] for i in range(0, docs, size)]
    for r in range(len(rows)):
        wide = [[jnp.broadcast_to(x[:, c:c + 1], (size, cols)) for c in range(r * size, (r + 1) * size)] for x in rows]
        pivot, line = wide[r], rows[r]
        scale_rows = jnp.ones((size, cols), jnp.float32)
        for j in range(size):
            inverse = reciprocal(pivot[j][j:j + 1])
            factor = jnp.where(here == j, 0.0, pivot[j]) * inverse
            pivot = [x if i <= j else x - factor * x[j:j + 1] for i, x in enumerate(pivot)]
            line = line - factor * line[j:j + 1]
            scale_rows = jnp.where(here == j, inverse, scale_rows)
        line = line * scale_rows
        for s in range(len(rows)):
            if s == r:
                rows[s] = line
            else:
                terms = [wide[s][j] * line[j:j + 1] for j in range(size)]
                rows[s] = rows[s] - (((terms[0] + terms[1]) + (terms[2] + terms[3]))
                                     + ((terms[4] + terms[5]) + (terms[6] + terms[7])))
    for r, x in enumerate(rows):
        done_ref[r * size:(r + 1) * size, :] = x * (mean_diag * scale)
    mine = pl.ds(pl.multiple_of(lax.axis_index("dp") * DOC_DEV, DOC_DEV), DOC_DEV)
    out_ref[...] = done_ref[mine, :][:, docs:docs + queries]


def solve(x, recv, docs, queries, scale):
    return pl.pallas_call(
        functools.partial(solve_kernel, docs, queries, scale),
        out_shape=jax.ShapeDtypeStruct((DOC_DEV, queries), jnp.float32),
        in_specs=[VMEM] * 2,
        out_specs=VMEM,
        scratch_shapes=[pltpu.VMEM((docs, -(-(docs + queries) // LANES) * LANES), jnp.float32)],
        compiler_params=vmem_params(16),
        name="solve",
    )(x, recv)


def solve_large(total, docs, queries, scale):
    kernel = total[:, :docs]
    mean_diag = jnp.trace(kernel) / docs
    factor = jnp.linalg.cholesky(kernel + 0.1 * mean_diag * jnp.eye(docs, dtype=jnp.float32))
    solved = jax.scipy.linalg.cho_solve((factor, True), total[:, docs:docs + queries]) * (mean_diag * scale)
    return lax.dynamic_slice_in_dim(solved, lax.axis_index("dp") * DOC_DEV, DOC_DEV, 0)


def swap_cores(x):
    cores = lax.axis_size("tensor")
    return lax.ppermute(x, "tensor", [(i, cores - 1 - i) for i in range(cores)])


def trade(xs, group):
    dp = lax.axis_size("dp")
    got = []
    for x, ms in zip(xs, zip(*partners(group))):
        pairs = [(i * 2 + k, (i ^ m) * 2 + k) for i in range(dp) for k, m in enumerate(ms)]
        got.append(lax.ppermute(x, ("dp", "tensor"), pairs))
    return got


def trade_shared(x):
    dp = lax.axis_size("dp")
    return lax.ppermute(x, "dp", [(i, i ^ SHARED) for i in range(dp)])


def local(hidden, out_grad, proj_in, proj_out, doc_ids, queries):
    dp = lax.axis_size("dp")
    docs, num_queries = DOC_DEV * dp, queries.shape[0] * dp
    ranks = proj_in.shape[1]
    owners = owners_of(dp)
    pa = 1
    while pa * pa < owners:
        pa *= 2
    pb = owners // pa
    rows_a, rows_b = ranks // pa, ranks // pb

    part = project(hidden, out_grad, proj_in.T, proj_out.T)
    recv = swap_cores(part)

    lanes = part.shape[1]
    ids = doc_ids.astype(jnp.float32)
    asked = queries.reshape(-1, pa, rows_a, pb, rows_b).transpose(1, 3, 0, 2, 4).reshape(owners, -1, lanes)
    extra = jnp.concatenate([jnp.broadcast_to(ids, (owners, 1, lanes)), asked], axis=1)
    extra = jnp.pad(extra, ((0, 0), (0, -extra.shape[1] % 8), (0, 0)))

    *blocks, shared, own = pack(part, recv, extra, dp, pa, pb)
    gaps = list(zip(*partners(dp)))
    sizes = (rows_a, rows_b, docs, num_queries, dp, lanes)
    blocks = trade(blocks, dp) + [trade_shared(shared), own]
    gaps += [(SHARED, SHARED), (0, 0)]
    count = len(blocks) - 2
    grads = ()
    for part in ([count + 1, 0], [1], [count, *range(2, count)]):
        grads = (grads_of([blocks[t] for t in part], [gaps[t] for t in part], grads, *sizes),)
    grads = grads[0]
    share = gram(grads, swap_cores(grads), docs)
    scale = float(ranks * ranks) ** -0.5
    if docs <= 64:
        others = sum(trade([share] * (owners // 2 - 1), owners))
        share = others + jnp.where(lax.axis_index("tensor") == 0, share, trade_shared(share))
        return solve(share, swap_cores(share), docs, num_queries, scale).T
    share = lax.psum(share, "dp") * (owners / dp)
    return solve_large(jnp.concatenate([share[:, :docs], share[:, docs:]], axis=0).T, docs, num_queries, scale).T


def solution(mesh):
    return jax.shard_map(
        local,
        mesh=mesh,
        in_specs=(
            P(("groups", "dp"), "tensor"),
            P(("groups", "dp"), "tensor"),
            P("tensor", None),
            P("tensor", None),
            P(("groups", "dp")),
            P(("groups", "dp"), None),
        ),
        out_specs=P("groups", "dp"),
        check_vma=False,
    )
```

```python
import functools

import jax
import jax.numpy as jnp
from jax import lax
from jax.experimental import pallas as pl
from jax.experimental.pallas import tpu as pltpu
from jax.sharding import PartitionSpec as P

TOK_DEV = 256
DOC_DEV = 8
LANES = 128
FLIGHT = 7
SHARED = 1
NT = (((1,), (1,)), ((), ()))
HIGHEST = lax.Precision.HIGHEST
VMEM = pl.BlockSpec(memory_space=pltpu.VMEM)
HBM = pl.BlockSpec(memory_space=pltpu.HBM)


def vmem_params(mib):
    return pltpu.CompilerParams(vmem_limit_bytes=int(mib * (1 << 20)))


def pieces(x):
    rows, units = x.shape
    split = x.reshape(rows // 8, 8, units // (2 * LANES), 2, LANES).transpose(0, 2, 3, 1, 4)
    return split.reshape(rows // 8, units // (2 * LANES), 16, LANES)


def chunks_of(length, ramp, tail):
    left = length - sum(ramp) - sum(tail)
    sizes = [*ramp, *([6] * (left // 6)), *([left % 6] if left % 6 else []), *tail]
    return [(sum(sizes[:i]), size) for i, size in enumerate(sizes)]


def project_kernel(g_chunks, h_chunks, h_ref, g_ref, pin_ref, pout_ref, out_ref, h_buf, g_buf, pin_buf, pout_buf, fold_ref, sems):
    plan = [(pout_ref, pout_buf, g_ref, g_buf, at) for at in g_chunks] + [(pin_ref, pin_buf, h_ref, h_buf, at) for at in h_chunks]
    copies = []
    for i, (proj, proj_buf, data, data_buf, (start, size)) in enumerate(plan):
        at = pl.ds(start, size)
        copies.append((
            pltpu.make_async_copy(proj.at[:, at], proj_buf.at[:, at], sems.at[2 * i]),
            pltpu.make_async_copy(data.at[:, at], data_buf.at[:, at], sems.at[2 * i + 1]),
        ))

    def start(i):
        if i < len(copies):
            for copy in copies[i]:
                copy.start()

    for i in range(FLIGHT):
        start(i)
    lane = lax.broadcasted_iota(jnp.int32, fold_ref.shape, 0)
    token = lax.broadcasted_iota(jnp.int32, fold_ref.shape, 1)
    fold_ref[...] = jnp.where(lane // 16 * 8 + lane % 8 == token, 1.0, 0.0).astype(jnp.bfloat16)

    def line_up(ref, first, size):
        blocks = [ref[:, j].reshape(ref.shape[0] * 16, LANES) for j in range(first, first + size)]
        return jnp.concatenate(blocks, axis=1)

    totals = [None, None]
    for i, (_, proj_buf, _, data_buf, (first, size)) in enumerate(plan):
        for copy in copies[i]:
            copy.wait()
        start(i + FLIGHT)
        which = 0 if i < len(g_chunks) else 1
        part = lax.dot_general(
            line_up(proj_buf, first, size), line_up(data_buf, first, size), NT, preferred_element_type=jnp.float32
        )
        totals[which] = part if totals[which] is None else totals[which] + part

    spread = totals[0].shape[1]
    even = lax.broadcasted_iota(jnp.int32, (8, spread), 1) % 16 < 8
    lines = []
    for total in totals:
        for g in range(total.shape[0] // 16):
            lines.append(jnp.where(even, total[16 * g:16 * g + 8], total[16 * g + 8:16 * g + 16]))
    lines = jnp.concatenate(lines, axis=0)
    split = []
    for _ in range(3):
        split.append(lines.astype(jnp.bfloat16))
        lines = lines - split[-1].astype(jnp.float32)
    rows = out_ref.shape[0]
    sums = jnp.dot(jnp.concatenate(split, axis=0), fold_ref[...], preferred_element_type=jnp.float32)
    out_ref[...] = sums[2 * rows:] + sums[rows:2 * rows] + sums[:rows]


def project(hidden, out_grad, pin_t, pout_t):
    tokens, units = hidden.shape
    width = out_grad.shape[1]
    ranks = pin_t.shape[0] + pout_t.shape[0]
    operands = [pieces(x) for x in (hidden, out_grad, pin_t, pout_t)]
    g_chunks = chunks_of(operands[1].shape[1], (1, 2, 3, 4), ())
    h_chunks = chunks_of(operands[0].shape[1], (), (4, 2, 2))
    return pl.pallas_call(
        functools.partial(project_kernel, g_chunks, h_chunks),
        out_shape=jax.ShapeDtypeStruct((ranks, tokens), jnp.float32),
        in_specs=[HBM] * 4,
        out_specs=VMEM,
        scratch_shapes=[pltpu.VMEM(x.shape, x.dtype) for x in operands]
        + [pltpu.VMEM((2 * tokens, tokens), jnp.bfloat16), pltpu.SemaphoreType.DMA((2 * len(g_chunks + h_chunks),))],
        compiler_params=vmem_params(53.5),
        cost_estimate=pl.CostEstimate(
            flops=2 * tokens * 64 * (units + width),
            bytes_accessed=2 * (tokens + 64) * (units + width),
            transcendentals=0,
        ),
        name="project",
    )(*operands)


def owners_of(dp):
    return max(dp // 2, 1)


def partners(dp):
    order = [m for far in (True, False) for m in range(1, dp) if m != SHARED and (2 * m >= dp) == far]
    return order[0::2], order[1::2]


def partner(dp, t):
    first, second = partners(dp)
    return jnp.where(lax.axis_index("tensor") == 0, first[t], second[t])


def pack_kernel(dp, pb, rows_a, rows_b, span, part_ref, recv_ref, extra_ref, *refs):
    outs, total_ref = refs[:-1], refs[-1]
    total_ref[...] = part_ref[...] + recv_ref[...]
    ranks = total_ref.shape[0] // 2
    rows = rows_a + rows_b
    owners, ids = extra_ref.shape[0], 2 * span
    me = lax.axis_index("dp")
    lead = lax.axis_index("tensor") == 0

    def slices(owner):
        p, q = owner // pb, owner % pb
        g = total_ref[pl.ds(pl.multiple_of(p * rows_a, rows_a), rows_a), :]
        b = total_ref[pl.ds(pl.multiple_of(ranks + q * rows_b, rows_b), rows_b), :]
        return [(g[:, i:i + LANES], b[:, i:i + LANES]) for i in (0, LANES)]

    for t, out_ref in enumerate(outs[:-2]):
        owner = (me ^ partner(dp, t)) % owners
        for i, (g, b) in enumerate(slices(owner)):
            out_ref[i * rows:i * rows + rows_a, :] = g
            out_ref[i * rows + rows_a:(i + 1) * rows, :] = b
        out_ref[2 * rows:, :] = extra_ref[owner]
    for out_ref, to in zip(outs[-2:], (me ^ SHARED, me)):
        owner = to % owners
        (g, b), (later_g, later_b) = slices(owner)
        extra = extra_ref[owner]
        out_ref[0:rows_a, :] = jnp.where(lead, g, later_g)
        out_ref[rows_a:rows, :] = jnp.where(lead, b, later_b)
        out_ref[rows:rows + span, :] = jnp.where(lead, extra[0:span], extra[span:ids])
        rest = out_ref.shape[0] - rows - span
        out_ref[rows + span:, :] = jnp.broadcast_to(jnp.where(lead, extra[ids:ids + 1], extra[ids + 1:ids + 2]), (rest, LANES))


def pack(part, recv, extra, dp, pa, pb):
    ranks = part.shape[0] // 2
    rows_a, rows_b = ranks // pa, ranks // pb
    rows, span = rows_a + rows_b, rows_a * rows_b // LANES
    whole = jax.ShapeDtypeStruct((2 * rows + extra.shape[1], LANES), jnp.float32)
    half = jax.ShapeDtypeStruct((rows + 8 * (span // 8 + 1), LANES), jnp.float32)
    count = dp // 2 - 1
    return pl.pallas_call(
        functools.partial(pack_kernel, dp, pb, rows_a, rows_b, span),
        out_shape=(whole,) * count + (half, half),
        in_specs=[VMEM] * 3,
        out_specs=(VMEM,) * (count + 2),
        scratch_shapes=[pltpu.VMEM(part.shape, jnp.float32)],
        compiler_params=vmem_params(16),
        name="pack",
    )(part, recv, extra)


def grads_kernel(rows_a, rows_b, docs, dp, gaps, wholes, *refs):
    xs, before, (out_ref, outer_ref, member_ref) = refs[:len(gaps)], refs[len(gaps):-3], refs[-3:]
    rows, wide = rows_a + rows_b, rows_a * rows_b
    span = wide // LANES
    queries = out_ref.shape[0] - docs
    doc = lax.broadcasted_iota(jnp.int32, (docs, LANES), 0)
    place = lax.broadcasted_iota(jnp.int32, (queries, LANES), 0)
    me = lax.axis_index("dp")
    core = lax.axis_index("tensor")
    asked = [jnp.zeros((queries, LANES), jnp.float32)] * span
    start = 0
    for x_ref, gap, whole in zip(xs, gaps, wholes):
        parts = 2 if whole else 1
        base = parts * rows
        for i in range(parts):
            at = slice(start, start + LANES)
            start += LANES
            g, b = x_ref[i * rows:i * rows + rows_a, :], x_ref[i * rows + rows_a:(i + 1) * rows, :]
            ids = base + parts * span + i
            member_ref[:, at] = jnp.where(doc == x_ref[ids:ids + 1, :].astype(jnp.int32), 1.0, 0.0).astype(jnp.bfloat16)
            outer = (g[:, None, :] * b[None, :, :]).reshape(wide, LANES)
            high = outer.astype(jnp.bfloat16)
            outer_ref[0:wide, at] = high
            outer_ref[wide:, at] = (outer - high.astype(jnp.float32)).astype(jnp.bfloat16)
        source = 2 * (me ^ jnp.where(core == 0, gap[0], gap[1]))
        for i in range(parts):
            held = place == source + (i if whole else core)
            for j in range(span):
                row = base + i * span + j
                asked[j] = jnp.where(held, x_ref[row:row + 1, :], asked[j])
    sums = lax.dot_general(member_ref[...], outer_ref[...], NT, preferred_element_type=jnp.float32)
    sums = (sums[:, wide:] + sums[:, :wide]) * (TOK_DEV ** -0.5)
    asked = jnp.concatenate(asked, axis=1)
    if before:
        sums, asked = sums + before[0][0:docs, :], asked + before[0][docs:, :]
    out_ref[0:docs, :] = sums
    out_ref[docs:, :] = asked


def grads_of(xs, gaps, wholes, before, rows_a, rows_b, docs, queries, dp):
    tokens = LANES * (len(xs) + sum(wholes))
    wide = rows_a * rows_b
    operands = (*xs, *before)
    return pl.pallas_call(
        functools.partial(grads_kernel, rows_a, rows_b, docs, dp, gaps, wholes),
        out_shape=jax.ShapeDtypeStruct((docs + queries, wide), jnp.float32),
        in_specs=[VMEM] * len(operands),
        out_specs=VMEM,
        scratch_shapes=[
            pltpu.VMEM((2 * wide, tokens), jnp.bfloat16),
            pltpu.VMEM((docs, tokens), jnp.bfloat16),
        ],
        compiler_params=vmem_params(40),
        cost_estimate=pl.CostEstimate(
            flops=4 * docs * wide * tokens, bytes_accessed=4 * (rows_a + rows_b) * tokens, transcendentals=0
        ),
        name="grads",
    )(*operands)


def gram_kernel(docs, part_ref, recv_ref, out_ref):
    both = part_ref[...] + recv_ref[...]
    share = lax.dot_general(both, both[:docs], NT, precision=HIGHEST, preferred_element_type=jnp.float32)
    half = share.shape[0] // 2
    out_ref[...] = jnp.concatenate([share[:half], share[half:]], axis=1)


def gram(part, recv, docs):
    return pl.pallas_call(
        functools.partial(gram_kernel, docs),
        out_shape=jax.ShapeDtypeStruct((part.shape[0] // 2, 2 * docs), jnp.float32),
        in_specs=[VMEM] * 2,
        out_specs=VMEM,
        compiler_params=vmem_params(16),
        name="gram",
    )(part, recv)


def solve_kernel(docs, queries, scale, x_ref, recv_ref, out_ref, done_ref):
    total = x_ref[...] + recv_ref[...]
    stack = jnp.concatenate([total[:, :docs], total[:, docs:]], axis=0)
    cols = done_ref.shape[1]
    diagonal = [lax.broadcasted_iota(jnp.int32, (docs, docs), i) for i in range(2)]
    mean_diag = jnp.sum(jnp.where(diagonal[0] == diagonal[1], stack[:docs], 0.0)) * (1.0 / docs)
    stack = jnp.concatenate([stack, jnp.zeros((cols - stack.shape[0], docs), jnp.float32)], axis=0)
    total = stack.T
    row = lax.broadcasted_iota(jnp.int32, (docs, cols), 0)
    col = lax.broadcasted_iota(jnp.int32, (docs, cols), 1)
    work = total + jnp.where(row == col, 0.1 * mean_diag, 0.0)
    size = 8
    here = lax.broadcasted_iota(jnp.int32, (size, cols), 0)
    rows = [work[i:i + size] for i in range(0, docs, size)]
    for r in range(len(rows)):
        wide = [[jnp.broadcast_to(x[:, c:c + 1], (size, cols)) for c in range(r * size, (r + 1) * size)] for x in rows]
        pivot, line = wide[r], rows[r]
        scale_rows = jnp.ones((size, cols), jnp.float32)
        for j in range(size):
            inverse = 1.0 / pivot[j][j:j + 1]
            factor = jnp.where(here == j, 0.0, pivot[j]) * inverse
            pivot = [x if i <= j else x - factor * x[j:j + 1] for i, x in enumerate(pivot)]
            line = line - factor * line[j:j + 1]
            scale_rows = jnp.where(here == j, inverse, scale_rows)
        line = line * scale_rows
        for s in range(len(rows)):
            if s == r:
                rows[s] = line
            else:
                terms = [wide[s][j] * line[j:j + 1] for j in range(size)]
                rows[s] = rows[s] - (((terms[0] + terms[1]) + (terms[2] + terms[3]))
                                     + ((terms[4] + terms[5]) + (terms[6] + terms[7])))
    for r, x in enumerate(rows):
        done_ref[r * size:(r + 1) * size, :] = x * (mean_diag * scale)
    mine = pl.ds(pl.multiple_of(lax.axis_index("dp") * DOC_DEV, DOC_DEV), DOC_DEV)
    out_ref[...] = done_ref[mine, :][:, docs:docs + queries]


def solve(x, recv, docs, queries, scale):
    return pl.pallas_call(
        functools.partial(solve_kernel, docs, queries, scale),
        out_shape=jax.ShapeDtypeStruct((DOC_DEV, queries), jnp.float32),
        in_specs=[VMEM] * 2,
        out_specs=VMEM,
        scratch_shapes=[pltpu.VMEM((docs, -(-(docs + queries) // LANES) * LANES), jnp.float32)],
        compiler_params=vmem_params(16),
        name="solve",
    )(x, recv)


def solve_large(total, docs, queries, scale):
    kernel = total[:, :docs]
    mean_diag = jnp.trace(kernel) / docs
    factor = jnp.linalg.cholesky(kernel + 0.1 * mean_diag * jnp.eye(docs, dtype=jnp.float32))
    solved = jax.scipy.linalg.cho_solve((factor, True), total[:, docs:docs + queries]) * (mean_diag * scale)
    return lax.dynamic_slice_in_dim(solved, lax.axis_index("dp") * DOC_DEV, DOC_DEV, 0)


def swap_cores(x):
    cores = lax.axis_size("tensor")
    return lax.ppermute(x, "tensor", [(i, cores - 1 - i) for i in range(cores)])


def trade(xs, group):
    dp = lax.axis_size("dp")
    got = []
    for x, ms in zip(xs, zip(*partners(group))):
        pairs = [(i * 2 + k, (i ^ m) * 2 + k) for i in range(dp) for k, m in enumerate(ms)]
        got.append(lax.ppermute(x, ("dp", "tensor"), pairs))
    return got


def trade_shared(x):
    dp = lax.axis_size("dp")
    return lax.ppermute(x, "dp", [(i, i ^ SHARED) for i in range(dp)])


def local(hidden, out_grad, proj_in, proj_out, doc_ids, queries):
    dp = lax.axis_size("dp")
    docs, num_queries = DOC_DEV * dp, queries.shape[0] * dp
    ranks = proj_in.shape[1]
    owners = owners_of(dp)
    pa = 1
    while pa * pa < owners:
        pa *= 2
    pb = owners // pa
    rows_a, rows_b = ranks // pa, ranks // pb

    part = project(hidden, out_grad, proj_in.T, proj_out.T)
    recv = swap_cores(part)

    ids = jnp.broadcast_to(doc_ids.astype(jnp.float32).reshape(2, LANES), (owners, 2, LANES))
    asked = queries.reshape(-1, pa, rows_a, pb, rows_b).transpose(1, 3, 0, 2, 4).reshape(owners, -1, LANES)
    extra = jnp.concatenate([asked, ids], axis=1)
    extra = jnp.pad(extra, ((0, 0), (0, -extra.shape[1] % 8), (0, 0)))

    *blocks, shared, own = pack(part, recv, extra, dp, pa, pb)
    blocks = trade(blocks, dp) + [trade_shared(shared), own]
    gaps = [*zip(*partners(dp)), (SHARED, SHARED), (0, 0)]
    wholes = [True] * (len(blocks) - 2) + [False, False]
    sizes = (rows_a, rows_b, docs, num_queries, dp)
    late = min(1, len(blocks) - 3)
    rest = [t for t in range(len(blocks)) if t != late]
    grads = ()
    for part in (rest, [late]):
        grads = (grads_of(*([x[t] for t in part] for x in (blocks, gaps, wholes)), grads, *sizes),)
    grads = grads[0]
    share = gram(grads, swap_cores(grads), docs)
    scale = float(ranks * ranks) ** -0.5
    if docs <= 64:
        others = sum(trade([share] * (owners // 2 - 1), owners))
        share = others + jnp.where(lax.axis_index("tensor") == 0, share, trade_shared(share))
        return solve(share, swap_cores(share), docs, num_queries, scale).T
    share = lax.psum(share, "dp") * (owners / dp)
    return solve_large(jnp.concatenate([share[:, :docs], share[:, docs:]], axis=0).T, docs, num_queries, scale).T


def solution(mesh):
    return jax.shard_map(
        local,
        mesh=mesh,
        in_specs=(
            P(("groups", "dp"), "tensor"),
            P(("groups", "dp"), "tensor"),
            P("tensor", None),
            P("tensor", None),
            P(("groups", "dp")),
            P(("groups", "dp"), None),
        ),
        out_specs=P("groups", "dp"),
        check_vma=False,
    )
```

```python
import functools

import jax
import jax.numpy as jnp
from jax import lax
from jax.experimental import pallas as pl
from jax.experimental.pallas import tpu as pltpu
from jax.sharding import PartitionSpec as P

TOK_DEV = 256
DOC_DEV = 8
LANES = 128
FLIGHT = 7
SHARED = 1
NT = (((1,), (1,)), ((), ()))
HIGHEST = lax.Precision.HIGHEST
VMEM = pl.BlockSpec(memory_space=pltpu.VMEM)
HBM = pl.BlockSpec(memory_space=pltpu.HBM)


def vmem_params(mib):
    return pltpu.CompilerParams(vmem_limit_bytes=int(mib * (1 << 20)))


def pieces(x):
    rows, units = x.shape
    split = x.reshape(rows // 8, 8, units // (2 * LANES), 2, LANES).transpose(0, 2, 3, 1, 4)
    return split.reshape(rows // 8, units // (2 * LANES), 16, LANES)


def chunks_of(length, ramp, tail):
    left = length - sum(ramp) - sum(tail)
    sizes = [*ramp, *([6] * (left // 6)), *([left % 6] if left % 6 else []), *tail]
    return [(sum(sizes[:i]), size) for i, size in enumerate(sizes)]


def project_kernel(g_chunks, h_chunks, h_ref, g_ref, pin_ref, pout_ref, out_ref, h_buf, g_buf, pin_buf, pout_buf, sems):
    plan = [(pout_ref, pout_buf, g_ref, g_buf, at) for at in g_chunks] + [(pin_ref, pin_buf, h_ref, h_buf, at) for at in h_chunks]
    copies = []
    for i, (proj, proj_buf, data, data_buf, (start, size)) in enumerate(plan):
        at = pl.ds(start, size)
        copies.append((
            pltpu.make_async_copy(proj.at[:, at], proj_buf.at[:, at], sems.at[2 * i]),
            pltpu.make_async_copy(data.at[:, at], data_buf.at[:, at], sems.at[2 * i + 1]),
        ))

    def start(i):
        if i < len(copies):
            for copy in copies[i]:
                copy.start()

    for i in range(FLIGHT):
        start(i)

    def line_up(ref, first, size):
        blocks = [ref[:, j].reshape(ref.shape[0] * 16, LANES) for j in range(first, first + size)]
        return jnp.concatenate(blocks, axis=1)

    totals = [None, None]
    for i, (_, proj_buf, _, data_buf, (first, size)) in enumerate(plan):
        for copy in copies[i]:
            copy.wait()
        start(i + FLIGHT)
        which = 0 if i < len(g_chunks) else 1
        part = lax.dot_general(
            line_up(data_buf, first, size), line_up(proj_buf, first, size), NT, preferred_element_type=jnp.float32
        )
        totals[which] = part if totals[which] is None else totals[which] + part

    even = lax.broadcasted_iota(jnp.int32, (8, totals[0].shape[1]), 1) % 16 < 8
    done = 0
    for total in totals:
        lines = [jnp.where(even, total[j:j + 8], total[j + 8:j + 16]) for j in range(0, total.shape[0], 16)]
        lines = jnp.concatenate(lines, axis=0).T
        for j in range(0, lines.shape[0], 16):
            out_ref[done:done + 8, :] = lines[j:j + 8] + lines[j + 8:j + 16]
            done += 8


def project(hidden, out_grad, pin_t, pout_t):
    tokens, units = hidden.shape
    width = out_grad.shape[1]
    ranks = pin_t.shape[0] + pout_t.shape[0]
    operands = [pieces(x) for x in (hidden, out_grad, pin_t, pout_t)]
    g_chunks = chunks_of(operands[1].shape[1], (1, 2, 3, 4), ())
    h_chunks = chunks_of(operands[0].shape[1], (), (4, 2, 2))
    return pl.pallas_call(
        functools.partial(project_kernel, g_chunks, h_chunks),
        out_shape=jax.ShapeDtypeStruct((ranks, tokens), jnp.float32),
        in_specs=[HBM] * 4,
        out_specs=VMEM,
        scratch_shapes=[pltpu.VMEM(x.shape, x.dtype) for x in operands]
        + [pltpu.SemaphoreType.DMA((2 * len(g_chunks + h_chunks),))],
        compiler_params=vmem_params(53.5),
        cost_estimate=pl.CostEstimate(
            flops=2 * tokens * 64 * (units + width),
            bytes_accessed=2 * (tokens + 64) * (units + width),
            transcendentals=0,
        ),
        name="project",
    )(*operands)


def owners_of(dp):
    return max(dp // 2, 1)


def partners(dp):
    order = [m for far in (True, False) for m in range(1, dp) if m != SHARED and (2 * m >= dp) == far]
    return order[0::2], order[1::2]


def partner(dp, t):
    first, second = partners(dp)
    return jnp.where(lax.axis_index("tensor") == 0, first[t], second[t])


def pack_kernel(dp, pb, rows_a, rows_b, span, part_ref, recv_ref, extra_ref, *refs):
    outs, total_ref = refs[:-1], refs[-1]
    total_ref[...] = part_ref[...] + recv_ref[...]
    ranks = total_ref.shape[0] // 2
    rows = rows_a + rows_b
    owners, ids = extra_ref.shape[0], 2 * span
    me = lax.axis_index("dp")
    lead = lax.axis_index("tensor") == 0

    def slices(owner):
        p, q = owner // pb, owner % pb
        g = total_ref[pl.ds(pl.multiple_of(p * rows_a, rows_a), rows_a), :]
        b = total_ref[pl.ds(pl.multiple_of(ranks + q * rows_b, rows_b), rows_b), :]
        return [(g[:, i:i + LANES], b[:, i:i + LANES]) for i in (0, LANES)]

    for t, out_ref in enumerate(outs[:-2]):
        owner = (me ^ partner(dp, t)) % owners
        for i, (g, b) in enumerate(slices(owner)):
            out_ref[i * rows:i * rows + rows_a, :] = g
            out_ref[i * rows + rows_a:(i + 1) * rows, :] = b
        out_ref[2 * rows:, :] = extra_ref[owner]
    for out_ref, to in zip(outs[-2:], (me ^ SHARED, me)):
        owner = to % owners
        (g, b), (later_g, later_b) = slices(owner)
        extra = extra_ref[owner]
        out_ref[0:rows_a, :] = jnp.where(lead, g, later_g)
        out_ref[rows_a:rows, :] = jnp.where(lead, b, later_b)
        out_ref[rows:rows + span, :] = jnp.where(lead, extra[0:span], extra[span:ids])
        rest = out_ref.shape[0] - rows - span
        out_ref[rows + span:, :] = jnp.broadcast_to(jnp.where(lead, extra[ids:ids + 1], extra[ids + 1:ids + 2]), (rest, LANES))


def pack(part, recv, extra, dp, pa, pb):
    ranks = part.shape[0] // 2
    rows_a, rows_b = ranks // pa, ranks // pb
    rows, span = rows_a + rows_b, rows_a * rows_b // LANES
    whole = jax.ShapeDtypeStruct((2 * rows + extra.shape[1], LANES), jnp.float32)
    half = jax.ShapeDtypeStruct((rows + 8 * (span // 8 + 1), LANES), jnp.float32)
    count = dp // 2 - 1
    return pl.pallas_call(
        functools.partial(pack_kernel, dp, pb, rows_a, rows_b, span),
        out_shape=(whole,) * count + (half, half),
        in_specs=[VMEM] * 3,
        out_specs=(VMEM,) * (count + 2),
        scratch_shapes=[pltpu.VMEM(part.shape, jnp.float32)],
        compiler_params=vmem_params(16),
        name="pack",
    )(part, recv, extra)


def grads_kernel(rows_a, rows_b, docs, dp, gaps, wholes, *refs):
    xs, before, (out_ref, outer_ref, member_ref) = refs[:len(gaps)], refs[len(gaps):-3], refs[-3:]
    rows, wide = rows_a + rows_b, rows_a * rows_b
    span = wide // LANES
    queries = out_ref.shape[0] - docs
    doc = lax.broadcasted_iota(jnp.int32, (docs, LANES), 0)
    place = lax.broadcasted_iota(jnp.int32, (queries, LANES), 0)
    me = lax.axis_index("dp")
    core = lax.axis_index("tensor")
    asked = [jnp.zeros((queries, LANES), jnp.float32)] * span
    start = 0
    for x_ref, gap, whole in zip(xs, gaps, wholes):
        parts = 2 if whole else 1
        base = parts * rows
        for i in range(parts):
            at = slice(start, start + LANES)
            start += LANES
            g, b = x_ref[i * rows:i * rows + rows_a, :], x_ref[i * rows + rows_a:(i + 1) * rows, :]
            ids = base + parts * span + i
            member_ref[:, at] = jnp.where(doc == x_ref[ids:ids + 1, :].astype(jnp.int32), 1.0, 0.0).astype(jnp.bfloat16)
            outer = (g[:, None, :] * b[None, :, :]).reshape(wide, LANES)
            high = outer.astype(jnp.bfloat16)
            outer_ref[0:wide, at] = high
            outer_ref[wide:, at] = (outer - high.astype(jnp.float32)).astype(jnp.bfloat16)
        source = 2 * (me ^ jnp.where(core == 0, gap[0], gap[1]))
        for i in range(parts):
            held = place == source + (i if whole else core)
            for j in range(span):
                row = base + i * span + j
                asked[j] = jnp.where(held, x_ref[row:row + 1, :], asked[j])
    sums = lax.dot_general(member_ref[...], outer_ref[...], NT, preferred_element_type=jnp.float32)
    sums = (sums[:, wide:] + sums[:, :wide]) * (TOK_DEV ** -0.5)
    asked = jnp.concatenate(asked, axis=1)
    if before:
        sums, asked = sums + before[0][0:docs, :], asked + before[0][docs:, :]
    out_ref[0:docs, :] = sums
    out_ref[docs:, :] = asked


def grads_of(xs, gaps, wholes, before, rows_a, rows_b, docs, queries, dp):
    tokens = LANES * (len(xs) + sum(wholes))
    wide = rows_a * rows_b
    operands = (*xs, *before)
    return pl.pallas_call(
        functools.partial(grads_kernel, rows_a, rows_b, docs, dp, gaps, wholes),
        out_shape=jax.ShapeDtypeStruct((docs + queries, wide), jnp.float32),
        in_specs=[VMEM] * len(operands),
        out_specs=VMEM,
        scratch_shapes=[
            pltpu.VMEM((2 * wide, tokens), jnp.bfloat16),
            pltpu.VMEM((docs, tokens), jnp.bfloat16),
        ],
        compiler_params=vmem_params(40),
        cost_estimate=pl.CostEstimate(
            flops=4 * docs * wide * tokens, bytes_accessed=4 * (rows_a + rows_b) * tokens, transcendentals=0
        ),
        name="grads",
    )(*operands)


def gram_kernel(docs, part_ref, recv_ref, out_ref):
    both = part_ref[...] + recv_ref[...]
    share = lax.dot_general(both, both[:docs], NT, precision=HIGHEST, preferred_element_type=jnp.float32)
    half = share.shape[0] // 2
    out_ref[...] = jnp.concatenate([share[:half], share[half:]], axis=1)


def gram(part, recv, docs):
    return pl.pallas_call(
        functools.partial(gram_kernel, docs),
        out_shape=jax.ShapeDtypeStruct((part.shape[0] // 2, 2 * docs), jnp.float32),
        in_specs=[VMEM] * 2,
        out_specs=VMEM,
        compiler_params=vmem_params(16),
        name="gram",
    )(part, recv)


def solve_kernel(docs, queries, scale, *refs):
    xs, out_ref, done_ref = [x_ref[...] for x_ref in refs[:-2]], refs[-2], refs[-1]
    while len(xs) > 1:
        xs = [x + y for x, y in zip(xs[0::2], xs[1::2])]
    total = xs[0]
    stack = jnp.concatenate([total[:, :docs], total[:, docs:]], axis=0)
    cols = done_ref.shape[1]
    diagonal = [lax.broadcasted_iota(jnp.int32, (docs, docs), i) for i in range(2)]
    mean_diag = jnp.sum(jnp.where(diagonal[0] == diagonal[1], stack[:docs], 0.0)) * (1.0 / docs)
    stack = jnp.concatenate([stack, jnp.zeros((cols - stack.shape[0], docs), jnp.float32)], axis=0)
    total = stack.T
    row = lax.broadcasted_iota(jnp.int32, (docs, cols), 0)
    col = lax.broadcasted_iota(jnp.int32, (docs, cols), 1)
    work = total + jnp.where(row == col, 0.1 * mean_diag, 0.0)
    size = 8
    here = lax.broadcasted_iota(jnp.int32, (size, cols), 0)
    rows = [work[i:i + size] for i in range(0, docs, size)]
    for r in range(len(rows)):
        wide = [[jnp.broadcast_to(x[:, c:c + 1], (size, cols)) for c in range(r * size, (r + 1) * size)] for x in rows]
        pivot, line = wide[r], rows[r]
        scale_rows = jnp.ones((size, cols), jnp.float32)
        for j in range(size):
            inverse = 1.0 / pivot[j][j:j + 1]
            factor = jnp.where(here == j, 0.0, pivot[j]) * inverse
            pivot = [x if i <= j else x - factor * x[j:j + 1] for i, x in enumerate(pivot)]
            line = line - factor * line[j:j + 1]
            scale_rows = jnp.where(here == j, inverse, scale_rows)
        line = line * scale_rows
        for s in range(len(rows)):
            if s == r:
                rows[s] = line
            else:
                terms = [wide[s][j] * line[j:j + 1] for j in range(size)]
                rows[s] = rows[s] - (((terms[0] + terms[1]) + (terms[2] + terms[3]))
                                     + ((terms[4] + terms[5]) + (terms[6] + terms[7])))
    for r, x in enumerate(rows):
        done_ref[r * size:(r + 1) * size, :] = x * (mean_diag * scale)
    mine = pl.ds(pl.multiple_of(lax.axis_index("dp") * DOC_DEV, DOC_DEV), DOC_DEV)
    out_ref[...] = done_ref[mine, :][:, docs:docs + queries]


def solve(xs, docs, queries, scale):
    return pl.pallas_call(
        functools.partial(solve_kernel, docs, queries, scale),
        out_shape=jax.ShapeDtypeStruct((DOC_DEV, queries), jnp.float32),
        in_specs=[VMEM] * len(xs),
        out_specs=VMEM,
        scratch_shapes=[pltpu.VMEM((docs, -(-(docs + queries) // LANES) * LANES), jnp.float32)],
        compiler_params=vmem_params(16),
        name="solve",
    )(*xs)


def solve_large(total, docs, queries, scale):
    kernel = total[:, :docs]
    mean_diag = jnp.trace(kernel) / docs
    factor = jnp.linalg.cholesky(kernel + 0.1 * mean_diag * jnp.eye(docs, dtype=jnp.float32))
    solved = jax.scipy.linalg.cho_solve((factor, True), total[:, docs:docs + queries]) * (mean_diag * scale)
    return lax.dynamic_slice_in_dim(solved, lax.axis_index("dp") * DOC_DEV, DOC_DEV, 0)


def swap_cores(x):
    cores = lax.axis_size("tensor")
    return lax.ppermute(x, "tensor", [(i, cores - 1 - i) for i in range(cores)])


def trade(xs):
    dp = lax.axis_size("dp")
    got = []
    for x, ms in zip(xs, zip(*partners(dp))):
        pairs = [(i * 2 + k, (i ^ m) * 2 + k) for i in range(dp) for k, m in enumerate(ms)]
        got.append(lax.ppermute(x, ("dp", "tensor"), pairs))
    return got


def trade_shared(x):
    dp = lax.axis_size("dp")
    return lax.ppermute(x, "dp", [(i, i ^ SHARED) for i in range(dp)])


def local(hidden, out_grad, proj_in, proj_out, doc_ids, queries):
    dp = lax.axis_size("dp")
    docs, num_queries = DOC_DEV * dp, queries.shape[0] * dp
    ranks = proj_in.shape[1]
    owners = owners_of(dp)
    pa = 1
    while pa * pa < owners:
        pa *= 2
    pb = owners // pa
    rows_a, rows_b = ranks // pa, ranks // pb

    part = project(hidden, out_grad, proj_in.T, proj_out.T)
    recv = swap_cores(part)

    ids = jnp.broadcast_to(doc_ids.astype(jnp.float32).reshape(2, LANES), (owners, 2, LANES))
    asked = queries.reshape(-1, pa, rows_a, pb, rows_b).transpose(1, 3, 0, 2, 4).reshape(owners, -1, LANES)
    extra = jnp.concatenate([asked, ids], axis=1)
    extra = jnp.pad(extra, ((0, 0), (0, -extra.shape[1] % 8), (0, 0)))

    *blocks, shared, own = pack(part, recv, extra, dp, pa, pb)
    blocks = trade(blocks) + [trade_shared(shared), own]
    gaps = [*zip(*partners(dp)), (SHARED, SHARED), (0, 0)]
    wholes = [True] * (len(blocks) - 2) + [False, False]
    sizes = (rows_a, rows_b, docs, num_queries, dp)
    late = min(1, len(blocks) - 3)
    rest = [t for t in range(len(blocks)) if t != late]
    grads = ()
    for part in (rest, [late]):
        grads = (grads_of(*([x[t] for t in part] for x in (blocks, gaps, wholes)), grads, *sizes),)
    grads = grads[0]
    share = gram(grads, swap_cores(grads), docs)
    scale = float(ranks * ranks) ** -0.5
    if docs <= 64:
        others = [lax.ppermute(share, "dp", [(i, i ^ m) for i in range(dp)]) for m in range(owners - 1, 0, -1)]
        return solve([share] + others, docs, num_queries, scale).T
    share = lax.psum(share, "dp") * (owners / dp)
    return solve_large(jnp.concatenate([share[:, :docs], share[:, docs:]], axis=0).T, docs, num_queries, scale).T


def solution(mesh):
    return jax.shard_map(
        local,
        mesh=mesh,
        in_specs=(
            P(("groups", "dp"), "tensor"),
            P(("groups", "dp"), "tensor"),
            P("tensor", None),
            P("tensor", None),
            P(("groups", "dp")),
            P(("groups", "dp"), None),
        ),
        out_specs=P("groups", "dp"),
        check_vma=False,
    )
```

```python
import functools

import jax
import jax.numpy as jnp
from jax import lax
from jax.experimental import pallas as pl
from jax.experimental.pallas import tpu as pltpu
from jax.sharding import PartitionSpec as P

TOK_DEV = 256
DOC_DEV = 8
LANES = 128
FLIGHT = 7
SHARED = 1
NT = (((1,), (1,)), ((), ()))
HIGHEST = lax.Precision.HIGHEST
VMEM = pl.BlockSpec(memory_space=pltpu.VMEM)
HBM = pl.BlockSpec(memory_space=pltpu.HBM)


def vmem_params(mib):
    return pltpu.CompilerParams(vmem_limit_bytes=int(mib * (1 << 20)))


def tiles(x):
    rows, units = x.shape
    return x.reshape(rows // 16, 2, 8, units // LANES, LANES).transpose(0, 1, 3, 2, 4)


def chunks_of(length, ramp, tail):
    left = length - sum(ramp) - sum(tail)
    sizes = [*ramp, *([6] * (left // 6)), *([left % 6] if left % 6 else []), *tail]
    return [(2 * sum(sizes[:i]), 2 * size) for i, size in enumerate(sizes)]


def project_kernel(g_chunks, h_chunks, h_ref, g_ref, pin_ref, pout_ref, out_ref, h_buf, g_buf, pin_buf, pout_buf, sems):
    plan = [(pout_ref, pout_buf, g_ref, g_buf, at) for at in g_chunks] + [(pin_ref, pin_buf, h_ref, h_buf, at) for at in h_chunks]
    copies = []
    for i, (proj, proj_buf, data, data_buf, (start, size)) in enumerate(plan):
        at = pl.ds(start, size)
        copies.append([
            pltpu.make_async_copy(src.at[:, h, at], dst.at[:, at, pl.ds(8 * h, 8)], sems.at[4 * i + 2 * j + h])
            for j, (src, dst) in enumerate(((proj, proj_buf), (data, data_buf)))
            for h in range(2)
        ])

    def start(i):
        if i < len(copies):
            for copy in copies[i]:
                copy.start()

    for i in range(FLIGHT):
        start(i)

    def line_up(ref, first, size):
        blocks = [ref[:, j].reshape(ref.shape[0] * 16, LANES) for j in range(first, first + size)]
        return jnp.concatenate(blocks, axis=1)

    totals = [None, None]
    for i, (_, proj_buf, _, data_buf, (first, size)) in enumerate(plan):
        for copy in copies[i]:
            copy.wait()
        start(i + FLIGHT)
        which = 0 if i < len(g_chunks) else 1
        part = lax.dot_general(
            line_up(proj_buf, first, size), line_up(data_buf, first, size), NT, preferred_element_type=jnp.float32
        )
        totals[which] = part if totals[which] is None else totals[which] + part
    out_ref[...] = jnp.concatenate(totals, axis=0)


def project(hidden, out_grad, pin_t, pout_t):
    tokens, units = hidden.shape
    width = out_grad.shape[1]
    ranks = pin_t.shape[0] + pout_t.shape[0]
    operands = [tiles(x) for x in (hidden, out_grad, pin_t, pout_t)]
    g_chunks = chunks_of(operands[1].shape[2] // 2, (1, 2, 3, 4), ())
    h_chunks = chunks_of(operands[0].shape[2] // 2, (), (4, 2, 2))
    return pl.pallas_call(
        functools.partial(project_kernel, g_chunks, h_chunks),
        out_shape=jax.ShapeDtypeStruct((ranks, tokens), jnp.float32),
        in_specs=[HBM] * 4,
        out_specs=VMEM,
        scratch_shapes=[pltpu.VMEM((x.shape[0], x.shape[2], 16, LANES), x.dtype) for x in operands]
        + [pltpu.SemaphoreType.DMA((4 * len(g_chunks + h_chunks),))],
        compiler_params=vmem_params(53.5),
        cost_estimate=pl.CostEstimate(
            flops=2 * tokens * 64 * (units + width),
            bytes_accessed=2 * (tokens + 64) * (units + width),
            transcendentals=0,
        ),
        name="project",
    )(*operands)


def owners_of(dp):
    return max(dp // 2, 1)


def partners(dp):
    order = [m for far in (True, False) for m in range(1, dp) if m != SHARED and (2 * m >= dp) == far]
    return order[0::2], order[1::2]


def partner(dp, t):
    first, second = partners(dp)
    return jnp.where(lax.axis_index("tensor") == 0, first[t], second[t])


def pack_kernel(dp, pb, rows_a, rows_b, span, part_ref, recv_ref, extra_ref, *refs):
    outs, total_ref = refs[:-1], refs[-1]
    total_ref[...] = part_ref[...] + recv_ref[...]
    ranks = total_ref.shape[0] // 2
    rows = rows_a + rows_b
    owners, ids = extra_ref.shape[0], 2 * span
    me = lax.axis_index("dp")
    lead = lax.axis_index("tensor") == 0

    def slices(owner):
        p, q = owner // pb, owner % pb
        g = total_ref[pl.ds(pl.multiple_of(p * rows_a, rows_a), rows_a), :]
        b = total_ref[pl.ds(pl.multiple_of(ranks + q * rows_b, rows_b), rows_b), :]
        return [(g[:, i:i + LANES], b[:, i:i + LANES]) for i in (0, LANES)]

    for t, out_ref in enumerate(outs[:-2]):
        owner = (me ^ partner(dp, t)) % owners
        for i, (g, b) in enumerate(slices(owner)):
            out_ref[i * rows:i * rows + rows_a, :] = g
            out_ref[i * rows + rows_a:(i + 1) * rows, :] = b
        out_ref[2 * rows:, :] = extra_ref[owner]
    for out_ref, to in zip(outs[-2:], (me ^ SHARED, me)):
        owner = to % owners
        (g, b), (later_g, later_b) = slices(owner)
        extra = extra_ref[owner]
        out_ref[0:rows_a, :] = jnp.where(lead, g, later_g)
        out_ref[rows_a:rows, :] = jnp.where(lead, b, later_b)
        out_ref[rows:rows + span, :] = jnp.where(lead, extra[0:span], extra[span:ids])
        rest = out_ref.shape[0] - rows - span
        out_ref[rows + span:, :] = jnp.broadcast_to(jnp.where(lead, extra[ids:ids + 1], extra[ids + 1:ids + 2]), (rest, LANES))


def pack(part, recv, extra, dp, pa, pb):
    ranks = part.shape[0] // 2
    rows_a, rows_b = ranks // pa, ranks // pb
    rows, span = rows_a + rows_b, rows_a * rows_b // LANES
    whole = jax.ShapeDtypeStruct((2 * rows + extra.shape[1], LANES), jnp.float32)
    half = jax.ShapeDtypeStruct((rows + 8 * (span // 8 + 1), LANES), jnp.float32)
    count = dp // 2 - 1
    return pl.pallas_call(
        functools.partial(pack_kernel, dp, pb, rows_a, rows_b, span),
        out_shape=(whole,) * count + (half, half),
        in_specs=[VMEM] * 3,
        out_specs=(VMEM,) * (count + 2),
        scratch_shapes=[pltpu.VMEM(part.shape, jnp.float32)],
        compiler_params=vmem_params(16),
        name="pack",
    )(part, recv, extra)


def grads_kernel(rows_a, rows_b, docs, dp, gaps, wholes, *refs):
    xs, before, (out_ref, outer_ref, member_ref) = refs[:len(gaps)], refs[len(gaps):-3], refs[-3:]
    rows, wide = rows_a + rows_b, rows_a * rows_b
    span = wide // LANES
    queries = out_ref.shape[0] - docs
    doc = lax.broadcasted_iota(jnp.int32, (docs, LANES), 0)
    place = lax.broadcasted_iota(jnp.int32, (queries, LANES), 0)
    me = lax.axis_index("dp")
    core = lax.axis_index("tensor")
    asked = [jnp.zeros((queries, LANES), jnp.float32)] * span
    start = 0
    for x_ref, gap, whole in zip(xs, gaps, wholes):
        parts = 2 if whole else 1
        base = parts * rows
        for i in range(parts):
            at = slice(start, start + LANES)
            start += LANES
            g, b = x_ref[i * rows:i * rows + rows_a, :], x_ref[i * rows + rows_a:(i + 1) * rows, :]
            ids = base + parts * span + i
            member_ref[:, at] = jnp.where(doc == x_ref[ids:ids + 1, :].astype(jnp.int32), 1.0, 0.0).astype(jnp.bfloat16)
            outer = (g[:, None, :] * b[None, :, :]).reshape(wide, LANES)
            high = outer.astype(jnp.bfloat16)
            outer_ref[0:wide, at] = high
            outer_ref[wide:, at] = (outer - high.astype(jnp.float32)).astype(jnp.bfloat16)
        source = 2 * (me ^ jnp.where(core == 0, gap[0], gap[1]))
        for i in range(parts):
            held = place == source + (i if whole else core)
            for j in range(span):
                row = base + i * span + j
                asked[j] = jnp.where(held, x_ref[row:row + 1, :], asked[j])
    sums = lax.dot_general(member_ref[...], outer_ref[...], NT, preferred_element_type=jnp.float32)
    sums = (sums[:, wide:] + sums[:, :wide]) * (TOK_DEV ** -0.5)
    asked = jnp.concatenate(asked, axis=1)
    if before:
        sums, asked = sums + before[0][0:docs, :], asked + before[0][docs:, :]
    out_ref[0:docs, :] = sums
    out_ref[docs:, :] = asked


def grads_of(xs, gaps, wholes, before, rows_a, rows_b, docs, queries, dp):
    tokens = LANES * (len(xs) + sum(wholes))
    wide = rows_a * rows_b
    operands = (*xs, *before)
    return pl.pallas_call(
        functools.partial(grads_kernel, rows_a, rows_b, docs, dp, gaps, wholes),
        out_shape=jax.ShapeDtypeStruct((docs + queries, wide), jnp.float32),
        in_specs=[VMEM] * len(operands),
        out_specs=VMEM,
        scratch_shapes=[
            pltpu.VMEM((2 * wide, tokens), jnp.bfloat16),
            pltpu.VMEM((docs, tokens), jnp.bfloat16),
        ],
        compiler_params=vmem_params(40),
        cost_estimate=pl.CostEstimate(
            flops=4 * docs * wide * tokens, bytes_accessed=4 * (rows_a + rows_b) * tokens, transcendentals=0
        ),
        name="grads",
    )(*operands)


def gram_kernel(docs, part_ref, recv_ref, out_ref):
    both = part_ref[...] + recv_ref[...]
    rows = both.shape[0]
    split = []
    for _ in range(3):
        split.append(both.astype(jnp.bfloat16))
        both = both - split[-1].astype(jnp.float32)
    every = lax.dot_general(
        jnp.concatenate(split, axis=0),
        jnp.concatenate([x[:docs] for x in split], axis=0),
        NT,
        preferred_element_type=jnp.float32,
    )
    share = None
    for i, j in ((2, 0), (1, 1), (0, 2), (1, 0), (0, 1), (0, 0)):
        term = every[i * rows:(i + 1) * rows, j * docs:(j + 1) * docs]
        share = term if share is None else share + term
    half = share.shape[0] // 2
    out_ref[...] = jnp.concatenate([share[:half], share[half:]], axis=1)


def gram(part, recv, docs):
    return pl.pallas_call(
        functools.partial(gram_kernel, docs),
        out_shape=jax.ShapeDtypeStruct((part.shape[0] // 2, 2 * docs), jnp.float32),
        in_specs=[VMEM] * 2,
        out_specs=VMEM,
        compiler_params=vmem_params(16),
        name="gram",
    )(part, recv)


def solve_kernel(docs, queries, scale, x_ref, recv_ref, out_ref, done_ref):
    total = x_ref[...] + recv_ref[...]
    stack = jnp.concatenate([total[:, :docs], total[:, docs:]], axis=0)
    cols = done_ref.shape[1]
    diagonal = [lax.broadcasted_iota(jnp.int32, (docs, docs), i) for i in range(2)]
    mean_diag = jnp.sum(jnp.where(diagonal[0] == diagonal[1], stack[:docs], 0.0)) * (1.0 / docs)
    stack = jnp.concatenate([stack, jnp.zeros((cols - stack.shape[0], docs), jnp.float32)], axis=0)
    total = stack.T
    row = lax.broadcasted_iota(jnp.int32, (docs, cols), 0)
    col = lax.broadcasted_iota(jnp.int32, (docs, cols), 1)
    work = total + jnp.where(row == col, 0.1 * mean_diag, 0.0)
    size = 8
    here = lax.broadcasted_iota(jnp.int32, (size, cols), 0)
    rows = [work[i:i + size] for i in range(0, docs, size)]
    for r in range(len(rows)):
        wide = [[jnp.broadcast_to(x[:, c:c + 1], (size, cols)) for c in range(r * size, (r + 1) * size)] for x in rows]
        pivot, line = wide[r], rows[r]
        scale_rows = jnp.ones((size, cols), jnp.float32)
        for j in range(size):
            inverse = pltpu.reciprocal(pivot[j][j:j + 1], full_range=False)
            factor = jnp.where(here == j, 0.0, pivot[j]) * inverse
            pivot = [x if i <= j else x - factor * x[j:j + 1] for i, x in enumerate(pivot)]
            line = line - factor * line[j:j + 1]
            scale_rows = jnp.where(here == j, inverse, scale_rows)
        line = line * scale_rows
        for s in range(len(rows)):
            if s == r:
                rows[s] = line
            else:
                terms = [wide[s][j] * line[j:j + 1] for j in range(size)]
                rows[s] = rows[s] - (((terms[0] + terms[1]) + (terms[2] + terms[3]))
                                     + ((terms[4] + terms[5]) + (terms[6] + terms[7])))
    for r, x in enumerate(rows):
        done_ref[r * size:(r + 1) * size, :] = x * (mean_diag * scale)
    mine = pl.ds(pl.multiple_of(lax.axis_index("dp") * DOC_DEV, DOC_DEV), DOC_DEV)
    out_ref[...] = done_ref[mine, :][:, docs:docs + queries]


def solve(x, recv, docs, queries, scale):
    return pl.pallas_call(
        functools.partial(solve_kernel, docs, queries, scale),
        out_shape=jax.ShapeDtypeStruct((DOC_DEV, queries), jnp.float32),
        in_specs=[VMEM] * 2,
        out_specs=VMEM,
        scratch_shapes=[pltpu.VMEM((docs, -(-(docs + queries) // LANES) * LANES), jnp.float32)],
        compiler_params=vmem_params(16),
        name="solve",
    )(x, recv)


def solve_large(total, docs, queries, scale):
    kernel = total[:, :docs]
    mean_diag = jnp.trace(kernel) / docs
    factor = jnp.linalg.cholesky(kernel + 0.1 * mean_diag * jnp.eye(docs, dtype=jnp.float32))
    solved = jax.scipy.linalg.cho_solve((factor, True), total[:, docs:docs + queries]) * (mean_diag * scale)
    return lax.dynamic_slice_in_dim(solved, lax.axis_index("dp") * DOC_DEV, DOC_DEV, 0)


def swap_cores(x):
    cores = lax.axis_size("tensor")
    return lax.ppermute(x, "tensor", [(i, cores - 1 - i) for i in range(cores)])


def trade(xs, group):
    dp = lax.axis_size("dp")
    got = []
    for x, ms in zip(xs, zip(*partners(group))):
        pairs = [(i * 2 + k, (i ^ m) * 2 + k) for i in range(dp) for k, m in enumerate(ms)]
        got.append(lax.ppermute(x, ("dp", "tensor"), pairs))
    return got


def trade_shared(x):
    dp = lax.axis_size("dp")
    return lax.ppermute(x, "dp", [(i, i ^ SHARED) for i in range(dp)])


def local(hidden, out_grad, proj_in, proj_out, doc_ids, queries):
    dp = lax.axis_size("dp")
    docs, num_queries = DOC_DEV * dp, queries.shape[0] * dp
    ranks = proj_in.shape[1]
    owners = owners_of(dp)
    pa = 1
    while pa * pa < owners:
        pa *= 2
    pb = owners // pa
    rows_a, rows_b = ranks // pa, ranks // pb

    part = project(hidden, out_grad, proj_in.T, proj_out.T)
    recv = swap_cores(part)

    ids = jnp.broadcast_to(doc_ids.astype(jnp.float32).reshape(2, LANES), (owners, 2, LANES))
    asked = queries.reshape(-1, pa, rows_a, pb, rows_b).transpose(1, 3, 0, 2, 4).reshape(owners, -1, LANES)
    extra = jnp.concatenate([asked, ids], axis=1)
    extra = jnp.pad(extra, ((0, 0), (0, -extra.shape[1] % 8), (0, 0)))

    *blocks, shared, own = pack(part, recv, extra, dp, pa, pb)
    blocks = trade(blocks, dp) + [trade_shared(shared), own]
    gaps = [*zip(*partners(dp)), (SHARED, SHARED), (0, 0)]
    wholes = [True] * (len(blocks) - 2) + [False, False]
    sizes = (rows_a, rows_b, docs, num_queries, dp)
    late = min(1, len(blocks) - 3)
    rest = [t for t in range(len(blocks)) if t != late]
    grads = ()
    for part in (rest, [late]):
        grads = (grads_of(*([x[t] for t in part] for x in (blocks, gaps, wholes)), grads, *sizes),)
    grads = grads[0]
    share = gram(grads, swap_cores(grads), docs)
    scale = float(ranks * ranks) ** -0.5
    if docs <= 64:
        others = sum(trade([share] * (owners // 2 - 1), owners))
        share = others + jnp.where(lax.axis_index("tensor") == 0, share, trade_shared(share))
        return solve(share, swap_cores(share), docs, num_queries, scale).T
    share = lax.psum(share, "dp") * (owners / dp)
    return solve_large(jnp.concatenate([share[:, :docs], share[:, docs:]], axis=0).T, docs, num_queries, scale).T


def solution(mesh):
    return jax.shard_map(
        local,
        mesh=mesh,
        in_specs=(
            P(("groups", "dp"), "tensor"),
            P(("groups", "dp"), "tensor"),
            P("tensor", None),
            P("tensor", None),
            P(("groups", "dp")),
            P(("groups", "dp"), None),
        ),
        out_specs=P("groups", "dp"),
        check_vma=False,
    )
```

```python
import functools

import jax
import jax.numpy as jnp
from jax import lax
from jax.experimental import pallas as pl
from jax.experimental.pallas import tpu as pltpu
from jax.sharding import PartitionSpec as P

TOK_DEV = 256
DOC_DEV = 8
LANES = 128
FLIGHT = 7
SHARED = 1
NT = (((1,), (1,)), ((), ()))
VMEM = pl.BlockSpec(memory_space=pltpu.VMEM)
HBM = pl.BlockSpec(memory_space=pltpu.HBM)


def vmem_params(mib):
    return pltpu.CompilerParams(vmem_limit_bytes=int(mib * (1 << 20)))


def pieces(x):
    rows, units = x.shape
    split = x.reshape(rows // 8, 8, units // (2 * LANES), 2, LANES).transpose(0, 2, 3, 1, 4)
    return split.reshape(rows // 8, units // (2 * LANES), 16, LANES)


def chunks_of(length, ramp, tail):
    left = length - sum(ramp) - sum(tail)
    sizes = [*ramp, *([6] * (left // 6)), *([left % 6] if left % 6 else []), *tail]
    return [(sum(sizes[:i]), size) for i, size in enumerate(sizes)]


def project_kernel(g_chunks, h_chunks, h_ref, g_ref, pin_ref, pout_ref, out_ref, h_buf, g_buf, pin_buf, pout_buf, sems):
    plan = [(pout_ref, pout_buf, g_ref, g_buf, at) for at in g_chunks] + [(pin_ref, pin_buf, h_ref, h_buf, at) for at in h_chunks]
    copies = []
    for i, (proj, proj_buf, data, data_buf, (start, size)) in enumerate(plan):
        at = pl.ds(start, size)
        copies.append((
            pltpu.make_async_copy(proj.at[:, at], proj_buf.at[:, at], sems.at[2 * i]),
            pltpu.make_async_copy(data.at[:, at], data_buf.at[:, at], sems.at[2 * i + 1]),
        ))

    def start(i):
        if i < len(copies):
            for copy in copies[i]:
                copy.start()

    for i in range(FLIGHT):
        start(i)

    def line_up(ref, first, size):
        blocks = [ref[:, j].reshape(ref.shape[0] * 16, LANES) for j in range(first, first + size)]
        return jnp.concatenate(blocks, axis=1)

    totals = [None, None]
    for i, (_, proj_buf, _, data_buf, (first, size)) in enumerate(plan):
        for copy in copies[i]:
            copy.wait()
        start(i + FLIGHT)
        which = 0 if i < len(g_chunks) else 1
        part = lax.dot_general(
            line_up(proj_buf, first, size), line_up(data_buf, first, size), NT, preferred_element_type=jnp.float32
        )
        totals[which] = part if totals[which] is None else totals[which] + part

    lane = lax.broadcasted_iota(jnp.int32, (8, LANES), 1)
    even = lane % 16 < 8
    later = lane // (LANES // 2)
    order = lane % (LANES // 2) // 8 * 16 + lane % 8 + 8 * later
    done = 0
    for total in totals:
        for g in range(0, total.shape[0], 16):
            lines = []
            for i in range(0, total.shape[1], LANES):
                upper, lower = total[g:g + 8, i:i + LANES], total[g + 8:g + 16, i:i + LANES]
                lines.append(jnp.where(even, upper, lower))
            for i in range(0, len(lines), 2):
                first = lines[i] + pltpu.roll(lines[i], LANES - 8, 1)
                second = lines[i + 1] + pltpu.roll(lines[i + 1], 8, 1)
                both = jnp.where(even, first, second)
                at = i // 2 * LANES
                out_ref[done:done + 8, at:at + LANES] = jnp.take_along_axis(both, order, axis=1)
            done += 8


def project(hidden, out_grad, pin_t, pout_t):
    tokens, units = hidden.shape
    width = out_grad.shape[1]
    ranks = pin_t.shape[0] + pout_t.shape[0]
    operands = [pieces(x) for x in (hidden, out_grad, pin_t, pout_t)]
    g_chunks = chunks_of(operands[1].shape[1], (1, 2, 3, 4), ())
    h_chunks = chunks_of(operands[0].shape[1], (), (4, 2, 2))
    return pl.pallas_call(
        functools.partial(project_kernel, g_chunks, h_chunks),
        out_shape=jax.ShapeDtypeStruct((ranks, tokens), jnp.float32),
        in_specs=[HBM] * 4,
        out_specs=VMEM,
        scratch_shapes=[pltpu.VMEM(x.shape, x.dtype) for x in operands]
        + [pltpu.SemaphoreType.DMA((2 * len(g_chunks + h_chunks),))],
        compiler_params=vmem_params(53.5),
        cost_estimate=pl.CostEstimate(
            flops=2 * tokens * 64 * (units + width),
            bytes_accessed=2 * (tokens + 64) * (units + width),
            transcendentals=0,
        ),
        name="project",
    )(*operands)


def owners_of(dp):
    return max(dp // 2, 1)


def partners(dp):
    order = [m for far in (True, False) for m in range(1, dp) if m != SHARED and (2 * m >= dp) == far]
    return order[0::2], order[1::2]


def partner(dp, t):
    first, second = partners(dp)
    return jnp.where(lax.axis_index("tensor") == 0, first[t], second[t])


def pack_kernel(dp, pb, rows_a, rows_b, span, part_ref, recv_ref, extra_ref, *refs):
    outs, total_ref = refs[:-1], refs[-1]
    total_ref[...] = part_ref[...] + recv_ref[...]
    ranks = total_ref.shape[0] // 2
    rows = rows_a + rows_b
    owners, ids = extra_ref.shape[0], 2 * span
    me = lax.axis_index("dp")
    lead = lax.axis_index("tensor") == 0

    def slices(owner):
        p, q = owner // pb, owner % pb
        g = total_ref[pl.ds(pl.multiple_of(p * rows_a, rows_a), rows_a), :]
        b = total_ref[pl.ds(pl.multiple_of(ranks + q * rows_b, rows_b), rows_b), :]
        return [(g[:, i:i + LANES], b[:, i:i + LANES]) for i in (0, LANES)]

    for t, out_ref in enumerate(outs[:-2]):
        owner = (me ^ partner(dp, t)) % owners
        for i, (g, b) in enumerate(slices(owner)):
            out_ref[i * rows:i * rows + rows_a, :] = g
            out_ref[i * rows + rows_a:(i + 1) * rows, :] = b
        out_ref[2 * rows:, :] = extra_ref[owner]
    for out_ref, to in zip(outs[-2:], (me ^ SHARED, me)):
        owner = to % owners
        (g, b), (later_g, later_b) = slices(owner)
        extra = extra_ref[owner]
        out_ref[0:rows_a, :] = jnp.where(lead, g, later_g)
        out_ref[rows_a:rows, :] = jnp.where(lead, b, later_b)
        out_ref[rows:rows + span, :] = jnp.where(lead, extra[0:span], extra[span:ids])
        rest = out_ref.shape[0] - rows - span
        out_ref[rows + span:, :] = jnp.broadcast_to(jnp.where(lead, extra[ids:ids + 1], extra[ids + 1:ids + 2]), (rest, LANES))


def pack(part, recv, extra, dp, pa, pb):
    ranks = part.shape[0] // 2
    rows_a, rows_b = ranks // pa, ranks // pb
    rows, span = rows_a + rows_b, rows_a * rows_b // LANES
    whole = jax.ShapeDtypeStruct((2 * rows + extra.shape[1], LANES), jnp.float32)
    half = jax.ShapeDtypeStruct((rows + 8 * (span // 8 + 1), LANES), jnp.float32)
    count = dp // 2 - 1
    return pl.pallas_call(
        functools.partial(pack_kernel, dp, pb, rows_a, rows_b, span),
        out_shape=(whole,) * count + (half, half),
        in_specs=[VMEM] * 3,
        out_specs=(VMEM,) * (count + 2),
        scratch_shapes=[pltpu.VMEM(part.shape, jnp.float32)],
        compiler_params=vmem_params(16),
        name="pack",
    )(part, recv, extra)


def grads_kernel(rows_a, rows_b, docs, dp, gaps, wholes, *refs):
    xs, before, (out_ref, outer_ref, member_ref) = refs[:len(gaps)], refs[len(gaps):-3], refs[-3:]
    rows, wide = rows_a + rows_b, rows_a * rows_b
    span = wide // LANES
    queries = out_ref.shape[0] - docs
    doc = lax.broadcasted_iota(jnp.int32, (docs, LANES), 0)
    place = lax.broadcasted_iota(jnp.int32, (queries, LANES), 0)
    me = lax.axis_index("dp")
    core = lax.axis_index("tensor")
    asked = [jnp.zeros((queries, LANES), jnp.float32)] * span
    start = 0
    for x_ref, gap, whole in zip(xs, gaps, wholes):
        parts = 2 if whole else 1
        base = parts * rows
        for i in range(parts):
            at = slice(start, start + LANES)
            start += LANES
            g, b = x_ref[i * rows:i * rows + rows_a, :], x_ref[i * rows + rows_a:(i + 1) * rows, :]
            ids = base + parts * span + i
            member_ref[:, at] = jnp.where(doc == x_ref[ids:ids + 1, :].astype(jnp.int32), 1.0, 0.0).astype(jnp.bfloat16)
            outer = (g[:, None, :] * b[None, :, :]).reshape(wide, LANES)
            high = outer.astype(jnp.bfloat16)
            outer_ref[0:wide, at] = high
            outer_ref[wide:, at] = (outer - high.astype(jnp.float32)).astype(jnp.bfloat16)
        source = 2 * (me ^ jnp.where(core == 0, gap[0], gap[1]))
        for i in range(parts):
            held = place == source + (i if whole else core)
            for j in range(span):
                row = base + i * span + j
                asked[j] = jnp.where(held, x_ref[row:row + 1, :], asked[j])
    sums = lax.dot_general(member_ref[...], outer_ref[...], NT, preferred_element_type=jnp.float32)
    sums = (sums[:, wide:] + sums[:, :wide]) * (TOK_DEV ** -0.5)
    asked = jnp.concatenate(asked, axis=1)
    if before:
        sums, asked = sums + before[0][0:docs, :], asked + before[0][docs:, :]
    out_ref[0:docs, :] = sums
    out_ref[docs:, :] = asked


def grads_of(xs, gaps, wholes, before, rows_a, rows_b, docs, queries, dp):
    tokens = LANES * (len(xs) + sum(wholes))
    wide = rows_a * rows_b
    operands = (*xs, *before)
    return pl.pallas_call(
        functools.partial(grads_kernel, rows_a, rows_b, docs, dp, gaps, wholes),
        out_shape=jax.ShapeDtypeStruct((docs + queries, wide), jnp.float32),
        in_specs=[VMEM] * len(operands),
        out_specs=VMEM,
        scratch_shapes=[
            pltpu.VMEM((2 * wide, tokens), jnp.bfloat16),
            pltpu.VMEM((docs, tokens), jnp.bfloat16),
        ],
        compiler_params=vmem_params(40),
        cost_estimate=pl.CostEstimate(
            flops=4 * docs * wide * tokens, bytes_accessed=4 * (rows_a + rows_b) * tokens, transcendentals=0
        ),
        name="grads",
    )(*operands)


def gram_kernel(docs, part_ref, recv_ref, out_ref):
    both = part_ref[...] + recv_ref[...]
    rows = both.shape[0]
    split = []
    for _ in range(3):
        split.append(both.astype(jnp.bfloat16))
        both = both - split[-1].astype(jnp.float32)
    every = lax.dot_general(
        jnp.concatenate(split, axis=0),
        jnp.concatenate([x[:docs] for x in split], axis=0),
        NT,
        preferred_element_type=jnp.float32,
    )
    share = None
    for i, j in ((2, 0), (1, 1), (0, 2), (1, 0), (0, 1), (0, 0)):
        term = every[i * rows:(i + 1) * rows, j * docs:(j + 1) * docs]
        share = term if share is None else share + term
    half = share.shape[0] // 2
    out_ref[...] = jnp.concatenate([share[:half], share[half:]], axis=1)


def gram(part, recv, docs):
    return pl.pallas_call(
        functools.partial(gram_kernel, docs),
        out_shape=jax.ShapeDtypeStruct((part.shape[0] // 2, 2 * docs), jnp.float32),
        in_specs=[VMEM] * 2,
        out_specs=VMEM,
        compiler_params=vmem_params(16),
        name="gram",
    )(part, recv)


def solve_kernel(docs, queries, scale, x_ref, recv_ref, out_ref, done_ref):
    total = x_ref[...] + recv_ref[...]
    stack = jnp.concatenate([total[:, :docs], total[:, docs:]], axis=0)
    cols = done_ref.shape[1]
    diagonal = [lax.broadcasted_iota(jnp.int32, (docs, docs), i) for i in range(2)]
    mean_diag = jnp.sum(jnp.where(diagonal[0] == diagonal[1], stack[:docs], 0.0)) * (1.0 / docs)
    stack = jnp.concatenate([stack, jnp.zeros((cols - stack.shape[0], docs), jnp.float32)], axis=0)
    total = stack.T
    row = lax.broadcasted_iota(jnp.int32, (docs, cols), 0)
    col = lax.broadcasted_iota(jnp.int32, (docs, cols), 1)
    work = total + jnp.where(row == col, 0.1 * mean_diag, 0.0)
    size = 8
    here = lax.broadcasted_iota(jnp.int32, (size, cols), 0)
    rows = [work[i:i + size] for i in range(0, docs, size)]
    for r in range(len(rows)):
        wide = [[jnp.broadcast_to(x[:, c:c + 1], (size, cols)) for c in range(r * size, (r + 1) * size)] for x in rows]
        pivot, line = wide[r], rows[r]
        scale_rows = jnp.ones((size, cols), jnp.float32)
        for j in range(size):
            inverse = 1.0 / pivot[j][j:j + 1]
            factor = jnp.where(here == j, 0.0, pivot[j]) * inverse
            pivot = [x if i <= j else x - factor * x[j:j + 1] for i, x in enumerate(pivot)]
            line = line - factor * line[j:j + 1]
            scale_rows = jnp.where(here == j, inverse, scale_rows)
        line = line * scale_rows
        for s in range(len(rows)):
            if s == r:
                rows[s] = line
            else:
                terms = [wide[s][j] * line[j:j + 1] for j in range(size)]
                rows[s] = rows[s] - (((terms[0] + terms[1]) + (terms[2] + terms[3]))
                                     + ((terms[4] + terms[5]) + (terms[6] + terms[7])))
    for r, x in enumerate(rows):
        done_ref[r * size:(r + 1) * size, :] = x * (mean_diag * scale)
    mine = pl.ds(pl.multiple_of(lax.axis_index("dp") * DOC_DEV, DOC_DEV), DOC_DEV)
    out_ref[...] = done_ref[mine, :][:, docs:docs + queries]


def solve(x, recv, docs, queries, scale):
    return pl.pallas_call(
        functools.partial(solve_kernel, docs, queries, scale),
        out_shape=jax.ShapeDtypeStruct((DOC_DEV, queries), jnp.float32),
        in_specs=[VMEM] * 2,
        out_specs=VMEM,
        scratch_shapes=[pltpu.VMEM((docs, -(-(docs + queries) // LANES) * LANES), jnp.float32)],
        compiler_params=vmem_params(16),
        name="solve",
    )(x, recv)


def solve_large(total, docs, queries, scale):
    kernel = total[:, :docs]
    mean_diag = jnp.trace(kernel) / docs
    factor = jnp.linalg.cholesky(kernel + 0.1 * mean_diag * jnp.eye(docs, dtype=jnp.float32))
    solved = jax.scipy.linalg.cho_solve((factor, True), total[:, docs:docs + queries]) * (mean_diag * scale)
    return lax.dynamic_slice_in_dim(solved, lax.axis_index("dp") * DOC_DEV, DOC_DEV, 0)


def swap_cores(x):
    cores = lax.axis_size("tensor")
    return lax.ppermute(x, "tensor", [(i, cores - 1 - i) for i in range(cores)])


def trade(xs, group):
    dp = lax.axis_size("dp")
    got = []
    for x, ms in zip(xs, zip(*partners(group))):
        pairs = [(i * 2 + k, (i ^ m) * 2 + k) for i in range(dp) for k, m in enumerate(ms)]
        got.append(lax.ppermute(x, ("dp", "tensor"), pairs))
    return got


def trade_shared(x):
    dp = lax.axis_size("dp")
    return lax.ppermute(x, "dp", [(i, i ^ SHARED) for i in range(dp)])


def local(hidden, out_grad, proj_in, proj_out, doc_ids, queries):
    dp = lax.axis_size("dp")
    docs, num_queries = DOC_DEV * dp, queries.shape[0] * dp
    ranks = proj_in.shape[1]
    owners = owners_of(dp)
    pa = 1
    while pa * pa < owners:
        pa *= 2
    pb = owners // pa
    rows_a, rows_b = ranks // pa, ranks // pb

    part = project(hidden, out_grad, proj_in.T, proj_out.T)
    recv = swap_cores(part)

    ids = jnp.broadcast_to(doc_ids.astype(jnp.float32).reshape(2, LANES), (owners, 2, LANES))
    asked = queries.reshape(-1, pa, rows_a, pb, rows_b).transpose(1, 3, 0, 2, 4).reshape(owners, -1, LANES)
    extra = jnp.concatenate([asked, ids], axis=1)
    extra = jnp.pad(extra, ((0, 0), (0, -extra.shape[1] % 8), (0, 0)))

    *blocks, shared, own = pack(part, recv, extra, dp, pa, pb)
    blocks = trade(blocks, dp) + [trade_shared(shared), own]
    gaps = [*zip(*partners(dp)), (SHARED, SHARED), (0, 0)]
    wholes = [True] * (len(blocks) - 2) + [False, False]
    sizes = (rows_a, rows_b, docs, num_queries, dp)
    late = min(1, len(blocks) - 3)
    rest = [t for t in range(len(blocks)) if t != late]
    grads = ()
    for part in (rest, [late]):
        grads = (grads_of(*([x[t] for t in part] for x in (blocks, gaps, wholes)), grads, *sizes),)
    grads = grads[0]
    share = gram(grads, swap_cores(grads), docs)
    scale = float(ranks * ranks) ** -0.5
    if docs <= 64:
        others = sum(trade([share] * (owners // 2 - 1), owners))
        share = others + jnp.where(lax.axis_index("tensor") == 0, share, trade_shared(share))
        return solve(share, swap_cores(share), docs, num_queries, scale).T
    share = lax.psum(share, "dp") * (owners / dp)
    return solve_large(jnp.concatenate([share[:, :docs], share[:, docs:]], axis=0).T, docs, num_queries, scale).T


def solution(mesh):
    return jax.shard_map(
        local,
        mesh=mesh,
        in_specs=(
            P(("groups", "dp"), "tensor"),
            P(("groups", "dp"), "tensor"),
            P("tensor", None),
            P("tensor", None),
            P(("groups", "dp")),
            P(("groups", "dp"), None),
        ),
        out_specs=P("groups", "dp"),
        check_vma=False,
    )
```

```python
import functools

import jax
import jax.numpy as jnp
from jax import lax
from jax.experimental import pallas as pl
from jax.experimental.pallas import tpu as pltpu
from jax.sharding import PartitionSpec as P

TOK_DEV = 256
DOC_DEV = 8
LANES = 128
FLIGHT = 7
SHARED = 1
NT = (((1,), (1,)), ((), ()))
VMEM = pl.BlockSpec(memory_space=pltpu.VMEM)
HBM = pl.BlockSpec(memory_space=pltpu.HBM)


def vmem_params(mib):
    return pltpu.CompilerParams(vmem_limit_bytes=int(mib * (1 << 20)))


def tiles(x):
    rows, units = x.shape
    return x.reshape(rows // 16, 2, 8, units // LANES, LANES).transpose(0, 1, 3, 2, 4)


def chunks_of(length, ramp, tail):
    left = length - sum(ramp) - sum(tail)
    sizes = [*ramp, *([6] * (left // 6)), *([left % 6] if left % 6 else []), *tail]
    return [(2 * sum(sizes[:i]), 2 * size) for i, size in enumerate(sizes)]


def project_kernel(g_chunks, h_chunks, h_ref, g_ref, pin_ref, pout_ref, out_ref, *refs):
    bufs, sems = refs[:-1], refs[-1]
    plan = [(pout_ref, g_ref, at) for at in g_chunks] + [(pin_ref, h_ref, at) for at in h_chunks]
    copies = []
    for i, (proj, data, (start, size)) in enumerate(plan):
        at = pl.ds(start, size)
        copies.append([])
        for j, src in enumerate((proj, data)):
            for h in range(2):
                dst = bufs[4 * i + 2 * j + h].at[:, pl.ds(h, size)]
                copies[-1].append(pltpu.make_async_copy(src.at[:, h, at], dst, sems.at[4 * i + 2 * j + h]))

    def start(i):
        if i < len(copies):
            for copy in copies[i]:
                copy.start()

    for i in range(FLIGHT):
        start(i)

    def line_up(one_ref, two_ref):
        groups, count = one_ref.shape[0], one_ref.shape[1] // 2
        one_ref = one_ref.reshape(groups, count, 16, LANES)
        two_ref = two_ref.reshape(groups, count + 1, 16, LANES)
        top = lax.broadcasted_iota(jnp.int32, (groups, 16, LANES), 1) < 8
        one = [one_ref[:, k] for k in range(count)]
        two = [two_ref[:, k] for k in range(count + 1)]
        even = [jnp.where(top, one[k], two[k]).reshape(groups * 16, LANES) for k in range(count)]
        odd = [jnp.where(top, two[k + 1], one[k]).reshape(groups * 16, LANES) for k in range(count)]
        return jnp.concatenate(even, axis=1), jnp.concatenate(odd, axis=1)

    totals = [[None, None], [None, None]]
    for i in range(len(plan)):
        for copy in copies[i]:
            copy.wait()
        start(i + FLIGHT)
        total = totals[0 if i < len(g_chunks) else 1]
        sides = zip(line_up(*bufs[4 * i:4 * i + 2]), line_up(*bufs[4 * i + 2:4 * i + 4]))
        for j, (proj, data) in enumerate(sides):
            part = lax.dot_general(proj, data, NT, preferred_element_type=jnp.float32)
            total[j] = part if total[j] is None else total[j] + part

    lane = lax.broadcasted_iota(jnp.int32, (8, LANES), 1)
    first = lane % 16 < 8
    done = 0
    for even, odd in totals:
        for g in range(0, even.shape[0], 8):
            for i in range(0, even.shape[1], LANES):
                line = odd[g ^ 8:(g ^ 8) + 8, i:i + LANES]
                line = jnp.where(first, pltpu.roll(line, LANES - 8, 1), pltpu.roll(line, 8, 1))
                out_ref[done:done + 8, i:i + LANES] = even[g:g + 8, i:i + LANES] + line
            done += 8


def project(hidden, out_grad, pin_t, pout_t):
    tokens, units = hidden.shape
    width = out_grad.shape[1]
    ranks = pin_t.shape[0] + pout_t.shape[0]
    operands = [tiles(x) for x in (hidden, out_grad, pin_t, pout_t)]
    g_chunks = chunks_of(operands[1].shape[2] // 2, (1, 2, 3, 4), ())
    h_chunks = chunks_of(operands[0].shape[2] // 2, (), (4, 2, 2))
    bufs = [
        pltpu.VMEM((x.shape[0], size + 2 * h, 8, LANES), x.dtype)
        for chunks, pair in ((g_chunks, (operands[3], operands[1])), (h_chunks, (operands[2], operands[0])))
        for _, size in chunks
        for x in pair
        for h in range(2)
    ]
    return pl.pallas_call(
        functools.partial(project_kernel, g_chunks, h_chunks),
        out_shape=jax.ShapeDtypeStruct((ranks, tokens), jnp.float32),
        in_specs=[HBM] * 4,
        out_specs=VMEM,
        scratch_shapes=bufs + [pltpu.SemaphoreType.DMA((len(bufs),))],
        compiler_params=vmem_params(53.5),
        cost_estimate=pl.CostEstimate(
            flops=2 * tokens * 64 * (units + width),
            bytes_accessed=2 * (tokens + 64) * (units + width),
            transcendentals=0,
        ),
        name="project",
    )(*operands)


def owners_of(dp):
    return max(dp // 2, 1)


def partners(dp):
    order = [m for far in (True, False) for m in range(1, dp) if m != SHARED and (2 * m >= dp) == far]
    return order[0::2], order[1::2]


def partner(dp, t):
    first, second = partners(dp)
    return jnp.where(lax.axis_index("tensor") == 0, first[t], second[t])


def pack_kernel(dp, pb, rows_a, rows_b, span, part_ref, recv_ref, extra_ref, *refs):
    outs, total_ref = refs[:-1], refs[-1]
    total_ref[...] = part_ref[...] + recv_ref[...]
    ranks = total_ref.shape[0] // 2
    rows = rows_a + rows_b
    owners, ids = extra_ref.shape[0], 2 * span
    me = lax.axis_index("dp")
    lead = lax.axis_index("tensor") == 0

    def slices(owner):
        p, q = owner // pb, owner % pb
        g = total_ref[pl.ds(pl.multiple_of(p * rows_a, rows_a), rows_a), :]
        b = total_ref[pl.ds(pl.multiple_of(ranks + q * rows_b, rows_b), rows_b), :]
        return [(g[:, i:i + LANES], b[:, i:i + LANES]) for i in (0, LANES)]

    for t, out_ref in enumerate(outs[:-2]):
        owner = (me ^ partner(dp, t)) % owners
        for i, (g, b) in enumerate(slices(owner)):
            out_ref[i * rows:i * rows + rows_a, :] = g
            out_ref[i * rows + rows_a:(i + 1) * rows, :] = b
        out_ref[2 * rows:, :] = extra_ref[owner]
    for out_ref, to in zip(outs[-2:], (me ^ SHARED, me)):
        owner = to % owners
        (g, b), (later_g, later_b) = slices(owner)
        extra = extra_ref[owner]
        out_ref[0:rows_a, :] = jnp.where(lead, g, later_g)
        out_ref[rows_a:rows, :] = jnp.where(lead, b, later_b)
        out_ref[rows:rows + span, :] = jnp.where(lead, extra[0:span], extra[span:ids])
        rest = out_ref.shape[0] - rows - span
        out_ref[rows + span:, :] = jnp.broadcast_to(jnp.where(lead, extra[ids:ids + 1], extra[ids + 1:ids + 2]), (rest, LANES))


def pack(part, recv, extra, dp, pa, pb):
    ranks = part.shape[0] // 2
    rows_a, rows_b = ranks // pa, ranks // pb
    rows, span = rows_a + rows_b, rows_a * rows_b // LANES
    whole = jax.ShapeDtypeStruct((2 * rows + extra.shape[1], LANES), jnp.float32)
    half = jax.ShapeDtypeStruct((rows + 8 * (span // 8 + 1), LANES), jnp.float32)
    count = dp // 2 - 1
    return pl.pallas_call(
        functools.partial(pack_kernel, dp, pb, rows_a, rows_b, span),
        out_shape=(whole,) * count + (half, half),
        in_specs=[VMEM] * 3,
        out_specs=(VMEM,) * (count + 2),
        scratch_shapes=[pltpu.VMEM(part.shape, jnp.float32)],
        compiler_params=vmem_params(16),
        name="pack",
    )(part, recv, extra)


def grads_kernel(rows_a, rows_b, docs, dp, gaps, wholes, *refs):
    xs, before, (out_ref, outer_ref, member_ref) = refs[:len(gaps)], refs[len(gaps):-3], refs[-3:]
    rows, wide = rows_a + rows_b, rows_a * rows_b
    span = wide // LANES
    queries = out_ref.shape[0] - docs
    doc = lax.broadcasted_iota(jnp.int32, (docs, LANES), 0)
    place = lax.broadcasted_iota(jnp.int32, (queries, LANES), 0)
    me = lax.axis_index("dp")
    core = lax.axis_index("tensor")
    asked = [jnp.zeros((queries, LANES), jnp.float32)] * span
    start = 0
    for x_ref, gap, whole in zip(xs, gaps, wholes):
        parts = 2 if whole else 1
        base = parts * rows
        for i in range(parts):
            at = slice(start, start + LANES)
            start += LANES
            g, b = x_ref[i * rows:i * rows + rows_a, :], x_ref[i * rows + rows_a:(i + 1) * rows, :]
            ids = base + parts * span + i
            member_ref[:, at] = jnp.where(doc == x_ref[ids:ids + 1, :].astype(jnp.int32), 1.0, 0.0).astype(jnp.bfloat16)
            outer = (g[:, None, :] * b[None, :, :]).reshape(wide, LANES)
            high = outer.astype(jnp.bfloat16)
            outer_ref[0:wide, at] = high
            outer_ref[wide:, at] = (outer - high.astype(jnp.float32)).astype(jnp.bfloat16)
        source = 2 * (me ^ jnp.where(core == 0, gap[0], gap[1]))
        for i in range(parts):
            held = place == source + (i if whole else core)
            for j in range(span):
                row = base + i * span + j
                asked[j] = jnp.where(held, x_ref[row:row + 1, :], asked[j])
    sums = lax.dot_general(member_ref[...], outer_ref[...], NT, preferred_element_type=jnp.float32)
    sums = (sums[:, wide:] + sums[:, :wide]) * (TOK_DEV ** -0.5)
    asked = jnp.concatenate(asked, axis=1)
    if before:
        sums, asked = sums + before[0][0:docs, :], asked + before[0][docs:, :]
    out_ref[0:docs, :] = sums
    out_ref[docs:, :] = asked


def grads_of(xs, gaps, wholes, before, rows_a, rows_b, docs, queries, dp):
    tokens = LANES * (len(xs) + sum(wholes))
    wide = rows_a * rows_b
    operands = (*xs, *before)
    return pl.pallas_call(
        functools.partial(grads_kernel, rows_a, rows_b, docs, dp, gaps, wholes),
        out_shape=jax.ShapeDtypeStruct((docs + queries, wide), jnp.float32),
        in_specs=[VMEM] * len(operands),
        out_specs=VMEM,
        scratch_shapes=[
            pltpu.VMEM((2 * wide, tokens), jnp.bfloat16),
            pltpu.VMEM((docs, tokens), jnp.bfloat16),
        ],
        compiler_params=vmem_params(40),
        cost_estimate=pl.CostEstimate(
            flops=4 * docs * wide * tokens, bytes_accessed=4 * (rows_a + rows_b) * tokens, transcendentals=0
        ),
        name="grads",
    )(*operands)


def gram_kernel(docs, part_ref, recv_ref, out_ref):
    both = part_ref[...] + recv_ref[...]
    rows = both.shape[0]
    split = []
    for _ in range(3):
        split.append(both.astype(jnp.bfloat16))
        both = both - split[-1].astype(jnp.float32)
    every = lax.dot_general(
        jnp.concatenate(split, axis=0),
        jnp.concatenate([x[:docs] for x in split], axis=0),
        NT,
        preferred_element_type=jnp.float32,
    )
    share = None
    for i, j in ((2, 0), (1, 1), (0, 2), (1, 0), (0, 1), (0, 0)):
        term = every[i * rows:(i + 1) * rows, j * docs:(j + 1) * docs]
        share = term if share is None else share + term
    half = share.shape[0] // 2
    out_ref[...] = jnp.concatenate([share[:half], share[half:]], axis=1)


def gram(part, recv, docs):
    return pl.pallas_call(
        functools.partial(gram_kernel, docs),
        out_shape=jax.ShapeDtypeStruct((part.shape[0] // 2, 2 * docs), jnp.float32),
        in_specs=[VMEM] * 2,
        out_specs=VMEM,
        compiler_params=vmem_params(16),
        name="gram",
    )(part, recv)


def solve_kernel(docs, queries, scale, x_ref, recv_ref, out_ref, done_ref):
    total = x_ref[...] + recv_ref[...]
    stack = jnp.concatenate([total[:, :docs], total[:, docs:]], axis=0)
    cols = done_ref.shape[1]
    diagonal = [lax.broadcasted_iota(jnp.int32, (docs, docs), i) for i in range(2)]
    mean_diag = jnp.sum(jnp.where(diagonal[0] == diagonal[1], stack[:docs], 0.0)) * (1.0 / docs)
    stack = jnp.concatenate([stack, jnp.zeros((cols - stack.shape[0], docs), jnp.float32)], axis=0)
    total = stack.T
    row = lax.broadcasted_iota(jnp.int32, (docs, cols), 0)
    col = lax.broadcasted_iota(jnp.int32, (docs, cols), 1)
    work = total + jnp.where(row == col, 0.1 * mean_diag, 0.0)
    size = 8
    here = lax.broadcasted_iota(jnp.int32, (size, cols), 0)
    rows = [work[i:i + size] for i in range(0, docs, size)]
    for r in range(len(rows)):
        wide = [[jnp.broadcast_to(x[:, c:c + 1], (size, cols)) for c in range(r * size, (r + 1) * size)] for x in rows]
        pivot, line = wide[r], rows[r]
        scale_rows = jnp.ones((size, cols), jnp.float32)
        for j in range(size):
            inverse = 1.0 / pivot[j][j:j + 1]
            factor = jnp.where(here == j, 0.0, pivot[j]) * inverse
            pivot = [x if i <= j else x - factor * x[j:j + 1] for i, x in enumerate(pivot)]
            line = line - factor * line[j:j + 1]
            scale_rows = jnp.where(here == j, inverse, scale_rows)
        line = line * scale_rows
        for s in range(len(rows)):
            if s == r:
                rows[s] = line
            else:
                terms = [wide[s][j] * line[j:j + 1] for j in range(size)]
                rows[s] = rows[s] - (((terms[0] + terms[1]) + (terms[2] + terms[3]))
                                     + ((terms[4] + terms[5]) + (terms[6] + terms[7])))
    for r, x in enumerate(rows):
        done_ref[r * size:(r + 1) * size, :] = x * (mean_diag * scale)
    mine = pl.ds(pl.multiple_of(lax.axis_index("dp") * DOC_DEV, DOC_DEV), DOC_DEV)
    out_ref[...] = done_ref[mine, :][:, docs:docs + queries]


def solve(x, recv, docs, queries, scale):
    return pl.pallas_call(
        functools.partial(solve_kernel, docs, queries, scale),
        out_shape=jax.ShapeDtypeStruct((DOC_DEV, queries), jnp.float32),
        in_specs=[VMEM] * 2,
        out_specs=VMEM,
        scratch_shapes=[pltpu.VMEM((docs, -(-(docs + queries) // LANES) * LANES), jnp.float32)],
        compiler_params=vmem_params(16),
        name="solve",
    )(x, recv)


def solve_large(total, docs, queries, scale):
    kernel = total[:, :docs]
    mean_diag = jnp.trace(kernel) / docs
    factor = jnp.linalg.cholesky(kernel + 0.1 * mean_diag * jnp.eye(docs, dtype=jnp.float32))
    solved = jax.scipy.linalg.cho_solve((factor, True), total[:, docs:docs + queries]) * (mean_diag * scale)
    return lax.dynamic_slice_in_dim(solved, lax.axis_index("dp") * DOC_DEV, DOC_DEV, 0)


def swap_cores(x):
    cores = lax.axis_size("tensor")
    return lax.ppermute(x, "tensor", [(i, cores - 1 - i) for i in range(cores)])


def trade(xs, group):
    dp = lax.axis_size("dp")
    got = []
    for x, ms in zip(xs, zip(*partners(group))):
        pairs = [(i * 2 + k, (i ^ m) * 2 + k) for i in range(dp) for k, m in enumerate(ms)]
        got.append(lax.ppermute(x, ("dp", "tensor"), pairs))
    return got


def trade_shared(x):
    dp = lax.axis_size("dp")
    return lax.ppermute(x, "dp", [(i, i ^ SHARED) for i in range(dp)])


def local(hidden, out_grad, proj_in, proj_out, doc_ids, queries):
    dp = lax.axis_size("dp")
    docs, num_queries = DOC_DEV * dp, queries.shape[0] * dp
    ranks = proj_in.shape[1]
    owners = owners_of(dp)
    pa = 1
    while pa * pa < owners:
        pa *= 2
    pb = owners // pa
    rows_a, rows_b = ranks // pa, ranks // pb

    part = project(hidden, out_grad, proj_in.T, proj_out.T)
    recv = swap_cores(part)

    ids = jnp.broadcast_to(doc_ids.astype(jnp.float32).reshape(2, LANES), (owners, 2, LANES))
    asked = queries.reshape(-1, pa, rows_a, pb, rows_b).transpose(1, 3, 0, 2, 4).reshape(owners, -1, LANES)
    extra = jnp.concatenate([asked, ids], axis=1)
    extra = jnp.pad(extra, ((0, 0), (0, -extra.shape[1] % 8), (0, 0)))

    *blocks, shared, own = pack(part, recv, extra, dp, pa, pb)
    blocks = trade(blocks, dp) + [trade_shared(shared), own]
    gaps = [*zip(*partners(dp)), (SHARED, SHARED), (0, 0)]
    wholes = [True] * (len(blocks) - 2) + [False, False]
    sizes = (rows_a, rows_b, docs, num_queries, dp)
    late = min(1, len(blocks) - 3)
    rest = [t for t in range(len(blocks)) if t != late]
    grads = ()
    for part in (rest, [late]):
        grads = (grads_of(*([x[t] for t in part] for x in (blocks, gaps, wholes)), grads, *sizes),)
    grads = grads[0]
    share = gram(grads, swap_cores(grads), docs)
    scale = float(ranks * ranks) ** -0.5
    if docs <= 64:
        others = sum(trade([share] * (owners // 2 - 1), owners))
        share = others + jnp.where(lax.axis_index("tensor") == 0, share, trade_shared(share))
        return solve(share, swap_cores(share), docs, num_queries, scale).T
    share = lax.psum(share, "dp") * (owners / dp)
    return solve_large(jnp.concatenate([share[:, :docs], share[:, docs:]], axis=0).T, docs, num_queries, scale).T


def solution(mesh):
    return jax.shard_map(
        local,
        mesh=mesh,
        in_specs=(
            P(("groups", "dp"), "tensor"),
            P(("groups", "dp"), "tensor"),
            P("tensor", None),
            P("tensor", None),
            P(("groups", "dp")),
            P(("groups", "dp"), None),
        ),
        out_specs=P("groups", "dp"),
        check_vma=False,
    )
```

```python
import functools

import jax
import jax.numpy as jnp
from jax import lax
from jax.experimental import pallas as pl
from jax.experimental.pallas import tpu as pltpu
from jax.sharding import PartitionSpec as P

TOK_DEV = 256
DOC_DEV = 8
LANES = 128
FLIGHT = 10
SHARED = 1
NT = (((1,), (1,)), ((), ()))
VMEM = pl.BlockSpec(memory_space=pltpu.VMEM)
HBM = pl.BlockSpec(memory_space=pltpu.HBM)


def vmem_params(mib):
    return pltpu.CompilerParams(vmem_limit_bytes=int(mib * (1 << 20)))


def pieces(x):
    rows, units = x.shape
    split = x.reshape(rows // 8, 8, units // (2 * LANES), 2, LANES).transpose(0, 2, 3, 1, 4)
    return split.reshape(rows // 8, units // (2 * LANES), 16, LANES)


def chunks_of(length, ramp, tail):
    left = length - sum(ramp) - sum(tail)
    sizes = [*ramp, *([6] * (left // 6)), *([left % 6] if left % 6 else []), *tail]
    return [(sum(sizes[:i]), size) for i, size in enumerate(sizes)]


def project_kernel(g_chunks, h_chunks, h_ref, g_ref, pin_ref, pout_ref, out_ref, h_buf, g_buf, pin_buf, pout_buf, sems):
    plan = [(pout_ref, pout_buf, g_ref, g_buf, at) for at in g_chunks] + [(pin_ref, pin_buf, h_ref, h_buf, at) for at in h_chunks]
    copies = []
    for i, (proj, proj_buf, data, data_buf, (start, size)) in enumerate(plan):
        at = pl.ds(start, size)
        copies.append((
            pltpu.make_async_copy(proj.at[:, at], proj_buf.at[:, at], sems.at[2 * i]),
            pltpu.make_async_copy(data.at[:, at], data_buf.at[:, at], sems.at[2 * i + 1]),
        ))

    def start(i):
        if i < len(copies):
            for copy in copies[i]:
                copy.start()

    for i in range(FLIGHT):
        start(i)

    def line_up(ref, first, size):
        blocks = [ref[:, j].reshape(ref.shape[0] * 16, LANES) for j in range(first, first + size)]
        return jnp.concatenate(blocks, axis=1)

    totals = [None, None]
    for i, (_, proj_buf, _, data_buf, (first, size)) in enumerate(plan):
        for copy in copies[i]:
            copy.wait()
        start(i + FLIGHT)
        which = 0 if i < len(g_chunks) else 1
        part = lax.dot_general(
            line_up(proj_buf, first, size), line_up(data_buf, first, size), NT, preferred_element_type=jnp.float32
        )
        totals[which] = part if totals[which] is None else totals[which] + part

    lane = lax.broadcasted_iota(jnp.int32, (8, LANES), 1)
    even = lane % 16 < 8
    later = lane // (LANES // 2)
    order = lane % (LANES // 2) // 8 * 16 + lane % 8 + 8 * later
    done = 0
    for total in totals:
        for g in range(0, total.shape[0], 16):
            lines = []
            for i in range(0, total.shape[1], LANES):
                upper, lower = total[g:g + 8, i:i + LANES], total[g + 8:g + 16, i:i + LANES]
                lines.append(jnp.where(even, upper, lower))
            for i in range(0, len(lines), 2):
                first = lines[i] + pltpu.roll(lines[i], LANES - 8, 1)
                second = lines[i + 1] + pltpu.roll(lines[i + 1], 8, 1)
                both = jnp.where(even, first, second)
                at = i // 2 * LANES
                out_ref[done:done + 8, at:at + LANES] = jnp.take_along_axis(both, order, axis=1)
            done += 8


def project(hidden, out_grad, pin_t, pout_t):
    tokens, units = hidden.shape
    width = out_grad.shape[1]
    ranks = pin_t.shape[0] + pout_t.shape[0]
    operands = [pieces(x) for x in (hidden, out_grad, pin_t, pout_t)]
    g_chunks = chunks_of(operands[1].shape[1], (1, 2, 3, 4), ())
    h_chunks = chunks_of(operands[0].shape[1], (), (4, 2, 2))
    return pl.pallas_call(
        functools.partial(project_kernel, g_chunks, h_chunks),
        out_shape=jax.ShapeDtypeStruct((ranks, tokens), jnp.float32),
        in_specs=[HBM] * 4,
        out_specs=VMEM,
        scratch_shapes=[pltpu.VMEM(x.shape, x.dtype) for x in operands]
        + [pltpu.SemaphoreType.DMA((2 * len(g_chunks + h_chunks),))],
        compiler_params=vmem_params(53.5),
        cost_estimate=pl.CostEstimate(
            flops=2 * tokens * 64 * (units + width),
            bytes_accessed=2 * (tokens + 64) * (units + width),
            transcendentals=0,
        ),
        name="project",
    )(*operands)


def owners_of(dp):
    return max(dp // 2, 1)


def partners(dp):
    order = [m for far in (True, False) for m in range(1, dp) if m != SHARED and (2 * m >= dp) == far]
    return order[0::2], order[1::2]


def partner(dp, t):
    first, second = partners(dp)
    return jnp.where(lax.axis_index("tensor") == 0, first[t], second[t])


def pack_kernel(dp, pb, rows_a, rows_b, span, part_ref, recv_ref, extra_ref, *refs):
    outs, total_ref = refs[:-1], refs[-1]
    total_ref[...] = part_ref[...] + recv_ref[...]
    ranks = total_ref.shape[0] // 2
    rows = rows_a + rows_b
    owners, ids = extra_ref.shape[0], 2 * span
    me = lax.axis_index("dp")
    lead = lax.axis_index("tensor") == 0

    def slices(owner):
        p, q = owner // pb, owner % pb
        g = total_ref[pl.ds(pl.multiple_of(p * rows_a, rows_a), rows_a), :]
        b = total_ref[pl.ds(pl.multiple_of(ranks + q * rows_b, rows_b), rows_b), :]
        return [(g[:, i:i + LANES], b[:, i:i + LANES]) for i in (0, LANES)]

    for t, out_ref in enumerate(outs[:-2]):
        owner = (me ^ partner(dp, t)) % owners
        for i, (g, b) in enumerate(slices(owner)):
            out_ref[i * rows:i * rows + rows_a, :] = g
            out_ref[i * rows + rows_a:(i + 1) * rows, :] = b
        out_ref[2 * rows:, :] = extra_ref[owner]
    for out_ref, to in zip(outs[-2:], (me ^ SHARED, me)):
        owner = to % owners
        (g, b), (later_g, later_b) = slices(owner)
        extra = extra_ref[owner]
        out_ref[0:rows_a, :] = jnp.where(lead, g, later_g)
        out_ref[rows_a:rows, :] = jnp.where(lead, b, later_b)
        out_ref[rows:rows + span, :] = jnp.where(lead, extra[0:span], extra[span:ids])
        rest = out_ref.shape[0] - rows - span
        out_ref[rows + span:, :] = jnp.broadcast_to(jnp.where(lead, extra[ids:ids + 1], extra[ids + 1:ids + 2]), (rest, LANES))


def pack(part, recv, extra, dp, pa, pb):
    ranks = part.shape[0] // 2
    rows_a, rows_b = ranks // pa, ranks // pb
    rows, span = rows_a + rows_b, rows_a * rows_b // LANES
    whole = jax.ShapeDtypeStruct((2 * rows + extra.shape[1], LANES), jnp.float32)
    half = jax.ShapeDtypeStruct((rows + 8 * (span // 8 + 1), LANES), jnp.float32)
    count = dp // 2 - 1
    return pl.pallas_call(
        functools.partial(pack_kernel, dp, pb, rows_a, rows_b, span),
        out_shape=(whole,) * count + (half, half),
        in_specs=[VMEM] * 3,
        out_specs=(VMEM,) * (count + 2),
        scratch_shapes=[pltpu.VMEM(part.shape, jnp.float32)],
        compiler_params=vmem_params(16),
        name="pack",
    )(part, recv, extra)


def grads_kernel(rows_a, rows_b, docs, dp, gaps, wholes, *refs):
    xs, before, (out_ref, outer_ref, member_ref) = refs[:len(gaps)], refs[len(gaps):-3], refs[-3:]
    rows, wide = rows_a + rows_b, rows_a * rows_b
    span = wide // LANES
    queries = out_ref.shape[0] - docs
    doc = lax.broadcasted_iota(jnp.int32, (docs, LANES), 0)
    place = lax.broadcasted_iota(jnp.int32, (queries, LANES), 0)
    me = lax.axis_index("dp")
    core = lax.axis_index("tensor")
    asked = [jnp.zeros((queries, LANES), jnp.float32)] * span
    start = 0
    for x_ref, gap, whole in zip(xs, gaps, wholes):
        parts = 2 if whole else 1
        base = parts * rows
        for i in range(parts):
            at = slice(start, start + LANES)
            start += LANES
            g, b = x_ref[i * rows:i * rows + rows_a, :], x_ref[i * rows + rows_a:(i + 1) * rows, :]
            ids = base + parts * span + i
            member_ref[:, at] = jnp.where(doc == x_ref[ids:ids + 1, :].astype(jnp.int32), 1.0, 0.0).astype(jnp.bfloat16)
            outer = (g[:, None, :] * b[None, :, :]).reshape(wide, LANES)
            high = outer.astype(jnp.bfloat16)
            outer_ref[0:wide, at] = high
            outer_ref[wide:, at] = (outer - high.astype(jnp.float32)).astype(jnp.bfloat16)
        source = 2 * (me ^ jnp.where(core == 0, gap[0], gap[1]))
        for i in range(parts):
            held = place == source + (i if whole else core)
            for j in range(span):
                row = base + i * span + j
                asked[j] = jnp.where(held, x_ref[row:row + 1, :], asked[j])
    sums = lax.dot_general(member_ref[...], outer_ref[...], NT, preferred_element_type=jnp.float32)
    sums = (sums[:, wide:] + sums[:, :wide]) * (TOK_DEV ** -0.5)
    asked = jnp.concatenate(asked, axis=1)
    if before:
        sums, asked = sums + before[0][0:docs, :], asked + before[0][docs:, :]
    out_ref[0:docs, :] = sums
    out_ref[docs:, :] = asked


def grads_of(xs, gaps, wholes, before, rows_a, rows_b, docs, queries, dp):
    tokens = LANES * (len(xs) + sum(wholes))
    wide = rows_a * rows_b
    operands = (*xs, *before)
    return pl.pallas_call(
        functools.partial(grads_kernel, rows_a, rows_b, docs, dp, gaps, wholes),
        out_shape=jax.ShapeDtypeStruct((docs + queries, wide), jnp.float32),
        in_specs=[VMEM] * len(operands),
        out_specs=VMEM,
        scratch_shapes=[
            pltpu.VMEM((2 * wide, tokens), jnp.bfloat16),
            pltpu.VMEM((docs, tokens), jnp.bfloat16),
        ],
        compiler_params=vmem_params(40),
        cost_estimate=pl.CostEstimate(
            flops=4 * docs * wide * tokens, bytes_accessed=4 * (rows_a + rows_b) * tokens, transcendentals=0
        ),
        name="grads",
    )(*operands)


def gram_kernel(docs, part_ref, recv_ref, out_ref):
    both = part_ref[...] + recv_ref[...]
    rows = both.shape[0]
    split = []
    for _ in range(3):
        split.append(both.astype(jnp.bfloat16))
        both = both - split[-1].astype(jnp.float32)
    every = lax.dot_general(
        jnp.concatenate(split, axis=0),
        jnp.concatenate([x[:docs] for x in split], axis=0),
        NT,
        preferred_element_type=jnp.float32,
    )
    share = None
    for i, j in ((2, 0), (1, 1), (0, 2), (1, 0), (0, 1), (0, 0)):
        term = every[i * rows:(i + 1) * rows, j * docs:(j + 1) * docs]
        share = term if share is None else share + term
    half = share.shape[0] // 2
    out_ref[...] = jnp.concatenate([share[:half], share[half:]], axis=1)


def gram(part, recv, docs):
    return pl.pallas_call(
        functools.partial(gram_kernel, docs),
        out_shape=jax.ShapeDtypeStruct((part.shape[0] // 2, 2 * docs), jnp.float32),
        in_specs=[VMEM] * 2,
        out_specs=VMEM,
        compiler_params=vmem_params(16),
        name="gram",
    )(part, recv)


def solve_kernel(docs, queries, scale, x_ref, recv_ref, out_ref, done_ref):
    total = x_ref[...] + recv_ref[...]
    stack = jnp.concatenate([total[:, :docs], total[:, docs:]], axis=0)
    cols = done_ref.shape[1]
    diagonal = [lax.broadcasted_iota(jnp.int32, (docs, docs), i) for i in range(2)]
    mean_diag = jnp.sum(jnp.where(diagonal[0] == diagonal[1], stack[:docs], 0.0)) * (1.0 / docs)
    stack = jnp.concatenate([stack, jnp.zeros((cols - stack.shape[0], docs), jnp.float32)], axis=0)
    total = stack.T
    row = lax.broadcasted_iota(jnp.int32, (docs, cols), 0)
    col = lax.broadcasted_iota(jnp.int32, (docs, cols), 1)
    work = total + jnp.where(row == col, 0.1 * mean_diag, 0.0)
    size = 8
    here = lax.broadcasted_iota(jnp.int32, (size, cols), 0)
    rows = [work[i:i + size] for i in range(0, docs, size)]
    for r in range(len(rows)):
        wide = [[jnp.broadcast_to(x[:, c:c + 1], (size, cols)) for c in range(r * size, (r + 1) * size)] for x in rows]
        pivot = [[jnp.broadcast_to(x[i:i + 1], (size, cols)) for x in wide[r]] for i in range(size)]
        line = [jnp.broadcast_to(rows[r][i:i + 1], (size, cols)) for i in range(size)]
        inverses = []
        for j in range(size):
            inverse = 1.0 / pivot[j][j]
            inverses.append(inverse)
            for i in range(size):
                if i != j:
                    factor = pivot[i][j] * inverse
                    for k in range(j + 1, size):
                        pivot[i][k] = pivot[i][k] - factor * pivot[j][k]
                    line[i] = line[i] - factor * line[j]
        line = [x * inverse for x, inverse in zip(line, inverses)]
        for s in range(len(rows)):
            if s == r:
                rows[s] = line[0]
                for j in range(1, size):
                    rows[s] = jnp.where(here == j, line[j], rows[s])
            else:
                terms = [wide[s][j] * line[j] for j in range(size)]
                rows[s] = rows[s] - (((terms[0] + terms[1]) + (terms[2] + terms[3]))
                                     + ((terms[4] + terms[5]) + (terms[6] + terms[7])))
    for r, x in enumerate(rows):
        done_ref[r * size:(r + 1) * size, :] = x * (mean_diag * scale)
    mine = pl.ds(pl.multiple_of(lax.axis_index("dp") * DOC_DEV, DOC_DEV), DOC_DEV)
    out_ref[...] = done_ref[mine, :][:, docs:docs + queries]


def solve(x, recv, docs, queries, scale):
    return pl.pallas_call(
        functools.partial(solve_kernel, docs, queries, scale),
        out_shape=jax.ShapeDtypeStruct((DOC_DEV, queries), jnp.float32),
        in_specs=[VMEM] * 2,
        out_specs=VMEM,
        scratch_shapes=[pltpu.VMEM((docs, -(-(docs + queries) // LANES) * LANES), jnp.float32)],
        compiler_params=vmem_params(16),
        name="solve",
    )(x, recv)


def solve_large(total, docs, queries, scale):
    kernel = total[:, :docs]
    mean_diag = jnp.trace(kernel) / docs
    factor = jnp.linalg.cholesky(kernel + 0.1 * mean_diag * jnp.eye(docs, dtype=jnp.float32))
    solved = jax.scipy.linalg.cho_solve((factor, True), total[:, docs:docs + queries]) * (mean_diag * scale)
    return lax.dynamic_slice_in_dim(solved, lax.axis_index("dp") * DOC_DEV, DOC_DEV, 0)


def swap_cores(x):
    cores = lax.axis_size("tensor")
    return lax.ppermute(x, "tensor", [(i, cores - 1 - i) for i in range(cores)])


def trade(xs, group):
    dp = lax.axis_size("dp")
    got = []
    for x, ms in zip(xs, zip(*partners(group))):
        pairs = [(i * 2 + k, (i ^ m) * 2 + k) for i in range(dp) for k, m in enumerate(ms)]
        got.append(lax.ppermute(x, ("dp", "tensor"), pairs))
    return got


def trade_shared(x):
    dp = lax.axis_size("dp")
    return lax.ppermute(x, "dp", [(i, i ^ SHARED) for i in range(dp)])


def local(hidden, out_grad, proj_in, proj_out, doc_ids, queries):
    dp = lax.axis_size("dp")
    docs, num_queries = DOC_DEV * dp, queries.shape[0] * dp
    ranks = proj_in.shape[1]
    owners = owners_of(dp)
    pa = 1
    while pa * pa < owners:
        pa *= 2
    pb = owners // pa
    rows_a, rows_b = ranks // pa, ranks // pb

    part = project(hidden, out_grad, proj_in.T, proj_out.T)
    recv = swap_cores(part)

    ids = jnp.broadcast_to(doc_ids.astype(jnp.float32).reshape(2, LANES), (owners, 2, LANES))
    asked = queries.reshape(-1, pa, rows_a, pb, rows_b).transpose(1, 3, 0, 2, 4).reshape(owners, -1, LANES)
    extra = jnp.concatenate([asked, ids], axis=1)
    extra = jnp.pad(extra, ((0, 0), (0, -extra.shape[1] % 8), (0, 0)))

    *blocks, shared, own = pack(part, recv, extra, dp, pa, pb)
    blocks = trade(blocks, dp) + [trade_shared(shared), own]
    gaps = [*zip(*partners(dp)), (SHARED, SHARED), (0, 0)]
    wholes = [True] * (len(blocks) - 2) + [False, False]
    sizes = (rows_a, rows_b, docs, num_queries, dp)
    late = min(1, len(blocks) - 3)
    rest = [t for t in range(len(blocks)) if t != late]
    grads = ()
    for part in (rest, [late]):
        grads = (grads_of(*([x[t] for t in part] for x in (blocks, gaps, wholes)), grads, *sizes),)
    grads = grads[0]
    share = gram(grads, swap_cores(grads), docs)
    scale = float(ranks * ranks) ** -0.5
    if docs <= 64:
        others = sum(trade([share] * (owners // 2 - 1), owners))
        share = others + jnp.where(lax.axis_index("tensor") == 0, share, trade_shared(share))
        return solve(share, swap_cores(share), docs, num_queries, scale).T
    share = lax.psum(share, "dp") * (owners / dp)
    return solve_large(jnp.concatenate([share[:, :docs], share[:, docs:]], axis=0).T, docs, num_queries, scale).T


def solution(mesh):
    return jax.shard_map(
        local,
        mesh=mesh,
        in_specs=(
            P(("groups", "dp"), "tensor"),
            P(("groups", "dp"), "tensor"),
            P("tensor", None),
            P("tensor", None),
            P(("groups", "dp")),
            P(("groups", "dp"), None),
        ),
        out_specs=P("groups", "dp"),
        check_vma=False,
    )
```

```python
import functools

import jax
import jax.numpy as jnp
from jax import lax
from jax.experimental import pallas as pl
from jax.experimental.pallas import tpu as pltpu
from jax.sharding import PartitionSpec as P

TOK_DEV = 256
DOC_DEV = 8
LANES = 128
FLIGHT = 7
SHARED = 1
NT = (((1,), (1,)), ((), ()))
VMEM = pl.BlockSpec(memory_space=pltpu.VMEM)
HBM = pl.BlockSpec(memory_space=pltpu.HBM)


def vmem_params(mib):
    return pltpu.CompilerParams(vmem_limit_bytes=int(mib * (1 << 20)))


def pieces(x):
    rows, units = x.shape
    split = x.reshape(rows // 8, 8, units // (2 * LANES), 2, LANES).transpose(0, 2, 3, 1, 4)
    return split.reshape(rows // 8, units // (2 * LANES), 16, LANES)


def chunks_of(length, ramp, tail):
    left = length - sum(ramp) - sum(tail)
    sizes = [*ramp, *([6] * (left // 6)), *([left % 6] if left % 6 else []), *tail]
    return [(sum(sizes[:i]), size) for i, size in enumerate(sizes)]


def project_kernel(g_chunks, h_chunks, h_ref, g_ref, pin_ref, pout_ref, out_ref, h_buf, g_buf, pin_buf, pout_buf, sems):
    plan = [(pout_ref, pout_buf, g_ref, g_buf, at) for at in g_chunks] + [(pin_ref, pin_buf, h_ref, h_buf, at) for at in h_chunks]
    copies = []
    for i, (proj, proj_buf, data, data_buf, (start, size)) in enumerate(plan):
        at = pl.ds(start, size)
        copies.append((
            pltpu.make_async_copy(proj.at[:, at], proj_buf.at[:, at], sems.at[2 * i]),
            pltpu.make_async_copy(data.at[:, at], data_buf.at[:, at], sems.at[2 * i + 1]),
        ))

    def start(i):
        if i < len(copies):
            for copy in copies[i]:
                copy.start()

    for i in range(FLIGHT):
        start(i)

    def line_up(ref, first, size):
        blocks = [ref[:, j].reshape(ref.shape[0] * 16, LANES) for j in range(first, first + size)]
        return jnp.concatenate(blocks, axis=1)

    totals = [None, None]
    for i, (_, proj_buf, _, data_buf, (first, size)) in enumerate(plan):
        for copy in copies[i]:
            copy.wait()
        start(i + FLIGHT)
        which = 0 if i < len(g_chunks) else 1
        part = lax.dot_general(
            line_up(proj_buf, first, size), line_up(data_buf, first, size), NT, preferred_element_type=jnp.float32
        )
        totals[which] = part if totals[which] is None else totals[which] + part

    lane = lax.broadcasted_iota(jnp.int32, (8, LANES), 1)
    even = lane % 16 < 8
    later = lane // (LANES // 2)
    order = lane % (LANES // 2) // 8 * 16 + lane % 8 + 8 * later
    done = 0
    for total in totals:
        for g in range(0, total.shape[0], 16):
            lines = []
            for i in range(0, total.shape[1], LANES):
                upper, lower = total[g:g + 8, i:i + LANES], total[g + 8:g + 16, i:i + LANES]
                lines.append(jnp.where(even, upper, lower))
            for i in range(0, len(lines), 2):
                first = lines[i] + pltpu.roll(lines[i], LANES - 8, 1)
                second = lines[i + 1] + pltpu.roll(lines[i + 1], 8, 1)
                both = jnp.where(even, first, second)
                at = i // 2 * LANES
                out_ref[done:done + 8, at:at + LANES] = jnp.take_along_axis(both, order, axis=1)
            done += 8


def project(hidden, out_grad, pin_t, pout_t):
    tokens, units = hidden.shape
    width = out_grad.shape[1]
    ranks = pin_t.shape[0] + pout_t.shape[0]
    operands = [pieces(x) for x in (hidden, out_grad, pin_t, pout_t)]
    g_chunks = chunks_of(operands[1].shape[1], (1, 2, 3, 4), ())
    h_chunks = chunks_of(operands[0].shape[1], (), (4, 2, 2))
    return pl.pallas_call(
        functools.partial(project_kernel, g_chunks, h_chunks),
        out_shape=jax.ShapeDtypeStruct((ranks, tokens), jnp.float32),
        in_specs=[HBM] * 4,
        out_specs=VMEM,
        scratch_shapes=[pltpu.VMEM(x.shape, x.dtype) for x in operands]
        + [pltpu.SemaphoreType.DMA((2 * len(g_chunks + h_chunks),))],
        compiler_params=vmem_params(53.5),
        cost_estimate=pl.CostEstimate(
            flops=2 * tokens * 64 * (units + width),
            bytes_accessed=2 * (tokens + 64) * (units + width),
            transcendentals=0,
        ),
        name="project",
    )(*operands)


def owners_of(dp):
    return max(dp // 2, 1)


def partners(dp):
    order = [m for far in (True, False) for m in range(1, dp) if m != SHARED and (2 * m >= dp) == far]
    return order[0::2], order[1::2]


def partner(dp, t):
    first, second = partners(dp)
    return jnp.where(lax.axis_index("tensor") == 0, first[t], second[t])


def pack_kernel(dp, pb, rows_a, rows_b, span, part_ref, recv_ref, extra_ref, *refs):
    outs, total_ref = refs[:-1], refs[-1]
    total_ref[...] = part_ref[...] + recv_ref[...]
    ranks = total_ref.shape[0] // 2
    rows = rows_a + rows_b
    owners, ids = extra_ref.shape[0], 2 * span
    me = lax.axis_index("dp")
    lead = lax.axis_index("tensor") == 0

    def slices(owner):
        p, q = owner // pb, owner % pb
        g = total_ref[pl.ds(pl.multiple_of(p * rows_a, rows_a), rows_a), :]
        b = total_ref[pl.ds(pl.multiple_of(ranks + q * rows_b, rows_b), rows_b), :]
        return [(g[:, i:i + LANES], b[:, i:i + LANES]) for i in (0, LANES)]

    for t, out_ref in enumerate(outs[:-2]):
        owner = (me ^ partner(dp, t)) % owners
        for i, (g, b) in enumerate(slices(owner)):
            out_ref[i * rows:i * rows + rows_a, :] = g
            out_ref[i * rows + rows_a:(i + 1) * rows, :] = b
        out_ref[2 * rows:, :] = extra_ref[owner]
    for out_ref, to in zip(outs[-2:], (me ^ SHARED, me)):
        owner = to % owners
        (g, b), (later_g, later_b) = slices(owner)
        extra = extra_ref[owner]
        out_ref[0:rows_a, :] = jnp.where(lead, g, later_g)
        out_ref[rows_a:rows, :] = jnp.where(lead, b, later_b)
        out_ref[rows:rows + span, :] = jnp.where(lead, extra[0:span], extra[span:ids])
        rest = out_ref.shape[0] - rows - span
        out_ref[rows + span:, :] = jnp.broadcast_to(jnp.where(lead, extra[ids:ids + 1], extra[ids + 1:ids + 2]), (rest, LANES))


def pack(part, recv, extra, dp, pa, pb):
    ranks = part.shape[0] // 2
    rows_a, rows_b = ranks // pa, ranks // pb
    rows, span = rows_a + rows_b, rows_a * rows_b // LANES
    whole = jax.ShapeDtypeStruct((2 * rows + extra.shape[1], LANES), jnp.float32)
    half = jax.ShapeDtypeStruct((rows + 8 * (span // 8 + 1), LANES), jnp.float32)
    count = dp // 2 - 1
    return pl.pallas_call(
        functools.partial(pack_kernel, dp, pb, rows_a, rows_b, span),
        out_shape=(whole,) * count + (half, half),
        in_specs=[VMEM] * 3,
        out_specs=(VMEM,) * (count + 2),
        scratch_shapes=[pltpu.VMEM(part.shape, jnp.float32)],
        compiler_params=vmem_params(16),
        name="pack",
    )(part, recv, extra)


def grads_kernel(rows_a, rows_b, docs, dp, gaps, wholes, *refs):
    xs, before, (out_ref, outer_ref, member_ref) = refs[:len(gaps)], refs[len(gaps):-3], refs[-3:]
    rows, wide = rows_a + rows_b, rows_a * rows_b
    span = wide // LANES
    queries = out_ref.shape[0] - docs
    doc = lax.broadcasted_iota(jnp.int32, (docs, LANES), 0)
    place = lax.broadcasted_iota(jnp.int32, (queries, LANES), 0)
    me = lax.axis_index("dp")
    core = lax.axis_index("tensor")
    asked = [jnp.zeros((queries, LANES), jnp.float32)] * span
    start = 0
    for x_ref, gap, whole in zip(xs, gaps, wholes):
        parts = 2 if whole else 1
        base = parts * rows
        for i in range(parts):
            at = slice(start, start + LANES)
            start += LANES
            g, b = x_ref[i * rows:i * rows + rows_a, :], x_ref[i * rows + rows_a:(i + 1) * rows, :]
            ids = base + parts * span + i
            member_ref[:, at] = jnp.where(doc == x_ref[ids:ids + 1, :].astype(jnp.int32), 1.0, 0.0).astype(jnp.bfloat16)
            outer = (g[:, None, :] * b[None, :, :]).reshape(wide, LANES)
            high = outer.astype(jnp.bfloat16)
            outer_ref[0:wide, at] = high
            outer_ref[wide:, at] = (outer - high.astype(jnp.float32)).astype(jnp.bfloat16)
        source = 2 * (me ^ jnp.where(core == 0, gap[0], gap[1]))
        for i in range(parts):
            held = place == source + (i if whole else core)
            for j in range(span):
                row = base + i * span + j
                asked[j] = jnp.where(held, x_ref[row:row + 1, :], asked[j])
    sums = lax.dot_general(member_ref[...], outer_ref[...], NT, preferred_element_type=jnp.float32)
    sums = (sums[:, wide:] + sums[:, :wide]) * (TOK_DEV ** -0.5)
    asked = jnp.concatenate(asked, axis=1)
    if before:
        sums, asked = sums + before[0][0:docs, :], asked + before[0][docs:, :]
    out_ref[0:docs, :] = sums
    out_ref[docs:, :] = asked


def grads_of(xs, gaps, wholes, before, rows_a, rows_b, docs, queries, dp):
    tokens = LANES * (len(xs) + sum(wholes))
    wide = rows_a * rows_b
    operands = (*xs, *before)
    return pl.pallas_call(
        functools.partial(grads_kernel, rows_a, rows_b, docs, dp, gaps, wholes),
        out_shape=jax.ShapeDtypeStruct((docs + queries, wide), jnp.float32),
        in_specs=[VMEM] * len(operands),
        out_specs=VMEM,
        scratch_shapes=[
            pltpu.VMEM((2 * wide, tokens), jnp.bfloat16),
            pltpu.VMEM((docs, tokens), jnp.bfloat16),
        ],
        compiler_params=vmem_params(40),
        cost_estimate=pl.CostEstimate(
            flops=4 * docs * wide * tokens, bytes_accessed=4 * (rows_a + rows_b) * tokens, transcendentals=0
        ),
        name="grads",
    )(*operands)


def gram_kernel(docs, part_ref, recv_ref, out_ref):
    both = part_ref[...] + recv_ref[...]
    rows = both.shape[0]
    split = []
    for _ in range(3):
        split.append(both.astype(jnp.bfloat16))
        both = both - split[-1].astype(jnp.float32)
    every = lax.dot_general(
        jnp.concatenate(split, axis=0),
        jnp.concatenate([x[:docs] for x in split], axis=0),
        NT,
        preferred_element_type=jnp.float32,
    )
    share = None
    for i, j in ((2, 0), (1, 1), (0, 2), (1, 0), (0, 1), (0, 0)):
        term = every[i * rows:(i + 1) * rows, j * docs:(j + 1) * docs]
        share = term if share is None else share + term
    half = share.shape[0] // 2
    out_ref[...] = jnp.concatenate([share[:half], share[half:]], axis=1)


def gram(part, recv, docs):
    return pl.pallas_call(
        functools.partial(gram_kernel, docs),
        out_shape=jax.ShapeDtypeStruct((part.shape[0] // 2, 2 * docs), jnp.float32),
        in_specs=[VMEM] * 2,
        out_specs=VMEM,
        compiler_params=vmem_params(16),
        name="gram",
    )(part, recv)


def solve_kernel(docs, queries, scale, x_ref, recv_ref, out_ref, done_ref):
    total = x_ref[...] + recv_ref[...]
    stack = jnp.concatenate([total[:, :docs], total[:, docs:]], axis=0)
    cols = done_ref.shape[1]
    diagonal = [lax.broadcasted_iota(jnp.int32, (docs, docs), i) for i in range(2)]
    mean_diag = jnp.sum(jnp.where(diagonal[0] == diagonal[1], stack[:docs], 0.0)) * (1.0 / docs)
    stack = jnp.concatenate([stack, jnp.zeros((cols - stack.shape[0], docs), jnp.float32)], axis=0)
    total = stack.T
    row = lax.broadcasted_iota(jnp.int32, (docs, cols), 0)
    col = lax.broadcasted_iota(jnp.int32, (docs, cols), 1)
    work = total + jnp.where(row == col, 0.1 * mean_diag, 0.0)
    size = 8
    here = lax.broadcasted_iota(jnp.int32, (size, cols), 0)
    rows = [work[i:i + size] for i in range(0, docs, size)]
    for r in range(len(rows)):
        wide = [[jnp.broadcast_to(x[:, c:c + 1], (size, cols)) for c in range(r * size, (r + 1) * size)] for x in rows]
        pivot, line = wide[r], rows[r]
        scale_rows = jnp.ones((size, cols), jnp.float32)
        for j in range(size):
            inverse = 1.0 / pivot[j][j:j + 1]
            factor = jnp.where(here == j, 0.0, pivot[j]) * inverse
            pivot = [x if i <= j else x - factor * x[j:j + 1] for i, x in enumerate(pivot)]
            line = line - factor * line[j:j + 1]
            scale_rows = jnp.where(here == j, inverse, scale_rows)
        line = line * scale_rows
        for s in range(len(rows)):
            if s == r:
                rows[s] = line
            else:
                terms = [wide[s][j] * line[j:j + 1] for j in range(size)]
                rows[s] = rows[s] - (((terms[0] + terms[1]) + (terms[2] + terms[3]))
                                     + ((terms[4] + terms[5]) + (terms[6] + terms[7])))
    for r, x in enumerate(rows):
        done_ref[r * size:(r + 1) * size, :] = x * (mean_diag * scale)
    mine = pl.ds(pl.multiple_of(lax.axis_index("dp") * DOC_DEV, DOC_DEV), DOC_DEV)
    out_ref[...] = done_ref[mine, :][:, docs:docs + queries]


def solve(x, recv, docs, queries, scale):
    return pl.pallas_call(
        functools.partial(solve_kernel, docs, queries, scale),
        out_shape=jax.ShapeDtypeStruct((DOC_DEV, queries), jnp.float32),
        in_specs=[VMEM] * 2,
        out_specs=VMEM,
        scratch_shapes=[pltpu.VMEM((docs, -(-(docs + queries) // LANES) * LANES), jnp.float32)],
        compiler_params=vmem_params(16),
        name="solve",
    )(x, recv)


def solve_large(total, docs, queries, scale):
    kernel = total[:, :docs]
    mean_diag = jnp.trace(kernel) / docs
    factor = jnp.linalg.cholesky(kernel + 0.1 * mean_diag * jnp.eye(docs, dtype=jnp.float32))
    solved = jax.scipy.linalg.cho_solve((factor, True), total[:, docs:docs + queries]) * (mean_diag * scale)
    return lax.dynamic_slice_in_dim(solved, lax.axis_index("dp") * DOC_DEV, DOC_DEV, 0)


def swap_cores(x):
    cores = lax.axis_size("tensor")
    return lax.ppermute(x, "tensor", [(i, cores - 1 - i) for i in range(cores)])


def trade(xs, group):
    dp = lax.axis_size("dp")
    got = []
    for x, ms in zip(xs, zip(*partners(group))):
        pairs = [(i * 2 + k, (i ^ m) * 2 + k) for i in range(dp) for k, m in enumerate(ms)]
        got.append(lax.ppermute(x, ("dp", "tensor"), pairs))
    return got


def trade_shared(x):
    dp = lax.axis_size("dp")
    return lax.ppermute(x, "dp", [(i, i ^ SHARED) for i in range(dp)])


def local(hidden, out_grad, proj_in, proj_out, doc_ids, queries):
    dp = lax.axis_size("dp")
    docs, num_queries = DOC_DEV * dp, queries.shape[0] * dp
    ranks = proj_in.shape[1]
    owners = owners_of(dp)
    pa = 1
    while pa * pa < owners:
        pa *= 2
    pb = owners // pa
    rows_a, rows_b = ranks // pa, ranks // pb

    part = project(hidden, out_grad, proj_in.T, proj_out.T)
    recv = swap_cores(part)

    ids = jnp.broadcast_to(doc_ids.astype(jnp.float32).reshape(2, LANES), (owners, 2, LANES))
    asked = queries.reshape(-1, pa, rows_a, pb, rows_b).transpose(1, 3, 0, 2, 4).reshape(owners, -1, LANES)
    extra = jnp.concatenate([asked, ids], axis=1)
    extra = jnp.pad(extra, ((0, 0), (0, -extra.shape[1] % 8), (0, 0)))

    *blocks, shared, own = pack(part, recv, extra, dp, pa, pb)
    blocks = trade(blocks, dp) + [trade_shared(shared), own]
    gaps = [*zip(*partners(dp)), (SHARED, SHARED), (0, 0)]
    wholes = [True] * (len(blocks) - 2) + [False, False]
    sizes = (rows_a, rows_b, docs, num_queries, dp)
    count = len(blocks) - 2
    grads = ()
    for part in ([count + 1, *range(2, count)], [0, count], [1]):
        grads = (grads_of(*([x[t] for t in part] for x in (blocks, gaps, wholes)), grads, *sizes),)
    grads = grads[0]
    share = gram(grads, swap_cores(grads), docs)
    scale = float(ranks * ranks) ** -0.5
    if docs <= 64:
        others = sum(trade([share] * (owners // 2 - 1), owners))
        share = others + jnp.where(lax.axis_index("tensor") == 0, share, trade_shared(share))
        return solve(share, swap_cores(share), docs, num_queries, scale).T
    share = lax.psum(share, "dp") * (owners / dp)
    return solve_large(jnp.concatenate([share[:, :docs], share[:, docs:]], axis=0).T, docs, num_queries, scale).T


def solution(mesh):
    return jax.shard_map(
        local,
        mesh=mesh,
        in_specs=(
            P(("groups", "dp"), "tensor"),
            P(("groups", "dp"), "tensor"),
            P("tensor", None),
            P("tensor", None),
            P(("groups", "dp")),
            P(("groups", "dp"), None),
        ),
        out_specs=P("groups", "dp"),
        check_vma=False,
    )
```

```python
import functools

import jax
import jax.numpy as jnp
from jax import lax
from jax.experimental import pallas as pl
from jax.experimental.pallas import tpu as pltpu
from jax.sharding import PartitionSpec as P

TOK_DEV = 256
DOC_DEV = 8
LANES = 128
FLIGHT = 7
SHARED = 1
NT = (((1,), (1,)), ((), ()))
VMEM = pl.BlockSpec(memory_space=pltpu.VMEM)
HBM = pl.BlockSpec(memory_space=pltpu.HBM)


def vmem_params(mib):
    return pltpu.CompilerParams(vmem_limit_bytes=int(mib * (1 << 20)))


def pieces(x):
    rows, units = x.shape
    split = x.reshape(rows // 8, 8, units // (2 * LANES), 2, LANES).transpose(0, 2, 3, 1, 4)
    return split.reshape(rows // 8, units // (2 * LANES), 16, LANES)


def chunks_of(length, ramp, tail):
    left = length - sum(ramp) - sum(tail)
    sizes = [*ramp, *([6] * (left // 6)), *([left % 6] if left % 6 else []), *tail]
    return [(sum(sizes[:i]), size) for i, size in enumerate(sizes)]


def project_kernel(g_chunks, h_chunks, h_ref, g_ref, pin_ref, pout_ref, out_ref, h_buf, g_buf, pin_buf, pout_buf, sems):
    plan = [(pout_ref, pout_buf, g_ref, g_buf, at) for at in g_chunks] + [(pin_ref, pin_buf, h_ref, h_buf, at) for at in h_chunks]
    copies = []
    for i, (proj, proj_buf, data, data_buf, (start, size)) in enumerate(plan):
        at = pl.ds(start, size)
        copies.append((
            pltpu.make_async_copy(proj.at[:, at], proj_buf.at[:, at], sems.at[2 * i]),
            pltpu.make_async_copy(data.at[:, at], data_buf.at[:, at], sems.at[2 * i + 1]),
        ))

    def start(i):
        if i < len(copies):
            for copy in copies[i]:
                copy.start()

    for i in range(FLIGHT):
        start(i)

    def line_up(ref, first, size):
        blocks = [ref[:, j].reshape(ref.shape[0] * 16, LANES) for j in range(first, first + size)]
        return jnp.concatenate(blocks, axis=1)

    totals = [None, None]
    for i, (_, proj_buf, _, data_buf, (first, size)) in enumerate(plan):
        for copy in copies[i]:
            copy.wait()
        start(i + FLIGHT)
        which = 0 if i < len(g_chunks) else 1
        part = lax.dot_general(
            line_up(proj_buf, first, size), line_up(data_buf, first, size), NT, preferred_element_type=jnp.float32
        )
        totals[which] = part if totals[which] is None else totals[which] + part

    lane = lax.broadcasted_iota(jnp.int32, (8, LANES), 1)
    even = lane % 16 < 8
    later = lane // (LANES // 2)
    order = lane % (LANES // 2) // 8 * 16 + lane % 8 + 8 * later
    done = 0
    for total in totals:
        for g in range(0, total.shape[0], 16):
            lines = []
            for i in range(0, total.shape[1], LANES):
                upper, lower = total[g:g + 8, i:i + LANES], total[g + 8:g + 16, i:i + LANES]
                lines.append(jnp.where(even, upper, lower))
            for i in range(0, len(lines), 2):
                first = lines[i] + pltpu.roll(lines[i], LANES - 8, 1)
                second = lines[i + 1] + pltpu.roll(lines[i + 1], 8, 1)
                both = jnp.where(even, first, second)
                at = i // 2 * LANES
                out_ref[done:done + 8, at:at + LANES] = jnp.take_along_axis(both, order, axis=1)
            done += 8


def project(hidden, out_grad, pin_t, pout_t):
    tokens, units = hidden.shape
    width = out_grad.shape[1]
    ranks = pin_t.shape[0] + pout_t.shape[0]
    operands = [pieces(x) for x in (hidden, out_grad, pin_t, pout_t)]
    g_chunks = chunks_of(operands[1].shape[1], (1, 2, 3, 4), ())
    h_chunks = chunks_of(operands[0].shape[1], (), (4, 2, 2))
    return pl.pallas_call(
        functools.partial(project_kernel, g_chunks, h_chunks),
        out_shape=jax.ShapeDtypeStruct((ranks, tokens), jnp.float32),
        in_specs=[HBM] * 4,
        out_specs=VMEM,
        scratch_shapes=[pltpu.VMEM(x.shape, x.dtype) for x in operands]
        + [pltpu.SemaphoreType.DMA((2 * len(g_chunks + h_chunks),))],
        compiler_params=vmem_params(53.5),
        cost_estimate=pl.CostEstimate(
            flops=2 * tokens * 64 * (units + width),
            bytes_accessed=2 * (tokens + 64) * (units + width),
            transcendentals=0,
        ),
        name="project",
    )(*operands)


def owners_of(dp):
    return max(dp // 2, 1)


def partners(dp):
    order = [m for far in (True, False) for m in range(1, dp) if m != SHARED and (2 * m >= dp) == far]
    return order[0::2], order[1::2]


def partner(dp, t):
    first, second = partners(dp)
    return jnp.where(lax.axis_index("tensor") == 0, first[t], second[t])


def pack_kernel(dp, pb, rows_a, rows_b, span, part_ref, recv_ref, extra_ref, *refs):
    outs, total_ref = refs[:-1], refs[-1]
    total_ref[...] = part_ref[...] + recv_ref[...]
    ranks = total_ref.shape[0] // 2
    rows = rows_a + rows_b
    owners, ids = extra_ref.shape[0], 2 * span
    me = lax.axis_index("dp")
    lead = lax.axis_index("tensor") == 0

    def slices(owner):
        p, q = owner // pb, owner % pb
        g = total_ref[pl.ds(pl.multiple_of(p * rows_a, rows_a), rows_a), :]
        b = total_ref[pl.ds(pl.multiple_of(ranks + q * rows_b, rows_b), rows_b), :]
        return [(g[:, i:i + LANES], b[:, i:i + LANES]) for i in (0, LANES)]

    for t, out_ref in enumerate(outs[:-2]):
        owner = (me ^ partner(dp, t)) % owners
        for i, (g, b) in enumerate(slices(owner)):
            out_ref[i * rows:i * rows + rows_a, :] = g
            out_ref[i * rows + rows_a:(i + 1) * rows, :] = b
        out_ref[2 * rows:, :] = extra_ref[owner]
    for out_ref, to in zip(outs[-2:], (me ^ SHARED, me)):
        owner = to % owners
        (g, b), (later_g, later_b) = slices(owner)
        extra = extra_ref[owner]
        out_ref[0:rows_a, :] = jnp.where(lead, g, later_g)
        out_ref[rows_a:rows, :] = jnp.where(lead, b, later_b)
        out_ref[rows:rows + span, :] = jnp.where(lead, extra[0:span], extra[span:ids])
        rest = out_ref.shape[0] - rows - span
        out_ref[rows + span:, :] = jnp.broadcast_to(jnp.where(lead, extra[ids:ids + 1], extra[ids + 1:ids + 2]), (rest, LANES))


def pack(part, recv, extra, dp, pa, pb):
    ranks = part.shape[0] // 2
    rows_a, rows_b = ranks // pa, ranks // pb
    rows, span = rows_a + rows_b, rows_a * rows_b // LANES
    whole = jax.ShapeDtypeStruct((2 * rows + extra.shape[1], LANES), jnp.float32)
    half = jax.ShapeDtypeStruct((rows + 8 * (span // 8 + 1), LANES), jnp.float32)
    count = dp // 2 - 1
    return pl.pallas_call(
        functools.partial(pack_kernel, dp, pb, rows_a, rows_b, span),
        out_shape=(whole,) * count + (half, half),
        in_specs=[VMEM] * 3,
        out_specs=(VMEM,) * (count + 2),
        scratch_shapes=[pltpu.VMEM(part.shape, jnp.float32)],
        compiler_params=vmem_params(16),
        name="pack",
    )(part, recv, extra)


def grads_kernel(rows_a, rows_b, docs, dp, gaps, wholes, *refs):
    xs, before, (out_ref, outer_ref, member_ref) = refs[:len(gaps)], refs[len(gaps):-3], refs[-3:]
    rows, wide = rows_a + rows_b, rows_a * rows_b
    span = wide // LANES
    queries = out_ref.shape[0] - docs
    doc = lax.broadcasted_iota(jnp.int32, (docs, LANES), 0)
    place = lax.broadcasted_iota(jnp.int32, (queries, LANES), 0)
    me = lax.axis_index("dp")
    core = lax.axis_index("tensor")
    asked = [jnp.zeros((queries, LANES), jnp.float32)] * span
    start = 0
    for x_ref, gap, whole in zip(xs, gaps, wholes):
        parts = 2 if whole else 1
        base = parts * rows
        for i in range(parts):
            at = slice(start, start + LANES)
            start += LANES
            g, b = x_ref[i * rows:i * rows + rows_a, :], x_ref[i * rows + rows_a:(i + 1) * rows, :]
            ids = base + parts * span + i
            member_ref[:, at] = jnp.where(doc == x_ref[ids:ids + 1, :].astype(jnp.int32), 1.0, 0.0).astype(jnp.bfloat16)
            outer = (g[:, None, :] * b[None, :, :]).reshape(wide, LANES)
            high = outer.astype(jnp.bfloat16)
            outer_ref[0:wide, at] = high
            outer_ref[wide:, at] = (outer - high.astype(jnp.float32)).astype(jnp.bfloat16)
        source = 2 * (me ^ jnp.where(core == 0, gap[0], gap[1]))
        for i in range(parts):
            held = place == source + (i if whole else core)
            for j in range(span):
                row = base + i * span + j
                asked[j] = jnp.where(held, x_ref[row:row + 1, :], asked[j])
    sums = lax.dot_general(member_ref[...], outer_ref[...], NT, preferred_element_type=jnp.float32)
    sums = (sums[:, wide:] + sums[:, :wide]) * (TOK_DEV ** -0.5)
    asked = jnp.concatenate(asked, axis=1)
    if before:
        sums, asked = sums + before[0][0:docs, :], asked + before[0][docs:, :]
    out_ref[0:docs, :] = sums
    out_ref[docs:, :] = asked


def grads_of(xs, gaps, wholes, before, rows_a, rows_b, docs, queries, dp):
    tokens = LANES * (len(xs) + sum(wholes))
    wide = rows_a * rows_b
    operands = (*xs, *before)
    return pl.pallas_call(
        functools.partial(grads_kernel, rows_a, rows_b, docs, dp, gaps, wholes),
        out_shape=jax.ShapeDtypeStruct((docs + queries, wide), jnp.float32),
        in_specs=[VMEM] * len(operands),
        out_specs=VMEM,
        scratch_shapes=[
            pltpu.VMEM((2 * wide, tokens), jnp.bfloat16),
            pltpu.VMEM((docs, tokens), jnp.bfloat16),
        ],
        compiler_params=vmem_params(40),
        cost_estimate=pl.CostEstimate(
            flops=4 * docs * wide * tokens, bytes_accessed=4 * (rows_a + rows_b) * tokens, transcendentals=0
        ),
        name="grads",
    )(*operands)


def gram_kernel(docs, part_ref, recv_ref, out_ref):
    both = part_ref[...] + recv_ref[...]
    rows = both.shape[0]
    split = []
    for _ in range(3):
        split.append(both.astype(jnp.bfloat16))
        both = both - split[-1].astype(jnp.float32)
    every = lax.dot_general(
        jnp.concatenate(split, axis=0),
        jnp.concatenate([x[:docs] for x in split], axis=0),
        NT,
        preferred_element_type=jnp.float32,
    )
    share = None
    for i, j in ((2, 0), (1, 1), (0, 2), (1, 0), (0, 1), (0, 0)):
        term = every[i * rows:(i + 1) * rows, j * docs:(j + 1) * docs]
        share = term if share is None else share + term
    half = share.shape[0] // 2
    out_ref[...] = jnp.concatenate([share[:half], share[half:]], axis=1)


def gram(part, recv, docs):
    return pl.pallas_call(
        functools.partial(gram_kernel, docs),
        out_shape=jax.ShapeDtypeStruct((part.shape[0] // 2, 2 * docs), jnp.float32),
        in_specs=[VMEM] * 2,
        out_specs=VMEM,
        compiler_params=vmem_params(16),
        name="gram",
    )(part, recv)


def solve_kernel(docs, queries, scale, x_ref, recv_ref, out_ref, kernel_ref, work_ref):
    total = x_ref[...] + recv_ref[...]
    stack = jnp.concatenate([total[:, :docs], total[:, docs:]], axis=0)
    cols = work_ref.shape[1]
    turned = pl.ds(pl.multiple_of((lax.axis_index("dp") + 1) * DOC_DEV, DOC_DEV), docs)
    diagonal = [lax.broadcasted_iota(jnp.int32, (docs, docs), i) for i in range(2)]
    mean_diag = jnp.sum(jnp.where(diagonal[0] == diagonal[1], stack[:docs], 0.0)) * (1.0 / docs)
    for i in range(2):
        kernel_ref[i * docs:(i + 1) * docs, :] = stack[:docs]
    rest = jnp.zeros((cols - stack.shape[0], docs), jnp.float32)
    total = jnp.concatenate([kernel_ref[turned, :], stack[docs:], rest], axis=0).T
    for i in range(2):
        work_ref[i * docs:(i + 1) * docs, :] = total
    total = work_ref[turned, :]
    row = lax.broadcasted_iota(jnp.int32, (docs, cols), 0)
    col = lax.broadcasted_iota(jnp.int32, (docs, cols), 1)
    work = total + jnp.where(row == col, 0.1 * mean_diag, 0.0)
    size = 8
    here = lax.broadcasted_iota(jnp.int32, (size, cols), 0)
    rows = [work[i:i + size] for i in range(0, docs, size)]
    for r in range(len(rows)):
        wide = [[jnp.broadcast_to(x[:, c:c + 1], (size, cols)) for c in range(r * size, (r + 1) * size)] for x in rows[r:]]
        pivot, line = wide[0], rows[r]
        scale_rows = jnp.ones((size, cols), jnp.float32)
        for j in range(size):
            inverse = 1.0 / pivot[j][j:j + 1]
            factor = jnp.where(here == j, 0.0, pivot[j]) * inverse
            pivot = [x if i <= j else x - factor * x[j:j + 1] for i, x in enumerate(pivot)]
            line = line - factor * line[j:j + 1]
            scale_rows = jnp.where(here == j, inverse, scale_rows)
        line = line * scale_rows
        rows[r] = line
        for s in range(r + 1, len(rows)):
            terms = [wide[s - r][j] * line[j:j + 1] for j in range(size)]
            rows[s] = rows[s] - (((terms[0] + terms[1]) + (terms[2] + terms[3]))
                                 + ((terms[4] + terms[5]) + (terms[6] + terms[7])))
    out_ref[...] = rows[-1][:, docs:docs + queries] * (mean_diag * scale)


def solve(x, recv, docs, queries, scale):
    return pl.pallas_call(
        functools.partial(solve_kernel, docs, queries, scale),
        out_shape=jax.ShapeDtypeStruct((DOC_DEV, queries), jnp.float32),
        in_specs=[VMEM] * 2,
        out_specs=VMEM,
        scratch_shapes=[
            pltpu.VMEM((2 * docs, docs), jnp.float32),
            pltpu.VMEM((2 * docs, -(-(docs + queries) // LANES) * LANES), jnp.float32),
        ],
        compiler_params=vmem_params(16),
        name="solve",
    )(x, recv)


def solve_large(total, docs, queries, scale):
    kernel = total[:, :docs]
    mean_diag = jnp.trace(kernel) / docs
    factor = jnp.linalg.cholesky(kernel + 0.1 * mean_diag * jnp.eye(docs, dtype=jnp.float32))
    solved = jax.scipy.linalg.cho_solve((factor, True), total[:, docs:docs + queries]) * (mean_diag * scale)
    return lax.dynamic_slice_in_dim(solved, lax.axis_index("dp") * DOC_DEV, DOC_DEV, 0)


def swap_cores(x):
    cores = lax.axis_size("tensor")
    return lax.ppermute(x, "tensor", [(i, cores - 1 - i) for i in range(cores)])


def trade(xs, group):
    dp = lax.axis_size("dp")
    got = []
    for x, ms in zip(xs, zip(*partners(group))):
        pairs = [(i * 2 + k, (i ^ m) * 2 + k) for i in range(dp) for k, m in enumerate(ms)]
        got.append(lax.ppermute(x, ("dp", "tensor"), pairs))
    return got


def trade_shared(x):
    dp = lax.axis_size("dp")
    return lax.ppermute(x, "dp", [(i, i ^ SHARED) for i in range(dp)])


def local(hidden, out_grad, proj_in, proj_out, doc_ids, queries):
    dp = lax.axis_size("dp")
    docs, num_queries = DOC_DEV * dp, queries.shape[0] * dp
    ranks = proj_in.shape[1]
    owners = owners_of(dp)
    pa = 1
    while pa * pa < owners:
        pa *= 2
    pb = owners // pa
    rows_a, rows_b = ranks // pa, ranks // pb

    part = project(hidden, out_grad, proj_in.T, proj_out.T)
    recv = swap_cores(part)

    ids = jnp.broadcast_to(doc_ids.astype(jnp.float32).reshape(2, LANES), (owners, 2, LANES))
    asked = queries.reshape(-1, pa, rows_a, pb, rows_b).transpose(1, 3, 0, 2, 4).reshape(owners, -1, LANES)
    extra = jnp.concatenate([asked, ids], axis=1)
    extra = jnp.pad(extra, ((0, 0), (0, -extra.shape[1] % 8), (0, 0)))

    *blocks, shared, own = pack(part, recv, extra, dp, pa, pb)
    blocks = trade(blocks, dp) + [trade_shared(shared), own]
    gaps = [*zip(*partners(dp)), (SHARED, SHARED), (0, 0)]
    wholes = [True] * (len(blocks) - 2) + [False, False]
    sizes = (rows_a, rows_b, docs, num_queries, dp)
    late = min(1, len(blocks) - 3)
    rest = [t for t in range(len(blocks)) if t != late]
    grads = ()
    for part in (rest, [late]):
        grads = (grads_of(*([x[t] for t in part] for x in (blocks, gaps, wholes)), grads, *sizes),)
    grads = grads[0]
    share = gram(grads, swap_cores(grads), docs)
    scale = float(ranks * ranks) ** -0.5
    if docs <= 64:
        others = sum(trade([share] * (owners // 2 - 1), owners))
        share = others + jnp.where(lax.axis_index("tensor") == 0, share, trade_shared(share))
        return solve(share, swap_cores(share), docs, num_queries, scale).T
    share = lax.psum(share, "dp") * (owners / dp)
    return solve_large(jnp.concatenate([share[:, :docs], share[:, docs:]], axis=0).T, docs, num_queries, scale).T


def solution(mesh):
    return jax.shard_map(
        local,
        mesh=mesh,
        in_specs=(
            P(("groups", "dp"), "tensor"),
            P(("groups", "dp"), "tensor"),
            P("tensor", None),
            P("tensor", None),
            P(("groups", "dp")),
            P(("groups", "dp"), None),
        ),
        out_specs=P("groups", "dp"),
        check_vma=False,
    )
```

```python
import functools

import jax
import jax.numpy as jnp
from jax import lax
from jax.experimental import pallas as pl
from jax.experimental.pallas import tpu as pltpu
from jax.sharding import PartitionSpec as P

TOK_DEV = 256
DOC_DEV = 8
LANES = 128
FLIGHT = 7
SHARED = 1
NT = (((1,), (1,)), ((), ()))
VMEM = pl.BlockSpec(memory_space=pltpu.VMEM)
HBM = pl.BlockSpec(memory_space=pltpu.HBM)


def vmem_params(mib):
    return pltpu.CompilerParams(vmem_limit_bytes=int(mib * (1 << 20)))


def pieces(x):
    rows, units = x.shape
    split = x.reshape(rows // 8, 8, units // (2 * LANES), 2, LANES).transpose(0, 2, 3, 1, 4)
    return split.reshape(rows // 8, units // (2 * LANES), 16, LANES)


def chunks_of(length, ramp, tail):
    left = length - sum(ramp) - sum(tail)
    sizes = [*ramp, *([6] * (left // 6)), *([left % 6] if left % 6 else []), *tail]
    return [(sum(sizes[:i]), size) for i, size in enumerate(sizes)]


def project_kernel(g_chunks, h_chunks, h_ref, g_ref, pin_ref, pout_ref, out_ref, h_buf, g_buf, pin_buf, pout_buf, sems):
    plan = [(pout_ref, pout_buf, g_ref, g_buf, at) for at in g_chunks] + [(pin_ref, pin_buf, h_ref, h_buf, at) for at in h_chunks]
    copies = []
    for i, (proj, proj_buf, data, data_buf, (start, size)) in enumerate(plan):
        at = pl.ds(start, size)
        copies.append((
            pltpu.make_async_copy(proj.at[:, at], proj_buf.at[:, at], sems.at[2 * i]),
            pltpu.make_async_copy(data.at[:, at], data_buf.at[:, at], sems.at[2 * i + 1]),
        ))

    def start(i):
        if i < len(copies):
            for copy in copies[i]:
                copy.start()

    for i in range(FLIGHT):
        start(i)

    def line_up(ref, first, size):
        blocks = [ref[:, j].reshape(ref.shape[0] * 16, LANES) for j in range(first, first + size)]
        return jnp.concatenate(blocks, axis=1)

    totals = [None, None]
    for i, (_, proj_buf, _, data_buf, (first, size)) in enumerate(plan):
        for copy in copies[i]:
            copy.wait()
        start(i + FLIGHT)
        which = 0 if i < len(g_chunks) else 1
        part = lax.dot_general(
            line_up(proj_buf, first, size), line_up(data_buf, first, size), NT, preferred_element_type=jnp.float32
        )
        totals[which] = part if totals[which] is None else totals[which] + part

    lane = lax.broadcasted_iota(jnp.int32, (8, LANES), 1)
    even = lane % 16 < 8
    later = lane // (LANES // 2)
    order = lane % (LANES // 2) // 8 * 16 + lane % 8 + 8 * later
    done = 0
    for total in totals:
        for g in range(0, total.shape[0], 16):
            lines = []
            for i in range(0, total.shape[1], LANES):
                upper, lower = total[g:g + 8, i:i + LANES], total[g + 8:g + 16, i:i + LANES]
                lines.append(jnp.where(even, upper, lower))
            for i in range(0, len(lines), 2):
                first = lines[i] + pltpu.roll(lines[i], LANES - 8, 1)
                second = lines[i + 1] + pltpu.roll(lines[i + 1], 8, 1)
                both = jnp.where(even, first, second)
                at = i // 2 * LANES
                out_ref[done:done + 8, at:at + LANES] = jnp.take_along_axis(both, order, axis=1)
            done += 8


def project(hidden, out_grad, pin_t, pout_t):
    tokens, units = hidden.shape
    width = out_grad.shape[1]
    ranks = pin_t.shape[0] + pout_t.shape[0]
    operands = [pieces(x) for x in (hidden, out_grad, pin_t, pout_t)]
    g_chunks = chunks_of(operands[1].shape[1], (1, 2, 3, 4), ())
    h_chunks = chunks_of(operands[0].shape[1], (), (4, 2, 2))
    return pl.pallas_call(
        functools.partial(project_kernel, g_chunks, h_chunks),
        out_shape=jax.ShapeDtypeStruct((ranks, tokens), jnp.float32),
        in_specs=[HBM] * 4,
        out_specs=VMEM,
        scratch_shapes=[pltpu.VMEM(x.shape, x.dtype) for x in operands]
        + [pltpu.SemaphoreType.DMA((2 * len(g_chunks + h_chunks),))],
        compiler_params=vmem_params(53.5),
        cost_estimate=pl.CostEstimate(
            flops=2 * tokens * 64 * (units + width),
            bytes_accessed=2 * (tokens + 64) * (units + width),
            transcendentals=0,
        ),
        name="project",
    )(*operands)


def owners_of(dp):
    return max(dp // 2, 1)


def partners(dp):
    order = [m for far in (True, False) for m in range(1, dp) if m != SHARED and (2 * m >= dp) == far]
    return order[0::2], order[1::2]


def partner(dp, t):
    first, second = partners(dp)
    return jnp.where(lax.axis_index("tensor") == 0, first[t], second[t])


def pack_kernel(dp, pb, rows_a, rows_b, span, part_ref, recv_ref, extra_ref, *refs):
    outs, total_ref = refs[:-1], refs[-1]
    total_ref[...] = part_ref[...] + recv_ref[...]
    ranks = total_ref.shape[0] // 2
    rows = rows_a + rows_b
    owners, ids = extra_ref.shape[0], 2 * span
    me = lax.axis_index("dp")
    lead = lax.axis_index("tensor") == 0

    def slices(owner):
        p, q = owner // pb, owner % pb
        g = total_ref[pl.ds(pl.multiple_of(p * rows_a, rows_a), rows_a), :]
        b = total_ref[pl.ds(pl.multiple_of(ranks + q * rows_b, rows_b), rows_b), :]
        return [(g[:, i:i + LANES], b[:, i:i + LANES]) for i in (0, LANES)]

    for t, out_ref in enumerate(outs[:-2]):
        owner = (me ^ partner(dp, t)) % owners
        for i, (g, b) in enumerate(slices(owner)):
            out_ref[i * rows:i * rows + rows_a, :] = g
            out_ref[i * rows + rows_a:(i + 1) * rows, :] = b
        out_ref[2 * rows:, :] = extra_ref[owner]
    for out_ref, to in zip(outs[-2:], (me ^ SHARED, me)):
        owner = to % owners
        (g, b), (later_g, later_b) = slices(owner)
        extra = extra_ref[owner]
        out_ref[0:rows_a, :] = jnp.where(lead, g, later_g)
        out_ref[rows_a:rows, :] = jnp.where(lead, b, later_b)
        out_ref[rows:rows + span, :] = jnp.where(lead, extra[0:span], extra[span:ids])
        rest = out_ref.shape[0] - rows - span
        out_ref[rows + span:, :] = jnp.broadcast_to(jnp.where(lead, extra[ids:ids + 1], extra[ids + 1:ids + 2]), (rest, LANES))


def pack(part, recv, extra, dp, pa, pb):
    ranks = part.shape[0] // 2
    rows_a, rows_b = ranks // pa, ranks // pb
    rows, span = rows_a + rows_b, rows_a * rows_b // LANES
    whole = jax.ShapeDtypeStruct((2 * rows + extra.shape[1], LANES), jnp.float32)
    half = jax.ShapeDtypeStruct((rows + 8 * (span // 8 + 1), LANES), jnp.float32)
    count = dp // 2 - 1
    return pl.pallas_call(
        functools.partial(pack_kernel, dp, pb, rows_a, rows_b, span),
        out_shape=(whole,) * count + (half, half),
        in_specs=[VMEM] * 3,
        out_specs=(VMEM,) * (count + 2),
        scratch_shapes=[pltpu.VMEM(part.shape, jnp.float32)],
        compiler_params=vmem_params(16),
        name="pack",
    )(part, recv, extra)


def grads_kernel(rows_a, rows_b, docs, dp, gaps, wholes, *refs):
    xs, before, (out_ref, outer_ref, member_ref) = refs[:len(gaps)], refs[len(gaps):-3], refs[-3:]
    rows, wide = rows_a + rows_b, rows_a * rows_b
    span = wide // LANES
    queries = out_ref.shape[0] - docs
    doc = lax.broadcasted_iota(jnp.int32, (docs, LANES), 0)
    place = lax.broadcasted_iota(jnp.int32, (queries, LANES), 0)
    me = lax.axis_index("dp")
    core = lax.axis_index("tensor")
    asked = [jnp.zeros((queries, LANES), jnp.float32)] * span
    start = 0
    for x_ref, gap, whole in zip(xs, gaps, wholes):
        parts = 2 if whole else 1
        base = parts * rows
        for i in range(parts):
            at = slice(start, start + LANES)
            start += LANES
            g, b = x_ref[i * rows:i * rows + rows_a, :], x_ref[i * rows + rows_a:(i + 1) * rows, :]
            ids = base + parts * span + i
            member_ref[:, at] = jnp.where(doc == x_ref[ids:ids + 1, :].astype(jnp.int32), 1.0, 0.0).astype(jnp.bfloat16)
            outer = (g[:, None, :] * b[None, :, :]).reshape(wide, LANES)
            high = outer.astype(jnp.bfloat16)
            outer_ref[0:wide, at] = high
            outer_ref[wide:, at] = (outer - high.astype(jnp.float32)).astype(jnp.bfloat16)
        source = 2 * (me ^ jnp.where(core == 0, gap[0], gap[1]))
        for i in range(parts):
            held = place == source + (i if whole else core)
            for j in range(span):
                row = base + i * span + j
                asked[j] = jnp.where(held, x_ref[row:row + 1, :], asked[j])
    sums = lax.dot_general(member_ref[...], outer_ref[...], NT, preferred_element_type=jnp.float32)
    sums = (sums[:, wide:] + sums[:, :wide]) * (TOK_DEV ** -0.5)
    asked = jnp.concatenate(asked, axis=1)
    if before:
        sums, asked = sums + before[0][0:docs, :], asked + before[0][docs:, :]
    out_ref[0:docs, :] = sums
    out_ref[docs:, :] = asked


def grads_of(xs, gaps, wholes, before, rows_a, rows_b, docs, queries, dp):
    tokens = LANES * (len(xs) + sum(wholes))
    wide = rows_a * rows_b
    operands = (*xs, *before)
    return pl.pallas_call(
        functools.partial(grads_kernel, rows_a, rows_b, docs, dp, gaps, wholes),
        out_shape=jax.ShapeDtypeStruct((docs + queries, wide), jnp.float32),
        in_specs=[VMEM] * len(operands),
        out_specs=VMEM,
        scratch_shapes=[
            pltpu.VMEM((2 * wide, tokens), jnp.bfloat16),
            pltpu.VMEM((docs, tokens), jnp.bfloat16),
        ],
        compiler_params=vmem_params(40),
        cost_estimate=pl.CostEstimate(
            flops=4 * docs * wide * tokens, bytes_accessed=4 * (rows_a + rows_b) * tokens, transcendentals=0
        ),
        name="grads",
    )(*operands)


def gram_kernel(docs, part_ref, recv_ref, out_ref):
    both = part_ref[...] + recv_ref[...]
    rows = both.shape[0]
    split = []
    for _ in range(3):
        split.append(both.astype(jnp.bfloat16))
        both = both - split[-1].astype(jnp.float32)
    every = lax.dot_general(
        jnp.concatenate(split, axis=0),
        jnp.concatenate([x[:docs] for x in split], axis=0),
        NT,
        preferred_element_type=jnp.float32,
    )
    share = None
    for i, j in ((2, 0), (1, 1), (0, 2), (1, 0), (0, 1), (0, 0)):
        term = every[i * rows:(i + 1) * rows, j * docs:(j + 1) * docs]
        share = term if share is None else share + term
    half = share.shape[0] // 2
    out_ref[...] = jnp.concatenate([share[:half], share[half:]], axis=1)


def gram(part, recv, docs):
    return pl.pallas_call(
        functools.partial(gram_kernel, docs),
        out_shape=jax.ShapeDtypeStruct((part.shape[0] // 2, 2 * docs), jnp.float32),
        in_specs=[VMEM] * 2,
        out_specs=VMEM,
        compiler_params=vmem_params(16),
        name="gram",
    )(part, recv)


def solve_kernel(docs, queries, scale, x_ref, recv_ref, out_ref, done_ref):
    total = x_ref[...] + recv_ref[...]
    stack = jnp.concatenate([total[:, :docs], total[:, docs:]], axis=0)
    cols = done_ref.shape[1]
    diagonal = [lax.broadcasted_iota(jnp.int32, (docs, docs), i) for i in range(2)]
    mean_diag = jnp.sum(jnp.where(diagonal[0] == diagonal[1], stack[:docs], 0.0)) * (1.0 / docs)
    stack = jnp.concatenate([stack, jnp.zeros((cols - stack.shape[0], docs), jnp.float32)], axis=0)
    total = stack.T
    row = lax.broadcasted_iota(jnp.int32, (docs, cols), 0)
    col = lax.broadcasted_iota(jnp.int32, (docs, cols), 1)
    work = total + jnp.where(row == col, 0.1 * mean_diag, 0.0)
    size = 8
    here = lax.broadcasted_iota(jnp.int32, (size, cols), 0)
    rows = [work[i:i + size] for i in range(0, docs, size)]
    for r in range(len(rows)):
        wide = [[jnp.broadcast_to(x[:, c:c + 1], (size, cols)) for c in range(r * size, (r + 1) * size)] for x in rows]
        pivot, line = list(wide[r]), rows[r]
        scale_rows = jnp.ones((size, cols), jnp.float32)
        diagonals = [jnp.broadcast_to(x[i:i + 1], (size, cols)) for i, x in enumerate(pivot)]
        for j in range(size):
            inverse = 1.0 / diagonals[j]
            factor = jnp.where(here == j, 0.0, pivot[j]) * inverse
            for k in range(j + 1, size):
                across = jnp.broadcast_to(pivot[k][j:j + 1], (size, cols))
                diagonals[k] = diagonals[k] - (across * across) * inverse
                pivot[k] = pivot[k] - factor * across
            line = line - factor * line[j:j + 1]
            scale_rows = jnp.where(here == j, inverse, scale_rows)
        line = line * scale_rows
        for s in range(len(rows)):
            if s == r:
                rows[s] = line
            else:
                terms = [wide[s][j] * line[j:j + 1] for j in range(size)]
                rows[s] = rows[s] - (((terms[0] + terms[1]) + (terms[2] + terms[3]))
                                     + ((terms[4] + terms[5]) + (terms[6] + terms[7])))
    for r, x in enumerate(rows):
        done_ref[r * size:(r + 1) * size, :] = x * (mean_diag * scale)
    mine = pl.ds(pl.multiple_of(lax.axis_index("dp") * DOC_DEV, DOC_DEV), DOC_DEV)
    out_ref[...] = done_ref[mine, :][:, docs:docs + queries]


def solve(x, recv, docs, queries, scale):
    return pl.pallas_call(
        functools.partial(solve_kernel, docs, queries, scale),
        out_shape=jax.ShapeDtypeStruct((DOC_DEV, queries), jnp.float32),
        in_specs=[VMEM] * 2,
        out_specs=VMEM,
        scratch_shapes=[pltpu.VMEM((docs, -(-(docs + queries) // LANES) * LANES), jnp.float32)],
        compiler_params=vmem_params(16),
        name="solve",
    )(x, recv)


def solve_large(total, docs, queries, scale):
    kernel = total[:, :docs]
    mean_diag = jnp.trace(kernel) / docs
    factor = jnp.linalg.cholesky(kernel + 0.1 * mean_diag * jnp.eye(docs, dtype=jnp.float32))
    solved = jax.scipy.linalg.cho_solve((factor, True), total[:, docs:docs + queries]) * (mean_diag * scale)
    return lax.dynamic_slice_in_dim(solved, lax.axis_index("dp") * DOC_DEV, DOC_DEV, 0)


def swap_cores(x):
    cores = lax.axis_size("tensor")
    return lax.ppermute(x, "tensor", [(i, cores - 1 - i) for i in range(cores)])


def trade(xs, group):
    dp = lax.axis_size("dp")
    got = []
    for x, ms in zip(xs, zip(*partners(group))):
        pairs = [(i * 2 + k, (i ^ m) * 2 + k) for i in range(dp) for k, m in enumerate(ms)]
        got.append(lax.ppermute(x, ("dp", "tensor"), pairs))
    return got


def trade_shared(x):
    dp = lax.axis_size("dp")
    return lax.ppermute(x, "dp", [(i, i ^ SHARED) for i in range(dp)])


def local(hidden, out_grad, proj_in, proj_out, doc_ids, queries):
    dp = lax.axis_size("dp")
    docs, num_queries = DOC_DEV * dp, queries.shape[0] * dp
    ranks = proj_in.shape[1]
    owners = owners_of(dp)
    pa = 1
    while pa * pa < owners:
        pa *= 2
    pb = owners // pa
    rows_a, rows_b = ranks // pa, ranks // pb

    part = project(hidden, out_grad, proj_in.T, proj_out.T)
    recv = swap_cores(part)

    ids = jnp.broadcast_to(doc_ids.astype(jnp.float32).reshape(2, LANES), (owners, 2, LANES))
    asked = queries.reshape(-1, pa, rows_a, pb, rows_b).transpose(1, 3, 0, 2, 4).reshape(owners, -1, LANES)
    extra = jnp.concatenate([asked, ids], axis=1)
    extra = jnp.pad(extra, ((0, 0), (0, -extra.shape[1] % 8), (0, 0)))

    *blocks, shared, own = pack(part, recv, extra, dp, pa, pb)
    blocks = trade(blocks, dp) + [trade_shared(shared), own]
    gaps = [*zip(*partners(dp)), (SHARED, SHARED), (0, 0)]
    wholes = [True] * (len(blocks) - 2) + [False, False]
    sizes = (rows_a, rows_b, docs, num_queries, dp)
    late = min(1, len(blocks) - 3)
    rest = [t for t in range(len(blocks)) if t != late]
    grads = ()
    for part in (rest, [late]):
        grads = (grads_of(*([x[t] for t in part] for x in (blocks, gaps, wholes)), grads, *sizes),)
    grads = grads[0]
    share = gram(grads, swap_cores(grads), docs)
    scale = float(ranks * ranks) ** -0.5
    if docs <= 64:
        others = sum(trade([share] * (owners // 2 - 1), owners))
        share = others + jnp.where(lax.axis_index("tensor") == 0, share, trade_shared(share))
        return solve(share, swap_cores(share), docs, num_queries, scale).T
    share = lax.psum(share, "dp") * (owners / dp)
    return solve_large(jnp.concatenate([share[:, :docs], share[:, docs:]], axis=0).T, docs, num_queries, scale).T


def solution(mesh):
    return jax.shard_map(
        local,
        mesh=mesh,
        in_specs=(
            P(("groups", "dp"), "tensor"),
            P(("groups", "dp"), "tensor"),
            P("tensor", None),
            P("tensor", None),
            P(("groups", "dp")),
            P(("groups", "dp"), None),
        ),
        out_specs=P("groups", "dp"),
        check_vma=False,
    )
```

```python
import functools

import jax
import jax.numpy as jnp
from jax import lax
from jax.experimental import pallas as pl
from jax.experimental.pallas import tpu as pltpu
from jax.sharding import PartitionSpec as P

TOK_DEV = 256
DOC_DEV = 8
LANES = 128
FLIGHT = 7
SHARED = 1
NT = (((1,), (1,)), ((), ()))
VMEM = pl.BlockSpec(memory_space=pltpu.VMEM)
HBM = pl.BlockSpec(memory_space=pltpu.HBM)


def vmem_params(mib):
    return pltpu.CompilerParams(vmem_limit_bytes=int(mib * (1 << 20)))


def pieces(x):
    rows, units = x.shape
    split = x.reshape(rows // 8, 8, units // (2 * LANES), 2, LANES).transpose(0, 2, 3, 1, 4)
    return split.reshape(rows // 8, units // (2 * LANES), 16, LANES)


def chunks_of(length, ramp, tail):
    left = length - sum(ramp) - sum(tail)
    sizes = [*ramp, *([6] * (left // 6)), *([left % 6] if left % 6 else []), *tail]
    return [(sum(sizes[:i]), size) for i, size in enumerate(sizes)]


def project_kernel(g_chunks, h_chunks, h_ref, g_ref, pin_ref, pout_ref, out_ref, h_buf, g_buf, pin_buf, pout_buf, sems):
    plan = [(pout_ref, pout_buf, g_ref, g_buf, at) for at in g_chunks] + [(pin_ref, pin_buf, h_ref, h_buf, at) for at in h_chunks]
    copies = []
    for i, (proj, proj_buf, data, data_buf, (start, size)) in enumerate(plan):
        at = pl.ds(start, size)
        copies.append((
            pltpu.make_async_copy(proj.at[:, at], proj_buf.at[:, at], sems.at[2 * i]),
            pltpu.make_async_copy(data.at[:, at], data_buf.at[:, at], sems.at[2 * i + 1]),
        ))

    def start(i):
        if i < len(copies):
            for copy in copies[i]:
                copy.start()

    for i in range(FLIGHT):
        start(i)

    def line_up(ref, first, size):
        blocks = [ref[:, j].reshape(ref.shape[0] * 16, LANES) for j in range(first, first + size)]
        return jnp.concatenate(blocks, axis=1)

    totals = [None, None]
    for i, (_, proj_buf, _, data_buf, (first, size)) in enumerate(plan):
        for copy in copies[i]:
            copy.wait()
        start(i + FLIGHT)
        which = 0 if i < len(g_chunks) else 1
        part = lax.dot_general(
            line_up(proj_buf, first, size), line_up(data_buf, first, size), NT, preferred_element_type=jnp.float32
        )
        totals[which] = part if totals[which] is None else totals[which] + part

    lane = lax.broadcasted_iota(jnp.int32, (8, LANES), 1)
    even = lane % 16 < 8
    later = lane // (LANES // 2)
    order = lane % (LANES // 2) // 8 * 16 + lane % 8 + 8 * later
    done = 0
    for total in totals:
        for g in range(0, total.shape[0], 16):
            lines = []
            for i in range(0, total.shape[1], LANES):
                upper, lower = total[g:g + 8, i:i + LANES], total[g + 8:g + 16, i:i + LANES]
                lines.append(jnp.where(even, upper, lower))
            for i in range(0, len(lines), 2):
                first = lines[i] + pltpu.roll(lines[i], LANES - 8, 1)
                second = lines[i + 1] + pltpu.roll(lines[i + 1], 8, 1)
                both = jnp.where(even, first, second)
                at = i // 2 * LANES
                out_ref[done:done + 8, at:at + LANES] = jnp.take_along_axis(both, order, axis=1)
            done += 8


def project(hidden, out_grad, pin_t, pout_t):
    tokens, units = hidden.shape
    width = out_grad.shape[1]
    ranks = pin_t.shape[0] + pout_t.shape[0]
    operands = [pieces(x) for x in (hidden, out_grad, pin_t, pout_t)]
    g_chunks = chunks_of(operands[1].shape[1], (1, 2, 3, 4), ())
    h_chunks = chunks_of(operands[0].shape[1], (), (4, 2, 2))
    return pl.pallas_call(
        functools.partial(project_kernel, g_chunks, h_chunks),
        out_shape=jax.ShapeDtypeStruct((ranks, tokens), jnp.float32),
        in_specs=[HBM] * 4,
        out_specs=VMEM,
        scratch_shapes=[pltpu.VMEM(x.shape, x.dtype) for x in operands]
        + [pltpu.SemaphoreType.DMA((2 * len(g_chunks + h_chunks),))],
        compiler_params=vmem_params(53.5),
        cost_estimate=pl.CostEstimate(
            flops=2 * tokens * 64 * (units + width),
            bytes_accessed=2 * (tokens + 64) * (units + width),
            transcendentals=0,
        ),
        name="project",
    )(*operands)


def owners_of(dp):
    return max(dp // 2, 1)


def partners(dp):
    order = [m for m in range(dp - 1, 0, -1) if m != SHARED]
    return order[0::2], order[1::2]


def partner(dp, t):
    first, second = partners(dp)
    return jnp.where(lax.axis_index("tensor") == 0, first[t], second[t])


def pack_kernel(dp, pb, rows_a, rows_b, span, part_ref, recv_ref, extra_ref, *refs):
    outs, total_ref = refs[:-1], refs[-1]
    total_ref[...] = part_ref[...] + recv_ref[...]
    ranks = total_ref.shape[0] // 2
    rows = rows_a + rows_b
    owners, ids = extra_ref.shape[0], 2 * span
    me = lax.axis_index("dp")
    lead = lax.axis_index("tensor") == 0

    def slices(owner):
        p, q = owner // pb, owner % pb
        g = total_ref[pl.ds(pl.multiple_of(p * rows_a, rows_a), rows_a), :]
        b = total_ref[pl.ds(pl.multiple_of(ranks + q * rows_b, rows_b), rows_b), :]
        return [(g[:, i:i + LANES], b[:, i:i + LANES]) for i in (0, LANES)]

    for t, out_ref in enumerate(outs[:-2]):
        owner = (me ^ partner(dp, t)) % owners
        for i, (g, b) in enumerate(slices(owner)):
            out_ref[i * rows:i * rows + rows_a, :] = g
            out_ref[i * rows + rows_a:(i + 1) * rows, :] = b
        out_ref[2 * rows:, :] = extra_ref[owner]
    for out_ref, to in zip(outs[-2:], (me ^ SHARED, me)):
        owner = to % owners
        (g, b), (later_g, later_b) = slices(owner)
        extra = extra_ref[owner]
        out_ref[0:rows_a, :] = jnp.where(lead, g, later_g)
        out_ref[rows_a:rows, :] = jnp.where(lead, b, later_b)
        out_ref[rows:rows + span, :] = jnp.where(lead, extra[0:span], extra[span:ids])
        rest = out_ref.shape[0] - rows - span
        out_ref[rows + span:, :] = jnp.broadcast_to(jnp.where(lead, extra[ids:ids + 1], extra[ids + 1:ids + 2]), (rest, LANES))


def pack(part, recv, extra, dp, pa, pb):
    ranks = part.shape[0] // 2
    rows_a, rows_b = ranks // pa, ranks // pb
    rows, span = rows_a + rows_b, rows_a * rows_b // LANES
    whole = jax.ShapeDtypeStruct((2 * rows + extra.shape[1], LANES), jnp.float32)
    half = jax.ShapeDtypeStruct((rows + 8 * (span // 8 + 1), LANES), jnp.float32)
    count = dp // 2 - 1
    return pl.pallas_call(
        functools.partial(pack_kernel, dp, pb, rows_a, rows_b, span),
        out_shape=(whole,) * count + (half, half),
        in_specs=[VMEM] * 3,
        out_specs=(VMEM,) * (count + 2),
        scratch_shapes=[pltpu.VMEM(part.shape, jnp.float32)],
        compiler_params=vmem_params(16),
        name="pack",
    )(part, recv, extra)


def grads_kernel(rows_a, rows_b, docs, dp, gaps, wholes, *refs):
    xs, before, (out_ref, outer_ref, member_ref) = refs[:len(gaps)], refs[len(gaps):-3], refs[-3:]
    rows, wide = rows_a + rows_b, rows_a * rows_b
    span = wide // LANES
    queries = out_ref.shape[0] - docs
    doc = lax.broadcasted_iota(jnp.int32, (docs, LANES), 0)
    place = lax.broadcasted_iota(jnp.int32, (queries, LANES), 0)
    me = lax.axis_index("dp")
    core = lax.axis_index("tensor")
    asked = [jnp.zeros((queries, LANES), jnp.float32)] * span
    start = 0
    for x_ref, gap, whole in zip(xs, gaps, wholes):
        parts = 2 if whole else 1
        base = parts * rows
        for i in range(parts):
            at = slice(start, start + LANES)
            start += LANES
            g, b = x_ref[i * rows:i * rows + rows_a, :], x_ref[i * rows + rows_a:(i + 1) * rows, :]
            ids = base + parts * span + i
            member_ref[:, at] = jnp.where(doc == x_ref[ids:ids + 1, :].astype(jnp.int32), 1.0, 0.0).astype(jnp.bfloat16)
            outer = (g[:, None, :] * b[None, :, :]).reshape(wide, LANES)
            high = outer.astype(jnp.bfloat16)
            outer_ref[0:wide, at] = high
            outer_ref[wide:, at] = (outer - high.astype(jnp.float32)).astype(jnp.bfloat16)
        source = 2 * (me ^ jnp.where(core == 0, gap[0], gap[1]))
        for i in range(parts):
            held = place == source + (i if whole else core)
            for j in range(span):
                row = base + i * span + j
                asked[j] = jnp.where(held, x_ref[row:row + 1, :], asked[j])
    sums = lax.dot_general(member_ref[...], outer_ref[...], NT, preferred_element_type=jnp.float32)
    sums = (sums[:, wide:] + sums[:, :wide]) * (TOK_DEV ** -0.5)
    asked = jnp.concatenate(asked, axis=1)
    if before:
        sums, asked = sums + before[0][0:docs, :], asked + before[0][docs:, :]
    out_ref[0:docs, :] = sums
    out_ref[docs:, :] = asked


def grads_of(xs, gaps, wholes, before, rows_a, rows_b, docs, queries, dp):
    tokens = LANES * (len(xs) + sum(wholes))
    wide = rows_a * rows_b
    operands = (*xs, *before)
    return pl.pallas_call(
        functools.partial(grads_kernel, rows_a, rows_b, docs, dp, gaps, wholes),
        out_shape=jax.ShapeDtypeStruct((docs + queries, wide), jnp.float32),
        in_specs=[VMEM] * len(operands),
        out_specs=VMEM,
        scratch_shapes=[
            pltpu.VMEM((2 * wide, tokens), jnp.bfloat16),
            pltpu.VMEM((docs, tokens), jnp.bfloat16),
        ],
        compiler_params=vmem_params(40),
        cost_estimate=pl.CostEstimate(
            flops=4 * docs * wide * tokens, bytes_accessed=4 * (rows_a + rows_b) * tokens, transcendentals=0
        ),
        name="grads",
    )(*operands)


def gram_kernel(docs, part_ref, recv_ref, out_ref):
    both = part_ref[...] + recv_ref[...]
    rows = both.shape[0]
    split = []
    for _ in range(3):
        split.append(both.astype(jnp.bfloat16))
        both = both - split[-1].astype(jnp.float32)
    every = lax.dot_general(
        jnp.concatenate(split, axis=0),
        jnp.concatenate([x[:docs] for x in split], axis=0),
        NT,
        preferred_element_type=jnp.float32,
    )
    share = None
    for i, j in ((2, 0), (1, 1), (0, 2), (1, 0), (0, 1), (0, 0)):
        term = every[i * rows:(i + 1) * rows, j * docs:(j + 1) * docs]
        share = term if share is None else share + term
    half = share.shape[0] // 2
    out_ref[...] = jnp.concatenate([share[:half], share[half:]], axis=1)


def gram(part, recv, docs):
    return pl.pallas_call(
        functools.partial(gram_kernel, docs),
        out_shape=jax.ShapeDtypeStruct((part.shape[0] // 2, 2 * docs), jnp.float32),
        in_specs=[VMEM] * 2,
        out_specs=VMEM,
        compiler_params=vmem_params(16),
        name="gram",
    )(part, recv)


def solve_kernel(docs, queries, scale, x_ref, recv_ref, out_ref, done_ref):
    total = x_ref[...] + recv_ref[...]
    stack = jnp.concatenate([total[:, :docs], total[:, docs:]], axis=0)
    cols = done_ref.shape[1]
    diagonal = [lax.broadcasted_iota(jnp.int32, (docs, docs), i) for i in range(2)]
    mean_diag = jnp.sum(jnp.where(diagonal[0] == diagonal[1], stack[:docs], 0.0)) * (1.0 / docs)
    stack = jnp.concatenate([stack, jnp.zeros((cols - stack.shape[0], docs), jnp.float32)], axis=0)
    total = stack.T
    row = lax.broadcasted_iota(jnp.int32, (docs, cols), 0)
    col = lax.broadcasted_iota(jnp.int32, (docs, cols), 1)
    work = total + jnp.where(row == col, 0.1 * mean_diag, 0.0)
    size = 8
    here = lax.broadcasted_iota(jnp.int32, (size, cols), 0)
    rows = [work[i:i + size] for i in range(0, docs, size)]
    for r in range(len(rows)):
        wide = [[jnp.broadcast_to(x[:, c:c + 1], (size, cols)) for c in range(r * size, (r + 1) * size)] for x in rows]
        pivot, line = wide[r], rows[r]
        scale_rows = jnp.ones((size, cols), jnp.float32)
        for j in range(size):
            inverse = 1.0 / pivot[j][j:j + 1]
            factor = jnp.where(here == j, 0.0, pivot[j]) * inverse
            pivot = [x if i <= j else x - factor * x[j:j + 1] for i, x in enumerate(pivot)]
            line = line - factor * line[j:j + 1]
            scale_rows = jnp.where(here == j, inverse, scale_rows)
        line = line * scale_rows
        for s in range(len(rows)):
            if s == r:
                rows[s] = line
            else:
                terms = [wide[s][j] * line[j:j + 1] for j in range(size)]
                rows[s] = rows[s] - (((terms[0] + terms[1]) + (terms[2] + terms[3]))
                                     + ((terms[4] + terms[5]) + (terms[6] + terms[7])))
    for r, x in enumerate(rows):
        done_ref[r * size:(r + 1) * size, :] = x * (mean_diag * scale)
    mine = pl.ds(pl.multiple_of(lax.axis_index("dp") * DOC_DEV, DOC_DEV), DOC_DEV)
    out_ref[...] = done_ref[mine, :][:, docs:docs + queries]


def solve(x, recv, docs, queries, scale):
    return pl.pallas_call(
        functools.partial(solve_kernel, docs, queries, scale),
        out_shape=jax.ShapeDtypeStruct((DOC_DEV, queries), jnp.float32),
        in_specs=[VMEM] * 2,
        out_specs=VMEM,
        scratch_shapes=[pltpu.VMEM((docs, -(-(docs + queries) // LANES) * LANES), jnp.float32)],
        compiler_params=vmem_params(16),
        name="solve",
    )(x, recv)


def solve_large(total, docs, queries, scale):
    kernel = total[:, :docs]
    mean_diag = jnp.trace(kernel) / docs
    factor = jnp.linalg.cholesky(kernel + 0.1 * mean_diag * jnp.eye(docs, dtype=jnp.float32))
    solved = jax.scipy.linalg.cho_solve((factor, True), total[:, docs:docs + queries]) * (mean_diag * scale)
    return lax.dynamic_slice_in_dim(solved, lax.axis_index("dp") * DOC_DEV, DOC_DEV, 0)


def swap_cores(x):
    cores = lax.axis_size("tensor")
    return lax.ppermute(x, "tensor", [(i, cores - 1 - i) for i in range(cores)])


def trade(xs, group):
    dp = lax.axis_size("dp")
    got = []
    for x, ms in zip(xs, zip(*partners(group))):
        pairs = [(i * 2 + k, (i ^ m) * 2 + k) for i in range(dp) for k, m in enumerate(ms)]
        got.append(lax.ppermute(x, ("dp", "tensor"), pairs))
    return got


def trade_shared(x):
    dp = lax.axis_size("dp")
    return lax.ppermute(x, "dp", [(i, i ^ SHARED) for i in range(dp)])


def local(hidden, out_grad, proj_in, proj_out, doc_ids, queries):
    dp = lax.axis_size("dp")
    docs, num_queries = DOC_DEV * dp, queries.shape[0] * dp
    ranks = proj_in.shape[1]
    owners = owners_of(dp)
    pa = 1
    while pa * pa < owners:
        pa *= 2
    pb = owners // pa
    rows_a, rows_b = ranks // pa, ranks // pb

    part = project(hidden, out_grad, proj_in.T, proj_out.T)
    recv = swap_cores(part)

    ids = jnp.broadcast_to(doc_ids.astype(jnp.float32).reshape(2, LANES), (owners, 2, LANES))
    asked = queries.reshape(-1, pa, rows_a, pb, rows_b).transpose(1, 3, 0, 2, 4).reshape(owners, -1, LANES)
    extra = jnp.concatenate([asked, ids], axis=1)
    extra = jnp.pad(extra, ((0, 0), (0, -extra.shape[1] % 8), (0, 0)))

    *blocks, shared, own = pack(part, recv, extra, dp, pa, pb)
    blocks = trade(blocks, dp) + [trade_shared(shared), own]
    gaps = [*zip(*partners(dp)), (SHARED, SHARED), (0, 0)]
    wholes = [True] * (len(blocks) - 2) + [False, False]
    sizes = (rows_a, rows_b, docs, num_queries, dp)
    late = min(1, len(blocks) - 3)
    rest = [t for t in range(len(blocks)) if t != late]
    grads = ()
    for part in (rest, [late]):
        grads = (grads_of(*([x[t] for t in part] for x in (blocks, gaps, wholes)), grads, *sizes),)
    grads = grads[0]
    share = gram(grads, swap_cores(grads), docs)
    scale = float(ranks * ranks) ** -0.5
    if docs <= 64:
        both = jnp.where(lax.axis_index("tensor") == 0, share, trade_shared(share))
        share = both + sum(trade([share] * (owners // 2 - 1), owners))
        return solve(share, swap_cores(share), docs, num_queries, scale).T
    share = lax.psum(share, "dp") * (owners / dp)
    return solve_large(jnp.concatenate([share[:, :docs], share[:, docs:]], axis=0).T, docs, num_queries, scale).T


def solution(mesh):
    return jax.shard_map(
        local,
        mesh=mesh,
        in_specs=(
            P(("groups", "dp"), "tensor"),
            P(("groups", "dp"), "tensor"),
            P("tensor", None),
            P("tensor", None),
            P(("groups", "dp")),
            P(("groups", "dp"), None),
        ),
        out_specs=P("groups", "dp"),
        check_vma=False,
    )
```

```python
import functools

import jax
import jax.numpy as jnp
from jax import lax
from jax.experimental import pallas as pl
from jax.experimental.pallas import tpu as pltpu
from jax.sharding import PartitionSpec as P

TOK_DEV = 256
DOC_DEV = 8
LANES = 128
FLIGHT = 7
SHARED = 1
NT = (((1,), (1,)), ((), ()))
VMEM = pl.BlockSpec(memory_space=pltpu.VMEM)
HBM = pl.BlockSpec(memory_space=pltpu.HBM)


def vmem_params(mib):
    return pltpu.CompilerParams(vmem_limit_bytes=int(mib * (1 << 20)))


def pieces(x):
    rows, units = x.shape
    split = x.reshape(rows // 8, 8, units // (2 * LANES), 2, LANES).transpose(0, 2, 3, 1, 4)
    return split.reshape(rows // 8, units // (2 * LANES), 16, LANES)


def chunks_of(length, ramp, tail):
    left = length - sum(ramp) - sum(tail)
    sizes = [*ramp, *([6] * (left // 6)), *([left % 6] if left % 6 else []), *tail]
    return [(sum(sizes[:i]), size) for i, size in enumerate(sizes)]


def project_kernel(g_chunks, h_chunks, h_ref, g_ref, pin_ref, pout_ref, out_ref, h_buf, g_buf, pin_buf, pout_buf, sems):
    plan = [(pout_ref, pout_buf, g_ref, g_buf, at) for at in g_chunks] + [(pin_ref, pin_buf, h_ref, h_buf, at) for at in h_chunks]
    copies = []
    for i, (proj, proj_buf, data, data_buf, (start, size)) in enumerate(plan):
        at = pl.ds(start, size)
        copies.append((
            pltpu.make_async_copy(proj.at[:, at], proj_buf.at[:, at], sems.at[2 * i]),
            pltpu.make_async_copy(data.at[:, at], data_buf.at[:, at], sems.at[2 * i + 1]),
        ))

    def start(i):
        if i < len(copies):
            for copy in copies[i]:
                copy.start()

    for i in range(FLIGHT):
        start(i)

    def line_up(ref, first, size):
        blocks = [ref[:, j].reshape(ref.shape[0] * 16, LANES) for j in range(first, first + size)]
        return jnp.concatenate(blocks, axis=1)

    totals = [None, None]
    for i, (_, proj_buf, _, data_buf, (first, size)) in enumerate(plan):
        for copy in copies[i]:
            copy.wait()
        start(i + FLIGHT)
        which = 0 if i < len(g_chunks) else 1
        part = lax.dot_general(
            line_up(proj_buf, first, size), line_up(data_buf, first, size), NT, preferred_element_type=jnp.float32
        )
        totals[which] = part if totals[which] is None else totals[which] + part

    lane = lax.broadcasted_iota(jnp.int32, (8, LANES), 1)
    even = lane % 16 < 8
    later = lane // (LANES // 2)
    order = lane % (LANES // 2) // 8 * 16 + lane % 8 + 8 * later
    done = 0
    for total in totals:
        for g in range(0, total.shape[0], 16):
            lines = []
            for i in range(0, total.shape[1], LANES):
                upper, lower = total[g:g + 8, i:i + LANES], total[g + 8:g + 16, i:i + LANES]
                lines.append(jnp.where(even, upper, lower))
            for i in range(0, len(lines), 2):
                first = lines[i] + pltpu.roll(lines[i], LANES - 8, 1)
                second = lines[i + 1] + pltpu.roll(lines[i + 1], 8, 1)
                both = jnp.where(even, first, second)
                at = i // 2 * LANES
                out_ref[done:done + 8, at:at + LANES] = jnp.take_along_axis(both, order, axis=1)
            done += 8


def project(hidden, out_grad, pin_t, pout_t):
    tokens, units = hidden.shape
    width = out_grad.shape[1]
    ranks = pin_t.shape[0] + pout_t.shape[0]
    operands = [pieces(x) for x in (hidden, out_grad, pin_t, pout_t)]
    g_chunks = chunks_of(operands[1].shape[1], (1, 2, 3, 4), ())
    h_chunks = chunks_of(operands[0].shape[1], (), (4, 2, 2))
    return pl.pallas_call(
        functools.partial(project_kernel, g_chunks, h_chunks),
        out_shape=jax.ShapeDtypeStruct((ranks, tokens), jnp.float32),
        in_specs=[HBM] * 4,
        out_specs=VMEM,
        scratch_shapes=[pltpu.VMEM(x.shape, x.dtype) for x in operands]
        + [pltpu.SemaphoreType.DMA((2 * len(g_chunks + h_chunks),))],
        compiler_params=vmem_params(53.5),
        cost_estimate=pl.CostEstimate(
            flops=2 * tokens * 64 * (units + width),
            bytes_accessed=2 * (tokens + 64) * (units + width),
            transcendentals=0,
        ),
        name="project",
    )(*operands)


def owners_of(dp):
    return max(dp // 2, 1)


def partners(dp):
    order = [m for far in (True, False) for m in range(1, dp) if m != SHARED and (2 * m >= dp) == far]
    pairs = [order[i:i + 2] if i % 4 == 0 else order[i:i + 2][::-1] for i in range(0, len(order), 2)]
    return [x for x, _ in pairs], [y for _, y in pairs]


def partner(dp, t):
    first, second = partners(dp)
    return jnp.where(lax.axis_index("tensor") == 0, first[t], second[t])


def pack_kernel(dp, pb, rows_a, rows_b, span, part_ref, recv_ref, extra_ref, *refs):
    outs, total_ref = refs[:-1], refs[-1]
    total_ref[...] = part_ref[...] + recv_ref[...]
    ranks = total_ref.shape[0] // 2
    rows = rows_a + rows_b
    owners, ids = extra_ref.shape[0], 2 * span
    me = lax.axis_index("dp")
    lead = lax.axis_index("tensor") == 0

    def slices(owner):
        p, q = owner // pb, owner % pb
        g = total_ref[pl.ds(pl.multiple_of(p * rows_a, rows_a), rows_a), :]
        b = total_ref[pl.ds(pl.multiple_of(ranks + q * rows_b, rows_b), rows_b), :]
        return [(g[:, i:i + LANES], b[:, i:i + LANES]) for i in (0, LANES)]

    for t, out_ref in enumerate(outs[:-2]):
        owner = (me ^ partner(dp, t)) % owners
        for i, (g, b) in enumerate(slices(owner)):
            out_ref[i * rows:i * rows + rows_a, :] = g
            out_ref[i * rows + rows_a:(i + 1) * rows, :] = b
        out_ref[2 * rows:, :] = extra_ref[owner]
    for out_ref, to in zip(outs[-2:], (me ^ SHARED, me)):
        owner = to % owners
        (g, b), (later_g, later_b) = slices(owner)
        extra = extra_ref[owner]
        out_ref[0:rows_a, :] = jnp.where(lead, g, later_g)
        out_ref[rows_a:rows, :] = jnp.where(lead, b, later_b)
        out_ref[rows:rows + span, :] = jnp.where(lead, extra[0:span], extra[span:ids])
        rest = out_ref.shape[0] - rows - span
        out_ref[rows + span:, :] = jnp.broadcast_to(jnp.where(lead, extra[ids:ids + 1], extra[ids + 1:ids + 2]), (rest, LANES))


def pack(part, recv, extra, dp, pa, pb):
    ranks = part.shape[0] // 2
    rows_a, rows_b = ranks // pa, ranks // pb
    rows, span = rows_a + rows_b, rows_a * rows_b // LANES
    whole = jax.ShapeDtypeStruct((2 * rows + extra.shape[1], LANES), jnp.float32)
    half = jax.ShapeDtypeStruct((rows + 8 * (span // 8 + 1), LANES), jnp.float32)
    count = dp // 2 - 1
    return pl.pallas_call(
        functools.partial(pack_kernel, dp, pb, rows_a, rows_b, span),
        out_shape=(whole,) * count + (half, half),
        in_specs=[VMEM] * 3,
        out_specs=(VMEM,) * (count + 2),
        scratch_shapes=[pltpu.VMEM(part.shape, jnp.float32)],
        compiler_params=vmem_params(16),
        name="pack",
    )(part, recv, extra)


def grads_kernel(rows_a, rows_b, docs, dp, gaps, wholes, *refs):
    xs, before, (out_ref, outer_ref, member_ref) = refs[:len(gaps)], refs[len(gaps):-3], refs[-3:]
    rows, wide = rows_a + rows_b, rows_a * rows_b
    span = wide // LANES
    queries = out_ref.shape[0] - docs
    doc = lax.broadcasted_iota(jnp.int32, (docs, LANES), 0)
    place = lax.broadcasted_iota(jnp.int32, (queries, LANES), 0)
    me = lax.axis_index("dp")
    core = lax.axis_index("tensor")
    asked = [jnp.zeros((queries, LANES), jnp.float32)] * span
    start = 0
    for x_ref, gap, whole in zip(xs, gaps, wholes):
        parts = 2 if whole else 1
        base = parts * rows
        for i in range(parts):
            at = slice(start, start + LANES)
            start += LANES
            g, b = x_ref[i * rows:i * rows + rows_a, :], x_ref[i * rows + rows_a:(i + 1) * rows, :]
            ids = base + parts * span + i
            member_ref[:, at] = jnp.where(doc == x_ref[ids:ids + 1, :].astype(jnp.int32), 1.0, 0.0).astype(jnp.bfloat16)
            outer = (g[:, None, :] * b[None, :, :]).reshape(wide, LANES)
            high = outer.astype(jnp.bfloat16)
            outer_ref[0:wide, at] = high
            outer_ref[wide:, at] = (outer - high.astype(jnp.float32)).astype(jnp.bfloat16)
        source = 2 * (me ^ jnp.where(core == 0, gap[0], gap[1]))
        for i in range(parts):
            held = place == source + (i if whole else core)
            for j in range(span):
                row = base + i * span + j
                asked[j] = jnp.where(held, x_ref[row:row + 1, :], asked[j])
    sums = lax.dot_general(member_ref[...], outer_ref[...], NT, preferred_element_type=jnp.float32)
    sums = (sums[:, wide:] + sums[:, :wide]) * (TOK_DEV ** -0.5)
    asked = jnp.concatenate(asked, axis=1)
    if before:
        sums, asked = sums + before[0][0:docs, :], asked + before[0][docs:, :]
    out_ref[0:docs, :] = sums
    out_ref[docs:, :] = asked


def grads_of(xs, gaps, wholes, before, rows_a, rows_b, docs, queries, dp):
    tokens = LANES * (len(xs) + sum(wholes))
    wide = rows_a * rows_b
    operands = (*xs, *before)
    return pl.pallas_call(
        functools.partial(grads_kernel, rows_a, rows_b, docs, dp, gaps, wholes),
        out_shape=jax.ShapeDtypeStruct((docs + queries, wide), jnp.float32),
        in_specs=[VMEM] * len(operands),
        out_specs=VMEM,
        scratch_shapes=[
            pltpu.VMEM((2 * wide, tokens), jnp.bfloat16),
            pltpu.VMEM((docs, tokens), jnp.bfloat16),
        ],
        compiler_params=vmem_params(40),
        cost_estimate=pl.CostEstimate(
            flops=4 * docs * wide * tokens, bytes_accessed=4 * (rows_a + rows_b) * tokens, transcendentals=0
        ),
        name="grads",
    )(*operands)


def gram_kernel(docs, part_ref, recv_ref, out_ref):
    both = part_ref[...] + recv_ref[...]
    rows = both.shape[0]
    split = []
    for _ in range(3):
        split.append(both.astype(jnp.bfloat16))
        both = both - split[-1].astype(jnp.float32)
    every = lax.dot_general(
        jnp.concatenate(split, axis=0),
        jnp.concatenate([x[:docs] for x in split], axis=0),
        NT,
        preferred_element_type=jnp.float32,
    )
    share = None
    for i, j in ((2, 0), (1, 1), (0, 2), (1, 0), (0, 1), (0, 0)):
        term = every[i * rows:(i + 1) * rows, j * docs:(j + 1) * docs]
        share = term if share is None else share + term
    half = share.shape[0] // 2
    out_ref[...] = jnp.concatenate([share[:half], share[half:]], axis=1)


def gram(part, recv, docs):
    return pl.pallas_call(
        functools.partial(gram_kernel, docs),
        out_shape=jax.ShapeDtypeStruct((part.shape[0] // 2, 2 * docs), jnp.float32),
        in_specs=[VMEM] * 2,
        out_specs=VMEM,
        compiler_params=vmem_params(16),
        name="gram",
    )(part, recv)


def solve_kernel(docs, queries, scale, x_ref, recv_ref, out_ref, done_ref):
    total = x_ref[...] + recv_ref[...]
    stack = jnp.concatenate([total[:, :docs], total[:, docs:]], axis=0)
    cols = done_ref.shape[1]
    diagonal = [lax.broadcasted_iota(jnp.int32, (docs, docs), i) for i in range(2)]
    mean_diag = jnp.sum(jnp.where(diagonal[0] == diagonal[1], stack[:docs], 0.0)) * (1.0 / docs)
    stack = jnp.concatenate([stack, jnp.zeros((cols - stack.shape[0], docs), jnp.float32)], axis=0)
    total = stack.T
    row = lax.broadcasted_iota(jnp.int32, (docs, cols), 0)
    col = lax.broadcasted_iota(jnp.int32, (docs, cols), 1)
    work = total + jnp.where(row == col, 0.1 * mean_diag, 0.0)
    size = 8
    here = lax.broadcasted_iota(jnp.int32, (size, cols), 0)
    rows = [work[i:i + size] for i in range(0, docs, size)]
    for r in range(len(rows)):
        wide = [[jnp.broadcast_to(x[:, c:c + 1], (size, cols)) for c in range(r * size, (r + 1) * size)] for x in rows]
        pivot, line = wide[r], rows[r]
        scale_rows = jnp.ones((size, cols), jnp.float32)
        for j in range(size):
            inverse = 1.0 / pivot[j][j:j + 1]
            factor = jnp.where(here == j, 0.0, pivot[j]) * inverse
            pivot = [x if i <= j else x - factor * x[j:j + 1] for i, x in enumerate(pivot)]
            line = line - factor * line[j:j + 1]
            scale_rows = jnp.where(here == j, inverse, scale_rows)
        line = line * scale_rows
        for s in range(len(rows)):
            if s == r:
                rows[s] = line
            else:
                terms = [wide[s][j] * line[j:j + 1] for j in range(size)]
                rows[s] = rows[s] - (((terms[0] + terms[1]) + (terms[2] + terms[3]))
                                     + ((terms[4] + terms[5]) + (terms[6] + terms[7])))
    for r, x in enumerate(rows):
        done_ref[r * size:(r + 1) * size, :] = x * (mean_diag * scale)
    mine = pl.ds(pl.multiple_of(lax.axis_index("dp") * DOC_DEV, DOC_DEV), DOC_DEV)
    out_ref[...] = done_ref[mine, :][:, docs:docs + queries]


def solve(x, recv, docs, queries, scale):
    return pl.pallas_call(
        functools.partial(solve_kernel, docs, queries, scale),
        out_shape=jax.ShapeDtypeStruct((DOC_DEV, queries), jnp.float32),
        in_specs=[VMEM] * 2,
        out_specs=VMEM,
        scratch_shapes=[pltpu.VMEM((docs, -(-(docs + queries) // LANES) * LANES), jnp.float32)],
        compiler_params=vmem_params(16),
        name="solve",
    )(x, recv)


def solve_large(total, docs, queries, scale):
    kernel = total[:, :docs]
    mean_diag = jnp.trace(kernel) / docs
    factor = jnp.linalg.cholesky(kernel + 0.1 * mean_diag * jnp.eye(docs, dtype=jnp.float32))
    solved = jax.scipy.linalg.cho_solve((factor, True), total[:, docs:docs + queries]) * (mean_diag * scale)
    return lax.dynamic_slice_in_dim(solved, lax.axis_index("dp") * DOC_DEV, DOC_DEV, 0)


def swap_cores(x):
    cores = lax.axis_size("tensor")
    return lax.ppermute(x, "tensor", [(i, cores - 1 - i) for i in range(cores)])


def trade(xs, group):
    dp = lax.axis_size("dp")
    got = []
    for x, ms in zip(xs, zip(*partners(group))):
        pairs = [(i * 2 + k, (i ^ m) * 2 + k) for i in range(dp) for k, m in enumerate(ms)]
        got.append(lax.ppermute(x, ("dp", "tensor"), pairs))
    return got


def trade_shared(x):
    dp = lax.axis_size("dp")
    return lax.ppermute(x, "dp", [(i, i ^ SHARED) for i in range(dp)])


def local(hidden, out_grad, proj_in, proj_out, doc_ids, queries):
    dp = lax.axis_size("dp")
    docs, num_queries = DOC_DEV * dp, queries.shape[0] * dp
    ranks = proj_in.shape[1]
    owners = owners_of(dp)
    pa = 1
    while pa * pa < owners:
        pa *= 2
    pb = owners // pa
    rows_a, rows_b = ranks // pa, ranks // pb

    part = project(hidden, out_grad, proj_in.T, proj_out.T)
    recv = swap_cores(part)

    ids = jnp.broadcast_to(doc_ids.astype(jnp.float32).reshape(2, LANES), (owners, 2, LANES))
    asked = queries.reshape(-1, pa, rows_a, pb, rows_b).transpose(1, 3, 0, 2, 4).reshape(owners, -1, LANES)
    extra = jnp.concatenate([asked, ids], axis=1)
    extra = jnp.pad(extra, ((0, 0), (0, -extra.shape[1] % 8), (0, 0)))

    *blocks, shared, own = pack(part, recv, extra, dp, pa, pb)
    blocks = trade(blocks, dp) + [trade_shared(shared), own]
    gaps = [*zip(*partners(dp)), (SHARED, SHARED), (0, 0)]
    wholes = [True] * (len(blocks) - 2) + [False, False]
    sizes = (rows_a, rows_b, docs, num_queries, dp)
    late = min(1, len(blocks) - 3)
    rest = [t for t in range(len(blocks)) if t != late]
    grads = ()
    for part in (rest, [late]):
        grads = (grads_of(*([x[t] for t in part] for x in (blocks, gaps, wholes)), grads, *sizes),)
    grads = grads[0]
    share = gram(grads, swap_cores(grads), docs)
    scale = float(ranks * ranks) ** -0.5
    if docs <= 64:
        others = sum(trade([share] * (owners // 2 - 1), owners))
        share = others + jnp.where(lax.axis_index("tensor") == 0, share, trade_shared(share))
        return solve(share, swap_cores(share), docs, num_queries, scale).T
    share = lax.psum(share, "dp") * (owners / dp)
    return solve_large(jnp.concatenate([share[:, :docs], share[:, docs:]], axis=0).T, docs, num_queries, scale).T


def solution(mesh):
    return jax.shard_map(
        local,
        mesh=mesh,
        in_specs=(
            P(("groups", "dp"), "tensor"),
            P(("groups", "dp"), "tensor"),
            P("tensor", None),
            P("tensor", None),
            P(("groups", "dp")),
            P(("groups", "dp"), None),
        ),
        out_specs=P("groups", "dp"),
        check_vma=False,
    )
```

```python
import functools

import jax
import jax.numpy as jnp
from jax import lax
from jax.experimental import pallas as pl
from jax.experimental.pallas import tpu as pltpu
from jax.sharding import PartitionSpec as P

TOK_DEV = 256
DOC_DEV = 8
LANES = 128
FLIGHT = 7
SHARED = 1
NT = (((1,), (1,)), ((), ()))
VMEM = pl.BlockSpec(memory_space=pltpu.VMEM)
HBM = pl.BlockSpec(memory_space=pltpu.HBM)


def vmem_params(mib):
    return pltpu.CompilerParams(vmem_limit_bytes=int(mib * (1 << 20)))


def pieces(x):
    rows, units = x.shape
    split = x.reshape(rows // 8, 8, units // (2 * LANES), 2, LANES).transpose(0, 2, 3, 1, 4)
    return split.reshape(rows // 8, units // (2 * LANES), 16, LANES)


def chunks_of(length, ramp, tail):
    left = length - sum(ramp) - sum(tail)
    sizes = [*ramp, *([6] * (left // 6)), *([left % 6] if left % 6 else []), *tail]
    return [(sum(sizes[:i]), size) for i, size in enumerate(sizes)]


def project_kernel(g_chunks, h_chunks, h_ref, g_ref, pin_ref, pout_ref, out_ref, h_buf, g_buf, pin_buf, pout_buf, sems):
    plan = [(pout_ref, pout_buf, g_ref, g_buf, at) for at in g_chunks] + [(pin_ref, pin_buf, h_ref, h_buf, at) for at in h_chunks]
    copies = []
    for i, (proj, proj_buf, data, data_buf, (start, size)) in enumerate(plan):
        at = pl.ds(start, size)
        copies.append((
            pltpu.make_async_copy(proj.at[:, at], proj_buf.at[:, at], sems.at[2 * i]),
            pltpu.make_async_copy(data.at[:, at], data_buf.at[:, at], sems.at[2 * i + 1]),
        ))

    def start(i):
        if i < len(copies):
            for copy in copies[i]:
                copy.start()

    for i in range(FLIGHT):
        start(i)

    def line_up(ref, first, size):
        blocks = [ref[:, j].reshape(ref.shape[0] * 16, LANES) for j in range(first, first + size)]
        return jnp.concatenate(blocks, axis=1)

    totals, streamed = [None, None], None
    for i, (_, proj_buf, _, data_buf, (first, size)) in enumerate(plan):
        for copy in copies[i]:
            copy.wait()
        start(i + FLIGHT)
        which = 0 if i < len(g_chunks) else 1
        if which == 1 and (i - len(g_chunks)) % 5 == 2:
            part = lax.dot_general(
                line_up(data_buf, first, size), line_up(proj_buf, first, size), NT, preferred_element_type=jnp.float32
            )
            streamed = part if streamed is None else streamed + part
            continue
        part = lax.dot_general(
            line_up(proj_buf, first, size), line_up(data_buf, first, size), NT, preferred_element_type=jnp.float32
        )
        totals[which] = part if totals[which] is None else totals[which] + part

    lane = lax.broadcasted_iota(jnp.int32, (8, LANES), 1)
    even = lane % 16 < 8
    later = lane // (LANES // 2)
    order = lane % (LANES // 2) // 8 * 16 + lane % 8 + 8 * later
    done = 0
    for total in totals:
        for g in range(0, total.shape[0], 16):
            lines = []
            for i in range(0, total.shape[1], LANES):
                upper, lower = total[g:g + 8, i:i + LANES], total[g + 8:g + 16, i:i + LANES]
                lines.append(jnp.where(even, upper, lower))
            for i in range(0, len(lines), 2):
                first = lines[i] + pltpu.roll(lines[i], LANES - 8, 1)
                second = lines[i + 1] + pltpu.roll(lines[i + 1], 8, 1)
                both = jnp.where(even, first, second)
                at = i // 2 * LANES
                out_ref[done:done + 8, at:at + LANES] = jnp.take_along_axis(both, order, axis=1)
            done += 8
    if streamed is not None:
        side = lax.broadcasted_iota(jnp.int32, (8, streamed.shape[1]), 1) % 16 < 8
        lines = [jnp.where(side, streamed[j:j + 8], streamed[j + 8:j + 16]) for j in range(0, streamed.shape[0], 16)]
        lines = jnp.concatenate(lines, axis=0).T
        begin = out_ref.shape[0] - lines.shape[0] // 2
        for g in range(0, lines.shape[0], 16):
            at = slice(begin + g // 2, begin + g // 2 + 8)
            out_ref[at, :] = out_ref[at, :] + (lines[g:g + 8] + lines[g + 8:g + 16])


def project(hidden, out_grad, pin_t, pout_t):
    tokens, units = hidden.shape
    width = out_grad.shape[1]
    ranks = pin_t.shape[0] + pout_t.shape[0]
    operands = [pieces(x) for x in (hidden, out_grad, pin_t, pout_t)]
    g_chunks = chunks_of(operands[1].shape[1], (1, 2, 3, 4), ())
    h_chunks = chunks_of(operands[0].shape[1], (), (4, 2, 2))
    return pl.pallas_call(
        functools.partial(project_kernel, g_chunks, h_chunks),
        out_shape=jax.ShapeDtypeStruct((ranks, tokens), jnp.float32),
        in_specs=[HBM] * 4,
        out_specs=VMEM,
        scratch_shapes=[pltpu.VMEM(x.shape, x.dtype) for x in operands]
        + [pltpu.SemaphoreType.DMA((2 * len(g_chunks + h_chunks),))],
        compiler_params=vmem_params(53.5),
        cost_estimate=pl.CostEstimate(
            flops=2 * tokens * 64 * (units + width),
            bytes_accessed=2 * (tokens + 64) * (units + width),
            transcendentals=0,
        ),
        name="project",
    )(*operands)


def owners_of(dp):
    return max(dp // 2, 1)


def partners(dp):
    order = [m for far in (True, False) for m in range(1, dp) if m != SHARED and (2 * m >= dp) == far]
    return order[0::2], order[1::2]


def partner(dp, t):
    first, second = partners(dp)
    return jnp.where(lax.axis_index("tensor") == 0, first[t], second[t])


def pack_kernel(dp, pb, rows_a, rows_b, span, part_ref, recv_ref, extra_ref, *refs):
    outs, total_ref = refs[:-1], refs[-1]
    total_ref[...] = part_ref[...] + recv_ref[...]
    ranks = total_ref.shape[0] // 2
    rows = rows_a + rows_b
    owners, ids = extra_ref.shape[0], 2 * span
    me = lax.axis_index("dp")
    lead = lax.axis_index("tensor") == 0

    def slices(owner):
        p, q = owner // pb, owner % pb
        g = total_ref[pl.ds(pl.multiple_of(p * rows_a, rows_a), rows_a), :]
        b = total_ref[pl.ds(pl.multiple_of(ranks + q * rows_b, rows_b), rows_b), :]
        return [(g[:, i:i + LANES], b[:, i:i + LANES]) for i in (0, LANES)]

    for t, out_ref in enumerate(outs[:-2]):
        owner = (me ^ partner(dp, t)) % owners
        for i, (g, b) in enumerate(slices(owner)):
            out_ref[i * rows:i * rows + rows_a, :] = g
            out_ref[i * rows + rows_a:(i + 1) * rows, :] = b
        out_ref[2 * rows:, :] = extra_ref[owner]
    for out_ref, to in zip(outs[-2:], (me ^ SHARED, me)):
        owner = to % owners
        (g, b), (later_g, later_b) = slices(owner)
        extra = extra_ref[owner]
        out_ref[0:rows_a, :] = jnp.where(lead, g, later_g)
        out_ref[rows_a:rows, :] = jnp.where(lead, b, later_b)
        out_ref[rows:rows + span, :] = jnp.where(lead, extra[0:span], extra[span:ids])
        rest = out_ref.shape[0] - rows - span
        out_ref[rows + span:, :] = jnp.broadcast_to(jnp.where(lead, extra[ids:ids + 1], extra[ids + 1:ids + 2]), (rest, LANES))


def pack(part, recv, extra, dp, pa, pb):
    ranks = part.shape[0] // 2
    rows_a, rows_b = ranks // pa, ranks // pb
    rows, span = rows_a + rows_b, rows_a * rows_b // LANES
    whole = jax.ShapeDtypeStruct((2 * rows + extra.shape[1], LANES), jnp.float32)
    half = jax.ShapeDtypeStruct((rows + 8 * (span // 8 + 1), LANES), jnp.float32)
    count = dp // 2 - 1
    return pl.pallas_call(
        functools.partial(pack_kernel, dp, pb, rows_a, rows_b, span),
        out_shape=(whole,) * count + (half, half),
        in_specs=[VMEM] * 3,
        out_specs=(VMEM,) * (count + 2),
        scratch_shapes=[pltpu.VMEM(part.shape, jnp.float32)],
        compiler_params=vmem_params(16),
        name="pack",
    )(part, recv, extra)


def grads_kernel(rows_a, rows_b, docs, dp, gaps, wholes, *refs):
    xs, before, (out_ref, outer_ref, member_ref) = refs[:len(gaps)], refs[len(gaps):-3], refs[-3:]
    rows, wide = rows_a + rows_b, rows_a * rows_b
    span = wide // LANES
    queries = out_ref.shape[0] - docs
    doc = lax.broadcasted_iota(jnp.int32, (docs, LANES), 0)
    place = lax.broadcasted_iota(jnp.int32, (queries, LANES), 0)
    me = lax.axis_index("dp")
    core = lax.axis_index("tensor")
    asked = [jnp.zeros((queries, LANES), jnp.float32)] * span
    start = 0
    for x_ref, gap, whole in zip(xs, gaps, wholes):
        parts = 2 if whole else 1
        base = parts * rows
        for i in range(parts):
            at = slice(start, start + LANES)
            start += LANES
            g, b = x_ref[i * rows:i * rows + rows_a, :], x_ref[i * rows + rows_a:(i + 1) * rows, :]
            ids = base + parts * span + i
            member_ref[:, at] = jnp.where(doc == x_ref[ids:ids + 1, :].astype(jnp.int32), 1.0, 0.0).astype(jnp.bfloat16)
            outer = (g[:, None, :] * b[None, :, :]).reshape(wide, LANES)
            high = outer.astype(jnp.bfloat16)
            outer_ref[0:wide, at] = high
            outer_ref[wide:, at] = (outer - high.astype(jnp.float32)).astype(jnp.bfloat16)
        source = 2 * (me ^ jnp.where(core == 0, gap[0], gap[1]))
        for i in range(parts):
            held = place == source + (i if whole else core)
            for j in range(span):
                row = base + i * span + j
                asked[j] = jnp.where(held, x_ref[row:row + 1, :], asked[j])
    sums = lax.dot_general(member_ref[...], outer_ref[...], NT, preferred_element_type=jnp.float32)
    sums = (sums[:, wide:] + sums[:, :wide]) * (TOK_DEV ** -0.5)
    asked = jnp.concatenate(asked, axis=1)
    if before:
        sums, asked = sums + before[0][0:docs, :], asked + before[0][docs:, :]
    out_ref[0:docs, :] = sums
    out_ref[docs:, :] = asked


def grads_of(xs, gaps, wholes, before, rows_a, rows_b, docs, queries, dp):
    tokens = LANES * (len(xs) + sum(wholes))
    wide = rows_a * rows_b
    operands = (*xs, *before)
    return pl.pallas_call(
        functools.partial(grads_kernel, rows_a, rows_b, docs, dp, gaps, wholes),
        out_shape=jax.ShapeDtypeStruct((docs + queries, wide), jnp.float32),
        in_specs=[VMEM] * len(operands),
        out_specs=VMEM,
        scratch_shapes=[
            pltpu.VMEM((2 * wide, tokens), jnp.bfloat16),
            pltpu.VMEM((docs, tokens), jnp.bfloat16),
        ],
        compiler_params=vmem_params(40),
        cost_estimate=pl.CostEstimate(
            flops=4 * docs * wide * tokens, bytes_accessed=4 * (rows_a + rows_b) * tokens, transcendentals=0
        ),
        name="grads",
    )(*operands)


def gram_kernel(docs, part_ref, recv_ref, out_ref):
    both = part_ref[...] + recv_ref[...]
    rows = both.shape[0]
    split = []
    for _ in range(3):
        split.append(both.astype(jnp.bfloat16))
        both = both - split[-1].astype(jnp.float32)
    every = lax.dot_general(
        jnp.concatenate(split, axis=0),
        jnp.concatenate([x[:docs] for x in split], axis=0),
        NT,
        preferred_element_type=jnp.float32,
    )
    share = None
    for i, j in ((2, 0), (1, 1), (0, 2), (1, 0), (0, 1), (0, 0)):
        term = every[i * rows:(i + 1) * rows, j * docs:(j + 1) * docs]
        share = term if share is None else share + term
    half = share.shape[0] // 2
    out_ref[...] = jnp.concatenate([share[:half], share[half:]], axis=1)


def gram(part, recv, docs):
    return pl.pallas_call(
        functools.partial(gram_kernel, docs),
        out_shape=jax.ShapeDtypeStruct((part.shape[0] // 2, 2 * docs), jnp.float32),
        in_specs=[VMEM] * 2,
        out_specs=VMEM,
        compiler_params=vmem_params(16),
        name="gram",
    )(part, recv)


def solve_kernel(docs, queries, scale, x_ref, recv_ref, out_ref, done_ref):
    total = x_ref[...] + recv_ref[...]
    stack = jnp.concatenate([total[:, :docs], total[:, docs:]], axis=0)
    cols = done_ref.shape[1]
    diagonal = [lax.broadcasted_iota(jnp.int32, (docs, docs), i) for i in range(2)]
    mean_diag = jnp.sum(jnp.where(diagonal[0] == diagonal[1], stack[:docs], 0.0)) * (1.0 / docs)
    stack = jnp.concatenate([stack, jnp.zeros((cols - stack.shape[0], docs), jnp.float32)], axis=0)
    total = stack.T
    row = lax.broadcasted_iota(jnp.int32, (docs, cols), 0)
    col = lax.broadcasted_iota(jnp.int32, (docs, cols), 1)
    work = total + jnp.where(row == col, 0.1 * mean_diag, 0.0)
    size = 8
    here = lax.broadcasted_iota(jnp.int32, (size, cols), 0)
    rows = [work[i:i + size] for i in range(0, docs, size)]
    for r in range(len(rows)):
        wide = [[jnp.broadcast_to(x[:, c:c + 1], (size, cols)) for c in range(r * size, (r + 1) * size)] for x in rows]
        pivot, line = wide[r], rows[r]
        scale_rows = jnp.ones((size, cols), jnp.float32)
        for j in range(size):
            inverse = 1.0 / pivot[j][j:j + 1]
            factor = jnp.where(here == j, 0.0, pivot[j]) * inverse
            pivot = [x if i <= j else x - factor * x[j:j + 1] for i, x in enumerate(pivot)]
            line = line - factor * line[j:j + 1]
            scale_rows = jnp.where(here == j, inverse, scale_rows)
        line = line * scale_rows
        for s in range(len(rows)):
            if s == r:
                rows[s] = line
            else:
                terms = [wide[s][j] * line[j:j + 1] for j in range(size)]
                rows[s] = rows[s] - (((terms[0] + terms[1]) + (terms[2] + terms[3]))
                                     + ((terms[4] + terms[5]) + (terms[6] + terms[7])))
    for r, x in enumerate(rows):
        done_ref[r * size:(r + 1) * size, :] = x * (mean_diag * scale)
    mine = pl.ds(pl.multiple_of(lax.axis_index("dp") * DOC_DEV, DOC_DEV), DOC_DEV)
    out_ref[...] = done_ref[mine, :][:, docs:docs + queries]


def solve(x, recv, docs, queries, scale):
    return pl.pallas_call(
        functools.partial(solve_kernel, docs, queries, scale),
        out_shape=jax.ShapeDtypeStruct((DOC_DEV, queries), jnp.float32),
        in_specs=[VMEM] * 2,
        out_specs=VMEM,
        scratch_shapes=[pltpu.VMEM((docs, -(-(docs + queries) // LANES) * LANES), jnp.float32)],
        compiler_params=vmem_params(16),
        name="solve",
    )(x, recv)


def solve_large(total, docs, queries, scale):
    kernel = total[:, :docs]
    mean_diag = jnp.trace(kernel) / docs
    factor = jnp.linalg.cholesky(kernel + 0.1 * mean_diag * jnp.eye(docs, dtype=jnp.float32))
    solved = jax.scipy.linalg.cho_solve((factor, True), total[:, docs:docs + queries]) * (mean_diag * scale)
    return lax.dynamic_slice_in_dim(solved, lax.axis_index("dp") * DOC_DEV, DOC_DEV, 0)


def swap_cores(x):
    cores = lax.axis_size("tensor")
    return lax.ppermute(x, "tensor", [(i, cores - 1 - i) for i in range(cores)])


def trade(xs, group):
    dp = lax.axis_size("dp")
    got = []
    for x, ms in zip(xs, zip(*partners(group))):
        pairs = [(i * 2 + k, (i ^ m) * 2 + k) for i in range(dp) for k, m in enumerate(ms)]
        got.append(lax.ppermute(x, ("dp", "tensor"), pairs))
    return got


def trade_shared(x):
    dp = lax.axis_size("dp")
    return lax.ppermute(x, "dp", [(i, i ^ SHARED) for i in range(dp)])


def local(hidden, out_grad, proj_in, proj_out, doc_ids, queries):
    dp = lax.axis_size("dp")
    docs, num_queries = DOC_DEV * dp, queries.shape[0] * dp
    ranks = proj_in.shape[1]
    owners = owners_of(dp)
    pa = 1
    while pa * pa < owners:
        pa *= 2
    pb = owners // pa
    rows_a, rows_b = ranks // pa, ranks // pb

    part = project(hidden, out_grad, proj_in.T, proj_out.T)
    recv = swap_cores(part)

    ids = jnp.broadcast_to(doc_ids.astype(jnp.float32).reshape(2, LANES), (owners, 2, LANES))
    asked = queries.reshape(-1, pa, rows_a, pb, rows_b).transpose(1, 3, 0, 2, 4).reshape(owners, -1, LANES)
    extra = jnp.concatenate([asked, ids], axis=1)
    extra = jnp.pad(extra, ((0, 0), (0, -extra.shape[1] % 8), (0, 0)))

    *blocks, shared, own = pack(part, recv, extra, dp, pa, pb)
    blocks = trade(blocks, dp) + [trade_shared(shared), own]
    gaps = [*zip(*partners(dp)), (SHARED, SHARED), (0, 0)]
    wholes = [True] * (len(blocks) - 2) + [False, False]
    sizes = (rows_a, rows_b, docs, num_queries, dp)
    late = min(1, len(blocks) - 3)
    rest = [t for t in range(len(blocks)) if t != late]
    grads = ()
    for part in (rest, [late]):
        grads = (grads_of(*([x[t] for t in part] for x in (blocks, gaps, wholes)), grads, *sizes),)
    grads = grads[0]
    share = gram(grads, swap_cores(grads), docs)
    scale = float(ranks * ranks) ** -0.5
    if docs <= 64:
        others = sum(trade([share] * (owners // 2 - 1), owners))
        share = others + jnp.where(lax.axis_index("tensor") == 0, share, trade_shared(share))
        return solve(share, swap_cores(share), docs, num_queries, scale).T
    share = lax.psum(share, "dp") * (owners / dp)
    return solve_large(jnp.concatenate([share[:, :docs], share[:, docs:]], axis=0).T, docs, num_queries, scale).T


def solution(mesh):
    return jax.shard_map(
        local,
        mesh=mesh,
        in_specs=(
            P(("groups", "dp"), "tensor"),
            P(("groups", "dp"), "tensor"),
            P("tensor", None),
            P("tensor", None),
            P(("groups", "dp")),
            P(("groups", "dp"), None),
        ),
        out_specs=P("groups", "dp"),
        check_vma=False,
    )
```

```python
import functools

import jax
import jax.numpy as jnp
from jax import lax
from jax.experimental import pallas as pl
from jax.experimental.pallas import tpu as pltpu
from jax.sharding import PartitionSpec as P

TOK_DEV = 256
DOC_DEV = 8
LANES = 128
FLIGHT = 7
SHARED = 2
NT = (((1,), (1,)), ((), ()))
VMEM = pl.BlockSpec(memory_space=pltpu.VMEM)
HBM = pl.BlockSpec(memory_space=pltpu.HBM)


def vmem_params(mib):
    return pltpu.CompilerParams(vmem_limit_bytes=int(mib * (1 << 20)))


def pieces(x):
    rows, units = x.shape
    split = x.reshape(rows // 8, 8, units // (2 * LANES), 2, LANES).transpose(0, 2, 3, 1, 4)
    return split.reshape(rows // 8, units // (2 * LANES), 16, LANES)


def chunks_of(length, ramp, tail):
    left = length - sum(ramp) - sum(tail)
    sizes = [*ramp, *([6] * (left // 6)), *([left % 6] if left % 6 else []), *tail]
    return [(sum(sizes[:i]), size) for i, size in enumerate(sizes)]


def project_kernel(g_chunks, h_chunks, h_ref, g_ref, pin_ref, pout_ref, out_ref, h_buf, g_buf, pin_buf, pout_buf, sems):
    plan = [(pout_ref, pout_buf, g_ref, g_buf, at) for at in g_chunks] + [(pin_ref, pin_buf, h_ref, h_buf, at) for at in h_chunks]
    copies = []
    for i, (proj, proj_buf, data, data_buf, (start, size)) in enumerate(plan):
        at = pl.ds(start, size)
        copies.append((
            pltpu.make_async_copy(proj.at[:, at], proj_buf.at[:, at], sems.at[2 * i]),
            pltpu.make_async_copy(data.at[:, at], data_buf.at[:, at], sems.at[2 * i + 1]),
        ))

    def start(i):
        if i < len(copies):
            for copy in copies[i]:
                copy.start()

    for i in range(FLIGHT):
        start(i)

    def line_up(ref, first, size):
        blocks = [ref[:, j].reshape(ref.shape[0] * 16, LANES) for j in range(first, first + size)]
        return jnp.concatenate(blocks, axis=1)

    totals = [None, None]
    for i, (_, proj_buf, _, data_buf, (first, size)) in enumerate(plan):
        for copy in copies[i]:
            copy.wait()
        start(i + FLIGHT)
        which = 0 if i < len(g_chunks) else 1
        part = lax.dot_general(
            line_up(proj_buf, first, size), line_up(data_buf, first, size), NT, preferred_element_type=jnp.float32
        )
        totals[which] = part if totals[which] is None else totals[which] + part

    lane = lax.broadcasted_iota(jnp.int32, (8, LANES), 1)
    even = lane % 16 < 8
    later = lane // (LANES // 2)
    order = lane % (LANES // 2) // 8 * 16 + lane % 8 + 8 * later
    done = 0
    for total in totals:
        for g in range(0, total.shape[0], 16):
            lines = []
            for i in range(0, total.shape[1], LANES):
                upper, lower = total[g:g + 8, i:i + LANES], total[g + 8:g + 16, i:i + LANES]
                lines.append(jnp.where(even, upper, lower))
            for i in range(0, len(lines), 2):
                first = lines[i] + pltpu.roll(lines[i], LANES - 8, 1)
                second = lines[i + 1] + pltpu.roll(lines[i + 1], 8, 1)
                both = jnp.where(even, first, second)
                at = i // 2 * LANES
                out_ref[done:done + 8, at:at + LANES] = jnp.take_along_axis(both, order, axis=1)
            done += 8


def project(hidden, out_grad, pin_t, pout_t):
    tokens, units = hidden.shape
    width = out_grad.shape[1]
    ranks = pin_t.shape[0] + pout_t.shape[0]
    operands = [pieces(x) for x in (hidden, out_grad, pin_t, pout_t)]
    g_chunks = chunks_of(operands[1].shape[1], (1, 2, 3, 4), ())
    h_chunks = chunks_of(operands[0].shape[1], (), (4, 2, 2))
    return pl.pallas_call(
        functools.partial(project_kernel, g_chunks, h_chunks),
        out_shape=jax.ShapeDtypeStruct((ranks, tokens), jnp.float32),
        in_specs=[HBM] * 4,
        out_specs=VMEM,
        scratch_shapes=[pltpu.VMEM(x.shape, x.dtype) for x in operands]
        + [pltpu.SemaphoreType.DMA((2 * len(g_chunks + h_chunks),))],
        compiler_params=vmem_params(53.5),
        cost_estimate=pl.CostEstimate(
            flops=2 * tokens * 64 * (units + width),
            bytes_accessed=2 * (tokens + 64) * (units + width),
            transcendentals=0,
        ),
        name="project",
    )(*operands)


def owners_of(dp):
    return max(dp // 2, 1)


def partners(dp):
    order = [m for far in (True, False) for m in range(1, dp) if m != SHARED and (2 * m >= dp) == far]
    return order[0::2], order[1::2]


def partner(dp, t):
    first, second = partners(dp)
    return jnp.where(lax.axis_index("tensor") == 0, first[t], second[t])


def pack_kernel(dp, pb, rows_a, rows_b, span, part_ref, recv_ref, extra_ref, *refs):
    outs, total_ref = refs[:-1], refs[-1]
    total_ref[...] = part_ref[...] + recv_ref[...]
    ranks = total_ref.shape[0] // 2
    rows = rows_a + rows_b
    owners, ids = extra_ref.shape[0], 2 * span
    me = lax.axis_index("dp")
    lead = lax.axis_index("tensor") == 0

    def slices(owner):
        p, q = owner // pb, owner % pb
        g = total_ref[pl.ds(pl.multiple_of(p * rows_a, rows_a), rows_a), :]
        b = total_ref[pl.ds(pl.multiple_of(ranks + q * rows_b, rows_b), rows_b), :]
        return [(g[:, i:i + LANES], b[:, i:i + LANES]) for i in (0, LANES)]

    for t, out_ref in enumerate(outs[:-2]):
        owner = (me ^ partner(dp, t)) % owners
        for i, (g, b) in enumerate(slices(owner)):
            out_ref[i * rows:i * rows + rows_a, :] = g
            out_ref[i * rows + rows_a:(i + 1) * rows, :] = b
        out_ref[2 * rows:, :] = extra_ref[owner]
    for out_ref, to in zip(outs[-2:], (me ^ SHARED, me)):
        owner = to % owners
        (g, b), (later_g, later_b) = slices(owner)
        extra = extra_ref[owner]
        out_ref[0:rows_a, :] = jnp.where(lead, g, later_g)
        out_ref[rows_a:rows, :] = jnp.where(lead, b, later_b)
        out_ref[rows:rows + span, :] = jnp.where(lead, extra[0:span], extra[span:ids])
        rest = out_ref.shape[0] - rows - span
        out_ref[rows + span:, :] = jnp.broadcast_to(jnp.where(lead, extra[ids:ids + 1], extra[ids + 1:ids + 2]), (rest, LANES))


def pack(part, recv, extra, dp, pa, pb):
    ranks = part.shape[0] // 2
    rows_a, rows_b = ranks // pa, ranks // pb
    rows, span = rows_a + rows_b, rows_a * rows_b // LANES
    whole = jax.ShapeDtypeStruct((2 * rows + extra.shape[1], LANES), jnp.float32)
    half = jax.ShapeDtypeStruct((rows + 8 * (span // 8 + 1), LANES), jnp.float32)
    count = dp // 2 - 1
    return pl.pallas_call(
        functools.partial(pack_kernel, dp, pb, rows_a, rows_b, span),
        out_shape=(whole,) * count + (half, half),
        in_specs=[VMEM] * 3,
        out_specs=(VMEM,) * (count + 2),
        scratch_shapes=[pltpu.VMEM(part.shape, jnp.float32)],
        compiler_params=vmem_params(16),
        name="pack",
    )(part, recv, extra)


def grads_kernel(rows_a, rows_b, docs, dp, gaps, wholes, *refs):
    xs, before, (out_ref, outer_ref, member_ref) = refs[:len(gaps)], refs[len(gaps):-3], refs[-3:]
    rows, wide = rows_a + rows_b, rows_a * rows_b
    span = wide // LANES
    queries = out_ref.shape[0] - docs
    doc = lax.broadcasted_iota(jnp.int32, (docs, LANES), 0)
    place = lax.broadcasted_iota(jnp.int32, (queries, LANES), 0)
    me = lax.axis_index("dp")
    core = lax.axis_index("tensor")
    asked = [jnp.zeros((queries, LANES), jnp.float32)] * span
    start = 0
    for x_ref, gap, whole in zip(xs, gaps, wholes):
        parts = 2 if whole else 1
        base = parts * rows
        for i in range(parts):
            at = slice(start, start + LANES)
            start += LANES
            g, b = x_ref[i * rows:i * rows + rows_a, :], x_ref[i * rows + rows_a:(i + 1) * rows, :]
            ids = base + parts * span + i
            member_ref[:, at] = jnp.where(doc == x_ref[ids:ids + 1, :].astype(jnp.int32), 1.0, 0.0).astype(jnp.bfloat16)
            outer = (g[:, None, :] * b[None, :, :]).reshape(wide, LANES)
            high = outer.astype(jnp.bfloat16)
            outer_ref[0:wide, at] = high
            outer_ref[wide:, at] = (outer - high.astype(jnp.float32)).astype(jnp.bfloat16)
        source = 2 * (me ^ jnp.where(core == 0, gap[0], gap[1]))
        for i in range(parts):
            held = place == source + (i if whole else core)
            for j in range(span):
                row = base + i * span + j
                asked[j] = jnp.where(held, x_ref[row:row + 1, :], asked[j])
    sums = lax.dot_general(member_ref[...], outer_ref[...], NT, preferred_element_type=jnp.float32)
    sums = (sums[:, wide:] + sums[:, :wide]) * (TOK_DEV ** -0.5)
    asked = jnp.concatenate(asked, axis=1)
    if before:
        sums, asked = sums + before[0][0:docs, :], asked + before[0][docs:, :]
    out_ref[0:docs, :] = sums
    out_ref[docs:, :] = asked


def grads_of(xs, gaps, wholes, before, rows_a, rows_b, docs, queries, dp):
    tokens = LANES * (len(xs) + sum(wholes))
    wide = rows_a * rows_b
    operands = (*xs, *before)
    return pl.pallas_call(
        functools.partial(grads_kernel, rows_a, rows_b, docs, dp, gaps, wholes),
        out_shape=jax.ShapeDtypeStruct((docs + queries, wide), jnp.float32),
        in_specs=[VMEM] * len(operands),
        out_specs=VMEM,
        scratch_shapes=[
            pltpu.VMEM((2 * wide, tokens), jnp.bfloat16),
            pltpu.VMEM((docs, tokens), jnp.bfloat16),
        ],
        compiler_params=vmem_params(40),
        cost_estimate=pl.CostEstimate(
            flops=4 * docs * wide * tokens, bytes_accessed=4 * (rows_a + rows_b) * tokens, transcendentals=0
        ),
        name="grads",
    )(*operands)


def gram_kernel(docs, part_ref, recv_ref, out_ref):
    both = part_ref[...] + recv_ref[...]
    rows = both.shape[0]
    split = []
    for _ in range(3):
        split.append(both.astype(jnp.bfloat16))
        both = both - split[-1].astype(jnp.float32)
    every = lax.dot_general(
        jnp.concatenate(split, axis=0),
        jnp.concatenate([x[:docs] for x in split], axis=0),
        NT,
        preferred_element_type=jnp.float32,
    )
    share = None
    for i, j in ((2, 0), (1, 1), (0, 2), (1, 0), (0, 1), (0, 0)):
        term = every[i * rows:(i + 1) * rows, j * docs:(j + 1) * docs]
        share = term if share is None else share + term
    half = share.shape[0] // 2
    out_ref[...] = jnp.concatenate([share[:half], share[half:]], axis=1)


def gram(part, recv, docs):
    return pl.pallas_call(
        functools.partial(gram_kernel, docs),
        out_shape=jax.ShapeDtypeStruct((part.shape[0] // 2, 2 * docs), jnp.float32),
        in_specs=[VMEM] * 2,
        out_specs=VMEM,
        compiler_params=vmem_params(16),
        name="gram",
    )(part, recv)


def solve_kernel(docs, queries, scale, x_ref, recv_ref, out_ref, done_ref):
    total = x_ref[...] + recv_ref[...]
    stack = jnp.concatenate([total[:, :docs], total[:, docs:]], axis=0)
    cols = done_ref.shape[1]
    diagonal = [lax.broadcasted_iota(jnp.int32, (docs, docs), i) for i in range(2)]
    mean_diag = jnp.sum(jnp.where(diagonal[0] == diagonal[1], stack[:docs], 0.0)) * (1.0 / docs)
    stack = jnp.concatenate([stack, jnp.zeros((cols - stack.shape[0], docs), jnp.float32)], axis=0)
    total = stack.T
    row = lax.broadcasted_iota(jnp.int32, (docs, cols), 0)
    col = lax.broadcasted_iota(jnp.int32, (docs, cols), 1)
    work = total + jnp.where(row == col, 0.1 * mean_diag, 0.0)
    size = 8
    here = lax.broadcasted_iota(jnp.int32, (size, cols), 0)
    rows = [work[i:i + size] for i in range(0, docs, size)]
    for r in range(len(rows)):
        wide = [[jnp.broadcast_to(x[:, c:c + 1], (size, cols)) for c in range(r * size, (r + 1) * size)] for x in rows]
        pivot, line = wide[r], rows[r]
        scale_rows = jnp.ones((size, cols), jnp.float32)
        for j in range(size):
            inverse = 1.0 / pivot[j][j:j + 1]
            factor = jnp.where(here == j, 0.0, pivot[j]) * inverse
            pivot = [x if i <= j else x - factor * x[j:j + 1] for i, x in enumerate(pivot)]
            line = line - factor * line[j:j + 1]
            scale_rows = jnp.where(here == j, inverse, scale_rows)
        line = line * scale_rows
        for s in range(len(rows)):
            if s == r:
                rows[s] = line
            else:
                terms = [wide[s][j] * line[j:j + 1] for j in range(size)]
                rows[s] = rows[s] - (((terms[0] + terms[1]) + (terms[2] + terms[3]))
                                     + ((terms[4] + terms[5]) + (terms[6] + terms[7])))
    for r, x in enumerate(rows):
        done_ref[r * size:(r + 1) * size, :] = x * (mean_diag * scale)
    mine = pl.ds(pl.multiple_of(lax.axis_index("dp") * DOC_DEV, DOC_DEV), DOC_DEV)
    out_ref[...] = done_ref[mine, :][:, docs:docs + queries]


def solve(x, recv, docs, queries, scale):
    return pl.pallas_call(
        functools.partial(solve_kernel, docs, queries, scale),
        out_shape=jax.ShapeDtypeStruct((DOC_DEV, queries), jnp.float32),
        in_specs=[VMEM] * 2,
        out_specs=VMEM,
        scratch_shapes=[pltpu.VMEM((docs, -(-(docs + queries) // LANES) * LANES), jnp.float32)],
        compiler_params=vmem_params(16),
        name="solve",
    )(x, recv)


def solve_large(total, docs, queries, scale):
    kernel = total[:, :docs]
    mean_diag = jnp.trace(kernel) / docs
    factor = jnp.linalg.cholesky(kernel + 0.1 * mean_diag * jnp.eye(docs, dtype=jnp.float32))
    solved = jax.scipy.linalg.cho_solve((factor, True), total[:, docs:docs + queries]) * (mean_diag * scale)
    return lax.dynamic_slice_in_dim(solved, lax.axis_index("dp") * DOC_DEV, DOC_DEV, 0)


def swap_cores(x):
    cores = lax.axis_size("tensor")
    return lax.ppermute(x, "tensor", [(i, cores - 1 - i) for i in range(cores)])


def trade(xs, group):
    dp = lax.axis_size("dp")
    got = []
    for x, ms in zip(xs, zip(*partners(group))):
        pairs = [(i * 2 + k, (i ^ m) * 2 + k) for i in range(dp) for k, m in enumerate(ms)]
        got.append(lax.ppermute(x, ("dp", "tensor"), pairs))
    return got


def trade_shared(x):
    dp = lax.axis_size("dp")
    return lax.ppermute(x, "dp", [(i, i ^ SHARED) for i in range(dp)])


def local(hidden, out_grad, proj_in, proj_out, doc_ids, queries):
    dp = lax.axis_size("dp")
    docs, num_queries = DOC_DEV * dp, queries.shape[0] * dp
    ranks = proj_in.shape[1]
    owners = owners_of(dp)
    pa = 1
    while pa * pa < owners:
        pa *= 2
    pb = owners // pa
    rows_a, rows_b = ranks // pa, ranks // pb

    part = project(hidden, out_grad, proj_in.T, proj_out.T)
    recv = swap_cores(part)

    ids = jnp.broadcast_to(doc_ids.astype(jnp.float32).reshape(2, LANES), (owners, 2, LANES))
    asked = queries.reshape(-1, pa, rows_a, pb, rows_b).transpose(1, 3, 0, 2, 4).reshape(owners, -1, LANES)
    extra = jnp.concatenate([asked, ids], axis=1)
    extra = jnp.pad(extra, ((0, 0), (0, -extra.shape[1] % 8), (0, 0)))

    *blocks, shared, own = pack(part, recv, extra, dp, pa, pb)
    blocks = trade(blocks, dp) + [trade_shared(shared), own]
    gaps = [*zip(*partners(dp)), (SHARED, SHARED), (0, 0)]
    wholes = [True] * (len(blocks) - 2) + [False, False]
    sizes = (rows_a, rows_b, docs, num_queries, dp)
    late = min(1, len(blocks) - 3)
    rest = [t for t in range(len(blocks)) if t != late]
    grads = ()
    for part in (rest, [late]):
        grads = (grads_of(*([x[t] for t in part] for x in (blocks, gaps, wholes)), grads, *sizes),)
    grads = grads[0]
    share = gram(grads, swap_cores(grads), docs)
    scale = float(ranks * ranks) ** -0.5
    if docs <= 64:
        others = sum(trade([share] * (owners // 2 - 1), owners))
        share = others + jnp.where(lax.axis_index("tensor") == 0, share, trade_shared(share))
        return solve(share, swap_cores(share), docs, num_queries, scale).T
    share = lax.psum(share, "dp") * (owners / dp)
    return solve_large(jnp.concatenate([share[:, :docs], share[:, docs:]], axis=0).T, docs, num_queries, scale).T


def solution(mesh):
    return jax.shard_map(
        local,
        mesh=mesh,
        in_specs=(
            P(("groups", "dp"), "tensor"),
            P(("groups", "dp"), "tensor"),
            P("tensor", None),
            P("tensor", None),
            P(("groups", "dp")),
            P(("groups", "dp"), None),
        ),
        out_specs=P("groups", "dp"),
        check_vma=False,
    )
```

```python
import functools

import jax
import jax.numpy as jnp
from jax import lax
from jax.experimental import pallas as pl
from jax.experimental.pallas import tpu as pltpu
from jax.sharding import PartitionSpec as P

TOK_DEV = 256
DOC_DEV = 8
LANES = 128
FLIGHT = 7
SHARED = 1
NT = (((1,), (1,)), ((), ()))
VMEM = pl.BlockSpec(memory_space=pltpu.VMEM)
HBM = pl.BlockSpec(memory_space=pltpu.HBM)


def vmem_params(mib):
    return pltpu.CompilerParams(vmem_limit_bytes=int(mib * (1 << 20)))


def pieces(x):
    rows, units = x.shape
    split = x.reshape(rows // 8, 8, units // (2 * LANES), 2, LANES).transpose(0, 2, 3, 1, 4)
    return split.reshape(rows // 8, units // (2 * LANES), 16, LANES)


def chunks_of(length, ramp, tail):
    left = length - sum(ramp) - sum(tail)
    sizes = [*ramp, *([6] * (left // 6)), *([left % 6] if left % 6 else []), *tail]
    return [(sum(sizes[:i]), size) for i, size in enumerate(sizes)]


def project_kernel(g_chunks, h_chunks, h_ref, g_ref, pin_ref, pout_ref, out_ref, h_buf, g_buf, pin_buf, pout_buf, sems):
    plan = [(pout_ref, pout_buf, g_ref, g_buf, at) for at in g_chunks] + [(pin_ref, pin_buf, h_ref, h_buf, at) for at in h_chunks]
    copies = []
    for i, (proj, proj_buf, data, data_buf, (start, size)) in enumerate(plan):
        at = pl.ds(start, size)
        copies.append((
            pltpu.make_async_copy(proj.at[:, at], proj_buf.at[:, at], sems.at[2 * i]),
            pltpu.make_async_copy(data.at[:, at], data_buf.at[:, at], sems.at[2 * i + 1]),
        ))

    def start(i):
        if i < len(copies):
            for copy in copies[i]:
                copy.start()

    for i in range(FLIGHT):
        start(i)

    def line_up(ref, first, size):
        blocks = [ref[:, j].reshape(ref.shape[0] * 16, LANES) for j in range(first, first + size)]
        return jnp.concatenate(blocks, axis=1)

    totals = [None, None]
    for i, (_, proj_buf, _, data_buf, (first, size)) in enumerate(plan):
        for copy in copies[i]:
            copy.wait()
        start(i + FLIGHT)
        which = 0 if i < len(g_chunks) else 1
        part = lax.dot_general(
            line_up(proj_buf, first, size), line_up(data_buf, first, size), NT, preferred_element_type=jnp.float32
        )
        totals[which] = part if totals[which] is None else totals[which] + part

    lane = lax.broadcasted_iota(jnp.int32, (8, LANES), 1)
    even = lane % 16 < 8
    later = lane // (LANES // 2)
    order = lane % (LANES // 2) // 8 * 16 + lane % 8 + 8 * later
    done = 0
    for total in totals:
        for g in range(0, total.shape[0], 16):
            lines = []
            for i in range(0, total.shape[1], LANES):
                upper, lower = total[g:g + 8, i:i + LANES], total[g + 8:g + 16, i:i + LANES]
                lines.append(jnp.where(even, upper, lower))
            for i in range(0, len(lines), 2):
                first = lines[i] + pltpu.roll(lines[i], LANES - 8, 1)
                second = lines[i + 1] + pltpu.roll(lines[i + 1], 8, 1)
                both = jnp.where(even, first, second)
                at = i // 2 * LANES
                out_ref[done:done + 8, at:at + LANES] = jnp.take_along_axis(both, order, axis=1)
            done += 8


def project(hidden, out_grad, pin_t, pout_t):
    tokens, units = hidden.shape
    width = out_grad.shape[1]
    ranks = pin_t.shape[0] + pout_t.shape[0]
    operands = [pieces(x) for x in (hidden, out_grad, pin_t, pout_t)]
    g_chunks = chunks_of(operands[1].shape[1], (1, 2, 3, 4), ())
    h_chunks = chunks_of(operands[0].shape[1], (), (4, 2, 2))
    return pl.pallas_call(
        functools.partial(project_kernel, g_chunks, h_chunks),
        out_shape=jax.ShapeDtypeStruct((ranks, tokens), jnp.float32),
        in_specs=[HBM] * 4,
        out_specs=VMEM,
        scratch_shapes=[pltpu.VMEM(x.shape, x.dtype) for x in operands]
        + [pltpu.SemaphoreType.DMA((2 * len(g_chunks + h_chunks),))],
        compiler_params=vmem_params(53.5),
        cost_estimate=pl.CostEstimate(
            flops=2 * tokens * 64 * (units + width),
            bytes_accessed=2 * (tokens + 64) * (units + width),
            transcendentals=0,
        ),
        name="project",
    )(*operands)


def owners_of(dp):
    return max(dp // 2, 1)


def partners(dp):
    order = [m for far in (True, False) for m in range(1, dp) if m != SHARED and (2 * m >= dp) == far]
    return order[0::2], order[1::2]


def partner(dp, t):
    first, second = partners(dp)
    return jnp.where(lax.axis_index("tensor") == 0, first[t], second[t])


def pack_kernel(dp, pb, rows_a, rows_b, span, part_ref, recv_ref, extra_ref, *refs):
    outs, total_ref = refs[:-1], refs[-1]
    total_ref[...] = part_ref[...] + recv_ref[...]
    ranks = total_ref.shape[0] // 2
    rows = rows_a + rows_b
    owners, ids = extra_ref.shape[0], 2 * span
    me = lax.axis_index("dp")
    lead = lax.axis_index("tensor") == 0

    def slices(owner):
        p, q = owner // pb, owner % pb
        g = total_ref[pl.ds(pl.multiple_of(p * rows_a, rows_a), rows_a), :]
        b = total_ref[pl.ds(pl.multiple_of(ranks + q * rows_b, rows_b), rows_b), :]
        return [(g[:, i:i + LANES], b[:, i:i + LANES]) for i in (0, LANES)]

    for t, out_ref in enumerate(outs[:-2]):
        owner = (me ^ partner(dp, t)) % owners
        for i, (g, b) in enumerate(slices(owner)):
            out_ref[i * rows:i * rows + rows_a, :] = g
            out_ref[i * rows + rows_a:(i + 1) * rows, :] = b
        out_ref[2 * rows:, :] = extra_ref[owner]
    for out_ref, to in zip(outs[-2:], (me ^ SHARED, me)):
        owner = to % owners
        (g, b), (later_g, later_b) = slices(owner)
        extra = extra_ref[owner]
        out_ref[0:rows_a, :] = jnp.where(lead, g, later_g)
        out_ref[rows_a:rows, :] = jnp.where(lead, b, later_b)
        out_ref[rows:rows + span, :] = jnp.where(lead, extra[0:span], extra[span:ids])
        rest = out_ref.shape[0] - rows - span
        out_ref[rows + span:, :] = jnp.broadcast_to(jnp.where(lead, extra[ids:ids + 1], extra[ids + 1:ids + 2]), (rest, LANES))


def pack(part, recv, extra, dp, pa, pb):
    ranks = part.shape[0] // 2
    rows_a, rows_b = ranks // pa, ranks // pb
    rows, span = rows_a + rows_b, rows_a * rows_b // LANES
    whole = jax.ShapeDtypeStruct((2 * rows + extra.shape[1], LANES), jnp.float32)
    half = jax.ShapeDtypeStruct((rows + 8 * (span // 8 + 1), LANES), jnp.float32)
    count = dp // 2 - 1
    return pl.pallas_call(
        functools.partial(pack_kernel, dp, pb, rows_a, rows_b, span),
        out_shape=(whole,) * count + (half, half),
        in_specs=[VMEM] * 3,
        out_specs=(VMEM,) * (count + 2),
        scratch_shapes=[pltpu.VMEM(part.shape, jnp.float32)],
        compiler_params=vmem_params(16),
        name="pack",
    )(part, recv, extra)


def grads_kernel(rows_a, rows_b, docs, dp, gaps, wholes, *refs):
    xs, before, (out_ref, outer_ref, member_ref) = refs[:len(gaps)], refs[len(gaps):-3], refs[-3:]
    rows, wide = rows_a + rows_b, rows_a * rows_b
    span = wide // LANES
    queries = out_ref.shape[0] - docs
    doc = lax.broadcasted_iota(jnp.int32, (docs, LANES), 0)
    place = lax.broadcasted_iota(jnp.int32, (queries, LANES), 0)
    me = lax.axis_index("dp")
    core = lax.axis_index("tensor")
    asked = [jnp.zeros((queries, LANES), jnp.float32)] * span
    start, tokens = 0, outer_ref.shape[1] // 2
    for x_ref, gap, whole in zip(xs, gaps, wholes):
        parts = 2 if whole else 1
        base = parts * rows
        for i in range(parts):
            at = slice(start, start + LANES)
            start += LANES
            g, b = x_ref[i * rows:i * rows + rows_a, :], x_ref[i * rows + rows_a:(i + 1) * rows, :]
            ids = base + parts * span + i
            member = jnp.where(doc == x_ref[ids:ids + 1, :].astype(jnp.int32), 1.0, 0.0).astype(jnp.bfloat16)
            later = slice(at.start + tokens, at.stop + tokens)
            member_ref[:, at] = member
            member_ref[:, later] = member
            outer = (g[:, None, :] * b[None, :, :]).reshape(wide, LANES)
            high = outer.astype(jnp.bfloat16)
            outer_ref[:, at] = high
            outer_ref[:, later] = (outer - high.astype(jnp.float32)).astype(jnp.bfloat16)
        source = 2 * (me ^ jnp.where(core == 0, gap[0], gap[1]))
        for i in range(parts):
            held = place == source + (i if whole else core)
            for j in range(span):
                row = base + i * span + j
                asked[j] = jnp.where(held, x_ref[row:row + 1, :], asked[j])
    sums = lax.dot_general(member_ref[...], outer_ref[...], NT, preferred_element_type=jnp.float32)
    sums = sums * (TOK_DEV ** -0.5)
    asked = jnp.concatenate(asked, axis=1)
    if before:
        sums, asked = sums + before[0][0:docs, :], asked + before[0][docs:, :]
    out_ref[0:docs, :] = sums
    out_ref[docs:, :] = asked


def grads_of(xs, gaps, wholes, before, rows_a, rows_b, docs, queries, dp):
    tokens = LANES * (len(xs) + sum(wholes))
    wide = rows_a * rows_b
    operands = (*xs, *before)
    return pl.pallas_call(
        functools.partial(grads_kernel, rows_a, rows_b, docs, dp, gaps, wholes),
        out_shape=jax.ShapeDtypeStruct((docs + queries, wide), jnp.float32),
        in_specs=[VMEM] * len(operands),
        out_specs=VMEM,
        scratch_shapes=[
            pltpu.VMEM((wide, 2 * tokens), jnp.bfloat16),
            pltpu.VMEM((docs, 2 * tokens), jnp.bfloat16),
        ],
        compiler_params=vmem_params(40),
        cost_estimate=pl.CostEstimate(
            flops=4 * docs * wide * tokens, bytes_accessed=4 * (rows_a + rows_b) * tokens, transcendentals=0
        ),
        name="grads",
    )(*operands)


def gram_kernel(docs, part_ref, recv_ref, out_ref):
    both = part_ref[...] + recv_ref[...]
    rows = both.shape[0]
    split = []
    for _ in range(3):
        split.append(both.astype(jnp.bfloat16))
        both = both - split[-1].astype(jnp.float32)
    every = lax.dot_general(
        jnp.concatenate(split, axis=0),
        jnp.concatenate([x[:docs] for x in split], axis=0),
        NT,
        preferred_element_type=jnp.float32,
    )
    share = None
    for i, j in ((2, 0), (1, 1), (0, 2), (1, 0), (0, 1), (0, 0)):
        term = every[i * rows:(i + 1) * rows, j * docs:(j + 1) * docs]
        share = term if share is None else share + term
    half = share.shape[0] // 2
    out_ref[...] = jnp.concatenate([share[:half], share[half:]], axis=1)


def gram(part, recv, docs):
    return pl.pallas_call(
        functools.partial(gram_kernel, docs),
        out_shape=jax.ShapeDtypeStruct((part.shape[0] // 2, 2 * docs), jnp.float32),
        in_specs=[VMEM] * 2,
        out_specs=VMEM,
        compiler_params=vmem_params(16),
        name="gram",
    )(part, recv)


def solve_kernel(docs, queries, scale, x_ref, recv_ref, out_ref, done_ref):
    total = x_ref[...] + recv_ref[...]
    stack = jnp.concatenate([total[:, :docs], total[:, docs:]], axis=0)
    cols = done_ref.shape[1]
    diagonal = [lax.broadcasted_iota(jnp.int32, (docs, docs), i) for i in range(2)]
    mean_diag = jnp.sum(jnp.where(diagonal[0] == diagonal[1], stack[:docs], 0.0)) * (1.0 / docs)
    stack = jnp.concatenate([stack, jnp.zeros((cols - stack.shape[0], docs), jnp.float32)], axis=0)
    total = stack.T
    row = lax.broadcasted_iota(jnp.int32, (docs, cols), 0)
    col = lax.broadcasted_iota(jnp.int32, (docs, cols), 1)
    work = total + jnp.where(row == col, 0.1 * mean_diag, 0.0)
    size = 8
    here = lax.broadcasted_iota(jnp.int32, (size, cols), 0)
    rows = [work[i:i + size] for i in range(0, docs, size)]
    for r in range(len(rows)):
        wide = [[jnp.broadcast_to(x[:, c:c + 1], (size, cols)) for c in range(r * size, (r + 1) * size)] for x in rows]
        pivot, line = wide[r], rows[r]
        scale_rows = jnp.ones((size, cols), jnp.float32)
        for j in range(size):
            inverse = 1.0 / pivot[j][j:j + 1]
            factor = jnp.where(here == j, 0.0, pivot[j]) * inverse
            pivot = [x if i <= j else x - factor * x[j:j + 1] for i, x in enumerate(pivot)]
            line = line - factor * line[j:j + 1]
            scale_rows = jnp.where(here == j, inverse, scale_rows)
        line = line * scale_rows
        for s in range(len(rows)):
            if s == r:
                rows[s] = line
            else:
                terms = [wide[s][j] * line[j:j + 1] for j in range(size)]
                rows[s] = rows[s] - (((terms[0] + terms[1]) + (terms[2] + terms[3]))
                                     + ((terms[4] + terms[5]) + (terms[6] + terms[7])))
    for r, x in enumerate(rows):
        done_ref[r * size:(r + 1) * size, :] = x * (mean_diag * scale)
    mine = pl.ds(pl.multiple_of(lax.axis_index("dp") * DOC_DEV, DOC_DEV), DOC_DEV)
    out_ref[...] = done_ref[mine, :][:, docs:docs + queries]


def solve(x, recv, docs, queries, scale):
    return pl.pallas_call(
        functools.partial(solve_kernel, docs, queries, scale),
        out_shape=jax.ShapeDtypeStruct((DOC_DEV, queries), jnp.float32),
        in_specs=[VMEM] * 2,
        out_specs=VMEM,
        scratch_shapes=[pltpu.VMEM((docs, -(-(docs + queries) // LANES) * LANES), jnp.float32)],
        compiler_params=vmem_params(16),
        name="solve",
    )(x, recv)


def solve_large(total, docs, queries, scale):
    kernel = total[:, :docs]
    mean_diag = jnp.trace(kernel) / docs
    factor = jnp.linalg.cholesky(kernel + 0.1 * mean_diag * jnp.eye(docs, dtype=jnp.float32))
    solved = jax.scipy.linalg.cho_solve((factor, True), total[:, docs:docs + queries]) * (mean_diag * scale)
    return lax.dynamic_slice_in_dim(solved, lax.axis_index("dp") * DOC_DEV, DOC_DEV, 0)


def swap_cores(x):
    cores = lax.axis_size("tensor")
    return lax.ppermute(x, "tensor", [(i, cores - 1 - i) for i in range(cores)])


def trade(xs, group):
    dp = lax.axis_size("dp")
    got = []
    for x, ms in zip(xs, zip(*partners(group))):
        pairs = [(i * 2 + k, (i ^ m) * 2 + k) for i in range(dp) for k, m in enumerate(ms)]
        got.append(lax.ppermute(x, ("dp", "tensor"), pairs))
    return got


def trade_shared(x):
    dp = lax.axis_size("dp")
    return lax.ppermute(x, "dp", [(i, i ^ SHARED) for i in range(dp)])


def local(hidden, out_grad, proj_in, proj_out, doc_ids, queries):
    dp = lax.axis_size("dp")
    docs, num_queries = DOC_DEV * dp, queries.shape[0] * dp
    ranks = proj_in.shape[1]
    owners = owners_of(dp)
    pa = 1
    while pa * pa < owners:
        pa *= 2
    pb = owners // pa
    rows_a, rows_b = ranks // pa, ranks // pb

    part = project(hidden, out_grad, proj_in.T, proj_out.T)
    recv = swap_cores(part)

    ids = jnp.broadcast_to(doc_ids.astype(jnp.float32).reshape(2, LANES), (owners, 2, LANES))
    asked = queries.reshape(-1, pa, rows_a, pb, rows_b).transpose(1, 3, 0, 2, 4).reshape(owners, -1, LANES)
    extra = jnp.concatenate([asked, ids], axis=1)
    extra = jnp.pad(extra, ((0, 0), (0, -extra.shape[1] % 8), (0, 0)))

    *blocks, shared, own = pack(part, recv, extra, dp, pa, pb)
    blocks = trade(blocks, dp) + [trade_shared(shared), own]
    gaps = [*zip(*partners(dp)), (SHARED, SHARED), (0, 0)]
    wholes = [True] * (len(blocks) - 2) + [False, False]
    sizes = (rows_a, rows_b, docs, num_queries, dp)
    late = min(1, len(blocks) - 3)
    rest = [t for t in range(len(blocks)) if t != late]
    grads = ()
    for part in (rest, [late]):
        grads = (grads_of(*([x[t] for t in part] for x in (blocks, gaps, wholes)), grads, *sizes),)
    grads = grads[0]
    share = gram(grads, swap_cores(grads), docs)
    scale = float(ranks * ranks) ** -0.5
    if docs <= 64:
        others = sum(trade([share] * (owners // 2 - 1), owners))
        share = others + jnp.where(lax.axis_index("tensor") == 0, share, trade_shared(share))
        return solve(share, swap_cores(share), docs, num_queries, scale).T
    share = lax.psum(share, "dp") * (owners / dp)
    return solve_large(jnp.concatenate([share[:, :docs], share[:, docs:]], axis=0).T, docs, num_queries, scale).T


def solution(mesh):
    return jax.shard_map(
        local,
        mesh=mesh,
        in_specs=(
            P(("groups", "dp"), "tensor"),
            P(("groups", "dp"), "tensor"),
            P("tensor", None),
            P("tensor", None),
            P(("groups", "dp")),
            P(("groups", "dp"), None),
        ),
        out_specs=P("groups", "dp"),
        check_vma=False,
    )
```
